32 devices in a mesh: dp: 8 (over z, x), tensor: 4 (over y, core).
Axes of the slice: x: 2, y: 2, z: 4, core: 2. Of those that a mesh axis runs over, the one named last changes fastest.
Arguments:
- tokens: bfloat16 [8192, 2048], P('dp'), may hold values from -6 to 6
- mixer_gain: bfloat16 [2048], P('dp'), may hold values from 0.5 to 1.5
- query_weight: bfloat16 [2048, 2048], P('dp', 'tensor'), may hold values from -0.125 to 0.125
- key_weight: bfloat16 [2048, 2048], P('dp', 'tensor'), may hold values from -0.125 to 0.125
- value_weight: bfloat16 [2048, 4096], P('dp', 'tensor'), may hold values from -0.125 to 0.125
- gate_weight: bfloat16 [2048, 4096], P('dp', 'tensor'), may hold values from -0.125 to 0.125
- out_weight: bfloat16 [4096, 2048], P('tensor', 'dp'), may hold values from -0.1875 to 0.1875
- group_gain: bfloat16 [8, 512], P('tensor', 'dp'), may hold values from 0.5 to 1.5
- feed_gain: bfloat16 [2048], P('dp'), may hold values from 0.5 to 1.5
- hidden_weight: bfloat16 [2048, 4096], P('dp', 'tensor'), may hold values from -0.125 to 0.125
- up_weight: bfloat16 [2048, 4096], P('dp', 'tensor'), may hold values from -0.125 to 0.125
- down_weight: bfloat16 [4096, 2048], P('tensor', 'dp'), may hold values from -0.125 to 0.125
- cotangent: bfloat16 [8192, 2048], P('dp'), may hold values from -6 to 6
Outputs:
- output: bfloat16 [8192, 2048], P('dp')
- tokens_grad: float32 [8192, 2048], P('dp')
- mixer_gain_grad: float32 [2048], P('dp')
- query_weight_grad: float32 [2048, 2048], P('dp', 'tensor')
- key_weight_grad: float32 [2048, 2048], P('dp', 'tensor')
- value_weight_grad: float32 [2048, 4096], P('dp', 'tensor')
- gate_weight_grad: float32 [2048, 4096], P('dp', 'tensor')
- out_weight_grad: float32 [4096, 2048], P('tensor', 'dp')
- group_gain_grad: float32 [8, 512], P('tensor', 'dp')
- feed_gain_grad: float32 [2048], P('dp')
- hidden_weight_grad: float32 [2048, 4096], P('dp', 'tensor')
- up_weight_grad: float32 [2048, 4096], P('dp', 'tensor')
- down_weight_grad: float32 [4096, 2048], P('tensor', 'dp')
The draws below stay inside these ranges and needn't reach their ends.
All inputs are finite; a program needn't handle non-finite values.
Results may differ from the reference program's by a relative error of at most 0.017.
Values may be sent and summed in bfloat16 or wider, within the bound.
A program may use at most 256 MiB of HBM per device.

```python
from functools import partial
import jax
import jax.numpy as jnp
from jax import lax

D = 2048
H = 8
DK = 256
DV = 512
FF = 4096
LEN = 1024
TOK_DEV = 1024
TOKENS = 8192
N_DP = 8


def unit_field(key, shape, limit):
    return jnp.clip(jax.random.normal(key, shape, jnp.float32), -limit, limit)


def draw_tokens(key, part):
    key = jax.random.fold_in(key, 11)
    return unit_field(key, (TOKENS, D), 6.0).astype(jnp.bfloat16)


def draw_cotangent(key, part):
    key = jax.random.fold_in(key, 23)
    field_key, pair_key = jax.random.split(key)
    base = unit_field(field_key, (TOKENS, D), 2.0)
    pairing = jax.random.permutation(pair_key, N_DP)
    row_block = jnp.arange(TOKENS) // TOK_DEV
    col_block = jnp.arange(D) // (D // N_DP)
    hit = pairing[row_block][:, None] == col_block[None, :]
    return (base * jnp.where(hit, 3.0, 1.0)).astype(jnp.bfloat16)


def shard_levels(key, dims, shards, low, top_value):
    def one(axis_at, parts):
        steps = jax.random.uniform(jax.random.fold_in(jax.random.fold_in(key, 6), axis_at), (parts,), jnp.float32, low / len(shards), top_value / len(shards))
        return jnp.repeat(jnp.exp(steps), dims[axis_at] // parts).reshape((-1,) + (1,) * (len(dims) - axis_at - 1))

    loudness = one(*shards[0])
    for cut in shards[1:]:
        loudness = loudness * one(*cut)
    return loudness


def centred(rng, extent, scale, reach, cuts=(), kind=jnp.bfloat16):
    gain = shard_levels(rng, extent, cuts, -0.22, 0.18) if cuts else 1.0
    values = jax.random.normal(rng, extent, jnp.float32) * scale * gain
    return jnp.minimum(jnp.maximum(values, -reach), reach).astype(kind)


def setup_inputs(seed: int = 0) -> dict:
    seeds = jax.random.split(jax.random.key(seed), 14)
    return {
        "tokens": draw_tokens(jax.random.fold_in(seeds[13], 71), 0),
        "mixer_gain": jnp.clip(1.0 + 0.1 * jax.random.normal(seeds[1], (D,), jnp.float32), 0.5, 1.5).astype(jnp.bfloat16),
        "query_weight": centred(seeds[2], (D, H * DK), D ** -0.5, 0.125, ((0, 8), (1, 4))),
        "key_weight": centred(seeds[3], (D, H * DK), D ** -0.5, 0.125, ((0, 8), (1, 4))),
        "value_weight": centred(seeds[4], (D, H * DV), D ** -0.5, 0.125, ((0, 8), (1, 4))),
        "gate_weight": centred(seeds[5], (D, H * DV), D ** -0.5, 0.125, ((0, 8), (1, 4))),
        "out_weight": centred(seeds[6], (H * DV, D), (H * DV // 4) ** -0.5, 0.1875, ((0, 4), (1, 8))),
        "group_gain": jnp.clip(1.0 + 0.1 * jax.random.normal(seeds[7], (H, DV), jnp.float32), 0.5, 1.5).astype(jnp.bfloat16),
        "feed_gain": jnp.clip(1.0 + 0.1 * jax.random.normal(seeds[8], (D,), jnp.float32), 0.5, 1.5).astype(jnp.bfloat16),
        "hidden_weight": centred(seeds[9], (D, FF), D ** -0.5, 0.125, ((0, 8), (1, 4))),
        "up_weight": centred(seeds[10], (D, FF), D ** -0.5, 0.125, ((0, 8), (1, 4))),
        "down_weight": centred(seeds[11], (FF, D), (FF // 2) ** -0.5, 0.125, ((0, 4), (1, 8))),
        "cotangent": draw_cotangent(jax.random.fold_in(seeds[13], 71), 0),
    }


norm_epsilon = 1e-05
group_epsilon = 0.01

@jax.custom_vjp
def low(v):
    return lax.optimization_barrier(v.astype(jnp.bfloat16)).astype(jnp.float32)

@jax.custom_vjp
def low_back(v):
    return v

def low_keep(v):
    return (low(v), None)

def low_pass(kept, grad):
    return (grad,)

def back_keep(v):
    return (v, None)

def back_low(kept, grad):
    return (low(grad),)
low.defvjp(low_keep, low_pass)
low_back.defvjp(back_keep, back_low)

def exact_dot(left, right):
    return jnp.dot(left, right, precision=lax.Precision.HIGHEST, preferred_element_type=jnp.float32)

def layer_norm(values, scale_gain, epsilon=norm_epsilon):
    center = values - lax.optimization_barrier(jnp.mean(values, axis=-1, keepdims=True))
    spread = lax.optimization_barrier(jnp.mean(center * center, axis=-1, keepdims=True))
    return center * lax.rsqrt(spread + epsilon) * scale_gain

def group_norm(retained, scale_gain):
    shaped = retained.reshape(retained.shape[0], scale_gain.shape[0], scale_gain.shape[1])
    return layer_norm(shaped, scale_gain, group_epsilon).reshape(retained.shape)

def rotate(values, head_count, direction):
    length = values.shape[0]
    head_width = values.shape[1] // head_count
    half_width = head_width // 2
    places = jnp.arange(length, dtype=jnp.float32)[:, None]
    speeds = 10000.0 ** (-jnp.arange(half_width, dtype=jnp.float32) / half_width)
    angles = places * speeds[None, :]
    cosine = jnp.cos(angles)[:, None, :]
    sine_part = direction * jnp.sin(angles)[:, None, :]
    shaped = values.reshape(length, head_count, 2, half_width)
    front_half = shaped[:, :, 0]
    back_half = shaped[:, :, 1]
    turned = jnp.stack([front_half * cosine - back_half * sine_part, front_half * sine_part + back_half * cosine], axis=2)
    return turned.reshape(length, head_count * head_width)

def decay_table(head_ids, length):
    log_rates = jnp.log1p(-jnp.exp2(-5.0 - head_ids))
    row_place = jnp.arange(length)[:, None]
    key_place = jnp.arange(length)[None, :]
    distance = jnp.maximum(row_place - key_place, 0).astype(jnp.float32)
    decays = jnp.where((row_place >= key_place)[None], jnp.exp(log_rates[:, None, None] * distance[None]), 0.0)
    return decays * lax.rsqrt(lax.optimization_barrier(jnp.sum(decays, axis=-1, keepdims=True)))

def mixer_core(decays, pieces):
    query_seq, key_seq, value_seq = pieces
    length = query_seq.shape[0]
    turned_query = low(rotate(query_seq, H, 1.0)).reshape(length, H, DK)
    turned_keys = low(rotate(key_seq, H, 1.0)).reshape(length, H, DK)
    value_heads = value_seq.reshape(length, H, DV)
    raw_scores = low_back(jnp.einsum('qhd,khd->hqk', turned_query, turned_keys, precision=lax.Precision.HIGHEST))
    scores = raw_scores * DK ** (-0.5) * decays
    row_totals = lax.optimization_barrier(jnp.sum(scores, axis=-1, keepdims=True))
    denominators = jnp.sqrt(row_totals * row_totals + 1.0)
    weights = low(scores / denominators)
    retained = jnp.einsum('hqk,khd->qhd', weights, value_heads, precision=lax.Precision.HIGHEST)
    return low_back(retained.reshape(length, H * DV))

def forward(inputs, mixer_gain, query_weight, key_weight, value_weight, gate_weight, out_weight, group_gain, feed_gain, hidden_weight, up_weight, down_weight):
    decays = decay_table(jnp.arange(H, dtype=jnp.float32), LEN)
    mixer_input = low(layer_norm(inputs, mixer_gain))
    query = low_back(exact_dot(mixer_input, query_weight))
    keyset = low_back(exact_dot(mixer_input, key_weight))
    values = low(low_back(exact_dot(mixer_input, value_weight)))
    gate_in = low_back(exact_dot(mixer_input, gate_weight))
    sequences = TOKENS // LEN
    core_step = jax.checkpoint(partial(mixer_core, decays))
    retained = lax.map(core_step, (query.reshape(sequences, LEN, H * DK), keyset.reshape(sequences, LEN, H * DK), values.reshape(sequences, LEN, H * DV)))
    retained = retained.reshape(TOKENS, H * DV)
    normed = group_norm(retained, group_gain)
    mixed = low(jax.nn.silu(gate_in) * normed)
    branch = low_back(exact_dot(mixed, out_weight))
    residual = inputs + branch
    feed_input = low(layer_norm(residual, feed_gain))
    hidden_pre = low_back(exact_dot(feed_input, hidden_weight))
    up_pre = low_back(exact_dot(feed_input, up_weight))
    activity = low(jax.nn.gelu(hidden_pre) * up_pre)
    return residual + low_back(exact_dot(activity, down_weight))

def reference(tokens, mixer_gain, query_weight, key_weight, value_weight, gate_weight, out_weight, group_gain, feed_gain, hidden_weight, up_weight, down_weight, cotangent):
    result, pullback = jax.vjp(forward, tokens.astype(jnp.float32), mixer_gain.astype(jnp.float32), query_weight.astype(jnp.float32), key_weight.astype(jnp.float32), value_weight.astype(jnp.float32), gate_weight.astype(jnp.float32), out_weight.astype(jnp.float32), group_gain.astype(jnp.float32), feed_gain.astype(jnp.float32), hidden_weight.astype(jnp.float32), up_weight.astype(jnp.float32), down_weight.astype(jnp.float32))
    grads = pullback(cotangent.astype(jnp.float32))
    return (result.astype(jnp.bfloat16), grads[0], grads[1], grads[2], grads[3], grads[4], grads[5], grads[6], grads[7], grads[8], grads[9], grads[10], grads[11])
```

```python
import jax
import jax.numpy as jnp
from jax import lax
from jax.sharding import PartitionSpec as P

DK = 256
DV = 512

norm_epsilon = 1e-05
group_epsilon = 0.01
F32 = jnp.float32
BF16 = jnp.bfloat16


def layer_norm(values, scale_gain, epsilon=norm_epsilon):
    center = values - jnp.mean(values, axis=-1, keepdims=True)
    spread = jnp.mean(center * center, axis=-1, keepdims=True)
    return center * lax.rsqrt(spread + epsilon) * scale_gain


def group_norm(retained, scale_gain):
    shaped = retained.reshape(retained.shape[0], scale_gain.shape[0], scale_gain.shape[1])
    return layer_norm(shaped, scale_gain, group_epsilon).reshape(retained.shape)


def rotate(values, head_count, direction):
    length = values.shape[0]
    head_width = values.shape[1] // head_count
    half_width = head_width // 2
    places = jnp.arange(length, dtype=F32)[:, None]
    speeds = 10000.0 ** (-jnp.arange(half_width, dtype=F32) / half_width)
    angles = places * speeds[None, :]
    cosine = jnp.cos(angles)[:, None, :]
    sine_part = direction * jnp.sin(angles)[:, None, :]
    shaped = values.reshape(length, head_count, 2, half_width)
    front_half = shaped[:, :, 0]
    back_half = shaped[:, :, 1]
    turned = jnp.stack(
        [front_half * cosine - back_half * sine_part, front_half * sine_part + back_half * cosine],
        axis=2,
    )
    return turned.reshape(length, head_count * head_width)


def decay_table(head_ids, length):
    log_rates = jnp.log1p(-jnp.exp2(-5.0 - head_ids))
    row_place = jnp.arange(length)[:, None]
    key_place = jnp.arange(length)[None, :]
    distance = jnp.maximum(row_place - key_place, 0).astype(F32)
    decays = jnp.where(
        (row_place >= key_place)[None], jnp.exp(log_rates[:, None, None] * distance[None]), 0.0
    )
    return decays * lax.rsqrt(jnp.sum(decays, axis=-1, keepdims=True))


def plain_product(left, right):
    return jnp.dot(left, right, preferred_element_type=F32)


def row_product(left, right):
    return lax.dot_general(left, right, (((0,), (0,)), ((), ())), preferred_element_type=F32)


def back_product(left, right):
    return lax.dot_general(left, right, (((1,), (1,)), ((), ())), preferred_element_type=F32)


def core_scores(turned_query, turned_keys, decays):
    raw_scores = jnp.einsum("qhd,khd->hqk", turned_query, turned_keys, preferred_element_type=F32)
    scores = raw_scores * DK ** (-0.5) * decays
    row_totals = jnp.sum(scores, axis=-1, keepdims=True)
    denominators = jnp.sqrt(row_totals * row_totals + 1.0)
    return (scores, row_totals, denominators)


def feed_piece(hidden_pre, up_pre):
    return jax.nn.gelu(hidden_pre) * up_pre


def gate_piece(retained, gate_in, group_scale):
    return jax.nn.silu(gate_in) * group_norm(retained, group_scale)


class Ring:
    def __init__(self, name, size):
        self.name = name
        self.size = size
        self.outer = size // 2
        self.me = lax.axis_index(name)
        self.swap_pairs = [(i, i ^ 1) for i in range(size)]

    def swap(self, block):
        return lax.ppermute(block, self.name, self.swap_pairs)

    def shift(self, block, step):
        pairs = [
            (i, ((i // 2 + step) % self.outer) * 2 + i % 2) for i in range(self.size)
        ]
        return lax.ppermute(block, self.name, pairs)

    def block_at(self, place):
        turn, step = place // self.outer, place % self.outer
        outer = (self.me // 2 + self.outer - step) % self.outer
        return outer * 2 + (self.me % 2 + turn) % 2

    def place_of(self, block):
        turn = (block % 2 + self.me % 2) % 2
        step = (self.me // 2 + self.outer - block // 2) % self.outer
        return turn * self.outer + step

    def own_order(self, array, axis):
        width = array.shape[axis] // self.size
        return jnp.concatenate(
            [
                lax.dynamic_slice_in_dim(array, self.block_at(p) * width, width, axis)
                for p in range(self.size)
            ],
            axis=axis,
        )

    def true_order(self, array, axis):
        width = array.shape[axis] // self.size
        return jnp.concatenate(
            [
                lax.dynamic_slice_in_dim(array, self.place_of(b) * width, width, axis)
                for b in range(self.size)
            ],
            axis=axis,
        )

    def gather(self, block, axis):
        near = jnp.concatenate(
            [block] + [self.shift(block, s) for s in range(1, self.outer)], axis=axis
        )
        return jnp.concatenate([near, self.swap(near)], axis=axis)

    def scatter_sum(self, make_half, axis):
        far = self.swap(make_half(1).astype(BF16))
        near = make_half(0) + far.astype(F32)
        width = near.shape[axis] // self.outer
        total = lax.slice_in_dim(near, 0, width, axis=axis)
        for s in range(1, self.outer):
            part = lax.slice_in_dim(near, s * width, (s + 1) * width, axis=axis).astype(BF16)
            total = total + self.shift(part, -s).astype(F32)
        return total


def half_of(array, turn, axis):
    width = array.shape[axis] // 2
    return lax.slice_in_dim(array, turn * width, (turn + 1) * width, axis=axis)


def token_sum(ring, make_rows, rows):
    width = rows // ring.size
    outer, inner = ring.me // 2, ring.me % 2
    far = [make_rows((((outer + s) % ring.outer) * 2 + 1 - inner) * width, width) for s in range(ring.outer)]
    got = ring.swap(jnp.concatenate(far, axis=0).astype(BF16)).astype(F32)
    near = [
        make_rows((((outer + s) % ring.outer) * 2 + inner) * width, width)
        + lax.slice_in_dim(got, s * width, (s + 1) * width, axis=0)
        for s in range(ring.outer)
    ]
    total = near[0]
    for s in range(1, ring.outer):
        total = total + ring.shift(near[s].astype(BF16), s).astype(F32)
    return total


def token_gather(ring, block):
    return ring.true_order(ring.gather(block, 0), 0)


def on_device(
    dp_size,
    tensor_size,
    tokens,
    mixer_gain,
    query_weight,
    key_weight,
    value_weight,
    gate_weight,
    out_weight,
    group_gain,
    feed_gain,
    hidden_weight,
    up_weight,
    down_weight,
    cotangent,
):
    data = Ring("dp", dp_size)
    team = Ring("tensor", tensor_size)
    length, model = tokens.shape
    quarter = length // tensor_size
    heads_here = query_weight.shape[1] // DK

    block = mixer_gain.shape[0]
    gains = jnp.concatenate([mixer_gain, feed_gain, group_gain.reshape(-1)])[None, :]
    gains = data.gather(gains, 0)
    mixer_scale = gains[:, :block].reshape(-1).astype(F32)
    feed_scale = gains[:, block : 2 * block].reshape(-1).astype(F32)
    group_scale = data.true_order(gains[:, 2 * block :], 0).astype(F32)
    group_scale = group_scale.reshape(dp_size, heads_here, -1).swapaxes(0, 1).reshape(heads_here, -1)

    query_key = data.gather(jnp.concatenate([query_weight, key_weight], axis=1), 0)
    value_full = data.gather(value_weight, 0)
    gate_full = data.gather(gate_weight, 0)
    out_full = data.gather(out_weight, 1)
    hidden_full = data.gather(hidden_weight, 0)
    up_full = data.gather(up_weight, 0)
    down_full = data.gather(down_weight, 1)

    head_ids = (lax.axis_index("tensor") * heads_here + jnp.arange(heads_here)).astype(F32)
    decays = decay_table(head_ids, length)
    inputs = data.own_order(tokens, 1)
    cot = data.own_order(cotangent, 1)
    mixer_input = layer_norm(inputs.astype(F32), mixer_scale).astype(BF16)

    def my_rows(array):
        return lax.dynamic_slice_in_dim(array, team.me * quarter, quarter, 0)

    width = query_weight.shape[1]
    both = plain_product(mixer_input, query_key)
    query = both[:, :width]
    keyset = both[:, width:]
    values = plain_product(mixer_input, value_full).astype(BF16)
    gate_in = plain_product(mixer_input, gate_full)
    turned_query = rotate(query, heads_here, 1.0).astype(BF16).reshape(length, heads_here, DK)
    turned_keys = rotate(keyset, heads_here, 1.0).astype(BF16).reshape(length, heads_here, DK)
    scores, row_totals, denominators = core_scores(turned_query, turned_keys, decays)
    weights = (scores / denominators).astype(BF16)
    value_heads = values.reshape(length, heads_here, DV)
    retained = jnp.einsum("hqk,khd->qhd", weights, value_heads, preferred_element_type=F32)
    retained = retained.reshape(length, heads_here * DV)
    mixed = gate_piece(retained, gate_in, group_scale).astype(BF16)

    def row_terms(left, right):
        return lambda start, rows: plain_product(
            lax.dynamic_slice_in_dim(left, start, rows, 0), right
        )

    branch = token_sum(team, row_terms(mixed, out_full), length)
    residual = my_rows(inputs).astype(F32) + branch
    feed_input = token_gather(team, layer_norm(residual, feed_scale).astype(BF16))
    hidden_pre = plain_product(feed_input, hidden_full)
    up_pre = plain_product(feed_input, up_full)
    activity, feed_back = jax.vjp(feed_piece, hidden_pre, up_pre)
    activity = activity.astype(BF16)
    activity_grad = back_product(cot, down_full)
    hidden_grad, up_grad = feed_back(activity_grad)
    hidden_grad = hidden_grad.astype(BF16)
    up_grad = up_grad.astype(BF16)

    def feed_rows(start, rows):
        return back_product(
            lax.dynamic_slice_in_dim(hidden_grad, start, rows, 0), hidden_full
        ) + back_product(lax.dynamic_slice_in_dim(up_grad, start, rows, 0), up_full)

    feed_input_grad = token_sum(team, feed_rows, length)
    _, feed_norm_back = jax.vjp(layer_norm, residual, feed_scale)
    residual_part, feed_scale_grad = feed_norm_back(feed_input_grad)
    residual_grad = my_rows(cot).astype(F32) + residual_part
    branch_grad = token_gather(team, residual_grad.astype(BF16))

    hidden_weight_grad = data.scatter_sum(
        lambda turn: row_product(half_of(feed_input, turn, 1), hidden_grad), 0
    )
    up_weight_grad = data.scatter_sum(
        lambda turn: row_product(half_of(feed_input, turn, 1), up_grad), 0
    )
    down_grad = data.scatter_sum(lambda turn: row_product(activity, half_of(cot, turn, 1)), 1)

    feed_out = token_sum(team, row_terms(activity, down_full), length)
    output = token_gather(team, (residual + feed_out).astype(BF16))
    output = data.true_order(output, 1)

    mixed_grad = back_product(branch_grad, out_full)
    _, gate_back = jax.vjp(gate_piece, retained, gate_in, group_scale)
    retained_grad, gate_grad, group_scale_grad = gate_back(mixed_grad)
    retained_grad = retained_grad.astype(BF16)
    gate_grad = gate_grad.astype(BF16)
    out_weight_grad = data.scatter_sum(
        lambda turn: row_product(mixed, half_of(branch_grad, turn, 1)), 1
    )
    gate_weight_grad = data.scatter_sum(
        lambda turn: row_product(half_of(mixer_input, turn, 1), gate_grad), 0
    )

    grad_heads = retained_grad.reshape(length, heads_here, DV)
    weights_grad = jnp.einsum("qhd,khd->hqk", grad_heads, value_heads, preferred_element_type=F32)
    value_parts = jnp.einsum("hqk,qhd->khd", weights, grad_heads, preferred_element_type=F32)
    value_parts = value_parts.reshape(length, heads_here * DV).astype(BF16)
    value_weight_grad = data.scatter_sum(
        lambda turn: row_product(half_of(mixer_input, turn, 1), value_parts), 0
    )
    inner_totals = jnp.sum(weights_grad * scores, axis=-1, keepdims=True)
    slope = row_totals / denominators
    scores_grad = weights_grad / denominators - inner_totals / (denominators * denominators) * slope
    raw_grad = (scores_grad * DK ** (-0.5) * decays).astype(BF16)
    turned_query_grad = jnp.einsum("hqk,khd->qhd", raw_grad, turned_keys, preferred_element_type=F32)
    turned_key_grad = jnp.einsum("hqk,qhd->khd", raw_grad, turned_query, preferred_element_type=F32)
    query_parts = rotate(turned_query_grad.reshape(length, width), heads_here, -1.0).astype(BF16)
    key_parts = rotate(turned_key_grad.reshape(length, width), heads_here, -1.0).astype(BF16)
    both_parts = jnp.concatenate([query_parts, key_parts], axis=1)
    both_grad = data.scatter_sum(
        lambda turn: row_product(half_of(mixer_input, turn, 1), both_parts), 0
    )
    query_weight_grad = both_grad[:, :width]
    key_weight_grad = both_grad[:, width:]

    def mixer_rows(start, rows):
        def cut(array):
            return lax.dynamic_slice_in_dim(array, start, rows, 0)

        return (
            back_product(cut(both_parts), query_key)
            + back_product(cut(value_parts), value_full)
            + back_product(cut(gate_grad), gate_full)
        )

    mixer_input_grad = token_sum(team, mixer_rows, length)
    _, mixer_norm_back = jax.vjp(layer_norm, my_rows(inputs).astype(F32), mixer_scale)
    input_part, mixer_scale_grad = mixer_norm_back(mixer_input_grad)
    tokens_grad = token_gather(team, (residual_grad + input_part).astype(BF16))
    tokens_grad = data.true_order(tokens_grad, 1).astype(F32)

    norm_grads = jnp.concatenate([mixer_scale_grad, feed_scale_grad]).reshape(2, -1)
    norm_grads = lax.psum(data.true_order(norm_grads, 1), ("dp", "tensor"))
    norm_grads = lax.dynamic_slice_in_dim(norm_grads, data.me * block, block, 1)
    group_scale_grad = lax.psum(group_scale_grad, "dp")
    group_block = group_gain.shape[1]
    group_scale_grad = lax.dynamic_slice_in_dim(group_scale_grad, data.me * group_block, group_block, 1)
    return (
        output,
        tokens_grad,
        norm_grads[0],
        query_weight_grad,
        key_weight_grad,
        value_weight_grad,
        gate_weight_grad,
        out_weight_grad,
        group_scale_grad,
        norm_grads[1],
        hidden_weight_grad,
        up_weight_grad,
        down_grad,
    )


def solution(mesh):
    columns = P("dp", "tensor")
    rows = P("tensor", "dp")
    placed = (
        P("dp", None),
        P("dp"),
        columns,
        columns,
        columns,
        columns,
        rows,
        rows,
        P("dp"),
        columns,
        columns,
        rows,
        P("dp", None),
    )
    given = (
        P("dp", None),
        P("dp", None),
        P("dp"),
        columns,
        columns,
        columns,
        columns,
        rows,
        rows,
        P("dp"),
        columns,
        columns,
        rows,
    )

    def body(*arrays):
        return on_device(mesh.shape["dp"], mesh.shape["tensor"], *arrays)

    return jax.shard_map(body, mesh=mesh, in_specs=placed, out_specs=given, check_vma=False)
```

```python
import jax
import jax.numpy as jnp
from jax import lax
from jax.experimental import pallas as pl
from jax.experimental.pallas import tpu as pltpu
from jax.sharding import PartitionSpec as P

DK = 256
DV = 512

norm_epsilon = 1e-05
group_epsilon = 0.01
F32 = jnp.float32
BF16 = jnp.bfloat16


def layer_norm(values, scale_gain, epsilon=norm_epsilon):
    center = values - jnp.mean(values, axis=-1, keepdims=True)
    spread = jnp.mean(center * center, axis=-1, keepdims=True)
    return center * lax.rsqrt(spread + epsilon) * scale_gain


def group_norm(retained, scale_gain):
    shaped = retained.reshape(retained.shape[0], scale_gain.shape[0], scale_gain.shape[1])
    return layer_norm(shaped, scale_gain, group_epsilon).reshape(retained.shape)


def rotate(values, head_count, direction):
    length = values.shape[0]
    head_width = values.shape[1] // head_count
    half_width = head_width // 2
    places = jnp.arange(length, dtype=F32)[:, None]
    speeds = 10000.0 ** (-jnp.arange(half_width, dtype=F32) / half_width)
    angles = places * speeds[None, :]
    cosine = jnp.cos(angles)[:, None, :]
    sine_part = direction * jnp.sin(angles)[:, None, :]
    shaped = values.reshape(length, head_count, 2, half_width)
    front_half = shaped[:, :, 0]
    back_half = shaped[:, :, 1]
    turned = jnp.stack(
        [front_half * cosine - back_half * sine_part, front_half * sine_part + back_half * cosine],
        axis=2,
    )
    return turned.reshape(length, head_count * head_width)


def decays_plain(head_ids, length):
    log_rates = jnp.log1p(-jnp.exp2(-5.0 - head_ids))
    row_place = jnp.arange(length)[:, None]
    key_place = jnp.arange(length)[None, :]
    distance = jnp.maximum(row_place - key_place, 0).astype(F32)
    decays = jnp.where(
        (row_place >= key_place)[None], jnp.exp(log_rates[:, None, None] * distance[None]), 0.0
    )
    return decays


def decay_table(head_ids, length):
    decays = decays_plain(head_ids, length)
    return decays * lax.rsqrt(jnp.sum(decays, axis=-1, keepdims=True))


def plain_product(left, right):
    return jnp.dot(left, right, preferred_element_type=F32)


def row_product(left, right):
    return lax.dot_general(left, right, (((0,), (0,)), ((), ())), preferred_element_type=F32)


def back_product(left, right):
    return lax.dot_general(left, right, (((1,), (1,)), ((), ())), preferred_element_type=F32)


def core_scores(turned_query, turned_keys, decays):
    raw_scores = jnp.einsum("qhd,khd->hqk", turned_query, turned_keys, preferred_element_type=F32)
    scores = raw_scores * DK ** (-0.5) * decays
    row_totals = jnp.sum(scores, axis=-1, keepdims=True)
    denominators = jnp.sqrt(row_totals * row_totals + 1.0)
    return (scores, row_totals, denominators)


def feed_piece(hidden_pre, up_pre):
    return jax.nn.gelu(hidden_pre) * up_pre


def gate_piece(retained, gate_in, group_scale):
    return jax.nn.silu(gate_in) * group_norm(retained, group_scale)


class Ring:
    def __init__(self, name, size):
        self.name = name
        self.size = size
        self.outer = size // 2
        self.me = lax.axis_index(name)
        self.swap_pairs = [(i, i ^ 1) for i in range(size)]

    def swap(self, block):
        return lax.ppermute(block, self.name, self.swap_pairs)

    def shift(self, block, step):
        pairs = [
            (i, ((i // 2 + step) % self.outer) * 2 + i % 2) for i in range(self.size)
        ]
        return lax.ppermute(block, self.name, pairs)

    def block_at(self, place):
        turn, step = place // self.outer, place % self.outer
        outer = (self.me // 2 + self.outer - step) % self.outer
        return outer * 2 + (self.me % 2 + turn) % 2

    def place_of(self, block):
        turn = (block % 2 + self.me % 2) % 2
        step = (self.me // 2 + self.outer - block // 2) % self.outer
        return turn * self.outer + step

    def own_order(self, array, axis):
        width = array.shape[axis] // self.size
        return jnp.concatenate(
            [
                lax.dynamic_slice_in_dim(array, self.block_at(p) * width, width, axis)
                for p in range(self.size)
            ],
            axis=axis,
        )

    def true_order(self, array, axis):
        width = array.shape[axis] // self.size
        return jnp.concatenate(
            [
                lax.dynamic_slice_in_dim(array, self.place_of(b) * width, width, axis)
                for b in range(self.size)
            ],
            axis=axis,
        )

    def gather(self, block, axis):
        near = jnp.concatenate(
            [block] + [self.shift(block, s) for s in range(1, self.outer)], axis=axis
        )
        return jnp.concatenate([near, self.swap(near)], axis=axis)

    def scatter_sum(self, make_half, axis):
        far = self.swap(make_half(1).astype(BF16))
        near = make_half(0) + far.astype(F32)
        width = near.shape[axis] // self.outer
        total = lax.slice_in_dim(near, 0, width, axis=axis)
        for s in range(1, self.outer):
            part = lax.slice_in_dim(near, s * width, (s + 1) * width, axis=axis).astype(BF16)
            total = total + self.shift(part, -s).astype(F32)
        return total


def half_of(array, turn, axis):
    width = array.shape[axis] // 2
    return lax.slice_in_dim(array, turn * width, (turn + 1) * width, axis=axis)


def token_sum(ring, make_rows, rows):
    width = rows // ring.size
    outer, inner = ring.me // 2, ring.me % 2
    far = [make_rows((((outer + s) % ring.outer) * 2 + 1 - inner) * width, width) for s in range(ring.outer)]
    got = ring.swap(jnp.concatenate(far, axis=0).astype(BF16)).astype(F32)
    near = [
        make_rows((((outer + s) % ring.outer) * 2 + inner) * width, width)
        + lax.slice_in_dim(got, s * width, (s + 1) * width, axis=0)
        for s in range(ring.outer)
    ]
    total = near[0]
    for s in range(1, ring.outer):
        total = total + ring.shift(near[s].astype(BF16), s).astype(F32)
    return total


def token_gather(ring, block):
    return ring.true_order(ring.gather(block, 0), 0)


MESH = pl.DeviceIdType.MESH
ANY = pl.BlockSpec(memory_space=pl.ANY)


class Wires:
    def __init__(self, outer):
        self.outer = outer
        self.dp = lax.axis_index("dp")
        self.tensor = lax.axis_index("tensor")
        self.ring = self.dp // 2
        self.turn = self.dp % 2
        self.row = self.tensor // 2
        self.core = self.tensor % 2
        self.order = [1, outer - 1] + list(range(2, outer - 1))

    def far(self, step):
        return (lax.rem(self.ring + step, self.outer) * 2 + self.turn, self.tensor)

    def peer(self):
        return (self.ring * 2 + 1 - self.turn, self.tensor)

    def sibling(self):
        return (self.dp, self.row * 2 + 1 - self.core)

    def across(self):
        return (self.dp, (1 - self.row) * 2 + self.core)

    def block_at(self, place):
        turn, step = place // self.outer, place % self.outer
        return lax.rem(self.ring + self.outer - step, self.outer) * 2 + lax.rem(self.turn + turn, 2)

    def greet(self):
        barrier = pltpu.get_barrier_semaphore()
        partners = [self.far(s) for s in range(1, self.outer)]
        partners += [self.peer(), self.sibling(), self.across()]
        for partner in partners:
            pl.semaphore_signal(barrier, inc=1, device_id=partner, device_id_type=MESH)
        pl.semaphore_wait(barrier, len(partners))


def remote(src, dst, send, recv, device):
    return pltpu.make_async_remote_copy(
        src_ref=src, dst_ref=dst, send_sem=send, recv_sem=recv, device_id=device, device_id_type=MESH
    )


def tile(index, rows):
    return pl.ds(pl.multiple_of(index * rows, rows), rows)


def norm_rows(values, gain, epsilon):
    center = values - jnp.mean(values, axis=-1, keepdims=True)
    spread = jnp.mean(center * center, axis=-1, keepdims=True)
    return center * lax.rsqrt(spread + epsilon) * gain


def silu(v):
    return v * (1.0 / (1.0 + jnp.exp(-v)))


N_ITEMS = 9
GAINS, QUERY, KEY, VALUE, GATE, OUT, HIDDEN, UP, DOWN = range(N_ITEMS)
STEP = 256


def forward_kernel(outer, heads, dims, *refs):
    length, model, block = dims
    quarter = length // 4
    tokens, gains, cosine, sine, row_decay, key_decay = refs[:6]
    items = (gains,) + refs[6:14]
    fulls = refs[14:23]
    (mixer_out, query_out, key_out, value_out, retained_out, gate_out, mixed_out, residual_out,
     feed_out, hidden_out, up_out) = refs[23:34]
    (slot_a, slot_b, slot_o, wide, mixer, rq, rk, values, kept, gate_in, mixed, residual, csend, crecv, ysend,
     yrecv, cos_v, sin_v, rowd, keyd, gain_v, gain_m, gain_f, gain_g,
     loc, zs, zr, xs, xr, ts, tr, ls, os_) = refs[34:]
    wires = Wires(outer)
    rows = length // STEP

    def piece(item, place):
        if item in (OUT, DOWN):
            return fulls[item].at[:, pl.ds(place * block, block)]
        height = items[item].shape[0]
        return fulls[item].at[pl.ds(place * height, height)]

    def along(item, step):
        return remote(items[item], piece(item, step), zs.at[item, step], zr.at[item, step], wires.far(step))

    def beside(item, step):
        src = items[item] if step == 0 else piece(item, step)
        return remote(src, piece(item, outer + step), xs.at[item, step], xr.at[item, step], wires.peer())

    def own(item):
        return pltpu.make_async_copy(items[item], piece(item, 0), loc.at[item])

    def issue(item):
        if item < N_ITEMS:
            own(item).start()
            for step in wires.order:
                along(item, step).start()
            beside(item, 0).start()

    def pass_on(item):
        for step in wires.order:
            along(item, step).wait_recv()
            beside(item, step).start()

    def arrived(item):
        own(item).wait()
        for step in range(outer):
            beside(item, step).wait_recv()

    def load(src, dst, index):
        copy = pltpu.make_async_copy(src, dst, ls.at[index])
        copy.start()
        return copy

    stores = []

    def store(src, dst):
        copy = pltpu.make_async_copy(src, dst, os_.at[len(stores)])
        copy.start()
        stores.append(copy)
        return copy

    wires.greet()
    issue(GAINS)
    issue(QUERY)
    issue(KEY)
    loads = []
    for place in range(2 * outer):
        at = pl.multiple_of(wires.block_at(place) * block, block)
        loads.append(load(tokens.at[:, pl.ds(at, block)], wide.at[:, pl.ds(place * block, block)], place))
    first = 2 * outer
    loads.append(load(cosine, cos_v, first))
    loads.append(load(sine, sin_v, first + 1))
    loads.append(load(row_decay, rowd, first + 2))
    loads.append(load(key_decay, keyd, first + 3))
    pass_on(GAINS)
    issue(VALUE)
    arrived(GAINS)
    for copy in loads:
        copy.wait()
    copy = load(fulls[GAINS], gain_v, 0)
    copy.wait()
    group = jnp.zeros((1, heads * DV), F32)
    for place in range(2 * outer):
        line = gain_v[place * 16 : place * 16 + 1, :].astype(F32)
        gain_m[:, place * block : (place + 1) * block] = line[:, :block]
        gain_f[:, place * block : (place + 1) * block] = line[:, block : 2 * block]
        group = group + line[:, 2 * block :]
    gain_g[...] = group

    @pl.loop(0, length // 128)
    def _(r):
        at = tile(r, 128)
        mixer[at, :] = norm_rows(wide[at, :].astype(F32), gain_m[...], norm_epsilon).astype(BF16)

    mine = tile(wires.tensor, quarter)
    residual[...] = wide[mine, :].astype(F32)
    store(mixer, mixer_out)
    pass_on(QUERY)
    issue(GATE)
    pass_on(KEY)
    arrived(QUERY)
    arrived(KEY)
    narrow = heads * DK
    copy = load(fulls[QUERY], slot_a.at[:, pl.ds(0, narrow)], 0)
    other = load(fulls[KEY], slot_a.at[:, pl.ds(narrow, narrow)], 1)
    copy.wait()
    other.wait()

    @pl.loop(0, rows)
    def _(r):
        at = tile(r, STEP)
        both = jnp.dot(mixer[at, :], slot_a[...], preferred_element_type=F32)
        c, s = cos_v[at, :], sin_v[at, :]
        half = DK // 2
        for target, base in ((rq, 0), (rk, narrow)):
            for h in range(heads):
                lo = base + h * DK
                a, b = both[:, lo : lo + half], both[:, lo + half : lo + DK]
                target[at, h * DK : h * DK + half] = (a * c - b * s).astype(BF16)
                target[at, h * DK + half : (h + 1) * DK] = (a * s + b * c).astype(BF16)

    store(rq, query_out)
    store(rk, key_out)
    pass_on(VALUE)
    issue(OUT)
    arrived(VALUE)
    load(fulls[VALUE], slot_b, 0).wait()

    @pl.loop(0, rows)
    def _(r):
        at = tile(r, STEP)
        values[at, :] = jnp.dot(mixer[at, :], slot_b[...], preferred_element_type=F32).astype(BF16)

    store(values, value_out)
    for h in range(heads):
        for r in range(rows):
            at = slice(r * STEP, (r + 1) * STEP)
            upto = (r + 1) * STEP
            q = rq[at, h * DK : (h + 1) * DK]
            k = rk[:upto, h * DK : (h + 1) * DK]
            raw = lax.dot_general(q, k, (((1,), (1,)), ((), ())), preferred_element_type=F32)
            fade = rowd[at, h : h + 1] * keyd[h : h + 1, :upto]
            place = lax.broadcasted_iota(jnp.int32, (STEP, upto), 0) + r * STEP
            under = place >= lax.broadcasted_iota(jnp.int32, (STEP, upto), 1)
            scores = raw * jnp.where(under, fade, 0.0)
            total = jnp.sum(scores, axis=-1, keepdims=True)
            share = (scores * lax.rsqrt(total * total + 1.0)).astype(BF16)
            kept[at, h * DV : (h + 1) * DV] = jnp.dot(
                share, values[:upto, h * DV : (h + 1) * DV], preferred_element_type=F32
            )
    kept_store = store(kept, retained_out)
    pass_on(GATE)
    issue(HIDDEN)
    arrived(GATE)
    load(fulls[GATE], slot_a, 0).wait()

    @pl.loop(0, rows)
    def _(r):
        at = tile(r, STEP)
        gate = jnp.dot(mixer[at, :], slot_a[...], preferred_element_type=F32)
        gate_in[at, :] = gate
        for h in range(heads):
            cols = slice(h * DV, (h + 1) * DV)
            normed = norm_rows(kept[at, cols], gain_g[:, cols], group_epsilon)
            mixed[at, cols] = (silu(gate[:, cols]) * normed).astype(BF16)

    gate_store = store(gate_in, gate_out)
    store(mixed, mixed_out)
    pass_on(OUT)
    issue(UP)
    arrived(OUT)
    load(fulls[OUT], slot_o, 0).wait()

    def branch_rows(index):
        return jnp.dot(mixed[tile(index, quarter), :], slot_o[...], preferred_element_type=F32)

    def to_sibling(s):
        return remote(csend.at[s], crecv.at[s], ts.at[s], tr.at[s], wires.sibling())

    cross = remote(ysend, yrecv, ts.at[2], tr.at[2], wires.across())
    for s in (1, 0):
        owner = lax.rem(wires.row + s, 2) * 2 + 1 - wires.core
        csend[s] = branch_rows(owner).astype(BF16)
        to_sibling(s).start()
    part = branch_rows((1 - wires.row) * 2 + wires.core)
    to_sibling(1).wait_recv()
    ysend[...] = (part + crecv[1].astype(F32)).astype(BF16)
    cross.start()
    residual[...] += branch_rows(wires.tensor)
    to_sibling(0).wait_recv()
    residual[...] += crecv[0].astype(F32)
    pass_on(HIDDEN)
    issue(DOWN)
    cross.wait_recv()
    residual[...] += yrecv[...].astype(F32)
    store(residual, residual_out)
    feed_mine = wide.at[mine]

    @pl.loop(0, quarter // 128)
    def _(r):
        at = tile(r, 128)
        ysend_rows = norm_rows(residual[at, :], gain_f[...], norm_epsilon).astype(BF16)
        feed_mine[at, :] = ysend_rows

    feed_cross = remote(feed_mine, feed_mine, ts.at[3], tr.at[3], wires.across())
    feed_near = remote(feed_mine, feed_mine, ts.at[4], tr.at[4], wires.sibling())
    theirs = wide.at[tile((1 - wires.row) * 2 + wires.core, quarter)]
    feed_far = remote(theirs, theirs, ts.at[5], tr.at[5], wires.sibling())
    feed_cross.start()
    feed_near.start()
    arrived(HIDDEN)
    load(fulls[HIDDEN], slot_b, 0).wait()
    feed_cross.wait_recv()
    feed_far.start()
    feed_near.wait_recv()
    feed_far.wait_recv()
    store(wide, feed_out)
    kept_store.wait()
    gate_store.wait()

    @pl.loop(0, rows)
    def _(r):
        at = tile(r, STEP)
        kept[at, :] = jnp.dot(wide[at, :], slot_b[...], preferred_element_type=F32)

    hidden_store = pltpu.make_async_copy(kept, hidden_out, ls.at[1])
    hidden_store.start()
    pass_on(UP)
    arrived(UP)
    load(fulls[UP], slot_a, 0).wait()

    @pl.loop(0, rows)
    def _(r):
        at = tile(r, STEP)
        gate_in[at, :] = jnp.dot(wide[at, :], slot_a[...], preferred_element_type=F32)

    up_store = pltpu.make_async_copy(gate_in, up_out, ls.at[2])
    up_store.start()
    pass_on(DOWN)
    arrived(DOWN)
    hidden_store.wait()
    up_store.wait()
    for copy in stores:
        if copy is not kept_store and copy is not gate_store:
            copy.wait()
    for s in range(2):
        to_sibling(s).wait_send()
    for copy in (cross, feed_cross, feed_near, feed_far):
        copy.wait_send()
    for item in range(N_ITEMS):
        for step in range(1, outer):
            along(item, step).wait_send()
        for step in range(outer):
            beside(item, step).wait_send()


def forward_fast(dp_size, tokens, gains, tables, weights):
    outer = dp_size // 2
    length, model = tokens.shape
    block = model // dp_size
    heads = weights[0].shape[1] // DK
    units = weights[3].shape[1]
    wide = units
    shapes = [(gains.shape[0] * dp_size, gains.shape[1])]
    for place, weight in enumerate(weights):
        if place + 1 in (OUT, DOWN):
            shapes.append((weight.shape[0], model))
        else:
            shapes.append((model, weight.shape[1]))
    out_shape = [jax.ShapeDtypeStruct(s, BF16) for s in shapes]
    half = heads * DK
    for shape, kind in (
        ((length, model), BF16),
        ((length, half), BF16),
        ((length, half), BF16),
        ((length, wide), BF16),
        ((length, wide), F32),
        ((length, wide), F32),
        ((length, wide), BF16),
        ((length // 4, model), F32),
        ((length, model), BF16),
        ((length, units), F32),
        ((length, units), F32),
    ):
        out_shape.append(jax.ShapeDtypeStruct(shape, kind))
    quarter = length // 4
    dma = pltpu.SemaphoreType.DMA
    scratch = [
        pltpu.VMEM((model, wide), BF16),
        pltpu.VMEM((model, wide), BF16),
        pltpu.VMEM((wide, model), BF16),
        pltpu.VMEM((length, model), BF16),
        pltpu.VMEM((length, model), BF16),
        pltpu.VMEM((length, half), BF16),
        pltpu.VMEM((length, half), BF16),
        pltpu.VMEM((length, wide), BF16),
        pltpu.VMEM((length, wide), F32),
        pltpu.VMEM((length, wide), F32),
        pltpu.VMEM((length, wide), BF16),
        pltpu.VMEM((quarter, model), F32),
        pltpu.VMEM((2, quarter, model), BF16),
        pltpu.VMEM((2, quarter, model), BF16),
        pltpu.VMEM((quarter, model), BF16),
        pltpu.VMEM((quarter, model), BF16),
        pltpu.VMEM(tables[0].shape, F32),
        pltpu.VMEM(tables[1].shape, F32),
        pltpu.VMEM(tables[2].shape, F32),
        pltpu.VMEM(tables[3].shape, F32),
        pltpu.VMEM(shapes[0], BF16),
        pltpu.VMEM((1, model), F32),
        pltpu.VMEM((1, model), F32),
        pltpu.VMEM((1, heads * DV), F32),
        dma((N_ITEMS,)),
        dma((N_ITEMS, outer)),
        dma((N_ITEMS, outer)),
        dma((N_ITEMS, outer)),
        dma((N_ITEMS, outer)),
        dma((6,)),
        dma((6,)),
        dma((2 * outer + 4,)),
        dma((12,)),
    ]

    def kernel(*refs):
        forward_kernel(outer, heads, (length, model, block), *refs)

    results = pl.pallas_call(
        kernel,
        out_shape=out_shape,
        in_specs=[ANY] * (6 + len(weights)),
        out_specs=[ANY] * len(out_shape),
        scratch_shapes=scratch,
        compiler_params=pltpu.CompilerParams(
            collective_id=0, has_side_effects=True, vmem_limit_bytes=58 * 1024 * 1024
        ),
    )(tokens, gains, *tables, *weights)
    return results[: N_ITEMS], results[N_ITEMS:]


def on_device(
    dp_size,
    tensor_size,
    tokens,
    mixer_gain,
    query_weight,
    key_weight,
    value_weight,
    gate_weight,
    out_weight,
    group_gain,
    feed_gain,
    hidden_weight,
    up_weight,
    down_weight,
    cotangent,
):
    data = Ring("dp", dp_size)
    team = Ring("tensor", tensor_size)
    length, model = tokens.shape
    quarter = length // tensor_size
    heads_here = query_weight.shape[1] // DK

    block = mixer_gain.shape[0]
    width = query_weight.shape[1]
    group_block = group_gain.shape[1]
    head_ids = (lax.axis_index("tensor") * heads_here + jnp.arange(heads_here)).astype(F32)
    decays = decay_table(head_ids, length)
    inputs = data.own_order(tokens, 1)
    cot = data.own_order(cotangent, 1)

    def my_rows(array):
        return lax.dynamic_slice_in_dim(array, team.me * quarter, quarter, 0)

    def row_terms(left, right):
        return lambda start, rows: plain_product(
            lax.dynamic_slice_in_dim(left, start, rows, 0), right
        )

    if block % 128 == 0 and tensor_size == 4 and dp_size >= 8 and length % 1024 == 0:
        group_line = lax.dynamic_update_slice(
            jnp.zeros((heads_here, DV), BF16), group_gain, (0, data.me * group_block)
        )
        gains = jnp.concatenate([mixer_gain, feed_gain, group_line.reshape(-1)])
        gains = jnp.broadcast_to(gains[None, :], (16, gains.shape[0]))
        half = DK // 2
        angles = jnp.arange(length, dtype=F32)[:, None] * (
            10000.0 ** (-jnp.arange(half, dtype=F32) / half)
        )
        log_rates = jnp.log1p(-jnp.exp2(-5.0 - head_ids))
        steps = jnp.arange(length, dtype=F32)
        decay_sums = jnp.sum(decays_plain(head_ids, length), axis=-1)
        row_decay = jnp.exp(log_rates[:, None] * (steps - length // 2)) * lax.rsqrt(decay_sums) * DK ** (-0.5)
        key_decay = jnp.exp(log_rates[:, None] * (length // 2 - steps))
        tables = (jnp.cos(angles), jnp.sin(angles), row_decay.T, key_decay)
        fulls, kept = forward_fast(
            dp_size,
            tokens,
            gains,
            tables,
            (query_weight, key_weight, value_weight, gate_weight, out_weight, hidden_weight, up_weight, down_weight),
        )
        gains = fulls[0].reshape(dp_size, 16, -1)[:, 0].astype(F32)
        mixer_scale = gains[:, :block].reshape(-1)
        feed_scale = gains[:, block : 2 * block].reshape(-1)
        group_scale = jnp.sum(gains[:, 2 * block :], axis=0).reshape(heads_here, DV)
        _, query_full, key_full, value_full, gate_full, out_full, hidden_full, up_full, down_full = fulls
        query_key = jnp.concatenate([query_full, key_full], axis=1)
        (mixer_input, turned_query, turned_keys, values, retained, gate_in, mixed, residual, feed_input,
         hidden_pre, up_pre) = kept
        turned_query = turned_query.reshape(length, heads_here, DK)
        turned_keys = turned_keys.reshape(length, heads_here, DK)
        value_heads = values.reshape(length, heads_here, DV)
        scores, row_totals, denominators = core_scores(turned_query, turned_keys, decays)
        weights = (scores / denominators).astype(BF16)
    else:
        gains = jnp.concatenate([mixer_gain, feed_gain, group_gain.reshape(-1)])[None, :]
        gains = data.gather(gains, 0)
        mixer_scale = gains[:, :block].reshape(-1).astype(F32)
        feed_scale = gains[:, block : 2 * block].reshape(-1).astype(F32)
        group_scale = data.true_order(gains[:, 2 * block :], 0).astype(F32)
        group_scale = group_scale.reshape(dp_size, heads_here, -1).swapaxes(0, 1).reshape(heads_here, -1)

        query_key = data.gather(jnp.concatenate([query_weight, key_weight], axis=1), 0)
        value_full = data.gather(value_weight, 0)
        gate_full = data.gather(gate_weight, 0)
        out_full = data.gather(out_weight, 1)
        hidden_full = data.gather(hidden_weight, 0)
        up_full = data.gather(up_weight, 0)
        down_full = data.gather(down_weight, 1)

        mixer_input = layer_norm(inputs.astype(F32), mixer_scale).astype(BF16)

        both = plain_product(mixer_input, query_key)
        query = both[:, :width]
        keyset = both[:, width:]
        values = plain_product(mixer_input, value_full).astype(BF16)
        gate_in = plain_product(mixer_input, gate_full)
        turned_query = rotate(query, heads_here, 1.0).astype(BF16).reshape(length, heads_here, DK)
        turned_keys = rotate(keyset, heads_here, 1.0).astype(BF16).reshape(length, heads_here, DK)
        scores, row_totals, denominators = core_scores(turned_query, turned_keys, decays)
        weights = (scores / denominators).astype(BF16)
        value_heads = values.reshape(length, heads_here, DV)
        retained = jnp.einsum("hqk,khd->qhd", weights, value_heads, preferred_element_type=F32)
        retained = retained.reshape(length, heads_here * DV)
        mixed = gate_piece(retained, gate_in, group_scale).astype(BF16)

        branch = token_sum(team, row_terms(mixed, out_full), length)
        residual = my_rows(inputs).astype(F32) + branch
        feed_input = token_gather(team, layer_norm(residual, feed_scale).astype(BF16))
        hidden_pre = plain_product(feed_input, hidden_full)
        up_pre = plain_product(feed_input, up_full)

    activity, feed_back = jax.vjp(feed_piece, hidden_pre, up_pre)
    activity = activity.astype(BF16)
    activity_grad = back_product(cot, down_full)
    hidden_grad, up_grad = feed_back(activity_grad)
    hidden_grad = hidden_grad.astype(BF16)
    up_grad = up_grad.astype(BF16)

    def feed_rows(start, rows):
        return back_product(
            lax.dynamic_slice_in_dim(hidden_grad, start, rows, 0), hidden_full
        ) + back_product(lax.dynamic_slice_in_dim(up_grad, start, rows, 0), up_full)

    feed_input_grad = token_sum(team, feed_rows, length)
    _, feed_norm_back = jax.vjp(layer_norm, residual, feed_scale)
    residual_part, feed_scale_grad = feed_norm_back(feed_input_grad)
    residual_grad = my_rows(cot).astype(F32) + residual_part
    branch_grad = token_gather(team, residual_grad.astype(BF16))

    hidden_weight_grad = data.scatter_sum(
        lambda turn: row_product(half_of(feed_input, turn, 1), hidden_grad), 0
    )
    up_weight_grad = data.scatter_sum(
        lambda turn: row_product(half_of(feed_input, turn, 1), up_grad), 0
    )
    down_grad = data.scatter_sum(lambda turn: row_product(activity, half_of(cot, turn, 1)), 1)

    feed_out = token_sum(team, row_terms(activity, down_full), length)
    output = token_gather(team, (residual + feed_out).astype(BF16))
    output = data.true_order(output, 1)

    mixed_grad = back_product(branch_grad, out_full)
    _, gate_back = jax.vjp(gate_piece, retained, gate_in, group_scale)
    retained_grad, gate_grad, group_scale_grad = gate_back(mixed_grad)
    retained_grad = retained_grad.astype(BF16)
    gate_grad = gate_grad.astype(BF16)
    out_weight_grad = data.scatter_sum(
        lambda turn: row_product(mixed, half_of(branch_grad, turn, 1)), 1
    )
    gate_weight_grad = data.scatter_sum(
        lambda turn: row_product(half_of(mixer_input, turn, 1), gate_grad), 0
    )

    grad_heads = retained_grad.reshape(length, heads_here, DV)
    weights_grad = jnp.einsum("qhd,khd->hqk", grad_heads, value_heads, preferred_element_type=F32)
    value_parts = jnp.einsum("hqk,qhd->khd", weights, grad_heads, preferred_element_type=F32)
    value_parts = value_parts.reshape(length, heads_here * DV).astype(BF16)
    value_weight_grad = data.scatter_sum(
        lambda turn: row_product(half_of(mixer_input, turn, 1), value_parts), 0
    )
    inner_totals = jnp.sum(weights_grad * scores, axis=-1, keepdims=True)
    slope = row_totals / denominators
    scores_grad = weights_grad / denominators - inner_totals / (denominators * denominators) * slope
    raw_grad = (scores_grad * DK ** (-0.5) * decays).astype(BF16)
    turned_query_grad = jnp.einsum("hqk,khd->qhd", raw_grad, turned_keys, preferred_element_type=F32)
    turned_key_grad = jnp.einsum("hqk,qhd->khd", raw_grad, turned_query, preferred_element_type=F32)
    query_parts = rotate(turned_query_grad.reshape(length, width), heads_here, -1.0).astype(BF16)
    key_parts = rotate(turned_key_grad.reshape(length, width), heads_here, -1.0).astype(BF16)
    both_parts = jnp.concatenate([query_parts, key_parts], axis=1)
    both_grad = data.scatter_sum(
        lambda turn: row_product(half_of(mixer_input, turn, 1), both_parts), 0
    )
    query_weight_grad = both_grad[:, :width]
    key_weight_grad = both_grad[:, width:]

    def mixer_rows(start, rows):
        def cut(array):
            return lax.dynamic_slice_in_dim(array, start, rows, 0)

        return (
            back_product(cut(both_parts), query_key)
            + back_product(cut(value_parts), value_full)
            + back_product(cut(gate_grad), gate_full)
        )

    mixer_input_grad = token_sum(team, mixer_rows, length)
    _, mixer_norm_back = jax.vjp(layer_norm, my_rows(inputs).astype(F32), mixer_scale)
    input_part, mixer_scale_grad = mixer_norm_back(mixer_input_grad)
    tokens_grad = token_gather(team, (residual_grad + input_part).astype(BF16))
    tokens_grad = data.true_order(tokens_grad, 1).astype(F32)

    norm_grads = jnp.concatenate([mixer_scale_grad, feed_scale_grad]).reshape(2, -1)
    norm_grads = lax.psum(data.true_order(norm_grads, 1), ("dp", "tensor"))
    norm_grads = lax.dynamic_slice_in_dim(norm_grads, data.me * block, block, 1)
    group_scale_grad = lax.psum(group_scale_grad, "dp")
    group_scale_grad = lax.dynamic_slice_in_dim(group_scale_grad, data.me * group_block, group_block, 1)
    return (
        output,
        tokens_grad,
        norm_grads[0],
        query_weight_grad,
        key_weight_grad,
        value_weight_grad,
        gate_weight_grad,
        out_weight_grad,
        group_scale_grad,
        norm_grads[1],
        hidden_weight_grad,
        up_weight_grad,
        down_grad,
    )


def solution(mesh):
    columns = P("dp", "tensor")
    rows = P("tensor", "dp")
    placed = (
        P("dp", None),
        P("dp"),
        columns,
        columns,
        columns,
        columns,
        rows,
        rows,
        P("dp"),
        columns,
        columns,
        rows,
        P("dp", None),
    )
    given = (
        P("dp", None),
        P("dp", None),
        P("dp"),
        columns,
        columns,
        columns,
        columns,
        rows,
        rows,
        P("dp"),
        columns,
        columns,
        rows,
    )

    def body(*arrays):
        return on_device(mesh.shape["dp"], mesh.shape["tensor"], *arrays)

    return jax.shard_map(body, mesh=mesh, in_specs=placed, out_specs=given, check_vma=False)
```

```python
import jax
import jax.numpy as jnp
from jax import lax
from jax.experimental import pallas as pl
from jax.experimental.pallas import tpu as pltpu
from jax.sharding import PartitionSpec as P

DK = 256
DV = 512

norm_epsilon = 1e-05
group_epsilon = 0.01
F32 = jnp.float32
BF16 = jnp.bfloat16


def layer_norm(values, scale_gain, epsilon=norm_epsilon):
    center = values - jnp.mean(values, axis=-1, keepdims=True)
    spread = jnp.mean(center * center, axis=-1, keepdims=True)
    return center * lax.rsqrt(spread + epsilon) * scale_gain


def group_norm(retained, scale_gain):
    shaped = retained.reshape(retained.shape[0], scale_gain.shape[0], scale_gain.shape[1])
    return layer_norm(shaped, scale_gain, group_epsilon).reshape(retained.shape)


def rotate(values, head_count, direction):
    length = values.shape[0]
    head_width = values.shape[1] // head_count
    half_width = head_width // 2
    places = jnp.arange(length, dtype=F32)[:, None]
    speeds = 10000.0 ** (-jnp.arange(half_width, dtype=F32) / half_width)
    angles = places * speeds[None, :]
    cosine = jnp.cos(angles)[:, None, :]
    sine_part = direction * jnp.sin(angles)[:, None, :]
    shaped = values.reshape(length, head_count, 2, half_width)
    front_half = shaped[:, :, 0]
    back_half = shaped[:, :, 1]
    turned = jnp.stack(
        [front_half * cosine - back_half * sine_part, front_half * sine_part + back_half * cosine],
        axis=2,
    )
    return turned.reshape(length, head_count * head_width)


def decays_plain(head_ids, length):
    log_rates = jnp.log1p(-jnp.exp2(-5.0 - head_ids))
    row_place = jnp.arange(length)[:, None]
    key_place = jnp.arange(length)[None, :]
    distance = jnp.maximum(row_place - key_place, 0).astype(F32)
    decays = jnp.where(
        (row_place >= key_place)[None], jnp.exp(log_rates[:, None, None] * distance[None]), 0.0
    )
    return decays


def decay_table(head_ids, length):
    decays = decays_plain(head_ids, length)
    return decays * lax.rsqrt(jnp.sum(decays, axis=-1, keepdims=True))


def plain_product(left, right):
    return jnp.dot(left, right, preferred_element_type=F32)


def row_product(left, right):
    return lax.dot_general(left, right, (((0,), (0,)), ((), ())), preferred_element_type=F32)


def back_product(left, right):
    return lax.dot_general(left, right, (((1,), (1,)), ((), ())), preferred_element_type=F32)


def core_scores(turned_query, turned_keys, decays):
    raw_scores = jnp.einsum("qhd,khd->hqk", turned_query, turned_keys, preferred_element_type=F32)
    scores = raw_scores * DK ** (-0.5) * decays
    row_totals = jnp.sum(scores, axis=-1, keepdims=True)
    denominators = jnp.sqrt(row_totals * row_totals + 1.0)
    return (scores, row_totals, denominators)


def feed_piece(hidden_pre, up_pre):
    return jax.nn.gelu(hidden_pre) * up_pre


def gate_piece(retained, gate_in, group_scale):
    return jax.nn.silu(gate_in) * group_norm(retained, group_scale)


class Ring:
    def __init__(self, name, size):
        self.name = name
        self.size = size
        self.outer = size // 2
        self.me = lax.axis_index(name)
        self.swap_pairs = [(i, i ^ 1) for i in range(size)]

    def swap(self, block):
        return lax.ppermute(block, self.name, self.swap_pairs)

    def shift(self, block, step):
        pairs = [
            (i, ((i // 2 + step) % self.outer) * 2 + i % 2) for i in range(self.size)
        ]
        return lax.ppermute(block, self.name, pairs)

    def block_at(self, place):
        turn, step = place // self.outer, place % self.outer
        outer = (self.me // 2 + self.outer - step) % self.outer
        return outer * 2 + (self.me % 2 + turn) % 2

    def place_of(self, block):
        turn = (block % 2 + self.me % 2) % 2
        step = (self.me // 2 + self.outer - block // 2) % self.outer
        return turn * self.outer + step

    def own_order(self, array, axis):
        width = array.shape[axis] // self.size
        return jnp.concatenate(
            [
                lax.dynamic_slice_in_dim(array, self.block_at(p) * width, width, axis)
                for p in range(self.size)
            ],
            axis=axis,
        )

    def true_order(self, array, axis):
        width = array.shape[axis] // self.size
        return jnp.concatenate(
            [
                lax.dynamic_slice_in_dim(array, self.place_of(b) * width, width, axis)
                for b in range(self.size)
            ],
            axis=axis,
        )

    def gather(self, block, axis):
        near = jnp.concatenate(
            [block] + [self.shift(block, s) for s in range(1, self.outer)], axis=axis
        )
        return jnp.concatenate([near, self.swap(near)], axis=axis)

    def scatter_sum(self, make_half, axis):
        far = self.swap(make_half(1).astype(BF16))
        near = make_half(0) + far.astype(F32)
        width = near.shape[axis] // self.outer
        total = lax.slice_in_dim(near, 0, width, axis=axis)
        for s in range(1, self.outer):
            part = lax.slice_in_dim(near, s * width, (s + 1) * width, axis=axis).astype(BF16)
            total = total + self.shift(part, -s).astype(F32)
        return total


def half_of(array, turn, axis):
    width = array.shape[axis] // 2
    return lax.slice_in_dim(array, turn * width, (turn + 1) * width, axis=axis)


def token_sum(ring, make_rows, rows):
    width = rows // ring.size
    outer, inner = ring.me // 2, ring.me % 2
    far = [make_rows((((outer + s) % ring.outer) * 2 + 1 - inner) * width, width) for s in range(ring.outer)]
    got = ring.swap(jnp.concatenate(far, axis=0).astype(BF16)).astype(F32)
    near = [
        make_rows((((outer + s) % ring.outer) * 2 + inner) * width, width)
        + lax.slice_in_dim(got, s * width, (s + 1) * width, axis=0)
        for s in range(ring.outer)
    ]
    total = near[0]
    for s in range(1, ring.outer):
        total = total + ring.shift(near[s].astype(BF16), s).astype(F32)
    return total


def token_gather(ring, block):
    return ring.true_order(ring.gather(block, 0), 0)


MESH = pl.DeviceIdType.MESH
ANY = pl.BlockSpec(memory_space=pl.ANY)


class Wires:
    def __init__(self, outer):
        self.outer = outer
        self.dp = lax.axis_index("dp")
        self.tensor = lax.axis_index("tensor")
        self.ring = self.dp // 2
        self.turn = self.dp % 2
        self.row = self.tensor // 2
        self.core = self.tensor % 2
        self.order = [1, outer - 1] + list(range(2, outer - 1))

    def far(self, step):
        return (lax.rem(self.ring + step, self.outer) * 2 + self.turn, self.tensor)

    def peer(self):
        return (self.ring * 2 + 1 - self.turn, self.tensor)

    def sibling(self):
        return (self.dp, self.row * 2 + 1 - self.core)

    def across(self):
        return (self.dp, (1 - self.row) * 2 + self.core)

    def block_at(self, place):
        turn, step = place // self.outer, place % self.outer
        return lax.rem(self.ring + self.outer - step, self.outer) * 2 + lax.rem(self.turn + turn, 2)

    def corner(self):
        return (self.dp, (1 - self.row) * 2 + 1 - self.core)

    def greet_all(self):
        barrier = pltpu.get_barrier_semaphore()
        partners = [(self.block_at(place), self.tensor) for place in range(1, 2 * self.outer)]
        partners += [self.sibling(), self.across(), self.corner()]
        for partner in partners:
            pl.semaphore_signal(barrier, inc=1, device_id=partner, device_id_type=MESH)
        pl.semaphore_wait(barrier, len(partners))

    def greet(self):
        barrier = pltpu.get_barrier_semaphore()
        partners = [self.far(s) for s in range(1, self.outer)]
        partners += [self.peer(), self.sibling(), self.across()]
        for partner in partners:
            pl.semaphore_signal(barrier, inc=1, device_id=partner, device_id_type=MESH)
        pl.semaphore_wait(barrier, len(partners))


def remote(src, dst, send, recv, device):
    return pltpu.make_async_remote_copy(
        src_ref=src, dst_ref=dst, send_sem=send, recv_sem=recv, device_id=device, device_id_type=MESH
    )


def tile(index, rows):
    return pl.ds(pl.multiple_of(index * rows, rows), rows)


def norm_rows(values, gain, epsilon):
    center = values - jnp.mean(values, axis=-1, keepdims=True)
    spread = jnp.mean(center * center, axis=-1, keepdims=True)
    return center * lax.rsqrt(spread + epsilon) * gain


def silu(v):
    return v * (1.0 / (1.0 + jnp.exp(-v)))


N_ITEMS = 9
GAINS, QUERY, KEY, VALUE, GATE, OUT, HIDDEN, UP, DOWN = range(N_ITEMS)
STEP = 256
PART = 128


def forward_kernel(outer, heads, dims, *refs):
    length, model, block = dims
    quarter = length // 4
    tokens, gains, cosine, sine, row_decay, key_decay = refs[:6]
    items = (gains,) + refs[6:14]
    fulls = refs[14:23]
    (mixer_out, query_out, key_out, value_out, retained_out, gate_out, mixed_out, residual_out,
     feed_out, hidden_out, up_out) = refs[23:34]
    (slot_a, slot_b, slot_o, wide, mixer, rq, rk, values, kept, gate_in, mixed, residual, csend, crecv, ysend,
     yrecv, cos_v, sin_v, rowd, keyd, gain_v, gain_m, gain_f, gain_g,
     loc, zs, zr, xs, xr, ts, tr, ls, os_) = refs[34:]
    wires = Wires(outer)
    rows = length // STEP

    def piece(item, place):
        if item in (OUT, DOWN):
            return fulls[item].at[:, pl.ds(place * block, block)]
        height = items[item].shape[0]
        return fulls[item].at[pl.ds(place * height, height)]

    def along(item, step):
        return remote(items[item], piece(item, step), zs.at[item, step], zr.at[item, step], wires.far(step))

    def beside(item, step):
        src = items[item] if step == 0 else piece(item, step)
        return remote(src, piece(item, outer + step), xs.at[item, step], xr.at[item, step], wires.peer())

    def own(item):
        return pltpu.make_async_copy(items[item], piece(item, 0), loc.at[item])

    def issue(item):
        if item < N_ITEMS:
            own(item).start()
            for step in wires.order:
                along(item, step).start()
            beside(item, 0).start()

    def pass_on(item):
        for step in wires.order:
            along(item, step).wait_recv()
            beside(item, step).start()

    def arrived(item):
        own(item).wait()
        for step in range(outer):
            beside(item, step).wait_recv()

    def load(src, dst, index):
        copy = pltpu.make_async_copy(src, dst, ls.at[index])
        copy.start()
        return copy

    stores = []

    def store(src, dst):
        copy = pltpu.make_async_copy(src, dst, os_.at[len(stores)])
        copy.start()
        stores.append(copy)
        return copy

    wires.greet()
    issue(GAINS)
    issue(QUERY)
    issue(KEY)
    loads = []
    for place in range(2 * outer):
        at = pl.multiple_of(wires.block_at(place) * block, block)
        loads.append(load(tokens.at[:, pl.ds(at, block)], wide.at[:, pl.ds(place * block, block)], place))
    first = 2 * outer
    loads.append(load(cosine, cos_v, first))
    loads.append(load(sine, sin_v, first + 1))
    loads.append(load(row_decay, rowd, first + 2))
    loads.append(load(key_decay, keyd, first + 3))
    pass_on(GAINS)
    issue(VALUE)
    arrived(GAINS)
    for copy in loads:
        copy.wait()
    copy = load(fulls[GAINS], gain_v, 0)
    copy.wait()
    group = jnp.zeros((1, heads * DV), F32)
    for place in range(2 * outer):
        line = gain_v[place * 16 : place * 16 + 1, :].astype(F32)
        gain_m[:, place * block : (place + 1) * block] = line[:, :block]
        gain_f[:, place * block : (place + 1) * block] = line[:, block : 2 * block]
        group = group + line[:, 2 * block :]
    gain_g[...] = group

    @pl.loop(0, length // 128)
    def _(r):
        at = tile(r, 128)
        mixer[at, :] = norm_rows(wide[at, :].astype(F32), gain_m[...], norm_epsilon).astype(BF16)

    mine = tile(wires.tensor, quarter)
    residual[...] = wide[mine, :].astype(F32)
    store(mixer, mixer_out)
    pass_on(QUERY)
    issue(GATE)
    pass_on(KEY)
    arrived(QUERY)
    arrived(KEY)
    narrow = heads * DK
    copy = load(fulls[QUERY], slot_a.at[:, pl.ds(0, narrow)], 0)
    other = load(fulls[KEY], slot_a.at[:, pl.ds(narrow, narrow)], 1)
    copy.wait()
    other.wait()

    @pl.loop(0, rows)
    def _(r):
        at = tile(r, STEP)
        both = jnp.dot(mixer[at, :], slot_a[...], preferred_element_type=F32)
        c, s = cos_v[at, :], sin_v[at, :]
        half = DK // 2
        for target, base in ((rq, 0), (rk, narrow)):
            for h in range(heads):
                lo = base + h * DK
                a, b = both[:, lo : lo + half], both[:, lo + half : lo + DK]
                target[at, h * DK : h * DK + half] = (a * c - b * s).astype(BF16)
                target[at, h * DK + half : (h + 1) * DK] = (a * s + b * c).astype(BF16)

    store(rq, query_out)
    store(rk, key_out)
    pass_on(VALUE)
    issue(OUT)
    arrived(VALUE)
    load(fulls[VALUE], slot_b, 0).wait()

    @pl.loop(0, rows)
    def _(r):
        at = tile(r, STEP)
        values[at, :] = jnp.dot(mixer[at, :], slot_b[...], preferred_element_type=F32).astype(BF16)

    store(values, value_out)
    for h in range(heads):
        for r in range(rows):
            at = slice(r * STEP, (r + 1) * STEP)
            upto = (r + 1) * STEP
            q = rq[at, h * DK : (h + 1) * DK]
            k = rk[:upto, h * DK : (h + 1) * DK]
            raw = lax.dot_general(q, k, (((1,), (1,)), ((), ())), preferred_element_type=F32)
            fade = rowd[at, h : h + 1] * keyd[h : h + 1, :upto]
            place = lax.broadcasted_iota(jnp.int32, (STEP, upto), 0) + r * STEP
            under = place >= lax.broadcasted_iota(jnp.int32, (STEP, upto), 1)
            scores = raw * jnp.where(under, fade, 0.0)
            total = jnp.sum(scores, axis=-1, keepdims=True)
            share = (scores * lax.rsqrt(total * total + 1.0)).astype(BF16)
            kept[at, h * DV : (h + 1) * DV] = jnp.dot(
                share, values[:upto, h * DV : (h + 1) * DV], preferred_element_type=F32
            )
    kept_store = store(kept, retained_out)
    pass_on(GATE)
    issue(HIDDEN)
    arrived(GATE)
    load(fulls[GATE], slot_a, 0).wait()

    @pl.loop(0, rows)
    def _(r):
        at = tile(r, STEP)
        gate = jnp.dot(mixer[at, :], slot_a[...], preferred_element_type=F32)
        gate_in[at, :] = gate
        for h in range(heads):
            cols = slice(h * DV, (h + 1) * DV)
            normed = norm_rows(kept[at, cols], gain_g[:, cols], group_epsilon)
            mixed[at, cols] = (silu(gate[:, cols]) * normed).astype(BF16)

    gate_store = store(gate_in, gate_out)
    store(mixed, mixed_out)
    pass_on(OUT)
    issue(UP)
    arrived(OUT)
    load(fulls[OUT], slot_o, 0).wait()

    def branch_rows(index):
        return jnp.dot(mixed[tile(index, quarter), :], slot_o[...], preferred_element_type=F32)

    def to_sibling(s):
        return remote(csend.at[s], crecv.at[s], ts.at[s], tr.at[s], wires.sibling())

    cross = remote(ysend, yrecv, ts.at[2], tr.at[2], wires.across())
    for s in (1, 0):
        owner = lax.rem(wires.row + s, 2) * 2 + 1 - wires.core
        csend[s] = branch_rows(owner).astype(BF16)
        to_sibling(s).start()
    part = branch_rows((1 - wires.row) * 2 + wires.core)
    to_sibling(1).wait_recv()
    ysend[...] = (part + crecv[1].astype(F32)).astype(BF16)
    cross.start()
    residual[...] += branch_rows(wires.tensor)
    to_sibling(0).wait_recv()
    residual[...] += crecv[0].astype(F32)
    pass_on(HIDDEN)
    issue(DOWN)
    cross.wait_recv()
    residual[...] += yrecv[...].astype(F32)
    store(residual, residual_out)
    feed_mine = wide.at[mine]

    @pl.loop(0, quarter // 128)
    def _(r):
        at = tile(r, 128)
        ysend_rows = norm_rows(residual[at, :], gain_f[...], norm_epsilon).astype(BF16)
        feed_mine[at, :] = ysend_rows

    feed_cross = remote(feed_mine, feed_mine, ts.at[3], tr.at[3], wires.across())
    feed_near = remote(feed_mine, feed_mine, ts.at[4], tr.at[4], wires.sibling())
    theirs = wide.at[tile((1 - wires.row) * 2 + wires.core, quarter)]
    feed_far = remote(theirs, theirs, ts.at[5], tr.at[5], wires.sibling())
    feed_cross.start()
    feed_near.start()
    arrived(HIDDEN)
    load(fulls[HIDDEN], slot_b, 0).wait()
    feed_cross.wait_recv()
    feed_far.start()
    feed_near.wait_recv()
    feed_far.wait_recv()
    store(wide, feed_out)
    kept_store.wait()
    gate_store.wait()

    @pl.loop(0, rows)
    def _(r):
        at = tile(r, STEP)
        kept[at, :] = jnp.dot(wide[at, :], slot_b[...], preferred_element_type=F32)

    hidden_store = pltpu.make_async_copy(kept, hidden_out, ls.at[1])
    hidden_store.start()
    pass_on(UP)
    arrived(UP)
    load(fulls[UP], slot_a, 0).wait()

    @pl.loop(0, rows)
    def _(r):
        at = tile(r, STEP)
        gate_in[at, :] = jnp.dot(wide[at, :], slot_a[...], preferred_element_type=F32)

    up_store = pltpu.make_async_copy(gate_in, up_out, ls.at[2])
    up_store.start()
    pass_on(DOWN)
    arrived(DOWN)
    hidden_store.wait()
    up_store.wait()
    for copy in stores:
        if copy is not kept_store and copy is not gate_store:
            copy.wait()
    for s in range(2):
        to_sibling(s).wait_send()
    for copy in (cross, feed_cross, feed_near, feed_far):
        copy.wait_send()
    for item in range(N_ITEMS):
        for step in range(1, outer):
            along(item, step).wait_send()
        for step in range(outer):
            beside(item, step).wait_send()


def forward_fast(dp_size, tokens, gains, tables, weights):
    outer = dp_size // 2
    length, model = tokens.shape
    block = model // dp_size
    heads = weights[0].shape[1] // DK
    units = weights[3].shape[1]
    wide = units
    shapes = [(gains.shape[0] * dp_size, gains.shape[1])]
    for place, weight in enumerate(weights):
        if place + 1 in (OUT, DOWN):
            shapes.append((weight.shape[0], model))
        else:
            shapes.append((model, weight.shape[1]))
    out_shape = [jax.ShapeDtypeStruct(s, BF16) for s in shapes]
    half = heads * DK
    for shape, kind in (
        ((length, model), BF16),
        ((length, half), BF16),
        ((length, half), BF16),
        ((length, wide), BF16),
        ((length, wide), F32),
        ((length, wide), F32),
        ((length, wide), BF16),
        ((length // 4, model), F32),
        ((length, model), BF16),
        ((length, units), F32),
        ((length, units), F32),
    ):
        out_shape.append(jax.ShapeDtypeStruct(shape, kind))
    quarter = length // 4
    dma = pltpu.SemaphoreType.DMA
    scratch = [
        pltpu.VMEM((model, wide), BF16),
        pltpu.VMEM((model, wide), BF16),
        pltpu.VMEM((wide, model), BF16),
        pltpu.VMEM((length, model), BF16),
        pltpu.VMEM((length, model), BF16),
        pltpu.VMEM((length, half), BF16),
        pltpu.VMEM((length, half), BF16),
        pltpu.VMEM((length, wide), BF16),
        pltpu.VMEM((length, wide), F32),
        pltpu.VMEM((length, wide), F32),
        pltpu.VMEM((length, wide), BF16),
        pltpu.VMEM((quarter, model), F32),
        pltpu.VMEM((2, quarter, model), BF16),
        pltpu.VMEM((2, quarter, model), BF16),
        pltpu.VMEM((quarter, model), BF16),
        pltpu.VMEM((quarter, model), BF16),
        pltpu.VMEM(tables[0].shape, F32),
        pltpu.VMEM(tables[1].shape, F32),
        pltpu.VMEM(tables[2].shape, F32),
        pltpu.VMEM(tables[3].shape, F32),
        pltpu.VMEM(shapes[0], BF16),
        pltpu.VMEM((1, model), F32),
        pltpu.VMEM((1, model), F32),
        pltpu.VMEM((1, heads * DV), F32),
        dma((N_ITEMS,)),
        dma((N_ITEMS, outer)),
        dma((N_ITEMS, outer)),
        dma((N_ITEMS, outer)),
        dma((N_ITEMS, outer)),
        dma((6,)),
        dma((6,)),
        dma((2 * outer + 4,)),
        dma((12,)),
    ]

    def kernel(*refs):
        forward_kernel(outer, heads, (length, model, block), *refs)

    results = pl.pallas_call(
        kernel,
        out_shape=out_shape,
        in_specs=[ANY] * (6 + len(weights)),
        out_specs=[ANY] * len(out_shape),
        scratch_shapes=scratch,
        compiler_params=pltpu.CompilerParams(
            collective_id=0, has_side_effects=True, vmem_limit_bytes=58 * 1024 * 1024
        ),
    )(tokens, gains, *tables, *weights)
    return results[: N_ITEMS], results[N_ITEMS:]


N_GRADS = 7
(G_DOWN, G_HIDDEN, G_UP, G_OUT, G_GATE, G_VALUE, G_BOTH) = range(N_GRADS)
SQRT_2_PI = 0.7978845608028654
CUBIC = 0.044715


def rows_dot(left, right):
    return lax.dot_general(left, right, (((0,), (0,)), ((), ())), preferred_element_type=F32)


def back_dot(left, right):
    return lax.dot_general(left, right, (((1,), (1,)), ((), ())), preferred_element_type=F32)


def norm_back(values, grads, gain, epsilon):
    center = values - jnp.mean(values, axis=-1, keepdims=True)
    inverse = lax.rsqrt(jnp.mean(center * center, axis=-1, keepdims=True) + epsilon)
    unit = center * inverse
    u = grads * gain
    mean = jnp.mean(u, axis=-1, keepdims=True)
    slope = jnp.mean(u * unit, axis=-1, keepdims=True)
    return (u - mean - unit * slope) * inverse, grads * unit


def backward_kernel(outer, heads, dims, *refs):
    length, model, block, units = dims
    quarter = length // 4
    half = model // 2
    (tokens, cotangent, gains, query_full, key_full, value_full, gate_full, out_full, hidden_full, up_full,
     down_full, mixer_in, query_in, key_in, value_in, retained_in, gate_in, mixed_in, residual_in, feed_in,
     hidden_in, up_in, turns, key_decay) = refs[:24]
    (output, tokens_out, near_out, z_land, vector_out, x_land, branch_land) = refs[24:31]
    (u0, u1, u2, u3, u4, act, hid, upg, both, fa, fb, x_ring, z_ring, x_stage, acc, csend, crecv, ysend, yrecv,
     stage, grad_q, value_q, keyd, gain_v, gain_m, gain_f, gain_g,
     vec_t, vec_tr, vec_d, vec_dr, vec_g,
     xs, xr, zs, zr, ts, tr, gs, gr, vs, vr, ls, fs, st, ac) = refs[31:]
    wires = Wires(outer)
    rows = length // STEP
    mine = tile(wires.tensor, quarter)
    near_rows = tile(wires.row * 2 + 1 - wires.core, quarter)
    across_index = (1 - wires.row) * 2 + wires.core
    across_rows = tile(across_index, quarter)
    corner_rows = tile((1 - wires.row) * 2 + 1 - wires.core, quarter)

    def load(src, dst, index):
        copy = pltpu.make_async_copy(src, dst, ls.at[index])
        copy.start()
        return copy

    def load_tall(src, dst, index):
        return [load(src.at[pl.ds(h * half, half)], dst.at[:, pl.ds(h * half, half)], index + h) for h in range(2)]

    def wait_all(copies):
        for copy in copies:
            copy.wait()

    def own_blocks(src, dst, index):
        copies = []
        for place in range(2 * outer):
            at = pl.multiple_of(wires.block_at(place) * block, block)
            copies.append(load(src.at[:, pl.ds(at, block)], dst.at[:, pl.ds(place * block, block)], index + place))
        return copies

    def true_blocks(src, dst, index):
        copies = []
        for place in range(2 * outer):
            at = pl.multiple_of(wires.block_at(place) * block, block)
            copies.append(load(src.at[:, pl.ds(place * block, block)], dst.at[:, pl.ds(at, block)], index + place))
        return copies

    def x_copy(item, s):
        return remote(x_ring.at[(item % 2) * outer + s], x_land.at[item, s], xs.at[item, s], xr.at[item, s], wires.peer())

    def z_device(s):
        return (lax.rem(wires.ring + outer - s, outer) * 2 + wires.turn, wires.tensor)

    def z_copy(item, s):
        slot = (item % 2) * (outer - 1) + s - 1
        return remote(z_ring.at[slot], z_land.at[item, s - 1], zs.at[item, s], zr.at[item, s], z_device(s))

    def columns(place):
        return pl.ds(pl.multiple_of(place * block, block), block)

    def far(item, left, right):
        @pl.loop(0, outer)
        def _(i):
            s = lax.rem(i + 1, outer)
            if item >= 2:
                x_copy(item - 2, s).wait_send()
            product = rows_dot(left[:, columns(outer + s)], right[...])
            x_ring[(item % 2) * outer + s] = product.astype(BF16)
            x_copy(item, s).start()

    def acc_copy(item):
        return pltpu.make_async_copy(acc, near_out.at[item], ac.at[item])

    def near(item, left, right):
        def landed(s):
            x_copy(item, s).wait_recv()
            copy = pltpu.make_async_copy(x_land.at[item, s], x_stage.at[lax.rem(s, 2)], st.at[item, s])
            copy.start()
            return copy

        @pl.loop(1, outer)
        def _(s):
            copy = landed(s)
            if item >= 2:
                z_copy(item - 2, s).wait_send()
            product = rows_dot(left[:, columns(s)], right[...])
            copy.wait()
            z_ring[(item % 2) * (outer - 1) + s - 1] = (product + x_stage[lax.rem(s, 2)].astype(F32)).astype(BF16)
            z_copy(item, s).start()

        copy = landed(0)
        if item >= 1:
            acc_copy(item - 1).wait()
        product = rows_dot(left[:, columns(0)], right[...])
        copy.wait()
        acc[...] = product + x_stage[0].astype(F32)
        acc_copy(item).start()

    class Round:
        def __init__(self, index):
            self.index = index
            self.cross = remote(ysend, yrecv, ts.at[index, 2], tr.at[index, 2], wires.across())

        def to_sibling(self, s):
            return remote(csend.at[s], crecv.at[s], ts.at[self.index, s], tr.at[self.index, s], wires.sibling())

        def give(self, terms):
            for s in (1, 0):
                owner = lax.rem(wires.row + s, 2) * 2 + 1 - wires.core
                for h in range(2):
                    cols = slice(h * half, (h + 1) * half)
                    csend[s, :, cols] = terms(tile(owner, quarter), h).astype(BF16)
                self.to_sibling(s).start()

        def hand_over(self, terms):
            self.to_sibling(1).wait_recv()
            for h in range(2):
                cols = slice(h * half, (h + 1) * half)
                ysend[:, cols] = (terms(across_rows, h) + crecv[1, :, cols].astype(F32)).astype(BF16)
            self.cross.start()

        def keep(self, terms, totals, add):
            for h in range(2):
                part = terms(mine, h)
                totals[h][...] = totals[h][...] + part if add else part
            self.to_sibling(0).wait_recv()
            for h in range(2):
                totals[h][...] += crecv[0, :, h * half : (h + 1) * half].astype(F32)

        def finish(self, totals):
            self.cross.wait_recv()
            for h in range(2):
                totals[h][...] += yrecv[:, h * half : (h + 1) * half].astype(F32)
            for s in range(2):
                self.to_sibling(s).wait_send()
            self.cross.wait_send()

    class Spread:
        def __init__(self, index, source, land):
            self.cross = remote(source, land.at[mine], gs.at[index, 0], gr.at[index, 0], wires.across())
            self.near = remote(source, land.at[mine], gs.at[index, 1], gr.at[index, 1], wires.sibling())
            there = land.at[across_rows]
            self.far = remote(there, there, gs.at[index, 2], gr.at[index, 2], wires.sibling())
            self.own = pltpu.make_async_copy(source, land.at[mine], gs.at[index, 3])

        def start(self):
            self.cross.start()
            self.near.start()
            self.own.start()

        def pass_on(self):
            self.cross.wait_recv()
            self.far.start()

        def sent(self):
            self.cross.wait_send()
            self.near.wait_send()
            self.own.wait()

        def end(self):
            self.far.wait_recv()
            self.far.wait_send()

    def stream(src_a, src_b, body):
        def copies(r, slot):
            at = tile(r, PART)
            return (
                pltpu.make_async_copy(src_a.at[at], fa.at[slot, pl.ds(0, PART)], fs.at[0, slot]),
                pltpu.make_async_copy(src_b.at[at], fb.at[slot], fs.at[1, slot]),
            )

        for copy in copies(0, 0):
            copy.start()

        @pl.loop(0, length // PART)
        def _(r):
            slot = lax.rem(r, 2)

            @pl.when(r + 1 < length // PART)
            def _():
                for copy in copies(r + 1, 1 - slot):
                    copy.start()

            for copy in copies(r, slot):
                copy.wait()
            body(tile(r, PART), fa.at[slot, pl.ds(0, PART)], fb.at[slot])

    wires.greet_all()
    cot_loads = own_blocks(cotangent, u0, 0)
    n = 2 * outer
    down_load = load(down_full, u1, n)
    gain_load = load(gains, gain_v, n + 1)
    feed_load = load(feed_in, u2, n + 2)
    hidden_loads = load_tall(hidden_full, u3, n + 3)
    up_loads = load_tall(up_full, u4, n + 5)
    residual_load = load(residual_in, value_q, n + 7)
    table_load = load(key_decay, keyd, n + 8)
    wait_all(cot_loads)
    down_load.wait()

    def feed_tile(at, h_ref, u_ref):
        grads = back_dot(u0[at, :], u1[...])
        h, u = h_ref[...], u_ref[...]
        inner = SQRT_2_PI * (h + CUBIC * h * h * h)
        t = jnp.tanh(inner)
        gelu = 0.5 * h * (1.0 + t)
        slope = 0.5 * (1.0 + t) + 0.5 * h * (1.0 - t * t) * (SQRT_2_PI * (1.0 + 3.0 * CUBIC * h * h))
        act[at, :] = (gelu * u).astype(BF16)
        hid[at, :] = (grads * u * slope).astype(BF16)
        upg[at, :] = (grads * gelu).astype(BF16)

    stream(hidden_in, up_in, feed_tile)
    far(G_DOWN, u0, act)
    wait_all(hidden_loads)
    wait_all(up_loads)

    def tall_terms(pairs):
        def terms(at, h):
            cols = slice(h * half, (h + 1) * half)
            total = None
            for left, right in pairs:
                part = back_dot(left[at, :], right[:, cols])
                total = part if total is None else total + part
            return total

        return terms

    feed_terms = tall_terms(((hid, u3), (upg, u4)))
    feed_round, output_round, mixer_round = Round(0), Round(1), Round(2)
    feed_round.give(feed_terms)
    feed_load.wait()
    far(G_HIDDEN, u2, hid)
    feed_round.hand_over(feed_terms)
    grad_halves = [grad_q.at[:, pl.ds(h * half, half)] for h in range(2)]
    value_halves = [value_q.at[:, pl.ds(h * half, half)] for h in range(2)]
    mixer_halves = [fa.at[h] for h in range(2)]
    feed_round.keep(feed_terms, grad_halves, False)
    table_load.wait()
    gain_load.wait()
    group = jnp.zeros((1, heads * DV), F32)
    for place in range(2 * outer):
        line = gain_v[place * 16 : place * 16 + 1, :].astype(F32)
        gain_m[:, place * block : (place + 1) * block] = line[:, :block]
        gain_f[:, place * block : (place + 1) * block] = line[:, block : 2 * block]
        group = group + line[:, 2 * block :]
    gain_g[...] = group
    vec_t[...] = jnp.zeros_like(vec_t)
    vec_d[...] = jnp.zeros_like(vec_d)
    vec_g[...] = jnp.zeros_like(vec_g)
    mixer_load = load(mixer_in, u3, n + 3)
    narrow = heads * DK
    core_loads = [load(value_in, u4.at[:, pl.ds(0, half)], n + 4),
                  load(query_in, u4.at[:, pl.ds(half, narrow)], n + 5),
                  load(key_in, u4.at[:, pl.ds(half + narrow, narrow)], n + 6)]
    residual_load.wait()
    feed_round.finish(grad_halves)

    @pl.loop(0, quarter // 128)
    def _(r):
        at = tile(r, 128)
        part, gain_part = norm_back(value_q[at, :], grad_q[at, :], gain_f[...], norm_epsilon)
        cot_at = pl.ds(pl.multiple_of(wires.tensor * quarter + r * 128, 128), 128)
        total = u0[cot_at, :].astype(F32) + part
        grad_q[at, :] = total
        stage[at, :] = total.astype(BF16)
        vec_t[1:2, :] += jnp.sum(gain_part, axis=0, keepdims=True)

    branch_spread = Spread(0, stage, branch_land)
    branch_spread.start()
    near(G_DOWN, u0, act)
    far(G_UP, u2, upg)

    def output_terms(at, h):
        return jnp.dot(act[at, :], u1[:, h * half : (h + 1) * half], preferred_element_type=F32)

    branch_spread.near.wait_recv()
    output_round.give(output_terms)
    output_round.keep(output_terms, value_halves, True)
    branch_spread.pass_on()
    output_round.hand_over(output_terms)
    branch_spread.sent()
    out_load = load(out_full, u1, n)
    branch_loads = [load(branch_land.at[at], u0.at[at], n + 7 + i) for i, at in
                    enumerate((mine, near_rows, across_rows))]
    mixed_load = load(mixed_in, act, n + 1)
    branch_spread.far.wait_recv()
    branch_loads.append(load(branch_land.at[corner_rows], u0.at[corner_rows], n + 2))
    wait_all(branch_loads)
    out_load.wait()

    hold = both

    def gate_tile(at, r_ref, g_ref):
        grads = back_dot(u0[at, :], u1[...])
        for h in range(heads):
            cols = slice(h * DV, (h + 1) * DV)
            x, g, m = r_ref[:, cols], g_ref[:, cols], grads[:, cols]
            scale = gain_g[:, cols]
            sig = 1.0 / (1.0 + jnp.exp(-g))
            swish = g * sig
            center = x - jnp.mean(x, axis=-1, keepdims=True)
            inverse = lax.rsqrt(jnp.mean(center * center, axis=-1, keepdims=True) + group_epsilon)
            unit = center * inverse
            passed = m * swish
            hid[at, cols] = (m * unit * scale * (sig * (1.0 + g * (1.0 - sig)))).astype(BF16)
            vec_g[:, cols] += jnp.sum(passed * unit, axis=0, keepdims=True)
            u = passed * scale
            mean = jnp.mean(u, axis=-1, keepdims=True)
            slope = jnp.mean(u * unit, axis=-1, keepdims=True)
            hold[at, cols] = ((u - mean - unit * slope) * inverse).astype(BF16)

    near(G_HIDDEN, u2, hid)
    stream(retained_in, gate_in, gate_tile)
    mixed_load.wait()
    far(G_OUT, u0, act)
    mixer_load.wait()
    near(G_UP, u2, upg)
    value_loads = load_tall(value_full, u2, n + 1)
    far(G_GATE, u3, hid)
    wait_all(core_loads)

    side = DK // 2
    turn_load = load(turns, fb, n + 8)
    turn_load.wait()

    def turned_back(grads, r, count):
        a, b = grads[:, :side], grads[:, side:]
        c = jnp.concatenate([fb[0, :, (r + i) * side : (r + i + 1) * side] for i in range(count)], axis=0)
        s = jnp.concatenate([fb[1, :, (r + i) * side : (r + i + 1) * side] for i in range(count)], axis=0)
        return (a * c + b * s).astype(BF16), (b * c - a * s).astype(BF16)

    for h in range(heads):
        vcols = slice(h * DV, (h + 1) * DV)
        qcols = slice(half + h * DK, half + (h + 1) * DK)
        kcols = slice(half + narrow + h * DK, half + narrow + (h + 1) * DK)
        for r in range(length // PART):
            at = slice(r * PART, (r + 1) * PART)
            upto = (r + 1) * PART
            raw = back_dot(u4[at, qcols], u4[:upto, kcols])
            place = lax.broadcasted_iota(jnp.int32, (PART, upto), 0) + r * PART
            under = place >= lax.broadcasted_iota(jnp.int32, (PART, upto), 1)
            fade = keyd[heads + h : heads + h + 1, at].reshape(PART, 1) * keyd[h : h + 1, :upto]
            fade = jnp.where(under, fade, 0.0)
            scores = raw * fade
            total = jnp.sum(scores, axis=-1, keepdims=True)
            inverse = lax.rsqrt(total * total + 1.0)
            u1[at, :upto] = (scores * inverse).astype(BF16)
            grads = back_dot(hold[at, vcols], u4[:upto, vcols])
            inner = jnp.sum(grads * scores, axis=-1, keepdims=True)
            drop = inner * total * inverse * inverse * inverse
            raw_grad = ((grads * inverse - drop) * fade).astype(BF16)
            u1[at, half : half + upto] = raw_grad
            query_grad = jnp.dot(raw_grad, u4[:upto, kcols], preferred_element_type=F32)
            lo, hi = turned_back(query_grad, r, 1)
            upg[at, h * DK : h * DK + side] = lo
            upg[at, h * DK + side : (h + 1) * DK] = hi
        for c in range(rows):
            at = slice(c * STEP, (c + 1) * STEP)
            after = slice(c * STEP, length)
            for i in range(1, STEP // PART):
                spare = slice(c * STEP, c * STEP + i * PART)
                late = slice(c * STEP + i * PART, c * STEP + (i + 1) * PART)
                u1[spare, late] = jnp.zeros((i * PART, PART), BF16)
                u1[spare, half + c * STEP + i * PART : half + c * STEP + (i + 1) * PART] = jnp.zeros(
                    (i * PART, PART), BF16
                )
            hold_grad = rows_dot(u1[after, c * STEP : (c + 1) * STEP], hold[after, vcols])
            key_grad = rows_dot(u1[after, half + c * STEP : half + (c + 1) * STEP], u4[after, qcols])
            hold[at, vcols] = hold_grad.astype(BF16)
            lo, hi = turned_back(key_grad, c * (STEP // PART), STEP // PART)
            upg[at, narrow + h * DK : narrow + h * DK + side] = lo
            upg[at, narrow + h * DK + side : narrow + (h + 1) * DK] = hi

    gate_loads = load_tall(gate_full, u1, n + 3)
    both_loads = []
    for h in range(2):
        source = pl.ds(h * half, half)
        both_loads.append(load(query_full.at[source], u4.at[:, pl.ds(h * half, narrow)], n + 5 + 2 * h))
        both_loads.append(load(key_full.at[source], u4.at[:, pl.ds(h * half + narrow, narrow)], n + 6 + 2 * h))

    output_round.finish(value_halves)
    ysend[...] = value_q[...].astype(BF16)
    wait_all(true_blocks(ysend, stage, 0))
    output_spread = Spread(1, stage, output)
    output_spread.start()
    token_loads = []
    for place in range(2 * outer):
        at = pl.multiple_of(wires.block_at(place) * block, block)
        token_loads.append(load(tokens.at[mine, pl.ds(at, block)], ysend.at[:, pl.ds(place * block, block)], place))
    wait_all(token_loads)
    for r in range(2):
        at = slice(r * (quarter // 2), (r + 1) * (quarter // 2))
        value_q[at, :] = ysend[at, :].astype(F32)
    near(G_OUT, u0, act)
    far(G_VALUE, u3, hold)
    wait_all(gate_loads)
    wait_all(both_loads)
    wait_all(value_loads)
    mixer_terms = tall_terms(((upg, u4), (hold, u2), (hid, u1)))
    output_spread.near.wait_recv()
    mixer_round.give(mixer_terms)
    output_spread.pass_on()
    mixer_round.hand_over(mixer_terms)
    mixer_round.keep(mixer_terms, mixer_halves, False)
    near(G_GATE, u3, hid)
    far(G_BOTH, u3, upg)
    mixer_round.finish(mixer_halves)
    output_spread.sent()

    @pl.loop(0, quarter // 128)
    def _(r):
        at = tile(r, 128)
        grads = jnp.concatenate([fa[0, at, :], fa[1, at, :]], axis=1)
        part, gain_part = norm_back(value_q[at, :], grads, gain_m[...], norm_epsilon)
        ysend[at, :] = (grad_q[at, :] + part).astype(BF16)
        vec_t[0:1, :] += jnp.sum(gain_part, axis=0, keepdims=True)

    def vector_team(i, device):
        return remote(vec_t, vec_tr.at[i], vs.at[i], vr.at[i], device)

    team = (wires.sibling(), wires.across(), wires.corner())
    for i, device in enumerate(team):
        vector_team(i, device).start()
    wait_all(true_blocks(ysend, stage, 0))
    tokens_spread = Spread(2, stage, tokens_out)
    tokens_spread.start()
    for i, device in enumerate(team):
        vector_team(i, device).wait_recv()
    summed = vec_t[0:2, :]
    for i in range(3):
        summed = summed + vec_tr[i, 0:2, :]
    for place in range(2 * outer):
        vec_d[place, 0:2, :] = summed[:, place * block : (place + 1) * block]
        for i in range(heads * DV // block):
            vec_d[place, 2 + i : 3 + i, :] = vec_g[:, i * block : (i + 1) * block]

    def vector_data(place):
        device = (wires.block_at(place), wires.tensor)
        return remote(vec_d.at[place], vec_dr.at[place], vs.at[3 + place], vr.at[3 + place], device)

    for place in range(1, 2 * outer):
        vector_data(place).start()
    near(G_VALUE, u3, hold)
    tokens_spread.pass_on()
    vectors = vec_d[0]
    for place in range(1, 2 * outer):
        vector_data(place).wait_recv()
        vectors = vectors + vec_dr[place]
    vec_d[0] = vectors
    vector_store = load(vec_d.at[0], vector_out, 0)
    near(G_BOTH, u3, upg)

    vector_store.wait()
    branch_spread.far.wait_send()
    output_spread.end()
    tokens_spread.near.wait_recv()
    tokens_spread.end()
    tokens_spread.sent()
    for i, device in enumerate(team):
        vector_team(i, device).wait_send()
    for place in range(1, 2 * outer):
        vector_data(place).wait_send()
    acc_copy(N_GRADS - 1).wait()
    for item in (N_GRADS - 2, N_GRADS - 1):
        for s in range(outer):
            x_copy(item, s).wait_send()
        for s in range(1, outer):
            z_copy(item, s).wait_send()
    for item in range(N_GRADS):
        for s in range(1, outer):
            z_copy(item, s).wait_recv()


def backward_fast(dp_size, tokens, cotangent, fulls, kept, tables):
    outer = dp_size // 2
    length, model = tokens.shape
    block = model // dp_size
    gains, query_full, key_full, value_full, gate_full, out_full, hidden_full, up_full, down_full = fulls
    (mixer_input, turned_query, turned_keys, values, retained, gate_in, mixed, residual, feed_input, hidden_pre,
     up_pre) = kept
    heads = query_full.shape[1] // DK
    units = hidden_full.shape[1]
    quarter = length // 4
    shape = jax.ShapeDtypeStruct
    out_shape = [
        shape((length, model), BF16),
        shape((length, model), BF16),
        shape((N_GRADS, block, units), F32),
        shape((N_GRADS, outer - 1, block, units), BF16),
        shape((8, block), F32),
        shape((N_GRADS, outer, block, units), BF16),
        shape((length, model), BF16),
    ]
    dma = pltpu.SemaphoreType.DMA
    vmem = pltpu.VMEM
    scratch = [vmem((length, model), BF16)] * 5 + [vmem((length, units), BF16)] * 4
    scratch += [vmem((2, STEP, units), F32), vmem((2, PART, units), F32)]
    scratch += [
        vmem((2 * outer, block, units), BF16),
        vmem((2 * (outer - 1), block, units), BF16),
        vmem((2, block, units), BF16),
        vmem((block, units), F32),
        vmem((2, quarter, model), BF16),
        vmem((2, quarter, model), BF16),
        vmem((quarter, model), BF16),
        vmem((quarter, model), BF16),
        vmem((quarter, model), BF16),
        vmem((quarter, model), F32),
        vmem((quarter, model), F32),
        vmem(tables[1].shape, F32),
        vmem(gains.shape, BF16),
        vmem((1, model), F32),
        vmem((1, model), F32),
        vmem((1, heads * DV), F32),
        vmem((8, model), F32),
        vmem((3, 8, model), F32),
        vmem((dp_size, 8, block), F32),
        vmem((dp_size, 8, block), F32),
        vmem((1, heads * DV), F32),
        dma((N_GRADS, outer)),
        dma((N_GRADS, outer)),
        dma((N_GRADS, outer)),
        dma((N_GRADS, outer)),
        dma((3, 3)),
        dma((3, 3)),
        dma((3, 4)),
        dma((3, 4)),
        dma((3 + dp_size,)),
        dma((3 + dp_size,)),
        dma((dp_size + 12,)),
        dma((2, 2)),
        dma((N_GRADS, outer)),
        dma((N_GRADS,)),
    ]

    def kernel(*refs):
        backward_kernel(outer, heads, (length, model, block, units), *refs)

    operands = (tokens, cotangent, *fulls, *kept, *tables)
    return pl.pallas_call(
        kernel,
        out_shape=out_shape,
        in_specs=[ANY] * len(operands),
        out_specs=[ANY] * len(out_shape),
        scratch_shapes=scratch,
        compiler_params=pltpu.CompilerParams(
            collective_id=1, has_side_effects=True, vmem_limit_bytes=63 * 1024 * 1024
        ),
    )(*operands)


def on_device(
    dp_size,
    tensor_size,
    tokens,
    mixer_gain,
    query_weight,
    key_weight,
    value_weight,
    gate_weight,
    out_weight,
    group_gain,
    feed_gain,
    hidden_weight,
    up_weight,
    down_weight,
    cotangent,
):
    data = Ring("dp", dp_size)
    team = Ring("tensor", tensor_size)
    length, model = tokens.shape
    quarter = length // tensor_size
    heads_here = query_weight.shape[1] // DK

    block = mixer_gain.shape[0]
    width = query_weight.shape[1]
    group_block = group_gain.shape[1]
    head_ids = (lax.axis_index("tensor") * heads_here + jnp.arange(heads_here)).astype(F32)
    decays = decay_table(head_ids, length)
    inputs = data.own_order(tokens, 1)
    cot = data.own_order(cotangent, 1)

    def my_rows(array):
        return lax.dynamic_slice_in_dim(array, team.me * quarter, quarter, 0)

    def row_terms(left, right):
        return lambda start, rows: plain_product(
            lax.dynamic_slice_in_dim(left, start, rows, 0), right
        )

    units = hidden_weight.shape[1]
    even = units == 2 * width == heads_here * DV == model // 2 and heads_here * DV // block <= 6
    if even and block % 128 == 0 and tensor_size == 4 and dp_size >= 8 and length % 1024 == 0:
        group_line = lax.dynamic_update_slice(
            jnp.zeros((heads_here, DV), BF16), group_gain, (0, data.me * group_block)
        )
        gains = jnp.concatenate([mixer_gain, feed_gain, group_line.reshape(-1)])
        gains = jnp.broadcast_to(gains[None, :], (16, gains.shape[0]))
        half = DK // 2
        angles = jnp.arange(length, dtype=F32)[:, None] * (
            10000.0 ** (-jnp.arange(half, dtype=F32) / half)
        )
        log_rates = jnp.log1p(-jnp.exp2(-5.0 - head_ids))
        steps = jnp.arange(length, dtype=F32)
        decay_sums = jnp.sum(decays_plain(head_ids, length), axis=-1)
        row_decay = jnp.exp(log_rates[:, None] * (steps - length // 2)) * lax.rsqrt(decay_sums) * DK ** (-0.5)
        key_decay = jnp.exp(log_rates[:, None] * (length // 2 - steps))
        tables = (jnp.cos(angles), jnp.sin(angles), row_decay.T, key_decay)
        turns = [t.reshape(length // PART, PART, half).swapaxes(0, 1).reshape(PART, -1) for t in tables[:2]]
        back_tables = (jnp.stack(turns), jnp.concatenate([key_decay, row_decay]))
        fulls, kept = forward_fast(
            dp_size,
            tokens,
            gains,
            tables,
            (query_weight, key_weight, value_weight, gate_weight, out_weight, hidden_weight, up_weight, down_weight),
        )
        output, tokens_grad, near_sums, landed, vectors, _, _ = backward_fast(
            dp_size, tokens, cotangent, fulls, kept, back_tables
        )
        sums = [near_sums[k] + jnp.sum(landed[k].astype(F32), axis=0) for k in range(N_GRADS)]
        group_scale_grad = vectors[2 : 2 + heads_here * DV // block].reshape(heads_here, DV)
        return (
            output,
            tokens_grad.astype(F32),
            vectors[0],
            sums[G_BOTH][:, :width],
            sums[G_BOTH][:, width:],
            sums[G_VALUE],
            sums[G_GATE],
            sums[G_OUT].T,
            lax.dynamic_slice_in_dim(group_scale_grad, data.me * group_block, group_block, 1),
            vectors[1],
            sums[G_HIDDEN],
            sums[G_UP],
            sums[G_DOWN].T,
        )
    else:
        gains = jnp.concatenate([mixer_gain, feed_gain, group_gain.reshape(-1)])[None, :]
        gains = data.gather(gains, 0)
        mixer_scale = gains[:, :block].reshape(-1).astype(F32)
        feed_scale = gains[:, block : 2 * block].reshape(-1).astype(F32)
        group_scale = data.true_order(gains[:, 2 * block :], 0).astype(F32)
        group_scale = group_scale.reshape(dp_size, heads_here, -1).swapaxes(0, 1).reshape(heads_here, -1)

        query_key = data.gather(jnp.concatenate([query_weight, key_weight], axis=1), 0)
        value_full = data.gather(value_weight, 0)
        gate_full = data.gather(gate_weight, 0)
        out_full = data.gather(out_weight, 1)
        hidden_full = data.gather(hidden_weight, 0)
        up_full = data.gather(up_weight, 0)
        down_full = data.gather(down_weight, 1)

        mixer_input = layer_norm(inputs.astype(F32), mixer_scale).astype(BF16)

        both = plain_product(mixer_input, query_key)
        query = both[:, :width]
        keyset = both[:, width:]
        values = plain_product(mixer_input, value_full).astype(BF16)
        gate_in = plain_product(mixer_input, gate_full)
        turned_query = rotate(query, heads_here, 1.0).astype(BF16).reshape(length, heads_here, DK)
        turned_keys = rotate(keyset, heads_here, 1.0).astype(BF16).reshape(length, heads_here, DK)
        scores, row_totals, denominators = core_scores(turned_query, turned_keys, decays)
        weights = (scores / denominators).astype(BF16)
        value_heads = values.reshape(length, heads_here, DV)
        retained = jnp.einsum("hqk,khd->qhd", weights, value_heads, preferred_element_type=F32)
        retained = retained.reshape(length, heads_here * DV)
        mixed = gate_piece(retained, gate_in, group_scale).astype(BF16)

        branch = token_sum(team, row_terms(mixed, out_full), length)
        residual = my_rows(inputs).astype(F32) + branch
        feed_input = token_gather(team, layer_norm(residual, feed_scale).astype(BF16))
        hidden_pre = plain_product(feed_input, hidden_full)
        up_pre = plain_product(feed_input, up_full)

    activity, feed_back = jax.vjp(feed_piece, hidden_pre, up_pre)
    activity = activity.astype(BF16)
    activity_grad = back_product(cot, down_full)
    hidden_grad, up_grad = feed_back(activity_grad)
    hidden_grad = hidden_grad.astype(BF16)
    up_grad = up_grad.astype(BF16)

    def feed_rows(start, rows):
        return back_product(
            lax.dynamic_slice_in_dim(hidden_grad, start, rows, 0), hidden_full
        ) + back_product(lax.dynamic_slice_in_dim(up_grad, start, rows, 0), up_full)

    feed_input_grad = token_sum(team, feed_rows, length)
    _, feed_norm_back = jax.vjp(layer_norm, residual, feed_scale)
    residual_part, feed_scale_grad = feed_norm_back(feed_input_grad)
    residual_grad = my_rows(cot).astype(F32) + residual_part
    branch_grad = token_gather(team, residual_grad.astype(BF16))

    hidden_weight_grad = data.scatter_sum(
        lambda turn: row_product(half_of(feed_input, turn, 1), hidden_grad), 0
    )
    up_weight_grad = data.scatter_sum(
        lambda turn: row_product(half_of(feed_input, turn, 1), up_grad), 0
    )
    down_grad = data.scatter_sum(lambda turn: row_product(activity, half_of(cot, turn, 1)), 1)

    feed_out = token_sum(team, row_terms(activity, down_full), length)
    output = token_gather(team, (residual + feed_out).astype(BF16))
    output = data.true_order(output, 1)

    mixed_grad = back_product(branch_grad, out_full)
    _, gate_back = jax.vjp(gate_piece, retained, gate_in, group_scale)
    retained_grad, gate_grad, group_scale_grad = gate_back(mixed_grad)
    retained_grad = retained_grad.astype(BF16)
    gate_grad = gate_grad.astype(BF16)
    out_weight_grad = data.scatter_sum(
        lambda turn: row_product(mixed, half_of(branch_grad, turn, 1)), 1
    )
    gate_weight_grad = data.scatter_sum(
        lambda turn: row_product(half_of(mixer_input, turn, 1), gate_grad), 0
    )

    grad_heads = retained_grad.reshape(length, heads_here, DV)
    weights_grad = jnp.einsum("qhd,khd->hqk", grad_heads, value_heads, preferred_element_type=F32)
    value_parts = jnp.einsum("hqk,qhd->khd", weights, grad_heads, preferred_element_type=F32)
    value_parts = value_parts.reshape(length, heads_here * DV).astype(BF16)
    value_weight_grad = data.scatter_sum(
        lambda turn: row_product(half_of(mixer_input, turn, 1), value_parts), 0
    )
    inner_totals = jnp.sum(weights_grad * scores, axis=-1, keepdims=True)
    slope = row_totals / denominators
    scores_grad = weights_grad / denominators - inner_totals / (denominators * denominators) * slope
    raw_grad = (scores_grad * DK ** (-0.5) * decays).astype(BF16)
    turned_query_grad = jnp.einsum("hqk,khd->qhd", raw_grad, turned_keys, preferred_element_type=F32)
    turned_key_grad = jnp.einsum("hqk,qhd->khd", raw_grad, turned_query, preferred_element_type=F32)
    query_parts = rotate(turned_query_grad.reshape(length, width), heads_here, -1.0).astype(BF16)
    key_parts = rotate(turned_key_grad.reshape(length, width), heads_here, -1.0).astype(BF16)
    both_parts = jnp.concatenate([query_parts, key_parts], axis=1)
    both_grad = data.scatter_sum(
        lambda turn: row_product(half_of(mixer_input, turn, 1), both_parts), 0
    )
    query_weight_grad = both_grad[:, :width]
    key_weight_grad = both_grad[:, width:]

    def mixer_rows(start, rows):
        def cut(array):
            return lax.dynamic_slice_in_dim(array, start, rows, 0)

        return (
            back_product(cut(both_parts), query_key)
            + back_product(cut(value_parts), value_full)
            + back_product(cut(gate_grad), gate_full)
        )

    mixer_input_grad = token_sum(team, mixer_rows, length)
    _, mixer_norm_back = jax.vjp(layer_norm, my_rows(inputs).astype(F32), mixer_scale)
    input_part, mixer_scale_grad = mixer_norm_back(mixer_input_grad)
    tokens_grad = token_gather(team, (residual_grad + input_part).astype(BF16))
    tokens_grad = data.true_order(tokens_grad, 1).astype(F32)

    norm_grads = jnp.concatenate([mixer_scale_grad, feed_scale_grad]).reshape(2, -1)
    norm_grads = lax.psum(data.true_order(norm_grads, 1), ("dp", "tensor"))
    norm_grads = lax.dynamic_slice_in_dim(norm_grads, data.me * block, block, 1)
    group_scale_grad = lax.psum(group_scale_grad, "dp")
    group_scale_grad = lax.dynamic_slice_in_dim(group_scale_grad, data.me * group_block, group_block, 1)
    return (
        output,
        tokens_grad,
        norm_grads[0],
        query_weight_grad,
        key_weight_grad,
        value_weight_grad,
        gate_weight_grad,
        out_weight_grad,
        group_scale_grad,
        norm_grads[1],
        hidden_weight_grad,
        up_weight_grad,
        down_grad,
    )


def solution(mesh):
    columns = P("dp", "tensor")
    rows = P("tensor", "dp")
    placed = (
        P("dp", None),
        P("dp"),
        columns,
        columns,
        columns,
        columns,
        rows,
        rows,
        P("dp"),
        columns,
        columns,
        rows,
        P("dp", None),
    )
    given = (
        P("dp", None),
        P("dp", None),
        P("dp"),
        columns,
        columns,
        columns,
        columns,
        rows,
        rows,
        P("dp"),
        columns,
        columns,
        rows,
    )

    def body(*arrays):
        return on_device(mesh.shape["dp"], mesh.shape["tensor"], *arrays)

    return jax.shard_map(body, mesh=mesh, in_specs=placed, out_specs=given, check_vma=False)
```

```python
import jax
import jax.numpy as jnp
import numpy as np
from jax import lax
from jax.experimental import pallas as pl
from jax.experimental.pallas import tpu as pltpu
from jax.sharding import PartitionSpec as P

DK = 256
DV = 512

norm_epsilon = 1e-05
group_epsilon = 0.01
F32 = jnp.float32
BF16 = jnp.bfloat16


def layer_norm(values, scale_gain, epsilon=norm_epsilon):
    center = values - jnp.mean(values, axis=-1, keepdims=True)
    spread = jnp.mean(center * center, axis=-1, keepdims=True)
    return center * lax.rsqrt(spread + epsilon) * scale_gain


def group_norm(retained, scale_gain):
    shaped = retained.reshape(retained.shape[0], scale_gain.shape[0], scale_gain.shape[1])
    return layer_norm(shaped, scale_gain, group_epsilon).reshape(retained.shape)


def rotate(values, head_count, direction):
    length = values.shape[0]
    head_width = values.shape[1] // head_count
    half_width = head_width // 2
    places = jnp.arange(length, dtype=F32)[:, None]
    speeds = 10000.0 ** (-jnp.arange(half_width, dtype=F32) / half_width)
    angles = places * speeds[None, :]
    cosine = jnp.cos(angles)[:, None, :]
    sine_part = direction * jnp.sin(angles)[:, None, :]
    shaped = values.reshape(length, head_count, 2, half_width)
    front_half = shaped[:, :, 0]
    back_half = shaped[:, :, 1]
    turned = jnp.stack(
        [front_half * cosine - back_half * sine_part, front_half * sine_part + back_half * cosine],
        axis=2,
    )
    return turned.reshape(length, head_count * head_width)


def decays_plain(head_ids, length):
    log_rates = jnp.log1p(-jnp.exp2(-5.0 - head_ids))
    row_place = jnp.arange(length)[:, None]
    key_place = jnp.arange(length)[None, :]
    distance = jnp.maximum(row_place - key_place, 0).astype(F32)
    decays = jnp.where(
        (row_place >= key_place)[None], jnp.exp(log_rates[:, None, None] * distance[None]), 0.0
    )
    return decays


def decay_table(head_ids, length):
    decays = decays_plain(head_ids, length)
    return decays * lax.rsqrt(jnp.sum(decays, axis=-1, keepdims=True))


def plain_product(left, right):
    return jnp.dot(left, right, preferred_element_type=F32)


def row_product(left, right):
    return lax.dot_general(left, right, (((0,), (0,)), ((), ())), preferred_element_type=F32)


def back_product(left, right):
    return lax.dot_general(left, right, (((1,), (1,)), ((), ())), preferred_element_type=F32)


def core_scores(turned_query, turned_keys, decays):
    raw_scores = jnp.einsum("qhd,khd->hqk", turned_query, turned_keys, preferred_element_type=F32)
    scores = raw_scores * DK ** (-0.5) * decays
    row_totals = jnp.sum(scores, axis=-1, keepdims=True)
    denominators = jnp.sqrt(row_totals * row_totals + 1.0)
    return (scores, row_totals, denominators)


def feed_piece(hidden_pre, up_pre):
    return jax.nn.gelu(hidden_pre) * up_pre


def gate_piece(retained, gate_in, group_scale):
    return jax.nn.silu(gate_in) * group_norm(retained, group_scale)


class Ring:
    def __init__(self, name, size):
        self.name = name
        self.size = size
        self.outer = size // 2
        self.me = lax.axis_index(name)
        self.swap_pairs = [(i, i ^ 1) for i in range(size)]

    def swap(self, block):
        return lax.ppermute(block, self.name, self.swap_pairs)

    def shift(self, block, step):
        pairs = [
            (i, ((i // 2 + step) % self.outer) * 2 + i % 2) for i in range(self.size)
        ]
        return lax.ppermute(block, self.name, pairs)

    def block_at(self, place):
        turn, step = place // self.outer, place % self.outer
        outer = (self.me // 2 + self.outer - step) % self.outer
        return outer * 2 + (self.me % 2 + turn) % 2

    def place_of(self, block):
        turn = (block % 2 + self.me % 2) % 2
        step = (self.me // 2 + self.outer - block // 2) % self.outer
        return turn * self.outer + step

    def own_order(self, array, axis):
        width = array.shape[axis] // self.size
        return jnp.concatenate(
            [
                lax.dynamic_slice_in_dim(array, self.block_at(p) * width, width, axis)
                for p in range(self.size)
            ],
            axis=axis,
        )

    def true_order(self, array, axis):
        width = array.shape[axis] // self.size
        return jnp.concatenate(
            [
                lax.dynamic_slice_in_dim(array, self.place_of(b) * width, width, axis)
                for b in range(self.size)
            ],
            axis=axis,
        )

    def gather(self, block, axis):
        near = jnp.concatenate(
            [block] + [self.shift(block, s) for s in range(1, self.outer)], axis=axis
        )
        return jnp.concatenate([near, self.swap(near)], axis=axis)

    def scatter_sum(self, make_half, axis):
        far = self.swap(make_half(1).astype(BF16))
        near = make_half(0) + far.astype(F32)
        width = near.shape[axis] // self.outer
        total = lax.slice_in_dim(near, 0, width, axis=axis)
        for s in range(1, self.outer):
            part = lax.slice_in_dim(near, s * width, (s + 1) * width, axis=axis).astype(BF16)
            total = total + self.shift(part, -s).astype(F32)
        return total


def half_of(array, turn, axis):
    width = array.shape[axis] // 2
    return lax.slice_in_dim(array, turn * width, (turn + 1) * width, axis=axis)


def token_sum(ring, make_rows, rows):
    width = rows // ring.size
    outer, inner = ring.me // 2, ring.me % 2
    far = [make_rows((((outer + s) % ring.outer) * 2 + 1 - inner) * width, width) for s in range(ring.outer)]
    got = ring.swap(jnp.concatenate(far, axis=0).astype(BF16)).astype(F32)
    near = [
        make_rows((((outer + s) % ring.outer) * 2 + inner) * width, width)
        + lax.slice_in_dim(got, s * width, (s + 1) * width, axis=0)
        for s in range(ring.outer)
    ]
    total = near[0]
    for s in range(1, ring.outer):
        total = total + ring.shift(near[s].astype(BF16), s).astype(F32)
    return total


def token_gather(ring, block):
    return ring.true_order(ring.gather(block, 0), 0)


MESH = pl.DeviceIdType.MESH
ANY = pl.BlockSpec(memory_space=pl.ANY)


class Wires:
    def __init__(self, outer):
        self.outer = outer
        self.dp = lax.axis_index("dp")
        self.tensor = lax.axis_index("tensor")
        self.ring = self.dp // 2
        self.turn = self.dp % 2
        self.row = self.tensor // 2
        self.core = self.tensor % 2
        self.order = [1, outer - 1] + list(range(2, outer - 1))

    def far(self, step):
        return (lax.rem(self.ring + step, self.outer) * 2 + self.turn, self.tensor)

    def peer(self):
        return (self.ring * 2 + 1 - self.turn, self.tensor)

    def sibling(self):
        return (self.dp, self.row * 2 + 1 - self.core)

    def across(self):
        return (self.dp, (1 - self.row) * 2 + self.core)

    def block_at(self, place):
        turn, step = place // self.outer, place % self.outer
        return lax.rem(self.ring + self.outer - step, self.outer) * 2 + lax.rem(self.turn + turn, 2)

    def corner(self):
        return (self.dp, (1 - self.row) * 2 + 1 - self.core)

    def greet_all(self):
        barrier = pltpu.get_barrier_semaphore()
        partners = [(self.block_at(place), self.tensor) for place in range(1, 2 * self.outer)]
        partners += [self.sibling(), self.across(), self.corner()]
        for partner in partners:
            pl.semaphore_signal(barrier, inc=1, device_id=partner, device_id_type=MESH)
        pl.semaphore_wait(barrier, len(partners))

    def greet(self):
        barrier = pltpu.get_barrier_semaphore()
        partners = [self.far(s) for s in range(1, self.outer)]
        partners += [self.peer(), self.sibling(), self.across()]
        for partner in partners:
            pl.semaphore_signal(barrier, inc=1, device_id=partner, device_id_type=MESH)
        pl.semaphore_wait(barrier, len(partners))


def remote(src, dst, send, recv, device):
    return pltpu.make_async_remote_copy(
        src_ref=src, dst_ref=dst, send_sem=send, recv_sem=recv, device_id=device, device_id_type=MESH
    )


def tile(index, rows):
    return pl.ds(pl.multiple_of(index * rows, rows), rows)


def norm_rows(values, gain, epsilon):
    center = values - jnp.mean(values, axis=-1, keepdims=True)
    spread = jnp.mean(center * center, axis=-1, keepdims=True)
    return center * lax.rsqrt(spread + epsilon) * gain


def silu(v):
    return v * (1.0 / (1.0 + jnp.exp(-v)))


N_ITEMS = 9
GAINS, QUERY, KEY, VALUE, GATE, OUT, HIDDEN, UP, DOWN = range(N_ITEMS)
STEP = 256
PART = 128


def forward_kernel(outer, heads, dims, *refs):
    length, model, block = dims
    quarter = length // 4
    tokens, cotangent, gains, cosine, sine, row_decay, key_decay = refs[:7]
    items = (gains,) + refs[7:15]
    fulls = refs[15:24]
    (mixer_out, query_out, key_out, value_out, retained_out, gate_out, mixed_out, residual_out,
     feed_out, hidden_out, up_out, activity_out) = refs[24:36]
    (slot_a, slot_b, slot_o, wide, mixer, rq, rk, values, kept, gate_in, mixed, residual, csend, crecv, ysend,
     yrecv, cos_v, sin_v, rowd, keyd, gain_v, gain_m, gain_f, gain_g,
     loc, zs, zr, xs, xr, ts, tr, ls, os_) = refs[36:]
    wires = Wires(outer)
    rows = length // STEP
    units = slot_a.shape[1]

    def piece(item, place):
        if item in (OUT, DOWN):
            return fulls[item].at[:, pl.ds(place * block, block)]
        height = items[item].shape[0]
        return fulls[item].at[pl.ds(place * height, height)]

    last = outer - 1
    up = wires.ring < last
    down = wires.ring > 0

    def along(item, source, place, step):
        device = (jnp.clip(wires.ring + step, 0, last) * 2 + wires.turn, wires.tensor)
        return remote(source, piece(item, place), zs.at[item, place], zr.at[item, place], device)

    def climb(item, source, base):
        @pl.when(up)
        def _():
            along(item, source, base + 1, 1).start()

        @pl.when(down)
        def _():
            along(item, source, base + last, -1).start()

    def beside(item, step):
        src = items[item] if step == 0 else piece(item, step)
        return remote(src, piece(item, outer + step), xs.at[item, step], xr.at[item, step], wires.peer())

    def own(item):
        return pltpu.make_async_copy(items[item], piece(item, 0), loc.at[item])

    def issue(item, cross=True):
        own(item).start()
        climb(item, items[item], 0)
        if cross:
            beside(item, 0).start()

    def hops(item, base, cross, which=None):
        for hop in which or range(1, outer):
            @pl.when(hop <= wires.ring)
            def _():
                along(item, piece(item, base + hop), base + hop, 1).wait_recv()
                if hop < last:
                    @pl.when(up)
                    def _():
                        along(item, piece(item, base + hop), base + hop + 1, 1).start()
                if cross:
                    beside(item, hop).start()

            @pl.when(hop <= last - wires.ring)
            def _():
                place = outer - hop
                along(item, piece(item, base + place), base + place, 1).wait_recv()
                if hop < last:
                    @pl.when(down)
                    def _():
                        along(item, piece(item, base + place), base + place - 1, -1).start()
                if cross:
                    beside(item, place).start()

    def pass_on(item):
        hops(item, 0, item != DOWN)

    def climb_sent(item, base):
        @pl.when(up)
        def _():
            along(item, piece(item, base), base + 1, 1).wait_send()

        @pl.when(down)
        def _():
            along(item, piece(item, base), base + last, -1).wait_send()

        for hop in range(1, last):
            @pl.when((hop <= wires.ring) & up)
            def _():
                along(item, piece(item, base + hop), base + hop + 1, 1).wait_send()

            @pl.when((hop <= last - wires.ring) & down)
            def _():
                along(item, piece(item, base + outer - hop), base + outer - hop - 1, -1).wait_send()

    def arrived(item):
        own(item).wait()
        for step in range(outer if item != DOWN else 1):
            beside(item, step).wait_recv()

    def load(src, dst, index):
        copy = pltpu.make_async_copy(src, dst, ls.at[index])
        copy.start()
        return copy

    stores = []

    def store(src, dst):
        copy = pltpu.make_async_copy(src, dst, os_.at[len(stores)])
        copy.start()
        stores.append(copy)
        return copy

    wires.greet()
    issue(GAINS)
    issue(QUERY)
    issue(KEY)
    issue(VALUE)
    beside(DOWN, 0).start()

    def own_blocks(source, target):
        copies = []
        for place in range(2 * outer):
            at = pl.multiple_of(wires.block_at(place) * block, block)
            copies.append(load(source.at[:, pl.ds(at, block)], target.at[:, pl.ds(place * block, block)], place))
        return copies

    first = 2 * outer
    loads = own_blocks(tokens, wide)
    loads.append(load(cosine, cos_v, first))
    loads.append(load(sine, sin_v, first + 1))
    loads.append(load(row_decay, rowd, first + 2))
    loads.append(load(key_decay, keyd, first + 3))
    pass_on(GAINS)
    arrived(GAINS)
    for copy in loads:
        copy.wait()
    copy = load(fulls[GAINS], gain_v, 0)
    copy.wait()
    group = jnp.zeros((1, heads * DV), F32)
    for place in range(2 * outer):
        line = gain_v[place * 16 : place * 16 + 1, :].astype(F32)
        gain_m[:, place * block : (place + 1) * block] = line[:, :block]
        gain_f[:, place * block : (place + 1) * block] = line[:, block : 2 * block]
        group = group + line[:, 2 * block :]
    gain_g[...] = group

    @pl.loop(0, length // 128)
    def _(r):
        at = tile(r, 128)
        mixer[at, :] = norm_rows(wide[at, :].astype(F32), gain_m[...], norm_epsilon).astype(BF16)

    mine = tile(wires.tensor, quarter)
    residual[...] = wide[mine, :].astype(F32)
    mixer_store = store(mixer, mixer_out)
    pass_on(QUERY)
    pass_on(KEY)
    issue(GATE)
    pass_on(VALUE)
    issue(OUT)
    arrived(QUERY)
    arrived(KEY)
    narrow = heads * DK
    copy = load(fulls[QUERY], slot_a.at[:, pl.ds(0, narrow)], 0)
    other = load(fulls[KEY], slot_a.at[:, pl.ds(narrow, narrow)], 1)
    copy.wait()
    other.wait()

    @pl.loop(0, rows)
    def _(r):
        at = tile(r, STEP)
        both = jnp.dot(mixer[at, :], slot_a[...], preferred_element_type=F32)
        c, s = cos_v[at, :], sin_v[at, :]
        half = DK // 2
        for target, base in ((rq, 0), (rk, narrow)):
            for h in range(heads):
                lo = base + h * DK
                a, b = both[:, lo : lo + half], both[:, lo + half : lo + DK]
                target[at, h * DK : h * DK + half] = (a * c - b * s).astype(BF16)
                target[at, h * DK + half : (h + 1) * DK] = (a * s + b * c).astype(BF16)

    store(rq, query_out)
    store(rk, key_out)
    pass_on(GATE)
    issue(HIDDEN)
    arrived(VALUE)
    load(fulls[VALUE], slot_b, 0).wait()

    @pl.loop(0, rows)
    def _(r):
        at = tile(r, STEP)
        values[at, :] = jnp.dot(mixer[at, :], slot_b[...], preferred_element_type=F32).astype(BF16)

    store(values, value_out)
    for h in range(heads):
        for r in range(rows):
            at = slice(r * STEP, (r + 1) * STEP)
            upto = (r + 1) * STEP
            q = rq[at, h * DK : (h + 1) * DK]
            k = rk[:upto, h * DK : (h + 1) * DK]
            raw = lax.dot_general(q, k, (((1,), (1,)), ((), ())), preferred_element_type=F32)
            fade = rowd[at, h : h + 1] * keyd[h : h + 1, :upto]
            place = lax.broadcasted_iota(jnp.int32, (STEP, upto), 0) + r * STEP
            under = place >= lax.broadcasted_iota(jnp.int32, (STEP, upto), 1)
            scores = raw * jnp.where(under, fade, 0.0)
            total = jnp.sum(scores, axis=-1, keepdims=True)
            share = (scores * lax.rsqrt(total * total + 1.0)).astype(BF16)
            kept[at, h * DV : (h + 1) * DV] = jnp.dot(
                share, values[:upto, h * DV : (h + 1) * DV], preferred_element_type=F32
            )
    kept_store = store(kept, retained_out)
    pass_on(OUT)
    issue(UP)
    arrived(GATE)
    load(fulls[GATE], slot_a, 0).wait()

    @pl.loop(0, rows)
    def _(r):
        at = tile(r, STEP)
        gate = jnp.dot(mixer[at, :], slot_a[...], preferred_element_type=F32)
        gate_in[at, :] = gate
        for h in range(heads):
            cols = slice(h * DV, (h + 1) * DV)
            normed = norm_rows(kept[at, cols], gain_g[:, cols], group_epsilon)
            mixed[at, cols] = (silu(gate[:, cols]) * normed).astype(BF16)

    gate_store = store(gate_in, gate_out)
    mixed_store = store(mixed, mixed_out)
    pass_on(HIDDEN)
    issue(DOWN, False)
    arrived(DOWN)
    climb(DOWN, piece(DOWN, outer), outer)
    arrived(OUT)
    load(fulls[OUT], slot_o, 0).wait()

    def branch_rows(index):
        return jnp.dot(mixed[tile(index, quarter), :], slot_o[...], preferred_element_type=F32)

    def to_sibling(s):
        return remote(csend.at[s], crecv.at[s], ts.at[s], tr.at[s], wires.sibling())

    cross = remote(ysend, yrecv, ts.at[2], tr.at[2], wires.across())
    for s in (1, 0):
        owner = lax.rem(wires.row + s, 2) * 2 + 1 - wires.core
        csend[s] = branch_rows(owner).astype(BF16)
        to_sibling(s).start()
    part = branch_rows((1 - wires.row) * 2 + wires.core)
    to_sibling(1).wait_recv()
    ysend[...] = (part + crecv[1].astype(F32)).astype(BF16)
    cross.start()
    residual[...] += branch_rows(wires.tensor)
    to_sibling(0).wait_recv()
    residual[...] += crecv[0].astype(F32)
    pass_on(UP)
    hops(DOWN, 0, False, (1,))
    cross.wait_recv()
    residual[...] += yrecv[...].astype(F32)
    store(residual, residual_out)
    feed_mine = wide.at[mine]

    @pl.loop(0, quarter // 128)
    def _(r):
        at = tile(r, 128)
        ysend_rows = norm_rows(residual[at, :], gain_f[...], norm_epsilon).astype(BF16)
        feed_mine[at, :] = ysend_rows

    feed_cross = remote(feed_mine, feed_mine, ts.at[3], tr.at[3], wires.across())
    feed_near = remote(feed_mine, feed_mine, ts.at[4], tr.at[4], wires.sibling())
    theirs = wide.at[tile((1 - wires.row) * 2 + wires.core, quarter)]
    feed_far = remote(theirs, theirs, ts.at[5], tr.at[5], wires.sibling())
    feed_cross.start()
    feed_near.start()
    hops(DOWN, 0, False, (2, 3))
    hops(DOWN, outer, False, (1,))
    feed_cross.wait_recv()
    feed_far.start()
    mixer_store.wait()
    cot_loads = own_blocks(cotangent, mixer)
    hops(DOWN, outer, False, (2,))
    arrived(HIDDEN)
    load(fulls[HIDDEN], slot_b, first).wait()
    feed_near.wait_recv()
    feed_far.wait_recv()
    store(wide, feed_out)
    kept_store.wait()
    gate_store.wait()

    @pl.loop(0, rows)
    def _(r):
        at = tile(r, STEP)
        kept[at, :] = jnp.dot(wide[at, :], slot_b[...], preferred_element_type=F32)

    hops(DOWN, outer, False, (3,))
    load(fulls[DOWN], slot_o, first).wait()
    for copy in cot_loads:
        copy.wait()

    @pl.loop(0, rows)
    def _(r):
        at = tile(r, STEP)
        gate_in[at, :] = lax.dot_general(
            mixer[at, :], slot_o[...], (((1,), (1,)), ((), ())), preferred_element_type=F32
        )

    arrived(UP)
    load(fulls[UP], slot_a, first).wait()
    mixed_store.wait()

    @pl.loop(0, length // PART)
    def _(r):
        at = tile(r, PART)
        u = jnp.dot(wide[at, :], slot_a[...], preferred_element_type=F32)
        h, grads = kept[at, :], gate_in[at, :]
        t = jnp.tanh(SQRT_2_PI * (h + CUBIC * h * h * h))
        gelu = 0.5 * h * (1.0 + t)
        slope = 0.5 * (1.0 + t) + 0.5 * h * (1.0 - t * t) * (SQRT_2_PI * (1.0 + 3.0 * CUBIC * h * h))
        mixed[at, :] = (gelu * u).astype(BF16)
        slot_b[at, :] = (grads * u * slope).astype(BF16)
        slot_o[at, pl.ds(0, units)] = (grads * gelu).astype(BF16)

    store(mixed, activity_out)
    store(slot_b.at[pl.ds(0, length)], hidden_out)
    store(slot_o.at[:, pl.ds(0, units)], up_out)
    for copy in stores:
        if not any(copy is done for done in (kept_store, gate_store, mixer_store, mixed_store)):
            copy.wait()
    for s in range(2):
        to_sibling(s).wait_send()
    for copy in (cross, feed_cross, feed_near, feed_far):
        copy.wait_send()
    for item in range(N_ITEMS):
        climb_sent(item, 0)
        for step in range(outer if item != DOWN else 1):
            beside(item, step).wait_send()
    climb_sent(DOWN, outer)


def position_tables(length, heads):
    half = DK // 2
    speeds = 10000.0 ** (-np.arange(half, dtype=np.float32) / np.float32(half))
    angles = np.arange(length, dtype=np.float32)[:, None] * speeds.astype(np.float32)[None, :]
    pair = [np.cos(angles), np.sin(angles)]
    turns = [t.reshape(length // PART, PART, half).swapaxes(0, 1).reshape(PART, -1) for t in pair]
    rates = np.log1p(-np.exp2(-5.0 - np.arange(heads, dtype=np.float64)))[:, None]
    places = np.arange(length, dtype=np.float64)[None, :]
    sums = np.expm1(rates * (places + 1)) / np.expm1(rates)
    row_decay = np.exp(rates * (places - length // 2)) / np.sqrt(sums) * DK**-0.5
    key_decay = np.exp(rates * (length // 2 - places))
    return [jnp.asarray(np.asarray(t, np.float32)) for t in (*pair, np.stack(turns), row_decay, key_decay)]


def forward_fast(dp_size, tokens, cotangent, gains, tables, weights):
    outer = dp_size // 2
    length, model = tokens.shape
    block = model // dp_size
    heads = weights[0].shape[1] // DK
    units = weights[3].shape[1]
    wide = units
    shapes = [(gains.shape[0] * dp_size, gains.shape[1])]
    for place, weight in enumerate(weights):
        if place + 1 in (OUT, DOWN):
            shapes.append((weight.shape[0], model))
        else:
            shapes.append((model, weight.shape[1]))
    out_shape = [jax.ShapeDtypeStruct(s, BF16) for s in shapes]
    half = heads * DK
    for shape, kind in (
        ((length, model), BF16),
        ((length, half), BF16),
        ((length, half), BF16),
        ((length, wide), BF16),
        ((length, wide), F32),
        ((length, wide), F32),
        ((length, wide), BF16),
        ((length // 4, model), F32),
        ((length, model), BF16),
        ((length, units), BF16),
        ((length, units), BF16),
        ((length, units), BF16),
    ):
        out_shape.append(jax.ShapeDtypeStruct(shape, kind))
    quarter = length // 4
    dma = pltpu.SemaphoreType.DMA
    scratch = [
        pltpu.VMEM((model, wide), BF16),
        pltpu.VMEM((model, wide), BF16),
        pltpu.VMEM((wide, model), BF16),
        pltpu.VMEM((length, model), BF16),
        pltpu.VMEM((length, model), BF16),
        pltpu.VMEM((length, half), BF16),
        pltpu.VMEM((length, half), BF16),
        pltpu.VMEM((length, wide), BF16),
        pltpu.VMEM((length, wide), F32),
        pltpu.VMEM((length, wide), F32),
        pltpu.VMEM((length, wide), BF16),
        pltpu.VMEM((quarter, model), F32),
        pltpu.VMEM((2, quarter, model), BF16),
        pltpu.VMEM((2, quarter, model), BF16),
        pltpu.VMEM((quarter, model), BF16),
        pltpu.VMEM((quarter, model), BF16),
        pltpu.VMEM(tables[0].shape, F32),
        pltpu.VMEM(tables[1].shape, F32),
        pltpu.VMEM(tables[2].shape, F32),
        pltpu.VMEM(tables[3].shape, F32),
        pltpu.VMEM(shapes[0], BF16),
        pltpu.VMEM((1, model), F32),
        pltpu.VMEM((1, model), F32),
        pltpu.VMEM((1, heads * DV), F32),
        dma((N_ITEMS,)),
        dma((N_ITEMS, 2 * outer)),
        dma((N_ITEMS, 2 * outer)),
        dma((N_ITEMS, outer)),
        dma((N_ITEMS, outer)),
        dma((6,)),
        dma((6,)),
        dma((2 * outer + 4,)),
        dma((14,)),
    ]

    def kernel(*refs):
        forward_kernel(outer, heads, (length, model, block), *refs)

    results = pl.pallas_call(
        kernel,
        out_shape=out_shape,
        in_specs=[ANY] * (7 + len(weights)),
        out_specs=[ANY] * len(out_shape),
        scratch_shapes=scratch,
        compiler_params=pltpu.CompilerParams(
            collective_id=0, has_side_effects=True, vmem_limit_bytes=58 * 1024 * 1024
        ),
    )(tokens, cotangent, gains, *tables, *weights)
    return results[: N_ITEMS], results[N_ITEMS:]


N_GRADS = 7
(G_DOWN, G_HIDDEN, G_UP, G_OUT, G_GATE, G_VALUE, G_BOTH) = range(N_GRADS)
FLOW = (2, 3, 0, 1)
SQRT_2_PI = 0.7978845608028654
CUBIC = 0.044715


def rows_dot(left, right):
    return lax.dot_general(left, right, (((0,), (0,)), ((), ())), preferred_element_type=F32)


def back_dot(left, right):
    return lax.dot_general(left, right, (((1,), (1,)), ((), ())), preferred_element_type=F32)


def norm_back(values, grads, gain, epsilon):
    center = values - jnp.mean(values, axis=-1, keepdims=True)
    inverse = lax.rsqrt(jnp.mean(center * center, axis=-1, keepdims=True) + epsilon)
    unit = center * inverse
    u = grads * gain
    mean = jnp.mean(u, axis=-1, keepdims=True)
    slope = jnp.mean(u * unit, axis=-1, keepdims=True)
    return (u - mean - unit * slope) * inverse, grads * unit


def backward_kernel(outer, heads, dims, *refs):
    length, model, block, units = dims
    quarter = length // 4
    half = model // 2
    (tokens, cotangent, gains, query_full, key_full, value_full, gate_full, out_full, hidden_full, up_full,
     down_full, mixer_in, query_in, key_in, value_in, retained_in, gate_in, mixed_in, residual_in, feed_in,
     hidden_in, up_in, activity_in, turns, key_decay) = refs[:25]
    (output, tokens_out, near_out, z_land, vector_out, x_land, branch_land) = refs[25:32]
    (u0, u1, u2, u3, u4, act, hid, upg, both, fa, fb, x_ring, z_ring, x_stage, acc, csend, crecv, ysend, yrecv,
     stage, grad_q, value_q, keyd, gain_v, gain_m, gain_f, gain_g,
     vec_t, vec_tr, vec_d, vec_dr, vec_g,
     xs, xr, zs, zr, ts, tr, gs, gr, vs, vr, ls, fs, st, ac) = refs[32:]
    wires = Wires(outer)
    rows = length // STEP
    mine = tile(wires.tensor, quarter)
    near_rows = tile(wires.row * 2 + 1 - wires.core, quarter)
    across_index = (1 - wires.row) * 2 + wires.core
    across_rows = tile(across_index, quarter)
    corner_rows = tile((1 - wires.row) * 2 + 1 - wires.core, quarter)

    def load(src, dst, index):
        copy = pltpu.make_async_copy(src, dst, ls.at[index])
        copy.start()
        return copy

    def load_tall(src, dst, index):
        return [load(src.at[pl.ds(h * half, half)], dst.at[:, pl.ds(h * half, half)], index + h) for h in range(2)]

    def wait_all(copies):
        for copy in copies:
            copy.wait()

    def own_blocks(src, dst, index):
        copies = []
        for place in range(2 * outer):
            at = pl.multiple_of(wires.block_at(place) * block, block)
            copies.append(load(src.at[:, pl.ds(at, block)], dst.at[:, pl.ds(place * block, block)], index + place))
        return copies

    def true_blocks(src, dst, index):
        copies = []
        for place in range(2 * outer):
            at = pl.multiple_of(wires.block_at(place) * block, block)
            copies.append(load(src.at[:, pl.ds(place * block, block)], dst.at[:, pl.ds(at, block)], index + place))
        return copies

    def x_copy(item, s):
        return remote(x_ring.at[(item % 2) * outer + s], x_land.at[item, s], xs.at[item, s], xr.at[item, s], wires.peer())

    def z_copy(item, s):
        step = outer - 1 if s != outer - 1 else 1
        device = (lax.rem(wires.ring + step, outer) * 2 + wires.turn, wires.tensor)
        slot = (item % 2) * (outer - 1) + s - 1
        return remote(z_ring.at[slot], z_land.at[item, s - 1], zs.at[item, s], zr.at[item, s], device)

    def columns(place):
        return pl.ds(pl.multiple_of(place * block, block), block)

    def far(item, left, right):
        for s in FLOW:
            if item >= 2:
                x_copy(item - 2, s).wait_send()
            product = rows_dot(left[:, columns(outer + s)], right[...])
            x_ring[(item % 2) * outer + s] = product.astype(BF16)
            x_copy(item, s).start()

    def acc_copy(item):
        return pltpu.make_async_copy(acc, near_out.at[item], ac.at[item])

    def near(item, left, right):
        def staged(place, source):
            copy = pltpu.make_async_copy(source, x_stage.at[place], st.at[item, place])
            copy.start()
            return copy

        for s in FLOW:
            x_copy(item, s).wait_recv()
            copy = staged(s % 2, x_land.at[item, s])
            if s and item >= 2:
                z_copy(item - 2, s).wait_send()
            if s == 0 and item >= 1:
                acc_copy(item - 1).wait()
            product = rows_dot(left[:, columns(s)], right[...])
            copy.wait()
            product = product + x_stage[s % 2].astype(F32)
            if s == 0:
                acc[...] = product
                acc_copy(item).start()
                continue
            if s == 1:
                z_copy(item, 2).wait_recv()
                copy = staged(2, z_land.at[item, 1])
                copy.wait()
                product = product + x_stage[2].astype(F32)
            z_ring[(item % 2) * (outer - 1) + s - 1] = product.astype(BF16)
            z_copy(item, s).start()

    class Round:
        def __init__(self, index):
            self.index = index
            self.cross = remote(ysend, yrecv, ts.at[index, 2], tr.at[index, 2], wires.across())

        def to_sibling(self, s):
            return remote(csend.at[s], crecv.at[s], ts.at[self.index, s], tr.at[self.index, s], wires.sibling())

        def give(self, terms):
            for s in (1, 0):
                owner = lax.rem(wires.row + s, 2) * 2 + 1 - wires.core
                for h in range(2):
                    cols = slice(h * half, (h + 1) * half)
                    csend[s, :, cols] = terms(tile(owner, quarter), h).astype(BF16)
                self.to_sibling(s).start()

        def hand_over(self, terms):
            self.to_sibling(1).wait_recv()
            for h in range(2):
                cols = slice(h * half, (h + 1) * half)
                ysend[:, cols] = (terms(across_rows, h) + crecv[1, :, cols].astype(F32)).astype(BF16)
            self.cross.start()

        def keep(self, terms, totals, add):
            for h in range(2):
                part = terms(mine, h)
                totals[h][...] = totals[h][...] + part if add else part
            self.to_sibling(0).wait_recv()
            for h in range(2):
                totals[h][...] += crecv[0, :, h * half : (h + 1) * half].astype(F32)

        def finish(self, totals):
            self.cross.wait_recv()
            for h in range(2):
                totals[h][...] += yrecv[:, h * half : (h + 1) * half].astype(F32)
            for s in range(2):
                self.to_sibling(s).wait_send()
            self.cross.wait_send()

    class Spread:
        def __init__(self, index, source, land):
            self.cross = remote(source, land.at[mine], gs.at[index, 0], gr.at[index, 0], wires.across())
            self.near = remote(source, land.at[mine], gs.at[index, 1], gr.at[index, 1], wires.sibling())
            there = land.at[across_rows]
            self.far = remote(there, there, gs.at[index, 2], gr.at[index, 2], wires.sibling())
            self.own = pltpu.make_async_copy(source, land.at[mine], gs.at[index, 3])

        def start(self):
            self.cross.start()
            self.near.start()
            self.own.start()

        def pass_on(self):
            self.cross.wait_recv()
            self.far.start()

        def sent(self):
            self.cross.wait_send()
            self.near.wait_send()
            self.own.wait()

        def end(self):
            self.far.wait_recv()
            self.far.wait_send()

    def stream(src_a, src_b, body):
        def copies(r, slot):
            at = tile(r, PART)
            return (
                pltpu.make_async_copy(src_a.at[at], fa.at[slot, pl.ds(0, PART)], fs.at[0, slot]),
                pltpu.make_async_copy(src_b.at[at], fb.at[slot], fs.at[1, slot]),
            )

        for copy in copies(0, 0):
            copy.start()

        @pl.loop(0, length // PART)
        def _(r):
            slot = lax.rem(r, 2)

            @pl.when(r + 1 < length // PART)
            def _():
                for copy in copies(r + 1, 1 - slot):
                    copy.start()

            for copy in copies(r, slot):
                copy.wait()
            body(tile(r, PART), fa.at[slot, pl.ds(0, PART)], fb.at[slot])

    wires.greet_all()
    n = 2 * outer
    act_load = load(activity_in, act, n + 9)
    cot_loads = own_blocks(cotangent, u0, 0)
    hid_load = load(hidden_in, hid, n + 10)
    upg_load = load(up_in, upg, n + 11)
    hidden_loads = load_tall(hidden_full, u3, n + 3)
    up_loads = load_tall(up_full, u4, n + 5)
    feed_load = load(feed_in, u2, n + 2)
    down_load = load(down_full, u1, n)
    gain_load = load(gains, gain_v, n + 1)
    residual_load = load(residual_in, value_q, n + 7)
    table_load = load(key_decay, keyd, n + 8)
    act_load.wait()
    wait_all(cot_loads)
    far(G_DOWN, u0, act)
    hid_load.wait()
    upg_load.wait()
    wait_all(hidden_loads)
    wait_all(up_loads)

    def tall_terms(pairs):
        def terms(at, h):
            cols = slice(h * half, (h + 1) * half)
            total = None
            for left, right in pairs:
                part = back_dot(left[at, :], right[:, cols])
                total = part if total is None else total + part
            return total

        return terms

    feed_terms = tall_terms(((hid, u3), (upg, u4)))
    feed_round, output_round, mixer_round = Round(0), Round(1), Round(2)
    feed_round.give(feed_terms)
    feed_load.wait()
    far(G_HIDDEN, u2, hid)
    feed_round.hand_over(feed_terms)
    grad_halves = [grad_q.at[:, pl.ds(h * half, half)] for h in range(2)]
    value_halves = [value_q.at[:, pl.ds(h * half, half)] for h in range(2)]
    mixer_halves = [fa.at[h] for h in range(2)]
    feed_round.keep(feed_terms, grad_halves, False)
    table_load.wait()
    gain_load.wait()
    group = jnp.zeros((1, heads * DV), F32)
    for place in range(2 * outer):
        line = gain_v[place * 16 : place * 16 + 1, :].astype(F32)
        gain_m[:, place * block : (place + 1) * block] = line[:, :block]
        gain_f[:, place * block : (place + 1) * block] = line[:, block : 2 * block]
        group = group + line[:, 2 * block :]
    gain_g[...] = group
    vec_t[...] = jnp.zeros_like(vec_t)
    vec_d[...] = jnp.zeros_like(vec_d)
    vec_g[...] = jnp.zeros_like(vec_g)
    mixer_load = load(mixer_in, u3, n + 3)
    narrow = heads * DK
    core_loads = [load(value_in, u4.at[:, pl.ds(0, half)], n + 4),
                  load(query_in, u4.at[:, pl.ds(half, narrow)], n + 5),
                  load(key_in, u4.at[:, pl.ds(half + narrow, narrow)], n + 6)]
    residual_load.wait()
    feed_round.finish(grad_halves)

    @pl.loop(0, quarter // 128)
    def _(r):
        at = tile(r, 128)
        part, gain_part = norm_back(value_q[at, :], grad_q[at, :], gain_f[...], norm_epsilon)
        cot_at = pl.ds(pl.multiple_of(wires.tensor * quarter + r * 128, 128), 128)
        total = u0[cot_at, :].astype(F32) + part
        grad_q[at, :] = total
        stage[at, :] = total.astype(BF16)
        vec_t[1:2, :] += jnp.sum(gain_part, axis=0, keepdims=True)

    branch_spread = Spread(0, stage, branch_land)
    branch_spread.start()
    near(G_DOWN, u0, act)
    far(G_UP, u2, upg)

    down_load.wait()

    def output_terms(at, h):
        return jnp.dot(act[at, :], u1[:, h * half : (h + 1) * half], preferred_element_type=F32)

    branch_spread.near.wait_recv()
    output_round.give(output_terms)
    output_round.keep(output_terms, value_halves, True)
    branch_spread.pass_on()
    output_round.hand_over(output_terms)
    branch_spread.sent()
    out_load = load(out_full, u1, n)
    branch_loads = [load(branch_land.at[at], u0.at[at], n + 7 + i) for i, at in
                    enumerate((mine, near_rows, across_rows))]
    mixed_load = load(mixed_in, act, n + 1)
    branch_spread.far.wait_recv()
    branch_loads.append(load(branch_land.at[corner_rows], u0.at[corner_rows], n + 2))
    wait_all(branch_loads)
    out_load.wait()

    hold = both

    def gate_tile(at, r_ref, g_ref):
        grads = back_dot(u0[at, :], u1[...])
        for h in range(heads):
            cols = slice(h * DV, (h + 1) * DV)
            x, g, m = r_ref[:, cols], g_ref[:, cols], grads[:, cols]
            scale = gain_g[:, cols]
            sig = 1.0 / (1.0 + jnp.exp(-g))
            swish = g * sig
            center = x - jnp.mean(x, axis=-1, keepdims=True)
            inverse = lax.rsqrt(jnp.mean(center * center, axis=-1, keepdims=True) + group_epsilon)
            unit = center * inverse
            passed = m * swish
            hid[at, cols] = (m * unit * scale * (sig * (1.0 + g * (1.0 - sig)))).astype(BF16)
            vec_g[:, cols] += jnp.sum(passed * unit, axis=0, keepdims=True)
            u = passed * scale
            mean = jnp.mean(u, axis=-1, keepdims=True)
            slope = jnp.mean(u * unit, axis=-1, keepdims=True)
            hold[at, cols] = ((u - mean - unit * slope) * inverse).astype(BF16)

    near(G_HIDDEN, u2, hid)
    stream(retained_in, gate_in, gate_tile)
    mixed_load.wait()
    far(G_OUT, u0, act)
    mixer_load.wait()
    near(G_UP, u2, upg)
    value_loads = load_tall(value_full, u2, n + 1)
    far(G_GATE, u3, hid)
    wait_all(core_loads)

    side = DK // 2
    turn_load = load(turns, fb, n + 8)
    turn_load.wait()

    def turned_back(grads, r, count):
        a, b = grads[:, :side], grads[:, side:]
        c = jnp.concatenate([fb[0, :, (r + i) * side : (r + i + 1) * side] for i in range(count)], axis=0)
        s = jnp.concatenate([fb[1, :, (r + i) * side : (r + i + 1) * side] for i in range(count)], axis=0)
        return (a * c + b * s).astype(BF16), (b * c - a * s).astype(BF16)

    for h in range(heads):
        vcols = slice(h * DV, (h + 1) * DV)
        qcols = slice(half + h * DK, half + (h + 1) * DK)
        kcols = slice(half + narrow + h * DK, half + narrow + (h + 1) * DK)
        for r in range(length // PART):
            at = slice(r * PART, (r + 1) * PART)
            upto = (r + 1) * PART
            raw = back_dot(u4[at, qcols], u4[:upto, kcols])
            place = lax.broadcasted_iota(jnp.int32, (PART, upto), 0) + r * PART
            under = place >= lax.broadcasted_iota(jnp.int32, (PART, upto), 1)
            fade = keyd[heads + h : heads + h + 1, at].reshape(PART, 1) * keyd[h : h + 1, :upto]
            fade = jnp.where(under, fade, 0.0)
            scores = raw * fade
            total = jnp.sum(scores, axis=-1, keepdims=True)
            inverse = lax.rsqrt(total * total + 1.0)
            u1[at, :upto] = (scores * inverse).astype(BF16)
            grads = back_dot(hold[at, vcols], u4[:upto, vcols])
            inner = jnp.sum(grads * scores, axis=-1, keepdims=True)
            drop = inner * total * inverse * inverse * inverse
            raw_grad = ((grads * inverse - drop) * fade).astype(BF16)
            u1[at, half : half + upto] = raw_grad
            query_grad = jnp.dot(raw_grad, u4[:upto, kcols], preferred_element_type=F32)
            lo, hi = turned_back(query_grad, r, 1)
            upg[at, h * DK : h * DK + side] = lo
            upg[at, h * DK + side : (h + 1) * DK] = hi
        for c in range(rows):
            at = slice(c * STEP, (c + 1) * STEP)
            after = slice(c * STEP, length)
            for i in range(1, STEP // PART):
                spare = slice(c * STEP, c * STEP + i * PART)
                late = slice(c * STEP + i * PART, c * STEP + (i + 1) * PART)
                u1[spare, late] = jnp.zeros((i * PART, PART), BF16)
                u1[spare, half + c * STEP + i * PART : half + c * STEP + (i + 1) * PART] = jnp.zeros(
                    (i * PART, PART), BF16
                )
            hold_grad = rows_dot(u1[after, c * STEP : (c + 1) * STEP], hold[after, vcols])
            key_grad = rows_dot(u1[after, half + c * STEP : half + (c + 1) * STEP], u4[after, qcols])
            hold[at, vcols] = hold_grad.astype(BF16)
            lo, hi = turned_back(key_grad, c * (STEP // PART), STEP // PART)
            upg[at, narrow + h * DK : narrow + h * DK + side] = lo
            upg[at, narrow + h * DK + side : narrow + (h + 1) * DK] = hi

    gate_loads = load_tall(gate_full, u1, n + 3)
    both_loads = []
    for h in range(2):
        source = pl.ds(h * half, half)
        both_loads.append(load(query_full.at[source], u4.at[:, pl.ds(h * half, narrow)], n + 5 + 2 * h))
        both_loads.append(load(key_full.at[source], u4.at[:, pl.ds(h * half + narrow, narrow)], n + 6 + 2 * h))

    output_round.finish(value_halves)
    ysend[...] = value_q[...].astype(BF16)
    wait_all(true_blocks(ysend, stage, 0))
    output_spread = Spread(1, stage, output)
    output_spread.start()
    token_loads = []
    for place in range(2 * outer):
        at = pl.multiple_of(wires.block_at(place) * block, block)
        token_loads.append(load(tokens.at[mine, pl.ds(at, block)], ysend.at[:, pl.ds(place * block, block)], place))
    wait_all(token_loads)
    for r in range(2):
        at = slice(r * (quarter // 2), (r + 1) * (quarter // 2))
        value_q[at, :] = ysend[at, :].astype(F32)
    near(G_OUT, u0, act)
    far(G_VALUE, u3, hold)
    wait_all(gate_loads)
    wait_all(both_loads)
    wait_all(value_loads)
    mixer_terms = tall_terms(((upg, u4), (hold, u2), (hid, u1)))
    output_spread.near.wait_recv()
    mixer_round.give(mixer_terms)
    output_spread.pass_on()
    mixer_round.hand_over(mixer_terms)
    mixer_round.keep(mixer_terms, mixer_halves, False)
    near(G_GATE, u3, hid)
    far(G_BOTH, u3, upg)
    mixer_round.finish(mixer_halves)
    output_spread.sent()

    @pl.loop(0, quarter // 128)
    def _(r):
        at = tile(r, 128)
        grads = jnp.concatenate([fa[0, at, :], fa[1, at, :]], axis=1)
        part, gain_part = norm_back(value_q[at, :], grads, gain_m[...], norm_epsilon)
        ysend[at, :] = (grad_q[at, :] + part).astype(BF16)
        vec_t[0:1, :] += jnp.sum(gain_part, axis=0, keepdims=True)

    def vector_team(i, device):
        return remote(vec_t, vec_tr.at[i], vs.at[i], vr.at[i], device)

    team = (wires.sibling(), wires.across(), wires.corner())
    for i, device in enumerate(team):
        vector_team(i, device).start()
    wait_all(true_blocks(ysend, stage, 0))
    tokens_spread = Spread(2, stage, tokens_out)
    tokens_spread.start()
    for i, device in enumerate(team):
        vector_team(i, device).wait_recv()
    summed = vec_t[0:2, :]
    for i in range(3):
        summed = summed + vec_tr[i, 0:2, :]
    for place in range(2 * outer):
        vec_d[place, 0:2, :] = summed[:, place * block : (place + 1) * block]
        for i in range(heads * DV // block):
            vec_d[place, 2 + i : 3 + i, :] = vec_g[:, i * block : (i + 1) * block]

    def vector_data(place):
        device = (wires.block_at(place), wires.tensor)
        return remote(vec_d.at[place], vec_dr.at[place], vs.at[3 + place], vr.at[3 + place], device)

    for place in range(1, 2 * outer):
        vector_data(place).start()
    near(G_VALUE, u3, hold)
    tokens_spread.pass_on()
    vectors = vec_d[0]
    for place in range(1, 2 * outer):
        vector_data(place).wait_recv()
        vectors = vectors + vec_dr[place]
    vec_d[0] = vectors
    vector_store = load(vec_d.at[0], vector_out, 0)
    near(G_BOTH, u3, upg)

    vector_store.wait()
    branch_spread.far.wait_send()
    output_spread.end()
    tokens_spread.near.wait_recv()
    tokens_spread.end()
    tokens_spread.sent()
    for i, device in enumerate(team):
        vector_team(i, device).wait_send()
    for place in range(1, 2 * outer):
        vector_data(place).wait_send()
    acc_copy(N_GRADS - 1).wait()
    for item in (N_GRADS - 2, N_GRADS - 1):
        for s in range(outer):
            x_copy(item, s).wait_send()
        for s in range(1, outer):
            z_copy(item, s).wait_send()
    for item in range(N_GRADS):
        for s in (1, outer - 1):
            z_copy(item, s).wait_recv()


def backward_fast(dp_size, tokens, cotangent, fulls, kept, tables):
    outer = dp_size // 2
    length, model = tokens.shape
    block = model // dp_size
    gains, query_full, key_full, value_full, gate_full, out_full, hidden_full, up_full, down_full = fulls
    (mixer_input, turned_query, turned_keys, values, retained, gate_in, mixed, residual, feed_input, hidden_pre,
     up_pre, activity) = kept
    heads = query_full.shape[1] // DK
    units = hidden_full.shape[1]
    quarter = length // 4
    shape = jax.ShapeDtypeStruct
    out_shape = [
        shape((length, model), BF16),
        shape((length, model), BF16),
        shape((N_GRADS, block, units), F32),
        shape((N_GRADS, outer - 1, block, units), BF16),
        shape((8, block), F32),
        shape((N_GRADS, outer, block, units), BF16),
        shape((length, model), BF16),
    ]
    dma = pltpu.SemaphoreType.DMA
    vmem = pltpu.VMEM
    scratch = [vmem((length, model), BF16)] * 5 + [vmem((length, units), BF16)] * 4
    scratch += [vmem((2, STEP, units), F32), vmem((2, PART, units), F32)]
    scratch += [
        vmem((2 * outer, block, units), BF16),
        vmem((2 * (outer - 1), block, units), BF16),
        vmem((3, block, units), BF16),
        vmem((block, units), F32),
        vmem((2, quarter, model), BF16),
        vmem((2, quarter, model), BF16),
        vmem((quarter, model), BF16),
        vmem((quarter, model), BF16),
        vmem((quarter, model), BF16),
        vmem((quarter, model), F32),
        vmem((quarter, model), F32),
        vmem(tables[1].shape, F32),
        vmem(gains.shape, BF16),
        vmem((1, model), F32),
        vmem((1, model), F32),
        vmem((1, heads * DV), F32),
        vmem((8, model), F32),
        vmem((3, 8, model), F32),
        vmem((dp_size, 8, block), F32),
        vmem((dp_size, 8, block), F32),
        vmem((1, heads * DV), F32),
        dma((N_GRADS, outer)),
        dma((N_GRADS, outer)),
        dma((N_GRADS, outer)),
        dma((N_GRADS, outer)),
        dma((3, 3)),
        dma((3, 3)),
        dma((3, 4)),
        dma((3, 4)),
        dma((3 + dp_size,)),
        dma((3 + dp_size,)),
        dma((dp_size + 12,)),
        dma((2, 2)),
        dma((N_GRADS, outer)),
        dma((N_GRADS,)),
    ]

    def kernel(*refs):
        backward_kernel(outer, heads, (length, model, block, units), *refs)

    operands = (tokens, cotangent, *fulls, *kept, *tables)
    return pl.pallas_call(
        kernel,
        out_shape=out_shape,
        in_specs=[ANY] * len(operands),
        out_specs=[ANY] * len(out_shape),
        scratch_shapes=scratch,
        compiler_params=pltpu.CompilerParams(
            collective_id=1, has_side_effects=True, vmem_limit_bytes=63 * 1024 * 1024
        ),
    )(*operands)


def on_device(
    dp_size,
    tensor_size,
    tokens,
    mixer_gain,
    query_weight,
    key_weight,
    value_weight,
    gate_weight,
    out_weight,
    group_gain,
    feed_gain,
    hidden_weight,
    up_weight,
    down_weight,
    cotangent,
):
    data = Ring("dp", dp_size)
    team = Ring("tensor", tensor_size)
    length, model = tokens.shape
    quarter = length // tensor_size
    heads_here = query_weight.shape[1] // DK

    block = mixer_gain.shape[0]
    width = query_weight.shape[1]
    group_block = group_gain.shape[1]
    head_ids = (lax.axis_index("tensor") * heads_here + jnp.arange(heads_here)).astype(F32)
    decays = decay_table(head_ids, length)
    inputs = data.own_order(tokens, 1)
    cot = data.own_order(cotangent, 1)

    def my_rows(array):
        return lax.dynamic_slice_in_dim(array, team.me * quarter, quarter, 0)

    def row_terms(left, right):
        return lambda start, rows: plain_product(
            lax.dynamic_slice_in_dim(left, start, rows, 0), right
        )

    units = hidden_weight.shape[1]
    even = units == 2 * width == heads_here * DV == model // 2 and heads_here * DV // block <= 6
    if even and block % 128 == 0 and tensor_size == 4 and dp_size == 8 and length % 1024 == 0:
        group_line = lax.dynamic_update_slice(
            jnp.zeros((heads_here, DV), BF16), group_gain, (0, data.me * group_block)
        )
        gains = jnp.concatenate([mixer_gain, feed_gain, group_line.reshape(-1)])
        gains = jnp.broadcast_to(gains[None, :], (16, gains.shape[0]))
        cosine, sine, turns, row_decays, key_decays = position_tables(length, query_weight.shape[1] * tensor_size // DK)
        first = lax.axis_index("tensor") * heads_here
        row_decay = lax.dynamic_slice_in_dim(row_decays, first, heads_here, 0)
        key_decay = lax.dynamic_slice_in_dim(key_decays, first, heads_here, 0)
        tables = (cosine, sine, row_decay.T, key_decay)
        back_tables = (turns, jnp.concatenate([key_decay, row_decay]))
        fulls, kept = forward_fast(
            dp_size,
            tokens,
            cotangent,
            gains,
            tables,
            (query_weight, key_weight, value_weight, gate_weight, out_weight, hidden_weight, up_weight, down_weight),
        )
        output, tokens_grad, near_sums, landed, vectors, _, _ = backward_fast(
            dp_size, tokens, cotangent, fulls, kept, back_tables
        )
        sums = [near_sums[k] + landed[k, 0].astype(F32) + landed[k, 2].astype(F32) for k in range(N_GRADS)]
        group_scale_grad = vectors[2 : 2 + heads_here * DV // block].reshape(heads_here, DV)
        return (
            output,
            tokens_grad.astype(F32),
            vectors[0],
            sums[G_BOTH][:, :width],
            sums[G_BOTH][:, width:],
            sums[G_VALUE],
            sums[G_GATE],
            sums[G_OUT].T,
            lax.dynamic_slice_in_dim(group_scale_grad, data.me * group_block, group_block, 1),
            vectors[1],
            sums[G_HIDDEN],
            sums[G_UP],
            sums[G_DOWN].T,
        )
    else:
        gains = jnp.concatenate([mixer_gain, feed_gain, group_gain.reshape(-1)])[None, :]
        gains = data.gather(gains, 0)
        mixer_scale = gains[:, :block].reshape(-1).astype(F32)
        feed_scale = gains[:, block : 2 * block].reshape(-1).astype(F32)
        group_scale = data.true_order(gains[:, 2 * block :], 0).astype(F32)
        group_scale = group_scale.reshape(dp_size, heads_here, -1).swapaxes(0, 1).reshape(heads_here, -1)

        query_key = data.gather(jnp.concatenate([query_weight, key_weight], axis=1), 0)
        value_full = data.gather(value_weight, 0)
        gate_full = data.gather(gate_weight, 0)
        out_full = data.gather(out_weight, 1)
        hidden_full = data.gather(hidden_weight, 0)
        up_full = data.gather(up_weight, 0)
        down_full = data.gather(down_weight, 1)

        mixer_input = layer_norm(inputs.astype(F32), mixer_scale).astype(BF16)

        both = plain_product(mixer_input, query_key)
        query = both[:, :width]
        keyset = both[:, width:]
        values = plain_product(mixer_input, value_full).astype(BF16)
        gate_in = plain_product(mixer_input, gate_full)
        turned_query = rotate(query, heads_here, 1.0).astype(BF16).reshape(length, heads_here, DK)
        turned_keys = rotate(keyset, heads_here, 1.0).astype(BF16).reshape(length, heads_here, DK)
        scores, row_totals, denominators = core_scores(turned_query, turned_keys, decays)
        weights = (scores / denominators).astype(BF16)
        value_heads = values.reshape(length, heads_here, DV)
        retained = jnp.einsum("hqk,khd->qhd", weights, value_heads, preferred_element_type=F32)
        retained = retained.reshape(length, heads_here * DV)
        mixed = gate_piece(retained, gate_in, group_scale).astype(BF16)

        branch = token_sum(team, row_terms(mixed, out_full), length)
        residual = my_rows(inputs).astype(F32) + branch
        feed_input = token_gather(team, layer_norm(residual, feed_scale).astype(BF16))
        hidden_pre = plain_product(feed_input, hidden_full)
        up_pre = plain_product(feed_input, up_full)

    activity, feed_back = jax.vjp(feed_piece, hidden_pre, up_pre)
    activity = activity.astype(BF16)
    activity_grad = back_product(cot, down_full)
    hidden_grad, up_grad = feed_back(activity_grad)
    hidden_grad = hidden_grad.astype(BF16)
    up_grad = up_grad.astype(BF16)

    def feed_rows(start, rows):
        return back_product(
            lax.dynamic_slice_in_dim(hidden_grad, start, rows, 0), hidden_full
        ) + back_product(lax.dynamic_slice_in_dim(up_grad, start, rows, 0), up_full)

    feed_input_grad = token_sum(team, feed_rows, length)
    _, feed_norm_back = jax.vjp(layer_norm, residual, feed_scale)
    residual_part, feed_scale_grad = feed_norm_back(feed_input_grad)
    residual_grad = my_rows(cot).astype(F32) + residual_part
    branch_grad = token_gather(team, residual_grad.astype(BF16))

    hidden_weight_grad = data.scatter_sum(
        lambda turn: row_product(half_of(feed_input, turn, 1), hidden_grad), 0
    )
    up_weight_grad = data.scatter_sum(
        lambda turn: row_product(half_of(feed_input, turn, 1), up_grad), 0
    )
    down_grad = data.scatter_sum(lambda turn: row_product(activity, half_of(cot, turn, 1)), 1)

    feed_out = token_sum(team, row_terms(activity, down_full), length)
    output = token_gather(team, (residual + feed_out).astype(BF16))
    output = data.true_order(output, 1)

    mixed_grad = back_product(branch_grad, out_full)
    _, gate_back = jax.vjp(gate_piece, retained, gate_in, group_scale)
    retained_grad, gate_grad, group_scale_grad = gate_back(mixed_grad)
    retained_grad = retained_grad.astype(BF16)
    gate_grad = gate_grad.astype(BF16)
    out_weight_grad = data.scatter_sum(
        lambda turn: row_product(mixed, half_of(branch_grad, turn, 1)), 1
    )
    gate_weight_grad = data.scatter_sum(
        lambda turn: row_product(half_of(mixer_input, turn, 1), gate_grad), 0
    )

    grad_heads = retained_grad.reshape(length, heads_here, DV)
    weights_grad = jnp.einsum("qhd,khd->hqk", grad_heads, value_heads, preferred_element_type=F32)
    value_parts = jnp.einsum("hqk,qhd->khd", weights, grad_heads, preferred_element_type=F32)
    value_parts = value_parts.reshape(length, heads_here * DV).astype(BF16)
    value_weight_grad = data.scatter_sum(
        lambda turn: row_product(half_of(mixer_input, turn, 1), value_parts), 0
    )
    inner_totals = jnp.sum(weights_grad * scores, axis=-1, keepdims=True)
    slope = row_totals / denominators
    scores_grad = weights_grad / denominators - inner_totals / (denominators * denominators) * slope
    raw_grad = (scores_grad * DK ** (-0.5) * decays).astype(BF16)
    turned_query_grad = jnp.einsum("hqk,khd->qhd", raw_grad, turned_keys, preferred_element_type=F32)
    turned_key_grad = jnp.einsum("hqk,qhd->khd", raw_grad, turned_query, preferred_element_type=F32)
    query_parts = rotate(turned_query_grad.reshape(length, width), heads_here, -1.0).astype(BF16)
    key_parts = rotate(turned_key_grad.reshape(length, width), heads_here, -1.0).astype(BF16)
    both_parts = jnp.concatenate([query_parts, key_parts], axis=1)
    both_grad = data.scatter_sum(
        lambda turn: row_product(half_of(mixer_input, turn, 1), both_parts), 0
    )
    query_weight_grad = both_grad[:, :width]
    key_weight_grad = both_grad[:, width:]

    def mixer_rows(start, rows):
        def cut(array):
            return lax.dynamic_slice_in_dim(array, start, rows, 0)

        return (
            back_product(cut(both_parts), query_key)
            + back_product(cut(value_parts), value_full)
            + back_product(cut(gate_grad), gate_full)
        )

    mixer_input_grad = token_sum(team, mixer_rows, length)
    _, mixer_norm_back = jax.vjp(layer_norm, my_rows(inputs).astype(F32), mixer_scale)
    input_part, mixer_scale_grad = mixer_norm_back(mixer_input_grad)
    tokens_grad = token_gather(team, (residual_grad + input_part).astype(BF16))
    tokens_grad = data.true_order(tokens_grad, 1).astype(F32)

    norm_grads = jnp.concatenate([mixer_scale_grad, feed_scale_grad]).reshape(2, -1)
    norm_grads = lax.psum(data.true_order(norm_grads, 1), ("dp", "tensor"))
    norm_grads = lax.dynamic_slice_in_dim(norm_grads, data.me * block, block, 1)
    group_scale_grad = lax.psum(group_scale_grad, "dp")
    group_scale_grad = lax.dynamic_slice_in_dim(group_scale_grad, data.me * group_block, group_block, 1)
    return (
        output,
        tokens_grad,
        norm_grads[0],
        query_weight_grad,
        key_weight_grad,
        value_weight_grad,
        gate_weight_grad,
        out_weight_grad,
        group_scale_grad,
        norm_grads[1],
        hidden_weight_grad,
        up_weight_grad,
        down_grad,
    )


def solution(mesh):
    columns = P("dp", "tensor")
    rows = P("tensor", "dp")
    placed = (
        P("dp", None),
        P("dp"),
        columns,
        columns,
        columns,
        columns,
        rows,
        rows,
        P("dp"),
        columns,
        columns,
        rows,
        P("dp", None),
    )
    given = (
        P("dp", None),
        P("dp", None),
        P("dp"),
        columns,
        columns,
        columns,
        columns,
        rows,
        rows,
        P("dp"),
        columns,
        columns,
        rows,
    )

    def body(*arrays):
        return on_device(mesh.shape["dp"], mesh.shape["tensor"], *arrays)

    return jax.shard_map(body, mesh=mesh, in_specs=placed, out_specs=given, check_vma=False)
```

```python
import jax
import jax.numpy as jnp
import numpy as np
from jax import lax
from jax.experimental import pallas as pl
from jax.experimental.pallas import tpu as pltpu
from jax.sharding import PartitionSpec as P

DK = 256
DV = 512

norm_epsilon = 1e-05
group_epsilon = 0.01
F32 = jnp.float32
BF16 = jnp.bfloat16


def layer_norm(values, scale_gain, epsilon=norm_epsilon):
    center = values - jnp.mean(values, axis=-1, keepdims=True)
    spread = jnp.mean(center * center, axis=-1, keepdims=True)
    return center * lax.rsqrt(spread + epsilon) * scale_gain


def group_norm(retained, scale_gain):
    shaped = retained.reshape(retained.shape[0], scale_gain.shape[0], scale_gain.shape[1])
    return layer_norm(shaped, scale_gain, group_epsilon).reshape(retained.shape)


def rotate(values, head_count, direction):
    length = values.shape[0]
    head_width = values.shape[1] // head_count
    half_width = head_width // 2
    places = jnp.arange(length, dtype=F32)[:, None]
    speeds = 10000.0 ** (-jnp.arange(half_width, dtype=F32) / half_width)
    angles = places * speeds[None, :]
    cosine = jnp.cos(angles)[:, None, :]
    sine_part = direction * jnp.sin(angles)[:, None, :]
    shaped = values.reshape(length, head_count, 2, half_width)
    front_half = shaped[:, :, 0]
    back_half = shaped[:, :, 1]
    turned = jnp.stack(
        [front_half * cosine - back_half * sine_part, front_half * sine_part + back_half * cosine],
        axis=2,
    )
    return turned.reshape(length, head_count * head_width)


def decays_plain(head_ids, length):
    log_rates = jnp.log1p(-jnp.exp2(-5.0 - head_ids))
    row_place = jnp.arange(length)[:, None]
    key_place = jnp.arange(length)[None, :]
    distance = jnp.maximum(row_place - key_place, 0).astype(F32)
    decays = jnp.where(
        (row_place >= key_place)[None], jnp.exp(log_rates[:, None, None] * distance[None]), 0.0
    )
    return decays


def decay_table(head_ids, length):
    decays = decays_plain(head_ids, length)
    return decays * lax.rsqrt(jnp.sum(decays, axis=-1, keepdims=True))


def plain_product(left, right):
    return jnp.dot(left, right, preferred_element_type=F32)


def row_product(left, right):
    return lax.dot_general(left, right, (((0,), (0,)), ((), ())), preferred_element_type=F32)


def back_product(left, right):
    return lax.dot_general(left, right, (((1,), (1,)), ((), ())), preferred_element_type=F32)


def core_scores(turned_query, turned_keys, decays):
    raw_scores = jnp.einsum("qhd,khd->hqk", turned_query, turned_keys, preferred_element_type=F32)
    scores = raw_scores * DK ** (-0.5) * decays
    row_totals = jnp.sum(scores, axis=-1, keepdims=True)
    denominators = jnp.sqrt(row_totals * row_totals + 1.0)
    return (scores, row_totals, denominators)


def feed_piece(hidden_pre, up_pre):
    return jax.nn.gelu(hidden_pre) * up_pre


def gate_piece(retained, gate_in, group_scale):
    return jax.nn.silu(gate_in) * group_norm(retained, group_scale)


class Ring:
    def __init__(self, name, size):
        self.name = name
        self.size = size
        self.outer = size // 2
        self.me = lax.axis_index(name)
        self.swap_pairs = [(i, i ^ 1) for i in range(size)]

    def swap(self, block):
        return lax.ppermute(block, self.name, self.swap_pairs)

    def shift(self, block, step):
        pairs = [
            (i, ((i // 2 + step) % self.outer) * 2 + i % 2) for i in range(self.size)
        ]
        return lax.ppermute(block, self.name, pairs)

    def block_at(self, place):
        turn, step = place // self.outer, place % self.outer
        outer = (self.me // 2 + self.outer - step) % self.outer
        return outer * 2 + (self.me % 2 + turn) % 2

    def place_of(self, block):
        turn = (block % 2 + self.me % 2) % 2
        step = (self.me // 2 + self.outer - block // 2) % self.outer
        return turn * self.outer + step

    def own_order(self, array, axis):
        width = array.shape[axis] // self.size
        return jnp.concatenate(
            [
                lax.dynamic_slice_in_dim(array, self.block_at(p) * width, width, axis)
                for p in range(self.size)
            ],
            axis=axis,
        )

    def true_order(self, array, axis):
        width = array.shape[axis] // self.size
        return jnp.concatenate(
            [
                lax.dynamic_slice_in_dim(array, self.place_of(b) * width, width, axis)
                for b in range(self.size)
            ],
            axis=axis,
        )

    def gather(self, block, axis):
        near = jnp.concatenate(
            [block] + [self.shift(block, s) for s in range(1, self.outer)], axis=axis
        )
        return jnp.concatenate([near, self.swap(near)], axis=axis)

    def scatter_sum(self, make_half, axis):
        far = self.swap(make_half(1).astype(BF16))
        near = make_half(0) + far.astype(F32)
        width = near.shape[axis] // self.outer
        total = lax.slice_in_dim(near, 0, width, axis=axis)
        for s in range(1, self.outer):
            part = lax.slice_in_dim(near, s * width, (s + 1) * width, axis=axis).astype(BF16)
            total = total + self.shift(part, -s).astype(F32)
        return total


def half_of(array, turn, axis):
    width = array.shape[axis] // 2
    return lax.slice_in_dim(array, turn * width, (turn + 1) * width, axis=axis)


def token_sum(ring, make_rows, rows):
    width = rows // ring.size
    outer, inner = ring.me // 2, ring.me % 2
    far = [make_rows((((outer + s) % ring.outer) * 2 + 1 - inner) * width, width) for s in range(ring.outer)]
    got = ring.swap(jnp.concatenate(far, axis=0).astype(BF16)).astype(F32)
    near = [
        make_rows((((outer + s) % ring.outer) * 2 + inner) * width, width)
        + lax.slice_in_dim(got, s * width, (s + 1) * width, axis=0)
        for s in range(ring.outer)
    ]
    total = near[0]
    for s in range(1, ring.outer):
        total = total + ring.shift(near[s].astype(BF16), s).astype(F32)
    return total


def token_gather(ring, block):
    return ring.true_order(ring.gather(block, 0), 0)


MESH = pl.DeviceIdType.MESH
ANY = pl.BlockSpec(memory_space=pl.ANY)


class Wires:
    def __init__(self, outer):
        self.outer = outer
        self.dp = lax.axis_index("dp")
        self.tensor = lax.axis_index("tensor")
        self.ring = self.dp // 2
        self.turn = self.dp % 2
        self.row = self.tensor // 2
        self.core = self.tensor % 2
        self.order = [1, outer - 1] + list(range(2, outer - 1))

    def far(self, step):
        return (lax.rem(self.ring + step, self.outer) * 2 + self.turn, self.tensor)

    def peer(self):
        return (self.ring * 2 + 1 - self.turn, self.tensor)

    def sibling(self):
        return (self.dp, self.row * 2 + 1 - self.core)

    def across(self):
        return (self.dp, (1 - self.row) * 2 + self.core)

    def block_at(self, place):
        turn, step = place // self.outer, place % self.outer
        return lax.rem(self.ring + self.outer - step, self.outer) * 2 + lax.rem(self.turn + turn, 2)

    def corner(self):
        return (self.dp, (1 - self.row) * 2 + 1 - self.core)

    def greet_all(self):
        barrier = pltpu.get_barrier_semaphore()
        partners = [(self.block_at(place), self.tensor) for place in range(1, 2 * self.outer)]
        partners += [self.sibling(), self.across(), self.corner()]
        for partner in partners:
            pl.semaphore_signal(barrier, inc=1, device_id=partner, device_id_type=MESH)
        pl.semaphore_wait(barrier, len(partners))


def remote(src, dst, send, recv, device):
    return pltpu.make_async_remote_copy(
        src_ref=src, dst_ref=dst, send_sem=send, recv_sem=recv, device_id=device, device_id_type=MESH
    )


def tile(index, rows):
    return pl.ds(pl.multiple_of(index * rows, rows), rows)


def norm_rows(values, gain, epsilon):
    center = values - jnp.mean(values, axis=-1, keepdims=True)
    spread = jnp.mean(center * center, axis=-1, keepdims=True)
    return center * lax.rsqrt(spread + epsilon) * gain


def silu(v):
    return v * (1.0 / (1.0 + jnp.exp(-v)))


N_ITEMS = 9
GAINS, QUERY, KEY, VALUE, GATE, OUT, HIDDEN, UP, DOWN = range(N_ITEMS)
STEP = 256
PART = 128


def forward_kernel(outer, heads, dims, *refs):
    length, model, block = dims
    quarter = length // 4
    tokens, cotangent, gains, cosine, sine, row_decay, key_decay = refs[:7]
    items = (gains,) + refs[7:15]
    fulls = refs[15:24]
    (mixer_out, query_out, key_out, value_out, retained_out, gate_out, mixed_out, residual_out,
     feed_out, hidden_out, up_out, activity_out) = refs[24:36]
    (slot_a, slot_b, slot_o, wide, mixer, rq, rk, values, kept, gate_in, mixed, residual, csend, crecv, ysend,
     yrecv, cos_v, sin_v, rowd, keyd, gain_v, gain_m, gain_f, gain_g,
     loc, zs, zr, xs, xr, ts, tr, ls, os_) = refs[36:]
    wires = Wires(outer)
    rows = length // STEP
    units = slot_a.shape[1]

    def piece(item, place):
        if item in (OUT, DOWN):
            return fulls[item].at[:, pl.ds(place * block, block)]
        height = items[item].shape[0]
        return fulls[item].at[pl.ds(place * height, height)]

    last = outer - 1
    up = wires.ring < last
    down = wires.ring > 0

    def along(item, source, place, step):
        device = (jnp.clip(wires.ring + step, 0, last) * 2 + wires.turn, wires.tensor)
        return remote(source, piece(item, place), zs.at[item, place], zr.at[item, place], device)

    def climb(item, source, base):
        @pl.when(up)
        def _():
            along(item, source, base + 1, 1).start()

        @pl.when(down)
        def _():
            along(item, source, base + last, -1).start()

    def beside(item, step):
        src = items[item] if step == 0 else piece(item, step)
        return remote(src, piece(item, outer + step), xs.at[item, step], xr.at[item, step], wires.peer())

    def own(item):
        return pltpu.make_async_copy(items[item], piece(item, 0), loc.at[item])

    def issue(item, cross=True):
        climb(item, items[item], 0)
        if cross:
            beside(item, 0).start()

    def hops(item, base, cross, which=None):
        for hop in which or range(1, outer):
            @pl.when(hop <= wires.ring)
            def _():
                along(item, piece(item, base + hop), base + hop, 1).wait_recv()
                if hop < last:
                    @pl.when(up)
                    def _():
                        along(item, piece(item, base + hop), base + hop + 1, 1).start()
                if cross:
                    beside(item, hop).start()

            @pl.when(hop <= last - wires.ring)
            def _():
                place = outer - hop
                along(item, piece(item, base + place), base + place, 1).wait_recv()
                if hop < last:
                    @pl.when(down)
                    def _():
                        along(item, piece(item, base + place), base + place - 1, -1).start()
                if cross:
                    beside(item, place).start()

    def pass_on(item):
        hops(item, 0, item != DOWN)

    def climb_sent(item, base):
        @pl.when(up)
        def _():
            along(item, piece(item, base), base + 1, 1).wait_send()

        @pl.when(down)
        def _():
            along(item, piece(item, base), base + last, -1).wait_send()

        for hop in range(1, last):
            @pl.when((hop <= wires.ring) & up)
            def _():
                along(item, piece(item, base + hop), base + hop + 1, 1).wait_send()

            @pl.when((hop <= last - wires.ring) & down)
            def _():
                along(item, piece(item, base + outer - hop), base + outer - hop - 1, -1).wait_send()

    def arrived(item):
        own(item).wait()
        for step in range(outer if item != DOWN else 1):
            beside(item, step).wait_recv()

    def load(src, dst, index):
        copy = pltpu.make_async_copy(src, dst, ls.at[index])
        copy.start()
        return copy

    stores = []

    def store(src, dst):
        copy = pltpu.make_async_copy(src, dst, os_.at[len(stores)])
        copy.start()
        stores.append(copy)
        return copy

    def gain_copy(place):
        turn, step = place // outer, place % outer
        there = piece(GAINS, turn * outer + (outer - step) % outer)
        device = (wires.block_at(place), wires.tensor)
        return remote(gains, there, zs.at[GAINS, place], zr.at[GAINS, turn * outer + (outer - step) % outer], device)

    wires.greet_all()
    for place in range(1, 2 * outer):
        gain_copy(place).start()
    for item in range(N_ITEMS):
        own(item).start()
    issue(QUERY)
    issue(KEY)
    issue(VALUE)
    beside(DOWN, 0).start()

    def own_blocks(source, target):
        copies = []
        for place in range(2 * outer):
            at = pl.multiple_of(wires.block_at(place) * block, block)
            copies.append(load(source.at[:, pl.ds(at, block)], target.at[:, pl.ds(place * block, block)], place))
        return copies

    first = 2 * outer
    loads = own_blocks(tokens, wide)
    loads.append(load(cosine, cos_v, first))
    loads.append(load(sine, sin_v, first + 1))
    loads.append(load(row_decay, rowd, first + 2))
    loads.append(load(key_decay, keyd, first + 3))
    own(GAINS).wait()
    for place in range(1, 2 * outer):
        gain_copy(place).wait_recv()
    for copy in loads:
        copy.wait()
    copy = load(fulls[GAINS], gain_v, 0)
    copy.wait()
    group = jnp.zeros((1, heads * DV), F32)
    for place in range(2 * outer):
        line = gain_v[place * 16 : place * 16 + 1, :].astype(F32)
        gain_m[:, place * block : (place + 1) * block] = line[:, :block]
        gain_f[:, place * block : (place + 1) * block] = line[:, block : 2 * block]
        group = group + line[:, 2 * block :]
    gain_g[...] = group

    @pl.loop(0, length // 128)
    def _(r):
        at = tile(r, 128)
        mixer[at, :] = norm_rows(wide[at, :].astype(F32), gain_m[...], norm_epsilon).astype(BF16)

    mine = tile(wires.tensor, quarter)
    residual[...] = wide[mine, :].astype(F32)
    mixer_store = store(mixer, mixer_out)
    pass_on(QUERY)
    pass_on(KEY)
    issue(GATE)
    pass_on(VALUE)
    issue(OUT)
    arrived(QUERY)
    arrived(KEY)
    narrow = heads * DK
    copy = load(fulls[QUERY], slot_a.at[:, pl.ds(0, narrow)], 0)
    other = load(fulls[KEY], slot_a.at[:, pl.ds(narrow, narrow)], 1)
    copy.wait()
    other.wait()

    @pl.loop(0, rows)
    def _(r):
        at = tile(r, STEP)
        both = jnp.dot(mixer[at, :], slot_a[...], preferred_element_type=F32)
        c, s = cos_v[at, :], sin_v[at, :]
        half = DK // 2
        for target, base in ((rq, 0), (rk, narrow)):
            for h in range(heads):
                lo = base + h * DK
                a, b = both[:, lo : lo + half], both[:, lo + half : lo + DK]
                target[at, h * DK : h * DK + half] = (a * c - b * s).astype(BF16)
                target[at, h * DK + half : (h + 1) * DK] = (a * s + b * c).astype(BF16)

    store(rq, query_out)
    store(rk, key_out)
    pass_on(GATE)
    issue(HIDDEN)
    arrived(VALUE)
    load(fulls[VALUE], slot_b, 0).wait()

    @pl.loop(0, rows)
    def _(r):
        at = tile(r, STEP)
        values[at, :] = jnp.dot(mixer[at, :], slot_b[...], preferred_element_type=F32).astype(BF16)

    store(values, value_out)
    for h in range(heads):
        for r in range(rows):
            at = slice(r * STEP, (r + 1) * STEP)
            upto = (r + 1) * STEP
            q = rq[at, h * DK : (h + 1) * DK]
            k = rk[:upto, h * DK : (h + 1) * DK]
            raw = lax.dot_general(q, k, (((1,), (1,)), ((), ())), preferred_element_type=F32)
            fade = rowd[at, h : h + 1] * keyd[h : h + 1, :upto]
            place = lax.broadcasted_iota(jnp.int32, (STEP, upto), 0) + r * STEP
            under = place >= lax.broadcasted_iota(jnp.int32, (STEP, upto), 1)
            scores = raw * jnp.where(under, fade, 0.0)
            total = jnp.sum(scores, axis=-1, keepdims=True)
            share = (scores * lax.rsqrt(total * total + 1.0)).astype(BF16)
            kept[at, h * DV : (h + 1) * DV] = jnp.dot(
                share, values[:upto, h * DV : (h + 1) * DV], preferred_element_type=F32
            )
    kept_store = store(kept, retained_out)
    pass_on(OUT)
    issue(UP)
    arrived(GATE)
    load(fulls[GATE], slot_a, 0).wait()

    @pl.loop(0, rows)
    def _(r):
        at = tile(r, STEP)
        gate = jnp.dot(mixer[at, :], slot_a[...], preferred_element_type=F32)
        gate_in[at, :] = gate
        for h in range(heads):
            cols = slice(h * DV, (h + 1) * DV)
            normed = norm_rows(kept[at, cols], gain_g[:, cols], group_epsilon)
            mixed[at, cols] = (silu(gate[:, cols]) * normed).astype(BF16)

    gate_store = store(gate_in, gate_out)
    mixed_store = store(mixed, mixed_out)
    pass_on(HIDDEN)
    issue(DOWN, False)
    arrived(DOWN)
    climb(DOWN, piece(DOWN, outer), outer)
    arrived(OUT)
    load(fulls[OUT], slot_o, 0).wait()

    def branch_rows(index):
        return jnp.dot(mixed[tile(index, quarter), :], slot_o[...], preferred_element_type=F32)

    def to_sibling(s):
        return remote(csend.at[s], crecv.at[s], ts.at[s], tr.at[s], wires.sibling())

    cross = remote(ysend, yrecv, ts.at[2], tr.at[2], wires.across())
    for s in (1, 0):
        owner = lax.rem(wires.row + s, 2) * 2 + 1 - wires.core
        csend[s] = branch_rows(owner).astype(BF16)
        to_sibling(s).start()
    part = branch_rows((1 - wires.row) * 2 + wires.core)
    to_sibling(1).wait_recv()
    ysend[...] = (part + crecv[1].astype(F32)).astype(BF16)
    cross.start()
    residual[...] += branch_rows(wires.tensor)
    to_sibling(0).wait_recv()
    residual[...] += crecv[0].astype(F32)
    pass_on(UP)
    hops(DOWN, 0, False, (1,))
    cross.wait_recv()
    residual[...] += yrecv[...].astype(F32)
    store(residual, residual_out)
    feed_mine = wide.at[mine]

    @pl.loop(0, quarter // 128)
    def _(r):
        at = tile(r, 128)
        ysend_rows = norm_rows(residual[at, :], gain_f[...], norm_epsilon).astype(BF16)
        feed_mine[at, :] = ysend_rows

    feed_cross = remote(feed_mine, feed_mine, ts.at[3], tr.at[3], wires.across())
    feed_near = remote(feed_mine, feed_mine, ts.at[4], tr.at[4], wires.sibling())
    theirs = wide.at[tile((1 - wires.row) * 2 + wires.core, quarter)]
    feed_far = remote(theirs, theirs, ts.at[5], tr.at[5], wires.sibling())
    feed_cross.start()
    feed_near.start()
    hops(DOWN, 0, False, (2, 3))
    hops(DOWN, outer, False, (1,))
    feed_cross.wait_recv()
    feed_far.start()
    mixer_store.wait()
    cot_loads = own_blocks(cotangent, mixer)
    hops(DOWN, outer, False, (2,))
    arrived(HIDDEN)
    load(fulls[HIDDEN], slot_b, first).wait()
    feed_near.wait_recv()
    feed_far.wait_recv()
    store(wide, feed_out)
    kept_store.wait()
    gate_store.wait()

    @pl.loop(0, rows)
    def _(r):
        at = tile(r, STEP)
        kept[at, :] = jnp.dot(wide[at, :], slot_b[...], preferred_element_type=F32)

    hops(DOWN, outer, False, (3,))
    load(fulls[DOWN], slot_o, first).wait()
    for copy in cot_loads:
        copy.wait()

    @pl.loop(0, rows)
    def _(r):
        at = tile(r, STEP)
        gate_in[at, :] = lax.dot_general(
            mixer[at, :], slot_o[...], (((1,), (1,)), ((), ())), preferred_element_type=F32
        )

    arrived(UP)
    load(fulls[UP], slot_a, first).wait()
    mixed_store.wait()

    @pl.loop(0, length // PART)
    def _(r):
        at = tile(r, PART)
        u = jnp.dot(wide[at, :], slot_a[...], preferred_element_type=F32)
        h, grads = kept[at, :], gate_in[at, :]
        t = jnp.tanh(SQRT_2_PI * (h + CUBIC * h * h * h))
        gelu = 0.5 * h * (1.0 + t)
        slope = 0.5 * (1.0 + t) + 0.5 * h * (1.0 - t * t) * (SQRT_2_PI * (1.0 + 3.0 * CUBIC * h * h))
        mixed[at, :] = (gelu * u).astype(BF16)
        slot_b[at, :] = (grads * u * slope).astype(BF16)
        slot_o[at, pl.ds(0, units)] = (grads * gelu).astype(BF16)

    store(mixed, activity_out)
    store(slot_b.at[pl.ds(0, length)], hidden_out)
    store(slot_o.at[:, pl.ds(0, units)], up_out)
    for copy in stores:
        if not any(copy is done for done in (kept_store, gate_store, mixer_store, mixed_store)):
            copy.wait()
    for s in range(2):
        to_sibling(s).wait_send()
    for copy in (cross, feed_cross, feed_near, feed_far):
        copy.wait_send()
    for place in range(1, 2 * outer):
        gain_copy(place).wait_send()
    for item in range(1, N_ITEMS):
        climb_sent(item, 0)
        for step in range(outer if item != DOWN else 1):
            beside(item, step).wait_send()
    climb_sent(DOWN, outer)


def position_tables(length, heads):
    half = DK // 2
    speeds = 10000.0 ** (-np.arange(half, dtype=np.float32) / np.float32(half))
    angles = np.arange(length, dtype=np.float32)[:, None] * speeds.astype(np.float32)[None, :]
    pair = [np.cos(angles), np.sin(angles)]
    turns = [t.reshape(length // PART, PART, half).swapaxes(0, 1).reshape(PART, -1) for t in pair]
    rates = np.log1p(-np.exp2(-5.0 - np.arange(heads, dtype=np.float64)))[:, None]
    places = np.arange(length, dtype=np.float64)[None, :]
    sums = np.expm1(rates * (places + 1)) / np.expm1(rates)
    row_decay = np.exp(rates * (places - length // 2)) / np.sqrt(sums) * DK**-0.5
    key_decay = np.exp(rates * (length // 2 - places))
    return [jnp.asarray(np.asarray(t, np.float32)) for t in (*pair, np.stack(turns), row_decay, key_decay)]


def forward_fast(dp_size, tokens, cotangent, gains, tables, weights):
    outer = dp_size // 2
    length, model = tokens.shape
    block = model // dp_size
    heads = weights[0].shape[1] // DK
    units = weights[3].shape[1]
    wide = units
    shapes = [(gains.shape[0] * dp_size, gains.shape[1])]
    for place, weight in enumerate(weights):
        if place + 1 in (OUT, DOWN):
            shapes.append((weight.shape[0], model))
        else:
            shapes.append((model, weight.shape[1]))
    out_shape = [jax.ShapeDtypeStruct(s, BF16) for s in shapes]
    half = heads * DK
    for shape, kind in (
        ((length, model), BF16),
        ((length, half), BF16),
        ((length, half), BF16),
        ((length, wide), BF16),
        ((length, wide), F32),
        ((length, wide), F32),
        ((length, wide), BF16),
        ((length // 4, model), F32),
        ((length, model), BF16),
        ((length, units), BF16),
        ((length, units), BF16),
        ((length, units), BF16),
    ):
        out_shape.append(jax.ShapeDtypeStruct(shape, kind))
    quarter = length // 4
    dma = pltpu.SemaphoreType.DMA
    scratch = [
        pltpu.VMEM((model, wide), BF16),
        pltpu.VMEM((model, wide), BF16),
        pltpu.VMEM((wide, model), BF16),
        pltpu.VMEM((length, model), BF16),
        pltpu.VMEM((length, model), BF16),
        pltpu.VMEM((length, half), BF16),
        pltpu.VMEM((length, half), BF16),
        pltpu.VMEM((length, wide), BF16),
        pltpu.VMEM((length, wide), F32),
        pltpu.VMEM((length, wide), F32),
        pltpu.VMEM((length, wide), BF16),
        pltpu.VMEM((quarter, model), F32),
        pltpu.VMEM((2, quarter, model), BF16),
        pltpu.VMEM((2, quarter, model), BF16),
        pltpu.VMEM((quarter, model), BF16),
        pltpu.VMEM((quarter, model), BF16),
        pltpu.VMEM(tables[0].shape, F32),
        pltpu.VMEM(tables[1].shape, F32),
        pltpu.VMEM(tables[2].shape, F32),
        pltpu.VMEM(tables[3].shape, F32),
        pltpu.VMEM(shapes[0], BF16),
        pltpu.VMEM((1, model), F32),
        pltpu.VMEM((1, model), F32),
        pltpu.VMEM((1, heads * DV), F32),
        dma((N_ITEMS,)),
        dma((N_ITEMS, 2 * outer)),
        dma((N_ITEMS, 2 * outer)),
        dma((N_ITEMS, outer)),
        dma((N_ITEMS, outer)),
        dma((6,)),
        dma((6,)),
        dma((2 * outer + 4,)),
        dma((14,)),
    ]

    def kernel(*refs):
        forward_kernel(outer, heads, (length, model, block), *refs)

    results = pl.pallas_call(
        kernel,
        out_shape=out_shape,
        in_specs=[ANY] * (7 + len(weights)),
        out_specs=[ANY] * len(out_shape),
        scratch_shapes=scratch,
        compiler_params=pltpu.CompilerParams(
            collective_id=0, has_side_effects=True, vmem_limit_bytes=58 * 1024 * 1024
        ),
    )(tokens, cotangent, gains, *tables, *weights)
    return results[: N_ITEMS], results[N_ITEMS:]


N_GRADS = 7
(G_DOWN, G_HIDDEN, G_UP, G_OUT, G_GATE, G_VALUE, G_BOTH) = range(N_GRADS)
FLOW = (2, 3, 1, 0)
SQRT_2_PI = 0.7978845608028654
CUBIC = 0.044715


def rows_dot(left, right):
    return lax.dot_general(left, right, (((0,), (0,)), ((), ())), preferred_element_type=F32)


def back_dot(left, right):
    return lax.dot_general(left, right, (((1,), (1,)), ((), ())), preferred_element_type=F32)


def norm_back(values, grads, gain, epsilon):
    center = values - jnp.mean(values, axis=-1, keepdims=True)
    inverse = lax.rsqrt(jnp.mean(center * center, axis=-1, keepdims=True) + epsilon)
    unit = center * inverse
    u = grads * gain
    mean = jnp.mean(u, axis=-1, keepdims=True)
    slope = jnp.mean(u * unit, axis=-1, keepdims=True)
    return (u - mean - unit * slope) * inverse, grads * unit


def backward_kernel(outer, heads, dims, *refs):
    length, model, block, units = dims
    quarter = length // 4
    half = model // 2
    (tokens, cotangent, gains, query_full, key_full, value_full, gate_full, out_full, hidden_full, up_full,
     down_full, mixer_in, query_in, key_in, value_in, retained_in, gate_in, mixed_in, residual_in, feed_in,
     hidden_in, up_in, activity_in, turns, key_decay) = refs[:25]
    (output, tokens_out, near_out, z_land, vector_out, x_land, branch_land) = refs[25:32]
    (u0, u1, u2, u3, u4, act, hid, upg, both, fa, fb, x_ring, x_extra, z_ring, x_stage, acc, csend, crecv, ysend, yrecv,
     stage, grad_q, value_q, keyd, gain_v, gain_m, gain_f, gain_g,
     vec_t, vec_tr, vec_d, vec_dr, vec_g,
     xs, xr, zs, zr, ts, tr, gs, gr, vs, vr, ls, fs, st, ac) = refs[32:]
    wires = Wires(outer)
    rows = length // STEP
    mine = tile(wires.tensor, quarter)
    near_rows = tile(wires.row * 2 + 1 - wires.core, quarter)
    across_index = (1 - wires.row) * 2 + wires.core
    across_rows = tile(across_index, quarter)
    corner_rows = tile((1 - wires.row) * 2 + 1 - wires.core, quarter)

    def load(src, dst, index):
        copy = pltpu.make_async_copy(src, dst, ls.at[index])
        copy.start()
        return copy

    def load_tall(src, dst, index):
        return [load(src.at[pl.ds(h * half, half)], dst.at[:, pl.ds(h * half, half)], index + h) for h in range(2)]

    def wait_all(copies):
        for copy in copies:
            copy.wait()

    def own_blocks(src, dst, index):
        copies = []
        for place in range(2 * outer):
            at = pl.multiple_of(wires.block_at(place) * block, block)
            copies.append(load(src.at[:, pl.ds(at, block)], dst.at[:, pl.ds(place * block, block)], index + place))
        return copies

    def true_blocks(src, dst, index):
        copies = []
        for place in range(2 * outer):
            at = pl.multiple_of(wires.block_at(place) * block, block)
            copies.append(load(src.at[:, pl.ds(place * block, block)], dst.at[:, pl.ds(at, block)], index + place))
        return copies

    def x_copy(item, s):
        source = x_extra if item == G_DOWN else x_ring.at[(item % 2) * outer + s]
        return remote(source, x_land.at[item, s], xs.at[item, s], xr.at[item, s], wires.peer())

    def z_copy(item, s):
        step = outer - 1 if s != outer - 1 else 1
        device = (lax.rem(wires.ring + step, outer) * 2 + wires.turn, wires.tensor)
        slot = (item % 2) * (outer - 1) + s - 1
        return remote(z_ring.at[slot], z_land.at[item, s - 1], zs.at[item, s], zr.at[item, s], device)

    def columns(place):
        return pl.ds(pl.multiple_of(place * block, block), block)

    def far(item, left, right, flow=FLOW, behind=None):
        for s in flow:
            if item >= 3:
                x_copy(item - 2, s).wait_send()
            product = rows_dot(left[:, columns(outer + s)], right[...])
            x_ring[(item % 2) * outer + s] = product.astype(BF16)
            if behind is None:
                x_copy(item, s).start()
        if behind is not None:
            behind.wait_send()
            for s in flow:
                x_copy(item, s).start()

    def acc_copy(item):
        return pltpu.make_async_copy(acc, near_out.at[item], ac.at[item])

    def staged(item, place, source):
        copy = pltpu.make_async_copy(source, x_stage.at[place], st.at[item, place])
        copy.start()
        return copy

    sides = ((0, G_DOWN), (1, N_GRADS))

    def down_product(turn, s):
        return rows_dot(u0[:, columns(turn * outer + s)], act[...])

    def down_give(s):
        for turn, item in sides:
            z_ring[(item % 2) * (outer - 1) + s - 1] = down_product(turn, s).astype(BF16)
            z_copy(item, s).start()

    def down_first():
        down_give(2)
        for turn, item in sides:
            z_ring[(item % 2) * (outer - 1)] = down_product(turn, 1).astype(BF16)
        x_extra[...] = down_product(1, 0).astype(BF16)
        acc[...] = down_product(0, 0)
        acc_copy(G_DOWN).start()

    def relay(item):
        z_copy(item, 2).wait_recv()
        staged(item, 2, z_land.at[item, 1]).wait()
        slot = (item % 2) * (outer - 1)
        z_ring[slot] = (z_ring[slot].astype(F32) + x_stage[2].astype(F32)).astype(BF16)
        z_copy(item, 1).start()

    def down_sum():
        z_copy(N_GRADS, 3).wait_recv()
        copy = staged(N_GRADS, 2, z_land.at[N_GRADS, 2])
        z_copy(N_GRADS, 1).wait_recv()
        other = staged(N_GRADS, 3, z_land.at[N_GRADS, 0])
        copy.wait()
        other.wait()
        total = x_extra[...].astype(F32) + x_stage[2].astype(F32) + x_stage[3].astype(F32)
        x_extra[...] = total.astype(BF16)

    def near(item, left, right, flow=FLOW):
        before = N_GRADS if item == 1 else item - 2
        for s in flow:
            x_copy(item, s).wait_recv()
            copy = staged(item, s % 2, x_land.at[item, s])
            if s:
                z_copy(before, s).wait_send()
            if s == 0:
                acc_copy(item - 1).wait()
            product = rows_dot(left[:, columns(s)], right[...])
            copy.wait()
            product = product + x_stage[s % 2].astype(F32)
            if s == 0:
                acc[...] = product
                acc_copy(item).start()
                continue
            z_ring[(item % 2) * (outer - 1) + s - 1] = product.astype(BF16)
            if s > 1:
                z_copy(item, s).start()

    class Round:
        def __init__(self, index):
            self.index = index
            self.cross = remote(ysend, yrecv, ts.at[index, 2], tr.at[index, 2], wires.across())

        def to_sibling(self, s):
            return remote(csend.at[s], crecv.at[s], ts.at[self.index, s], tr.at[self.index, s], wires.sibling())

        def give(self, terms):
            for s in (1, 0):
                owner = lax.rem(wires.row + s, 2) * 2 + 1 - wires.core
                for h in range(2):
                    cols = slice(h * half, (h + 1) * half)
                    csend[s, :, cols] = terms(tile(owner, quarter), h).astype(BF16)
                self.to_sibling(s).start()

        def hand_over(self, terms):
            self.to_sibling(1).wait_recv()
            for h in range(2):
                cols = slice(h * half, (h + 1) * half)
                ysend[:, cols] = (terms(across_rows, h) + crecv[1, :, cols].astype(F32)).astype(BF16)
            self.cross.start()

        def keep(self, terms, totals, add):
            for h in range(2):
                part = terms(mine, h)
                totals[h][...] = totals[h][...] + part if add else part
            self.to_sibling(0).wait_recv()
            for h in range(2):
                totals[h][...] += crecv[0, :, h * half : (h + 1) * half].astype(F32)

        def finish(self, totals):
            self.cross.wait_recv()
            for h in range(2):
                totals[h][...] += yrecv[:, h * half : (h + 1) * half].astype(F32)
            for s in range(2):
                self.to_sibling(s).wait_send()
            self.cross.wait_send()

    class Spread:
        def __init__(self, index, source, land):
            self.cross = remote(source, land.at[mine], gs.at[index, 0], gr.at[index, 0], wires.across())
            self.near = remote(source, land.at[mine], gs.at[index, 1], gr.at[index, 1], wires.sibling())
            there = land.at[across_rows]
            self.far = remote(there, there, gs.at[index, 2], gr.at[index, 2], wires.sibling())
            self.own = pltpu.make_async_copy(source, land.at[mine], gs.at[index, 3])

        def start(self):
            self.cross.start()
            self.near.start()
            self.own.start()

        def pass_on(self):
            self.cross.wait_recv()
            self.far.start()

        def sent(self):
            self.cross.wait_send()
            self.near.wait_send()
            self.own.wait()

        def end(self):
            self.far.wait_recv()
            self.far.wait_send()

    def stream(src_a, src_b, body):
        def copies(r, slot):
            at = tile(r, PART)
            return (
                pltpu.make_async_copy(src_a.at[at], fa.at[slot, pl.ds(0, PART)], fs.at[0, slot]),
                pltpu.make_async_copy(src_b.at[at], fb.at[slot], fs.at[1, slot]),
            )

        for copy in copies(0, 0):
            copy.start()

        @pl.loop(0, length // PART)
        def _(r):
            slot = lax.rem(r, 2)

            @pl.when(r + 1 < length // PART)
            def _():
                for copy in copies(r + 1, 1 - slot):
                    copy.start()

            for copy in copies(r, slot):
                copy.wait()
            body(tile(r, PART), fa.at[slot, pl.ds(0, PART)], fb.at[slot])

    wires.greet_all()
    n = 2 * outer
    hid_load = load(hidden_in, hid, n + 10)
    feed_load = load(feed_in, u2, n + 2)
    act_load = load(activity_in, act, n + 9)
    cot_loads = own_blocks(cotangent, u0, 0)
    upg_load = load(up_in, upg, n + 11)
    hidden_loads = load_tall(hidden_full, u3, n + 3)
    up_loads = load_tall(up_full, u4, n + 5)
    down_load = load(down_full, u1, n)
    gain_load = load(gains, gain_v, n + 1)
    residual_load = load(residual_in, value_q, n + 7)
    table_load = load(key_decay, keyd, n + 8)
    hid_load.wait()
    feed_load.wait()
    far(G_HIDDEN, u2, hid)
    act_load.wait()
    wait_all(cot_loads)
    down_first()
    upg_load.wait()
    wait_all(hidden_loads)
    wait_all(up_loads)

    def tall_terms(pairs):
        def terms(at, h):
            cols = slice(h * half, (h + 1) * half)
            total = None
            for left, right in pairs:
                part = back_dot(left[at, :], right[:, cols])
                total = part if total is None else total + part
            return total

        return terms

    feed_terms = tall_terms(((hid, u3), (upg, u4)))
    feed_round, output_round, mixer_round = Round(0), Round(1), Round(2)
    feed_round.give(feed_terms)
    far(G_UP, u2, upg)
    feed_round.hand_over(feed_terms)
    grad_halves = [grad_q.at[:, pl.ds(h * half, half)] for h in range(2)]
    value_halves = [value_q.at[:, pl.ds(h * half, half)] for h in range(2)]
    mixer_halves = [fa.at[h] for h in range(2)]
    feed_round.keep(feed_terms, grad_halves, False)
    table_load.wait()
    gain_load.wait()
    group = jnp.zeros((1, heads * DV), F32)
    for place in range(2 * outer):
        line = gain_v[place * 16 : place * 16 + 1, :].astype(F32)
        gain_m[:, place * block : (place + 1) * block] = line[:, :block]
        gain_f[:, place * block : (place + 1) * block] = line[:, block : 2 * block]
        group = group + line[:, 2 * block :]
    gain_g[...] = group
    vec_t[...] = jnp.zeros_like(vec_t)
    vec_d[...] = jnp.zeros_like(vec_d)
    vec_g[...] = jnp.zeros_like(vec_g)
    mixer_load = load(mixer_in, u3, n + 3)
    narrow = heads * DK
    core_loads = [load(value_in, u4.at[:, pl.ds(0, half)], n + 4),
                  load(query_in, u4.at[:, pl.ds(half, narrow)], n + 5),
                  load(key_in, u4.at[:, pl.ds(half + narrow, narrow)], n + 6)]
    down_give(3)
    residual_load.wait()
    feed_round.finish(grad_halves)

    @pl.loop(0, quarter // 128)
    def _(r):
        at = tile(r, 128)
        part, gain_part = norm_back(value_q[at, :], grad_q[at, :], gain_f[...], norm_epsilon)
        cot_at = pl.ds(pl.multiple_of(wires.tensor * quarter + r * 128, 128), 128)
        total = u0[cot_at, :].astype(F32) + part
        grad_q[at, :] = total
        stage[at, :] = total.astype(BF16)
        vec_t[1:2, :] += jnp.sum(gain_part, axis=0, keepdims=True)

    branch_spread = Spread(0, stage, branch_land)
    branch_spread.start()
    relay(G_DOWN)
    relay(N_GRADS)
    near(G_HIDDEN, u2, hid, (2, 3, 0))

    down_load.wait()

    def output_terms(at, h):
        return jnp.dot(act[at, :], u1[:, h * half : (h + 1) * half], preferred_element_type=F32)

    branch_spread.near.wait_recv()
    output_round.give(output_terms)
    output_round.keep(output_terms, value_halves, True)
    branch_spread.pass_on()
    output_round.hand_over(output_terms)
    branch_spread.sent()
    out_load = load(out_full, u1, n)
    branch_loads = [load(branch_land.at[at], u0.at[at], n + 7 + i) for i, at in
                    enumerate((mine, near_rows, across_rows))]
    mixed_load = load(mixed_in, act, n + 1)
    branch_spread.far.wait_recv()
    branch_loads.append(load(branch_land.at[corner_rows], u0.at[corner_rows], n + 2))
    wait_all(branch_loads)
    out_load.wait()

    hold = both

    def gate_tile(at, r_ref, g_ref):
        grads = back_dot(u0[at, :], u1[...])
        for h in range(heads):
            cols = slice(h * DV, (h + 1) * DV)
            x, g, m = r_ref[:, cols], g_ref[:, cols], grads[:, cols]
            scale = gain_g[:, cols]
            sig = 1.0 / (1.0 + jnp.exp(-g))
            swish = g * sig
            center = x - jnp.mean(x, axis=-1, keepdims=True)
            inverse = lax.rsqrt(jnp.mean(center * center, axis=-1, keepdims=True) + group_epsilon)
            unit = center * inverse
            passed = m * swish
            hid[at, cols] = (m * unit * scale * (sig * (1.0 + g * (1.0 - sig)))).astype(BF16)
            vec_g[:, cols] += jnp.sum(passed * unit, axis=0, keepdims=True)
            u = passed * scale
            mean = jnp.mean(u, axis=-1, keepdims=True)
            slope = jnp.mean(u * unit, axis=-1, keepdims=True)
            hold[at, cols] = ((u - mean - unit * slope) * inverse).astype(BF16)

    mixed_load.wait()
    far(G_OUT, u0, act)
    near(G_HIDDEN, u2, hid, (1,))
    stream(retained_in, gate_in, gate_tile)
    relay(G_HIDDEN)
    mixer_load.wait()
    near(G_UP, u2, upg)
    value_loads = load_tall(value_full, u2, n + 1)
    far(G_GATE, u3, hid)
    wait_all(core_loads)

    side = DK // 2
    turn_load = load(turns, fb, n + 8)
    turn_load.wait()

    def turned_back(grads, r, count):
        a, b = grads[:, :side], grads[:, side:]
        c = jnp.concatenate([fb[0, :, (r + i) * side : (r + i + 1) * side] for i in range(count)], axis=0)
        s = jnp.concatenate([fb[1, :, (r + i) * side : (r + i + 1) * side] for i in range(count)], axis=0)
        return (a * c + b * s).astype(BF16), (b * c - a * s).astype(BF16)

    for h in range(heads):
        vcols = slice(h * DV, (h + 1) * DV)
        qcols = slice(half + h * DK, half + (h + 1) * DK)
        kcols = slice(half + narrow + h * DK, half + narrow + (h + 1) * DK)
        for r in range(length // PART):
            at = slice(r * PART, (r + 1) * PART)
            upto = (r + 1) * PART
            raw = back_dot(u4[at, qcols], u4[:upto, kcols])
            place = lax.broadcasted_iota(jnp.int32, (PART, upto), 0) + r * PART
            under = place >= lax.broadcasted_iota(jnp.int32, (PART, upto), 1)
            fade = keyd[heads + h : heads + h + 1, at].reshape(PART, 1) * keyd[h : h + 1, :upto]
            fade = jnp.where(under, fade, 0.0)
            scores = raw * fade
            total = jnp.sum(scores, axis=-1, keepdims=True)
            inverse = lax.rsqrt(total * total + 1.0)
            u1[at, :upto] = (scores * inverse).astype(BF16)
            grads = back_dot(hold[at, vcols], u4[:upto, vcols])
            inner = jnp.sum(grads * scores, axis=-1, keepdims=True)
            drop = inner * total * inverse * inverse * inverse
            raw_grad = ((grads * inverse - drop) * fade).astype(BF16)
            u1[at, half : half + upto] = raw_grad
            query_grad = jnp.dot(raw_grad, u4[:upto, kcols], preferred_element_type=F32)
            lo, hi = turned_back(query_grad, r, 1)
            upg[at, h * DK : h * DK + side] = lo
            upg[at, h * DK + side : (h + 1) * DK] = hi
        for c in range(rows):
            at = slice(c * STEP, (c + 1) * STEP)
            after = slice(c * STEP, length)
            for i in range(1, STEP // PART):
                spare = slice(c * STEP, c * STEP + i * PART)
                late = slice(c * STEP + i * PART, c * STEP + (i + 1) * PART)
                u1[spare, late] = jnp.zeros((i * PART, PART), BF16)
                u1[spare, half + c * STEP + i * PART : half + c * STEP + (i + 1) * PART] = jnp.zeros(
                    (i * PART, PART), BF16
                )
            hold_grad = rows_dot(u1[after, c * STEP : (c + 1) * STEP], hold[after, vcols])
            key_grad = rows_dot(u1[after, half + c * STEP : half + (c + 1) * STEP], u4[after, qcols])
            hold[at, vcols] = hold_grad.astype(BF16)
            lo, hi = turned_back(key_grad, c * (STEP // PART), STEP // PART)
            upg[at, narrow + h * DK : narrow + h * DK + side] = lo
            upg[at, narrow + h * DK + side : narrow + (h + 1) * DK] = hi

    gate_loads = load_tall(gate_full, u1, n + 3)
    both_loads = []
    for h in range(2):
        source = pl.ds(h * half, half)
        both_loads.append(load(query_full.at[source], u4.at[:, pl.ds(h * half, narrow)], n + 5 + 2 * h))
        both_loads.append(load(key_full.at[source], u4.at[:, pl.ds(h * half + narrow, narrow)], n + 6 + 2 * h))

    down_sum()
    relay(G_UP)

    output_round.finish(value_halves)
    ysend[...] = value_q[...].astype(BF16)
    wait_all(true_blocks(ysend, stage, 0))
    output_spread = Spread(1, stage, output)
    output_spread.start()
    token_loads = []
    for place in range(2 * outer):
        at = pl.multiple_of(wires.block_at(place) * block, block)
        token_loads.append(load(tokens.at[mine, pl.ds(at, block)], ysend.at[:, pl.ds(place * block, block)], place))
    wait_all(token_loads)
    for r in range(2):
        at = slice(r * (quarter // 2), (r + 1) * (quarter // 2))
        value_q[at, :] = ysend[at, :].astype(F32)
    near(G_OUT, u0, act)
    far(G_VALUE, u3, hold)
    wait_all(gate_loads)
    wait_all(both_loads)
    wait_all(value_loads)
    mixer_terms = tall_terms(((upg, u4), (hold, u2), (hid, u1)))
    output_spread.near.wait_recv()
    mixer_round.give(mixer_terms)
    output_spread.pass_on()
    mixer_round.hand_over(mixer_terms)
    mixer_round.keep(mixer_terms, mixer_halves, False)
    relay(G_OUT)
    mixer_round.finish(mixer_halves)
    output_spread.sent()

    @pl.loop(0, quarter // 128)
    def _(r):
        at = tile(r, 128)
        grads = jnp.concatenate([fa[0, at, :], fa[1, at, :]], axis=1)
        part, gain_part = norm_back(value_q[at, :], grads, gain_m[...], norm_epsilon)
        ysend[at, :] = (grad_q[at, :] + part).astype(BF16)
        vec_t[0:1, :] += jnp.sum(gain_part, axis=0, keepdims=True)

    def vector_team(i, device):
        return remote(vec_t, vec_tr.at[i], vs.at[i], vr.at[i], device)

    team = (wires.sibling(), wires.across(), wires.corner())
    for i, device in enumerate(team):
        vector_team(i, device).start()
    wait_all(true_blocks(ysend, stage, 0))
    tokens_spread = Spread(2, stage, tokens_out)
    tokens_spread.start()
    near(G_GATE, u3, hid)
    far(G_BOTH, u3, upg, (2, 3))
    for i, device in enumerate(team):
        vector_team(i, device).wait_recv()
    summed = vec_t[0:2, :]
    for i in range(3):
        summed = summed + vec_tr[i, 0:2, :]
    for place in range(2 * outer):
        vec_d[place, 0:2, :] = summed[:, place * block : (place + 1) * block]
        for i in range(heads * DV // block):
            vec_d[place, 2 + i : 3 + i, :] = vec_g[:, i * block : (i + 1) * block]

    def vector_data(place):
        device = (wires.block_at(place), wires.tensor)
        return remote(vec_d.at[place], vec_dr.at[place], vs.at[3 + place], vr.at[3 + place], device)

    for place in range(1, 2 * outer):
        vector_data(place).start()
    tokens_spread.pass_on()
    relay(G_GATE)
    near(G_VALUE, u3, hold)
    relay(G_VALUE)
    far(G_BOTH, u3, upg, (1, 0), x_copy(G_BOTH, 2))
    x_copy(G_DOWN, 0).start()
    near(G_BOTH, u3, upg, (2, 3))
    near(G_BOTH, u3, upg, (1,))
    relay(G_BOTH)
    near(G_BOTH, u3, upg, (0,))
    vectors = vec_d[0]
    for place in range(1, 2 * outer):
        vector_data(place).wait_recv()
        vectors = vectors + vec_dr[place]
    vec_d[0] = vectors
    vector_store = load(vec_d.at[0], vector_out, 0)

    vector_store.wait()
    branch_spread.far.wait_send()
    output_spread.end()
    tokens_spread.near.wait_recv()
    tokens_spread.end()
    tokens_spread.sent()
    for i, device in enumerate(team):
        vector_team(i, device).wait_send()
    for place in range(1, 2 * outer):
        vector_data(place).wait_send()
    acc_copy(N_GRADS - 1).wait()
    x_copy(G_DOWN, 0).wait()
    for item in (N_GRADS - 2, N_GRADS - 1):
        for s in range(outer):
            if (item, s) != (G_BOTH, 2):
                x_copy(item, s).wait_send()
        for s in range(1, outer):
            z_copy(item, s).wait_send()
    for item in range(N_GRADS):
        for s in (1, outer - 1):
            z_copy(item, s).wait_recv()


def backward_fast(dp_size, tokens, cotangent, fulls, kept, tables):
    outer = dp_size // 2
    length, model = tokens.shape
    block = model // dp_size
    gains, query_full, key_full, value_full, gate_full, out_full, hidden_full, up_full, down_full = fulls
    (mixer_input, turned_query, turned_keys, values, retained, gate_in, mixed, residual, feed_input, hidden_pre,
     up_pre, activity) = kept
    heads = query_full.shape[1] // DK
    units = hidden_full.shape[1]
    quarter = length // 4
    shape = jax.ShapeDtypeStruct
    out_shape = [
        shape((length, model), BF16),
        shape((length, model), BF16),
        shape((N_GRADS, block, units), F32),
        shape((N_GRADS + 1, outer - 1, block, units), BF16),
        shape((8, block), F32),
        shape((N_GRADS, outer, block, units), BF16),
        shape((length, model), BF16),
    ]
    dma = pltpu.SemaphoreType.DMA
    vmem = pltpu.VMEM
    scratch = [vmem((length, model), BF16)] * 5 + [vmem((length, units), BF16)] * 4
    scratch += [vmem((2, STEP, units), F32), vmem((2, PART, units), F32)]
    scratch += [
        vmem((2 * outer, block, units), BF16),
        vmem((block, units), BF16),
        vmem((2 * (outer - 1), block, units), BF16),
        vmem((4, block, units), BF16),
        vmem((block, units), F32),
        vmem((2, quarter, model), BF16),
        vmem((2, quarter, model), BF16),
        vmem((quarter, model), BF16),
        vmem((quarter, model), BF16),
        vmem((quarter, model), BF16),
        vmem((quarter, model), F32),
        vmem((quarter, model), F32),
        vmem(tables[1].shape, F32),
        vmem(gains.shape, BF16),
        vmem((1, model), F32),
        vmem((1, model), F32),
        vmem((1, heads * DV), F32),
        vmem((8, model), F32),
        vmem((3, 8, model), F32),
        vmem((dp_size, 8, block), F32),
        vmem((dp_size, 8, block), F32),
        vmem((1, heads * DV), F32),
        dma((N_GRADS, outer)),
        dma((N_GRADS, outer)),
        dma((N_GRADS + 1, outer)),
        dma((N_GRADS + 1, outer)),
        dma((3, 3)),
        dma((3, 3)),
        dma((3, 4)),
        dma((3, 4)),
        dma((3 + dp_size,)),
        dma((3 + dp_size,)),
        dma((dp_size + 12,)),
        dma((2, 2)),
        dma((N_GRADS + 1, outer)),
        dma((N_GRADS,)),
    ]

    def kernel(*refs):
        backward_kernel(outer, heads, (length, model, block, units), *refs)

    operands = (tokens, cotangent, *fulls, *kept, *tables)
    return pl.pallas_call(
        kernel,
        out_shape=out_shape,
        in_specs=[ANY] * len(operands),
        out_specs=[ANY] * len(out_shape),
        scratch_shapes=scratch,
        compiler_params=pltpu.CompilerParams(
            collective_id=1, has_side_effects=True, vmem_limit_bytes=63 * 1024 * 1024
        ),
    )(*operands)


def finish(near_sums, z_land, x_land, tokens_grad, output):
    steps = 8
    _, block, units = near_sums.shape
    length, model = output.shape
    rows, across = block // steps, block // 128
    side = units * across // steps
    turned = (G_DOWN, G_OUT)
    order = (G_BOTH, G_VALUE, G_GATE, G_OUT, G_HIDDEN, G_UP, G_DOWN)
    operands, in_specs, out_specs, out_shape = [], [], [], []

    def add(array, lead, item):
        operands.append(array)
        if item in turned:
            in_specs.append(pl.BlockSpec((1,) * len(lead) + (128, side), lambda i: (*lead, i % across, i // across)))
        else:
            in_specs.append(pl.BlockSpec((1,) * len(lead) + (rows, units), lambda i: (*lead, i, 0)))

    for item in order:
        add(near_sums, (item,), item)
        add(z_land, (item, 0), item)
        add(z_land, (item, 2), item)
        if item == G_DOWN:
            add(x_land, (item, 0), item)
        if item == G_BOTH:
            shapes = [((block, units // 2), (rows, units // 2))] * 2
        else:
            shapes = [((block, units), (rows, units))]
        for whole, part in shapes:
            if item in turned:
                out_shape.append(jax.ShapeDtypeStruct((units, block), F32))
                out_specs.append(pl.BlockSpec((side, 128), lambda i: (i // across, i % across)))
            else:
                out_shape.append(jax.ShapeDtypeStruct(whole, F32))
                out_specs.append(pl.BlockSpec(part, lambda i: (i, 0)))
    for array, kind in ((tokens_grad, F32), (output, BF16)):
        operands.append(array)
        spec = pl.BlockSpec((length // steps, model), lambda i: (i, 0))
        in_specs.append(spec)
        out_specs.append(spec)
        out_shape.append(jax.ShapeDtypeStruct(array.shape, kind))

    def kernel(*refs):
        ins, outs = list(refs[: len(operands)]), list(refs[len(operands) :])
        for item in order:
            total = ins.pop(0)[0]
            for _ in range(3 if item == G_DOWN else 2):
                total = total + ins.pop(0)[0, 0].astype(F32)
            if item == G_BOTH:
                outs.pop(0)[...] = total[:, : units // 2]
                outs.pop(0)[...] = total[:, units // 2 :]
            else:
                outs.pop(0)[...] = total.T if item in turned else total
        for source, target in zip(ins, outs):
            target[...] = source[...].astype(target.dtype)

    return pl.pallas_call(
        kernel,
        grid=(steps,),
        out_shape=out_shape,
        in_specs=in_specs,
        out_specs=out_specs,
        compiler_params=pltpu.CompilerParams(vmem_limit_bytes=62 * 1024 * 1024),
    )(*operands)


def on_device(
    dp_size,
    tensor_size,
    tokens,
    mixer_gain,
    query_weight,
    key_weight,
    value_weight,
    gate_weight,
    out_weight,
    group_gain,
    feed_gain,
    hidden_weight,
    up_weight,
    down_weight,
    cotangent,
):
    data = Ring("dp", dp_size)
    team = Ring("tensor", tensor_size)
    length, model = tokens.shape
    quarter = length // tensor_size
    heads_here = query_weight.shape[1] // DK

    block = mixer_gain.shape[0]
    width = query_weight.shape[1]
    group_block = group_gain.shape[1]
    head_ids = (lax.axis_index("tensor") * heads_here + jnp.arange(heads_here)).astype(F32)
    decays = decay_table(head_ids, length)
    inputs = data.own_order(tokens, 1)
    cot = data.own_order(cotangent, 1)

    def my_rows(array):
        return lax.dynamic_slice_in_dim(array, team.me * quarter, quarter, 0)

    def row_terms(left, right):
        return lambda start, rows: plain_product(
            lax.dynamic_slice_in_dim(left, start, rows, 0), right
        )

    units = hidden_weight.shape[1]
    even = units == 2 * width == heads_here * DV == model // 2 and heads_here * DV // block <= 6
    if even and block % 128 == 0 and tensor_size == 4 and dp_size == 8 and length % 1024 == 0:
        group_line = lax.dynamic_update_slice(
            jnp.zeros((heads_here, DV), BF16), group_gain, (0, data.me * group_block)
        )
        gains = jnp.concatenate([mixer_gain, feed_gain, group_line.reshape(-1)])
        gains = jnp.broadcast_to(gains[None, :], (16, gains.shape[0]))
        cosine, sine, turns, row_decays, key_decays = position_tables(length, query_weight.shape[1] * tensor_size // DK)
        first = lax.axis_index("tensor") * heads_here
        row_decay = lax.dynamic_slice_in_dim(row_decays, first, heads_here, 0)
        key_decay = lax.dynamic_slice_in_dim(key_decays, first, heads_here, 0)
        tables = (cosine, sine, row_decay.T, key_decay)
        back_tables = (turns, jnp.concatenate([key_decay, row_decay]))
        fulls, kept = forward_fast(
            dp_size,
            tokens,
            cotangent,
            gains,
            tables,
            (query_weight, key_weight, value_weight, gate_weight, out_weight, hidden_weight, up_weight, down_weight),
        )
        output, tokens_grad, near_sums, landed, vectors, crossed, _ = backward_fast(
            dp_size, tokens, cotangent, fulls, kept, back_tables
        )
        (query_grad, key_grad, value_grad, gate_grad, out_grad, hidden_grad, up_grad, down_grad, tokens_grad,
         output) = finish(near_sums, landed, crossed, tokens_grad, output)
        group_scale_grad = vectors[2 : 2 + heads_here * DV // block].reshape(heads_here, DV)
        return (
            output,
            tokens_grad,
            vectors[0],
            query_grad,
            key_grad,
            value_grad,
            gate_grad,
            out_grad,
            lax.dynamic_slice_in_dim(group_scale_grad, data.me * group_block, group_block, 1),
            vectors[1],
            hidden_grad,
            up_grad,
            down_grad,
        )
    else:
        gains = jnp.concatenate([mixer_gain, feed_gain, group_gain.reshape(-1)])[None, :]
        gains = data.gather(gains, 0)
        mixer_scale = gains[:, :block].reshape(-1).astype(F32)
        feed_scale = gains[:, block : 2 * block].reshape(-1).astype(F32)
        group_scale = data.true_order(gains[:, 2 * block :], 0).astype(F32)
        group_scale = group_scale.reshape(dp_size, heads_here, -1).swapaxes(0, 1).reshape(heads_here, -1)

        query_key = data.gather(jnp.concatenate([query_weight, key_weight], axis=1), 0)
        value_full = data.gather(value_weight, 0)
        gate_full = data.gather(gate_weight, 0)
        out_full = data.gather(out_weight, 1)
        hidden_full = data.gather(hidden_weight, 0)
        up_full = data.gather(up_weight, 0)
        down_full = data.gather(down_weight, 1)

        mixer_input = layer_norm(inputs.astype(F32), mixer_scale).astype(BF16)

        both = plain_product(mixer_input, query_key)
        query = both[:, :width]
        keyset = both[:, width:]
        values = plain_product(mixer_input, value_full).astype(BF16)
        gate_in = plain_product(mixer_input, gate_full)
        turned_query = rotate(query, heads_here, 1.0).astype(BF16).reshape(length, heads_here, DK)
        turned_keys = rotate(keyset, heads_here, 1.0).astype(BF16).reshape(length, heads_here, DK)
        scores, row_totals, denominators = core_scores(turned_query, turned_keys, decays)
        weights = (scores / denominators).astype(BF16)
        value_heads = values.reshape(length, heads_here, DV)
        retained = jnp.einsum("hqk,khd->qhd", weights, value_heads, preferred_element_type=F32)
        retained = retained.reshape(length, heads_here * DV)
        mixed = gate_piece(retained, gate_in, group_scale).astype(BF16)

        branch = token_sum(team, row_terms(mixed, out_full), length)
        residual = my_rows(inputs).astype(F32) + branch
        feed_input = token_gather(team, layer_norm(residual, feed_scale).astype(BF16))
        hidden_pre = plain_product(feed_input, hidden_full)
        up_pre = plain_product(feed_input, up_full)

    activity, feed_back = jax.vjp(feed_piece, hidden_pre, up_pre)
    activity = activity.astype(BF16)
    activity_grad = back_product(cot, down_full)
    hidden_grad, up_grad = feed_back(activity_grad)
    hidden_grad = hidden_grad.astype(BF16)
    up_grad = up_grad.astype(BF16)

    def feed_rows(start, rows):
        return back_product(
            lax.dynamic_slice_in_dim(hidden_grad, start, rows, 0), hidden_full
        ) + back_product(lax.dynamic_slice_in_dim(up_grad, start, rows, 0), up_full)

    feed_input_grad = token_sum(team, feed_rows, length)
    _, feed_norm_back = jax.vjp(layer_norm, residual, feed_scale)
    residual_part, feed_scale_grad = feed_norm_back(feed_input_grad)
    residual_grad = my_rows(cot).astype(F32) + residual_part
    branch_grad = token_gather(team, residual_grad.astype(BF16))

    hidden_weight_grad = data.scatter_sum(
        lambda turn: row_product(half_of(feed_input, turn, 1), hidden_grad), 0
    )
    up_weight_grad = data.scatter_sum(
        lambda turn: row_product(half_of(feed_input, turn, 1), up_grad), 0
    )
    down_grad = data.scatter_sum(lambda turn: row_product(activity, half_of(cot, turn, 1)), 1)

    feed_out = token_sum(team, row_terms(activity, down_full), length)
    output = token_gather(team, (residual + feed_out).astype(BF16))
    output = data.true_order(output, 1)

    mixed_grad = back_product(branch_grad, out_full)
    _, gate_back = jax.vjp(gate_piece, retained, gate_in, group_scale)
    retained_grad, gate_grad, group_scale_grad = gate_back(mixed_grad)
    retained_grad = retained_grad.astype(BF16)
    gate_grad = gate_grad.astype(BF16)
    out_weight_grad = data.scatter_sum(
        lambda turn: row_product(mixed, half_of(branch_grad, turn, 1)), 1
    )
    gate_weight_grad = data.scatter_sum(
        lambda turn: row_product(half_of(mixer_input, turn, 1), gate_grad), 0
    )

    grad_heads = retained_grad.reshape(length, heads_here, DV)
    weights_grad = jnp.einsum("qhd,khd->hqk", grad_heads, value_heads, preferred_element_type=F32)
    value_parts = jnp.einsum("hqk,qhd->khd", weights, grad_heads, preferred_element_type=F32)
    value_parts = value_parts.reshape(length, heads_here * DV).astype(BF16)
    value_weight_grad = data.scatter_sum(
        lambda turn: row_product(half_of(mixer_input, turn, 1), value_parts), 0
    )
    inner_totals = jnp.sum(weights_grad * scores, axis=-1, keepdims=True)
    slope = row_totals / denominators
    scores_grad = weights_grad / denominators - inner_totals / (denominators * denominators) * slope
    raw_grad = (scores_grad * DK ** (-0.5) * decays).astype(BF16)
    turned_query_grad = jnp.einsum("hqk,khd->qhd", raw_grad, turned_keys, preferred_element_type=F32)
    turned_key_grad = jnp.einsum("hqk,qhd->khd", raw_grad, turned_query, preferred_element_type=F32)
    query_parts = rotate(turned_query_grad.reshape(length, width), heads_here, -1.0).astype(BF16)
    key_parts = rotate(turned_key_grad.reshape(length, width), heads_here, -1.0).astype(BF16)
    both_parts = jnp.concatenate([query_parts, key_parts], axis=1)
    both_grad = data.scatter_sum(
        lambda turn: row_product(half_of(mixer_input, turn, 1), both_parts), 0
    )
    query_weight_grad = both_grad[:, :width]
    key_weight_grad = both_grad[:, width:]

    def mixer_rows(start, rows):
        def cut(array):
            return lax.dynamic_slice_in_dim(array, start, rows, 0)

        return (
            back_product(cut(both_parts), query_key)
            + back_product(cut(value_parts), value_full)
            + back_product(cut(gate_grad), gate_full)
        )

    mixer_input_grad = token_sum(team, mixer_rows, length)
    _, mixer_norm_back = jax.vjp(layer_norm, my_rows(inputs).astype(F32), mixer_scale)
    input_part, mixer_scale_grad = mixer_norm_back(mixer_input_grad)
    tokens_grad = token_gather(team, (residual_grad + input_part).astype(BF16))
    tokens_grad = data.true_order(tokens_grad, 1).astype(F32)

    norm_grads = jnp.concatenate([mixer_scale_grad, feed_scale_grad]).reshape(2, -1)
    norm_grads = lax.psum(data.true_order(norm_grads, 1), ("dp", "tensor"))
    norm_grads = lax.dynamic_slice_in_dim(norm_grads, data.me * block, block, 1)
    group_scale_grad = lax.psum(group_scale_grad, "dp")
    group_scale_grad = lax.dynamic_slice_in_dim(group_scale_grad, data.me * group_block, group_block, 1)
    return (
        output,
        tokens_grad,
        norm_grads[0],
        query_weight_grad,
        key_weight_grad,
        value_weight_grad,
        gate_weight_grad,
        out_weight_grad,
        group_scale_grad,
        norm_grads[1],
        hidden_weight_grad,
        up_weight_grad,
        down_grad,
    )


def solution(mesh):
    columns = P("dp", "tensor")
    rows = P("tensor", "dp")
    placed = (
        P("dp", None),
        P("dp"),
        columns,
        columns,
        columns,
        columns,
        rows,
        rows,
        P("dp"),
        columns,
        columns,
        rows,
        P("dp", None),
    )
    given = (
        P("dp", None),
        P("dp", None),
        P("dp"),
        columns,
        columns,
        columns,
        columns,
        rows,
        rows,
        P("dp"),
        columns,
        columns,
        rows,
    )

    def body(*arrays):
        return on_device(mesh.shape["dp"], mesh.shape["tensor"], *arrays)

    return jax.shard_map(body, mesh=mesh, in_specs=placed, out_specs=given, check_vma=False)
```

```python
import jax
import jax.numpy as jnp
import numpy as np
from jax import lax
from jax.experimental import pallas as pl
from jax.experimental.pallas import tpu as pltpu
from jax.sharding import PartitionSpec as P

DK = 256
DV = 512

norm_epsilon = 1e-05
group_epsilon = 0.01
F32 = jnp.float32
BF16 = jnp.bfloat16


def layer_norm(values, scale_gain, epsilon=norm_epsilon):
    center = values - jnp.mean(values, axis=-1, keepdims=True)
    spread = jnp.mean(center * center, axis=-1, keepdims=True)
    return center * lax.rsqrt(spread + epsilon) * scale_gain


def group_norm(retained, scale_gain):
    shaped = retained.reshape(retained.shape[0], scale_gain.shape[0], scale_gain.shape[1])
    return layer_norm(shaped, scale_gain, group_epsilon).reshape(retained.shape)


def rotate(values, head_count, direction):
    length = values.shape[0]
    head_width = values.shape[1] // head_count
    half_width = head_width // 2
    places = jnp.arange(length, dtype=F32)[:, None]
    speeds = 10000.0 ** (-jnp.arange(half_width, dtype=F32) / half_width)
    angles = places * speeds[None, :]
    cosine = jnp.cos(angles)[:, None, :]
    sine_part = direction * jnp.sin(angles)[:, None, :]
    shaped = values.reshape(length, head_count, 2, half_width)
    front_half = shaped[:, :, 0]
    back_half = shaped[:, :, 1]
    turned = jnp.stack(
        [front_half * cosine - back_half * sine_part, front_half * sine_part + back_half * cosine],
        axis=2,
    )
    return turned.reshape(length, head_count * head_width)


def decays_plain(head_ids, length):
    log_rates = jnp.log1p(-jnp.exp2(-5.0 - head_ids))
    row_place = jnp.arange(length)[:, None]
    key_place = jnp.arange(length)[None, :]
    distance = jnp.maximum(row_place - key_place, 0).astype(F32)
    decays = jnp.where(
        (row_place >= key_place)[None], jnp.exp(log_rates[:, None, None] * distance[None]), 0.0
    )
    return decays


def decay_table(head_ids, length):
    decays = decays_plain(head_ids, length)
    return decays * lax.rsqrt(jnp.sum(decays, axis=-1, keepdims=True))


def plain_product(left, right):
    return jnp.dot(left, right, preferred_element_type=F32)


def row_product(left, right):
    return lax.dot_general(left, right, (((0,), (0,)), ((), ())), preferred_element_type=F32)


def back_product(left, right):
    return lax.dot_general(left, right, (((1,), (1,)), ((), ())), preferred_element_type=F32)


def core_scores(turned_query, turned_keys, decays):
    raw_scores = jnp.einsum("qhd,khd->hqk", turned_query, turned_keys, preferred_element_type=F32)
    scores = raw_scores * DK ** (-0.5) * decays
    row_totals = jnp.sum(scores, axis=-1, keepdims=True)
    denominators = jnp.sqrt(row_totals * row_totals + 1.0)
    return (scores, row_totals, denominators)


def feed_piece(hidden_pre, up_pre):
    return jax.nn.gelu(hidden_pre) * up_pre


def gate_piece(retained, gate_in, group_scale):
    return jax.nn.silu(gate_in) * group_norm(retained, group_scale)


class Ring:
    def __init__(self, name, size):
        self.name = name
        self.size = size
        self.outer = size // 2
        self.me = lax.axis_index(name)
        self.swap_pairs = [(i, i ^ 1) for i in range(size)]

    def swap(self, block):
        return lax.ppermute(block, self.name, self.swap_pairs)

    def shift(self, block, step):
        pairs = [
            (i, ((i // 2 + step) % self.outer) * 2 + i % 2) for i in range(self.size)
        ]
        return lax.ppermute(block, self.name, pairs)

    def block_at(self, place):
        turn, step = place // self.outer, place % self.outer
        outer = (self.me // 2 + self.outer - step) % self.outer
        return outer * 2 + (self.me % 2 + turn) % 2

    def place_of(self, block):
        turn = (block % 2 + self.me % 2) % 2
        step = (self.me // 2 + self.outer - block // 2) % self.outer
        return turn * self.outer + step

    def own_order(self, array, axis):
        width = array.shape[axis] // self.size
        return jnp.concatenate(
            [
                lax.dynamic_slice_in_dim(array, self.block_at(p) * width, width, axis)
                for p in range(self.size)
            ],
            axis=axis,
        )

    def true_order(self, array, axis):
        width = array.shape[axis] // self.size
        return jnp.concatenate(
            [
                lax.dynamic_slice_in_dim(array, self.place_of(b) * width, width, axis)
                for b in range(self.size)
            ],
            axis=axis,
        )

    def gather(self, block, axis):
        near = jnp.concatenate(
            [block] + [self.shift(block, s) for s in range(1, self.outer)], axis=axis
        )
        return jnp.concatenate([near, self.swap(near)], axis=axis)

    def scatter_sum(self, make_half, axis):
        far = self.swap(make_half(1).astype(BF16))
        near = make_half(0) + far.astype(F32)
        width = near.shape[axis] // self.outer
        total = lax.slice_in_dim(near, 0, width, axis=axis)
        for s in range(1, self.outer):
            part = lax.slice_in_dim(near, s * width, (s + 1) * width, axis=axis).astype(BF16)
            total = total + self.shift(part, -s).astype(F32)
        return total


def half_of(array, turn, axis):
    width = array.shape[axis] // 2
    return lax.slice_in_dim(array, turn * width, (turn + 1) * width, axis=axis)


def token_sum(ring, make_rows, rows):
    width = rows // ring.size
    outer, inner = ring.me // 2, ring.me % 2
    far = [make_rows((((outer + s) % ring.outer) * 2 + 1 - inner) * width, width) for s in range(ring.outer)]
    got = ring.swap(jnp.concatenate(far, axis=0).astype(BF16)).astype(F32)
    near = [
        make_rows((((outer + s) % ring.outer) * 2 + inner) * width, width)
        + lax.slice_in_dim(got, s * width, (s + 1) * width, axis=0)
        for s in range(ring.outer)
    ]
    total = near[0]
    for s in range(1, ring.outer):
        total = total + ring.shift(near[s].astype(BF16), s).astype(F32)
    return total


def token_gather(ring, block):
    return ring.true_order(ring.gather(block, 0), 0)


MESH = pl.DeviceIdType.MESH
ANY = pl.BlockSpec(memory_space=pl.ANY)


class Wires:
    def __init__(self, outer):
        self.outer = outer
        self.dp = lax.axis_index("dp")
        self.tensor = lax.axis_index("tensor")
        self.ring = self.dp // 2
        self.turn = self.dp % 2
        self.row = self.tensor // 2
        self.core = self.tensor % 2
        self.order = [1, outer - 1] + list(range(2, outer - 1))

    def far(self, step):
        return (lax.rem(self.ring + step, self.outer) * 2 + self.turn, self.tensor)

    def peer(self):
        return (self.ring * 2 + 1 - self.turn, self.tensor)

    def sibling(self):
        return (self.dp, self.row * 2 + 1 - self.core)

    def across(self):
        return (self.dp, (1 - self.row) * 2 + self.core)

    def block_at(self, place):
        turn, step = place // self.outer, place % self.outer
        return lax.rem(self.ring + self.outer - step, self.outer) * 2 + lax.rem(self.turn + turn, 2)

    def corner(self):
        return (self.dp, (1 - self.row) * 2 + 1 - self.core)

    def greet_all(self):
        barrier = pltpu.get_barrier_semaphore()
        partners = [(self.block_at(place), self.tensor) for place in range(1, 2 * self.outer)]
        partners += [self.sibling(), self.across(), self.corner()]
        for partner in partners:
            pl.semaphore_signal(barrier, inc=1, device_id=partner, device_id_type=MESH)
        pl.semaphore_wait(barrier, len(partners))


def remote(src, dst, send, recv, device):
    return pltpu.make_async_remote_copy(
        src_ref=src, dst_ref=dst, send_sem=send, recv_sem=recv, device_id=device, device_id_type=MESH
    )


def tile(index, rows):
    return pl.ds(pl.multiple_of(index * rows, rows), rows)


def norm_rows(values, gain, epsilon):
    center = values - jnp.mean(values, axis=-1, keepdims=True)
    spread = jnp.mean(center * center, axis=-1, keepdims=True)
    return center * lax.rsqrt(spread + epsilon) * gain


def silu(v):
    return v * (1.0 / (1.0 + jnp.exp(-v)))


N_ITEMS = 9
GAINS, QUERY, KEY, VALUE, GATE, OUT, HIDDEN, UP, DOWN = range(N_ITEMS)
STEP = 256
PART = 128


def forward_kernel(outer, heads, dims, *refs):
    length, model, block = dims
    quarter = length // 4
    tokens, cotangent, gains, cosine, sine, row_decay, key_decay = refs[:7]
    items = (gains,) + refs[7:15]
    fulls = refs[15:24]
    (mixer_out, query_out, key_out, value_out, retained_out, gate_out, mixed_out, residual_out,
     feed_out, hidden_out, up_out, activity_out) = refs[24:36]
    (slot_a, slot_b, slot_o, wide, mixer, rq, rk, values, kept, gate_in, mixed, residual, csend, crecv, ysend,
     yrecv, cos_v, sin_v, rowd, keyd, gain_v, gain_m, gain_f, gain_g,
     loc, zs, zr, xs, xr, ts, tr, ls, os_) = refs[36:]
    wires = Wires(outer)
    rows = length // STEP
    units = slot_a.shape[1]

    def piece(item, place):
        if item in (OUT, DOWN):
            return fulls[item].at[:, pl.ds(place * block, block)]
        height = items[item].shape[0]
        return fulls[item].at[pl.ds(place * height, height)]

    last = outer - 1
    up = wires.ring < last
    down = wires.ring > 0

    def along(item, source, place, step):
        device = (jnp.clip(wires.ring + step, 0, last) * 2 + wires.turn, wires.tensor)
        return remote(source, piece(item, place), zs.at[item, place], zr.at[item, place], device)

    def climb(item, source, base):
        @pl.when(up)
        def _():
            along(item, source, base + 1, 1).start()

        @pl.when(down)
        def _():
            along(item, source, base + last, -1).start()

    def beside(item, step):
        src = items[item] if step == 0 else piece(item, step)
        return remote(src, piece(item, outer + step), xs.at[item, step], xr.at[item, step], wires.peer())

    def own(item):
        return pltpu.make_async_copy(items[item], piece(item, 0), loc.at[item])

    def issue(item, cross=True):
        climb(item, items[item], 0)
        if cross:
            beside(item, 0).start()

    def hops(item, base, cross, which=None):
        for hop in which or range(1, outer):
            @pl.when(hop <= wires.ring)
            def _():
                along(item, piece(item, base + hop), base + hop, 1).wait_recv()
                if hop < last:
                    @pl.when(up)
                    def _():
                        along(item, piece(item, base + hop), base + hop + 1, 1).start()
                if cross:
                    beside(item, hop).start()

            @pl.when(hop <= last - wires.ring)
            def _():
                place = outer - hop
                along(item, piece(item, base + place), base + place, 1).wait_recv()
                if hop < last:
                    @pl.when(down)
                    def _():
                        along(item, piece(item, base + place), base + place - 1, -1).start()
                if cross:
                    beside(item, place).start()

    def pass_on(item):
        hops(item, 0, item != DOWN)

    def climb_sent(item, base):
        @pl.when(up)
        def _():
            along(item, piece(item, base), base + 1, 1).wait_send()

        @pl.when(down)
        def _():
            along(item, piece(item, base), base + last, -1).wait_send()

        for hop in range(1, last):
            @pl.when((hop <= wires.ring) & up)
            def _():
                along(item, piece(item, base + hop), base + hop + 1, 1).wait_send()

            @pl.when((hop <= last - wires.ring) & down)
            def _():
                along(item, piece(item, base + outer - hop), base + outer - hop - 1, -1).wait_send()

    def arrived(item):
        if item != UP:
            own(item).wait()
        for step in range(outer if item != DOWN else 1):
            beside(item, step).wait_recv()

    def load(src, dst, index):
        copy = pltpu.make_async_copy(src, dst, ls.at[index])
        copy.start()
        return copy

    stores = []

    def store(src, dst):
        copy = pltpu.make_async_copy(src, dst, os_.at[len(stores)])
        copy.start()
        stores.append(copy)
        return copy

    def gain_copy(place):
        turn, step = place // outer, place % outer
        there = piece(GAINS, turn * outer + (outer - step) % outer)
        device = (wires.block_at(place), wires.tensor)
        return remote(gains, there, zs.at[GAINS, place], zr.at[GAINS, turn * outer + (outer - step) % outer], device)

    wires.greet_all()
    for place in range(1, 2 * outer):
        gain_copy(place).start()
    for item in range(N_ITEMS):
        own(item).start()
    issue(QUERY)
    issue(KEY)
    issue(VALUE)
    beside(DOWN, 0).start()

    def own_blocks(source, target):
        copies = []
        for place in range(2 * outer):
            at = pl.multiple_of(wires.block_at(place) * block, block)
            copies.append(load(source.at[:, pl.ds(at, block)], target.at[:, pl.ds(place * block, block)], place))
        return copies

    first = 2 * outer
    loads = own_blocks(tokens, wide)
    loads.append(load(cosine, cos_v, first))
    loads.append(load(sine, sin_v, first + 1))
    loads.append(load(row_decay, rowd, first + 2))
    loads.append(load(key_decay, keyd, first + 3))
    own(GAINS).wait()
    for place in range(1, 2 * outer):
        gain_copy(place).wait_recv()
    for copy in loads:
        copy.wait()
    copy = load(fulls[GAINS], gain_v, 0)
    copy.wait()
    group = jnp.zeros((1, heads * DV), F32)
    for place in range(2 * outer):
        line = gain_v[place * 16 : place * 16 + 1, :].astype(F32)
        gain_m[:, place * block : (place + 1) * block] = line[:, :block]
        gain_f[:, place * block : (place + 1) * block] = line[:, block : 2 * block]
        group = group + line[:, 2 * block :]
    gain_g[...] = group

    @pl.loop(0, length // 128)
    def _(r):
        at = tile(r, 128)
        mixer[at, :] = norm_rows(wide[at, :].astype(F32), gain_m[...], norm_epsilon).astype(BF16)

    mine = tile(wires.tensor, quarter)
    residual[...] = wide[mine, :].astype(F32)
    mixer_store = store(mixer, mixer_out)
    pass_on(QUERY)
    pass_on(KEY)
    issue(GATE)
    pass_on(VALUE)
    issue(OUT)
    hops(GATE, 0, True, (1,))
    arrived(QUERY)
    arrived(KEY)
    narrow = heads * DK
    copy = load(fulls[QUERY], slot_a.at[:, pl.ds(0, narrow)], 0)
    other = load(fulls[KEY], slot_a.at[:, pl.ds(narrow, narrow)], 1)
    copy.wait()
    other.wait()

    @pl.loop(0, rows)
    def _(r):
        at = tile(r, STEP)
        both = jnp.dot(mixer[at, :], slot_a[...], preferred_element_type=F32)
        c, s = cos_v[at, :], sin_v[at, :]
        half = DK // 2
        for target, base in ((rq, 0), (rk, narrow)):
            for h in range(heads):
                lo = base + h * DK
                a, b = both[:, lo : lo + half], both[:, lo + half : lo + DK]
                target[at, h * DK : h * DK + half] = (a * c - b * s).astype(BF16)
                target[at, h * DK + half : (h + 1) * DK] = (a * s + b * c).astype(BF16)

    store(rq, query_out)
    store(rk, key_out)
    hops(GATE, 0, True, (2, 3))
    issue(HIDDEN)
    hops(OUT, 0, True, (1,))
    arrived(VALUE)
    load(fulls[VALUE], slot_b, 0).wait()

    @pl.loop(0, rows)
    def _(r):
        at = tile(r, STEP)
        values[at, :] = jnp.dot(mixer[at, :], slot_b[...], preferred_element_type=F32).astype(BF16)

    store(values, value_out)
    for h in range(heads):
        for r in range(rows):
            at = slice(r * STEP, (r + 1) * STEP)
            upto = (r + 1) * STEP
            q = rq[at, h * DK : (h + 1) * DK]
            k = rk[:upto, h * DK : (h + 1) * DK]
            raw = lax.dot_general(q, k, (((1,), (1,)), ((), ())), preferred_element_type=F32)
            fade = rowd[at, h : h + 1] * keyd[h : h + 1, :upto]
            place = lax.broadcasted_iota(jnp.int32, (STEP, upto), 0) + r * STEP
            under = place >= lax.broadcasted_iota(jnp.int32, (STEP, upto), 1)
            scores = raw * jnp.where(under, fade, 0.0)
            total = jnp.sum(scores, axis=-1, keepdims=True)
            share = (scores * lax.rsqrt(total * total + 1.0)).astype(BF16)
            kept[at, h * DV : (h + 1) * DV] = jnp.dot(
                share, values[:upto, h * DV : (h + 1) * DV], preferred_element_type=F32
            )
    kept_store = store(kept, retained_out)
    hops(OUT, 0, True, (2, 3))
    issue(UP)
    hops(HIDDEN, 0, True, (1,))
    arrived(GATE)
    load(fulls[GATE], slot_a, 0).wait()

    @pl.loop(0, rows)
    def _(r):
        at = tile(r, STEP)
        gate = jnp.dot(mixer[at, :], slot_a[...], preferred_element_type=F32)
        gate_in[at, :] = gate
        for h in range(heads):
            cols = slice(h * DV, (h + 1) * DV)
            normed = norm_rows(kept[at, cols], gain_g[:, cols], group_epsilon)
            mixed[at, cols] = (silu(gate[:, cols]) * normed).astype(BF16)

    mixer_store.wait()
    cot_loads = own_blocks(cotangent, mixer)
    gate_store = store(gate_in, gate_out)
    mixed_store = store(mixed, mixed_out)
    hops(HIDDEN, 0, True, (2, 3))
    hops(UP, 0, True, (1,))
    issue(DOWN, False)
    arrived(DOWN)
    climb(DOWN, piece(DOWN, outer), outer)
    arrived(OUT)
    load(fulls[OUT], slot_o, first).wait()

    def branch_rows(index):
        return jnp.dot(mixed[tile(index, quarter), :], slot_o[...], preferred_element_type=F32)

    def to_sibling(s):
        return remote(csend.at[s], crecv.at[s], ts.at[s], tr.at[s], wires.sibling())

    cross = remote(ysend, yrecv, ts.at[2], tr.at[2], wires.across())
    for s in (1, 0):
        owner = lax.rem(wires.row + s, 2) * 2 + 1 - wires.core
        csend[s] = branch_rows(owner).astype(BF16)
        to_sibling(s).start()
    part = branch_rows((1 - wires.row) * 2 + wires.core)
    to_sibling(1).wait_recv()
    ysend[...] = (part + crecv[1].astype(F32)).astype(BF16)
    cross.start()
    residual[...] += branch_rows(wires.tensor)
    to_sibling(0).wait_recv()
    residual[...] += crecv[0].astype(F32)
    hops(UP, 0, True, (2, 3))
    hops(DOWN, 0, False, (1,))
    cross.wait_recv()
    residual[...] += yrecv[...].astype(F32)
    store(residual, residual_out)
    feed_mine = wide.at[mine]

    @pl.loop(0, quarter // 128)
    def _(r):
        at = tile(r, 128)
        ysend_rows = norm_rows(residual[at, :], gain_f[...], norm_epsilon).astype(BF16)
        feed_mine[at, :] = ysend_rows

    feed_cross = remote(feed_mine, feed_mine, ts.at[3], tr.at[3], wires.across())
    feed_near = remote(feed_mine, feed_mine, ts.at[4], tr.at[4], wires.sibling())
    theirs = wide.at[tile((1 - wires.row) * 2 + wires.core, quarter)]
    feed_far = remote(theirs, theirs, ts.at[5], tr.at[5], wires.sibling())
    feed_cross.start()
    feed_near.start()
    hops(DOWN, 0, False, (2, 3))
    hops(DOWN, outer, False, (1,))
    feed_cross.wait_recv()
    feed_far.start()
    near_cols, far_cols = pl.ds(0, model // 2), pl.ds(model // 2, model // 2)
    down_load = load(fulls[DOWN].at[:, near_cols], slot_o.at[:, near_cols], first + 1)
    own(UP).wait()
    up_load = load(fulls[UP].at[near_cols], slot_a.at[near_cols], first + 2)
    for copy in cot_loads:
        copy.wait()
    down_load.wait()
    gate_store.wait()

    def grads_half(at, cols):
        return lax.dot_general(
            mixer[at, cols], slot_o[:, cols], (((1,), (1,)), ((), ())), preferred_element_type=F32
        )

    @pl.loop(0, rows)
    def _(r):
        at = tile(r, STEP)
        gate_in[at, :] = grads_half(at, near_cols)

    hops(DOWN, outer, False, (2,))
    arrived(HIDDEN)
    load(fulls[HIDDEN], slot_b, first).wait()
    feed_near.wait_recv()
    feed_far.wait_recv()
    store(wide, feed_out)
    kept_store.wait()

    @pl.loop(0, rows)
    def _(r):
        at = tile(r, STEP)
        kept[at, :] = jnp.dot(wide[at, :], slot_b[...], preferred_element_type=F32)

    hops(DOWN, outer, False, (3,))
    load(fulls[DOWN].at[:, far_cols], slot_o.at[:, far_cols], first + 1).wait()

    @pl.loop(0, rows)
    def _(r):
        at = tile(r, STEP)
        gate_in[at, :] += grads_half(at, far_cols)

    arrived(UP)
    load(fulls[UP].at[far_cols], slot_a.at[far_cols], first).wait()
    up_load.wait()
    mixed_store.wait()

    @pl.loop(0, length // PART)
    def _(r):
        at = tile(r, PART)
        u = jnp.dot(wide[at, :], slot_a[...], preferred_element_type=F32)
        h, grads = kept[at, :], gate_in[at, :]
        t = jnp.tanh(SQRT_2_PI * (h + CUBIC * h * h * h))
        gelu = 0.5 * h * (1.0 + t)
        slope = 0.5 * (1.0 + t) + 0.5 * h * (1.0 - t * t) * (SQRT_2_PI * (1.0 + 3.0 * CUBIC * h * h))
        mixed[at, :] = (gelu * u).astype(BF16)
        slot_b[at, :] = (grads * u * slope).astype(BF16)
        slot_o[at, pl.ds(0, units)] = (grads * gelu).astype(BF16)

    store(mixed, activity_out)
    store(slot_b.at[pl.ds(0, length)], hidden_out)
    store(slot_o.at[:, pl.ds(0, units)], up_out)
    for copy in stores:
        if not any(copy is done for done in (kept_store, gate_store, mixer_store, mixed_store)):
            copy.wait()
    for s in range(2):
        to_sibling(s).wait_send()
    for copy in (cross, feed_cross, feed_near, feed_far):
        copy.wait_send()
    for place in range(1, 2 * outer):
        gain_copy(place).wait_send()
    for item in range(1, N_ITEMS):
        climb_sent(item, 0)
        for step in range(outer if item != DOWN else 1):
            beside(item, step).wait_send()
    climb_sent(DOWN, outer)


def position_tables(length, heads):
    half = DK // 2
    speeds = 10000.0 ** (-np.arange(half, dtype=np.float32) / np.float32(half))
    angles = np.arange(length, dtype=np.float32)[:, None] * speeds.astype(np.float32)[None, :]
    pair = [np.cos(angles), np.sin(angles)]
    turns = [t.reshape(length // PART, PART, half).swapaxes(0, 1).reshape(PART, -1) for t in pair]
    rates = np.log1p(-np.exp2(-5.0 - np.arange(heads, dtype=np.float64)))[:, None]
    places = np.arange(length, dtype=np.float64)[None, :]
    sums = np.expm1(rates * (places + 1)) / np.expm1(rates)
    row_decay = np.exp(rates * (places - length // 2)) / np.sqrt(sums) * DK**-0.5
    key_decay = np.exp(rates * (length // 2 - places))
    return [jnp.asarray(np.asarray(t, np.float32)) for t in (*pair, np.stack(turns), row_decay, key_decay)]


def forward_fast(dp_size, tokens, cotangent, gains, tables, weights):
    outer = dp_size // 2
    length, model = tokens.shape
    block = model // dp_size
    heads = weights[0].shape[1] // DK
    units = weights[3].shape[1]
    wide = units
    shapes = [(gains.shape[0] * dp_size, gains.shape[1])]
    for place, weight in enumerate(weights):
        if place + 1 in (OUT, DOWN):
            shapes.append((weight.shape[0], model))
        else:
            shapes.append((model, weight.shape[1]))
    out_shape = [jax.ShapeDtypeStruct(s, BF16) for s in shapes]
    half = heads * DK
    for shape, kind in (
        ((length, model), BF16),
        ((length, half), BF16),
        ((length, half), BF16),
        ((length, wide), BF16),
        ((length, wide), F32),
        ((length, wide), F32),
        ((length, wide), BF16),
        ((length // 4, model), F32),
        ((length, model), BF16),
        ((length, units), BF16),
        ((length, units), BF16),
        ((length, units), BF16),
    ):
        out_shape.append(jax.ShapeDtypeStruct(shape, kind))
    quarter = length // 4
    dma = pltpu.SemaphoreType.DMA
    scratch = [
        pltpu.VMEM((model, wide), BF16),
        pltpu.VMEM((model, wide), BF16),
        pltpu.VMEM((wide, model), BF16),
        pltpu.VMEM((length, model), BF16),
        pltpu.VMEM((length, model), BF16),
        pltpu.VMEM((length, half), BF16),
        pltpu.VMEM((length, half), BF16),
        pltpu.VMEM((length, wide), BF16),
        pltpu.VMEM((length, wide), F32),
        pltpu.VMEM((length, wide), F32),
        pltpu.VMEM((length, wide), BF16),
        pltpu.VMEM((quarter, model), F32),
        pltpu.VMEM((2, quarter, model), BF16),
        pltpu.VMEM((2, quarter, model), BF16),
        pltpu.VMEM((quarter, model), BF16),
        pltpu.VMEM((quarter, model), BF16),
        pltpu.VMEM(tables[0].shape, F32),
        pltpu.VMEM(tables[1].shape, F32),
        pltpu.VMEM(tables[2].shape, F32),
        pltpu.VMEM(tables[3].shape, F32),
        pltpu.VMEM(shapes[0], BF16),
        pltpu.VMEM((1, model), F32),
        pltpu.VMEM((1, model), F32),
        pltpu.VMEM((1, heads * DV), F32),
        dma((N_ITEMS,)),
        dma((N_ITEMS, 2 * outer)),
        dma((N_ITEMS, 2 * outer)),
        dma((N_ITEMS, outer)),
        dma((N_ITEMS, outer)),
        dma((6,)),
        dma((6,)),
        dma((2 * outer + 4,)),
        dma((14,)),
    ]

    def kernel(*refs):
        forward_kernel(outer, heads, (length, model, block), *refs)

    results = pl.pallas_call(
        kernel,
        out_shape=out_shape,
        in_specs=[ANY] * (7 + len(weights)),
        out_specs=[ANY] * len(out_shape),
        scratch_shapes=scratch,
        compiler_params=pltpu.CompilerParams(
            collective_id=0, has_side_effects=True, vmem_limit_bytes=58 * 1024 * 1024
        ),
    )(tokens, cotangent, gains, *tables, *weights)
    return results[: N_ITEMS], results[N_ITEMS:]


N_GRADS = 7
(G_DOWN, G_HIDDEN, G_UP, G_OUT, G_GATE, G_VALUE, G_BOTH) = range(N_GRADS)
FLOW = (2, 3, 1, 0)
SQRT_2_PI = 0.7978845608028654
CUBIC = 0.044715


def rows_dot(left, right):
    return lax.dot_general(left, right, (((0,), (0,)), ((), ())), preferred_element_type=F32)


def back_dot(left, right):
    return lax.dot_general(left, right, (((1,), (1,)), ((), ())), preferred_element_type=F32)


def norm_back(values, grads, gain, epsilon):
    center = values - jnp.mean(values, axis=-1, keepdims=True)
    inverse = lax.rsqrt(jnp.mean(center * center, axis=-1, keepdims=True) + epsilon)
    unit = center * inverse
    u = grads * gain
    mean = jnp.mean(u, axis=-1, keepdims=True)
    slope = jnp.mean(u * unit, axis=-1, keepdims=True)
    return (u - mean - unit * slope) * inverse, grads * unit


def backward_kernel(outer, heads, dims, *refs):
    length, model, block, units = dims
    quarter = length // 4
    half = model // 2
    (tokens, cotangent, gains, query_full, key_full, value_full, gate_full, out_full, hidden_full, up_full,
     down_full, mixer_in, query_in, key_in, value_in, retained_in, gate_in, mixed_in, residual_in, feed_in,
     hidden_in, up_in, activity_in, turns, key_decay) = refs[:25]
    (output, tokens_out, near_out, z_land, vector_out, x_land, branch_land) = refs[25:32]
    (u0, u1, u2, u3, u4, act, hid, upg, both, fa, fb, x_ring, x_extra, z_ring, x_stage, acc, csend, crecv, ysend, yrecv,
     stage, grad_q, value_q, keyd, gain_v, gain_m, gain_f, gain_g,
     vec_t, vec_tr, vec_d, vec_dr, vec_g,
     xs, xr, zs, zr, ts, tr, gs, gr, vs, vr, ls, fs, st, ac) = refs[32:]
    wires = Wires(outer)
    rows = length // STEP
    mine = tile(wires.tensor, quarter)
    near_rows = tile(wires.row * 2 + 1 - wires.core, quarter)
    across_index = (1 - wires.row) * 2 + wires.core
    across_rows = tile(across_index, quarter)
    corner_rows = tile((1 - wires.row) * 2 + 1 - wires.core, quarter)

    def load(src, dst, index):
        copy = pltpu.make_async_copy(src, dst, ls.at[index])
        copy.start()
        return copy

    def load_tall(src, dst, index):
        return [load(src.at[pl.ds(h * half, half)], dst.at[:, pl.ds(h * half, half)], index + h) for h in range(2)]

    def wait_all(copies):
        for copy in copies:
            copy.wait()

    def own_blocks(src, dst, index):
        copies = []
        for place in range(2 * outer):
            at = pl.multiple_of(wires.block_at(place) * block, block)
            copies.append(load(src.at[:, pl.ds(at, block)], dst.at[:, pl.ds(place * block, block)], index + place))
        return copies

    def true_blocks(src, dst, index):
        copies = []
        for place in range(2 * outer):
            at = pl.multiple_of(wires.block_at(place) * block, block)
            copies.append(load(src.at[:, pl.ds(place * block, block)], dst.at[:, pl.ds(at, block)], index + place))
        return copies

    def x_copy(item, s):
        source = x_extra if item == G_DOWN else x_ring.at[(item % 2) * outer + s]
        return remote(source, x_land.at[item, s], xs.at[item, s], xr.at[item, s], wires.peer())

    def z_copy(item, s):
        step = outer - 1 if s != outer - 1 else 1
        device = (lax.rem(wires.ring + step, outer) * 2 + wires.turn, wires.tensor)
        slot = (item % 2) * (outer - 1) + s - 1
        return remote(z_ring.at[slot], z_land.at[item, s - 1], zs.at[item, s], zr.at[item, s], device)

    def columns(place):
        return pl.ds(pl.multiple_of(place * block, block), block)

    def far(item, left, right, flow=FLOW, behind=None):
        for s in flow:
            if item >= 3:
                x_copy(item - 2, s).wait_send()
            product = rows_dot(left[:, columns(outer + s)], right[...])
            x_ring[(item % 2) * outer + s] = product.astype(BF16)
            if behind is None:
                x_copy(item, s).start()
        if behind is not None:
            behind.wait_send()
            for s in flow:
                x_copy(item, s).start()

    def acc_copy(item):
        return pltpu.make_async_copy(acc, near_out.at[item], ac.at[item])

    def staged(item, place, source):
        copy = pltpu.make_async_copy(source, x_stage.at[place], st.at[item, place])
        copy.start()
        return copy

    sides = ((0, G_DOWN), (1, N_GRADS))

    def down_product(turn, s):
        return rows_dot(u0[:, columns(turn * outer + s)], act[...])

    def down_give(s):
        for turn, item in sides:
            z_ring[(item % 2) * (outer - 1) + s - 1] = down_product(turn, s).astype(BF16)
            z_copy(item, s).start()

    def down_first():
        down_give(2)
        for turn, item in sides:
            z_ring[(item % 2) * (outer - 1)] = down_product(turn, 1).astype(BF16)
        x_extra[...] = down_product(1, 0).astype(BF16)
        acc[...] = down_product(0, 0)
        acc_copy(G_DOWN).start()

    def relay(item):
        z_copy(item, 2).wait_recv()
        staged(item, 2, z_land.at[item, 1]).wait()
        slot = (item % 2) * (outer - 1)
        z_ring[slot] = (z_ring[slot].astype(F32) + x_stage[2].astype(F32)).astype(BF16)
        z_copy(item, 1).start()

    def down_sum():
        z_copy(N_GRADS, 3).wait_recv()
        copy = staged(N_GRADS, 2, z_land.at[N_GRADS, 2])
        z_copy(N_GRADS, 1).wait_recv()
        other = staged(N_GRADS, 3, z_land.at[N_GRADS, 0])
        copy.wait()
        other.wait()
        total = x_extra[...].astype(F32) + x_stage[2].astype(F32) + x_stage[3].astype(F32)
        x_extra[...] = total.astype(BF16)

    def near(item, left, right, flow=FLOW):
        before = N_GRADS if item == 1 else item - 2
        for s in flow:
            x_copy(item, s).wait_recv()
            copy = staged(item, s % 2, x_land.at[item, s])
            if s:
                z_copy(before, s).wait_send()
            if s == 0:
                acc_copy(item - 1).wait()
            product = rows_dot(left[:, columns(s)], right[...])
            copy.wait()
            product = product + x_stage[s % 2].astype(F32)
            if s == 0:
                acc[...] = product
                acc_copy(item).start()
                continue
            z_ring[(item % 2) * (outer - 1) + s - 1] = product.astype(BF16)
            if s > 1:
                z_copy(item, s).start()

    class Round:
        def __init__(self, index):
            self.index = index
            self.cross = remote(ysend, yrecv, ts.at[index, 2], tr.at[index, 2], wires.across())

        def to_sibling(self, s):
            return remote(csend.at[s], crecv.at[s], ts.at[self.index, s], tr.at[self.index, s], wires.sibling())

        def give(self, terms):
            for s in (1, 0):
                owner = lax.rem(wires.row + s, 2) * 2 + 1 - wires.core
                for h in range(2):
                    cols = slice(h * half, (h + 1) * half)
                    csend[s, :, cols] = terms(tile(owner, quarter), h).astype(BF16)
                self.to_sibling(s).start()

        def hand_over(self, terms):
            self.to_sibling(1).wait_recv()
            for h in range(2):
                cols = slice(h * half, (h + 1) * half)
                ysend[:, cols] = (terms(across_rows, h) + crecv[1, :, cols].astype(F32)).astype(BF16)
            self.cross.start()

        def keep(self, terms, totals, add):
            for h in range(2):
                part = terms(mine, h)
                totals[h][...] = totals[h][...] + part if add else part
            self.to_sibling(0).wait_recv()
            for h in range(2):
                totals[h][...] += crecv[0, :, h * half : (h + 1) * half].astype(F32)

        def finish(self, totals):
            self.cross.wait_recv()
            for h in range(2):
                totals[h][...] += yrecv[:, h * half : (h + 1) * half].astype(F32)
            for s in range(2):
                self.to_sibling(s).wait_send()
            self.cross.wait_send()

    class Spread:
        def __init__(self, index, source, land):
            self.cross = remote(source, land.at[mine], gs.at[index, 0], gr.at[index, 0], wires.across())
            self.near = remote(source, land.at[mine], gs.at[index, 1], gr.at[index, 1], wires.sibling())
            there = land.at[across_rows]
            self.far = remote(there, there, gs.at[index, 2], gr.at[index, 2], wires.sibling())
            self.own = pltpu.make_async_copy(source, land.at[mine], gs.at[index, 3])

        def start(self):
            self.cross.start()
            self.near.start()
            self.own.start()

        def pass_on(self):
            self.cross.wait_recv()
            self.far.start()

        def sent(self):
            self.cross.wait_send()
            self.near.wait_send()
            self.own.wait()

        def end(self):
            self.far.wait_recv()
            self.far.wait_send()

    def stream(src_a, src_b, body):
        def copies(r, slot):
            at = tile(r, PART)
            return (
                pltpu.make_async_copy(src_a.at[at], fa.at[slot, pl.ds(0, PART)], fs.at[0, slot]),
                pltpu.make_async_copy(src_b.at[at], fb.at[slot], fs.at[1, slot]),
            )

        for copy in copies(0, 0):
            copy.start()

        @pl.loop(0, length // PART)
        def _(r):
            slot = lax.rem(r, 2)

            @pl.when(r + 1 < length // PART)
            def _():
                for copy in copies(r + 1, 1 - slot):
                    copy.start()

            for copy in copies(r, slot):
                copy.wait()
            body(tile(r, PART), fa.at[slot, pl.ds(0, PART)], fb.at[slot])

    wires.greet_all()
    n = 2 * outer
    hid_load = load(hidden_in, hid, n + 10)
    far_half, near_half = pl.ds(half, half), pl.ds(0, half)
    feed_load = load(feed_in.at[:, far_half], u2.at[:, far_half], n + 2)
    act_load = load(activity_in, act, n + 9)
    cot_loads = own_blocks(cotangent, u0, 0)
    upg_load = load(up_in, upg, n + 11)
    hidden_loads = load_tall(hidden_full, u3, n + 3)
    up_loads = load_tall(up_full, u4, n + 5)
    down_load = load(down_full, u1, n)
    gain_load = load(gains, gain_v, n + 1)
    residual_load = load(residual_in, value_q, n + 7)
    table_load = load(key_decay, keyd, n + 8)
    near_load = load(feed_in.at[:, near_half], u2.at[:, near_half], n + 12)
    hid_load.wait()
    feed_load.wait()
    far(G_HIDDEN, u2, hid)
    act_load.wait()
    wait_all(cot_loads)
    down_first()
    upg_load.wait()
    wait_all(hidden_loads)
    wait_all(up_loads)
    near_load.wait()

    def tall_terms(pairs):
        def terms(at, h):
            cols = slice(h * half, (h + 1) * half)
            total = None
            for left, right in pairs:
                part = back_dot(left[at, :], right[:, cols])
                total = part if total is None else total + part
            return total

        return terms

    feed_terms = tall_terms(((hid, u3), (upg, u4)))
    feed_round, output_round, mixer_round = Round(0), Round(1), Round(2)
    feed_round.give(feed_terms)
    far(G_UP, u2, upg)
    feed_round.hand_over(feed_terms)
    grad_halves = [grad_q.at[:, pl.ds(h * half, half)] for h in range(2)]
    value_halves = [value_q.at[:, pl.ds(h * half, half)] for h in range(2)]
    mixer_halves = [fa.at[h] for h in range(2)]
    feed_round.keep(feed_terms, grad_halves, False)
    table_load.wait()
    gain_load.wait()
    group = jnp.zeros((1, heads * DV), F32)
    for place in range(2 * outer):
        line = gain_v[place * 16 : place * 16 + 1, :].astype(F32)
        gain_m[:, place * block : (place + 1) * block] = line[:, :block]
        gain_f[:, place * block : (place + 1) * block] = line[:, block : 2 * block]
        group = group + line[:, 2 * block :]
    gain_g[...] = group
    vec_t[...] = jnp.zeros_like(vec_t)
    vec_d[...] = jnp.zeros_like(vec_d)
    vec_g[...] = jnp.zeros_like(vec_g)
    mixer_load = load(mixer_in, u3, n + 3)
    narrow = heads * DK
    core_loads = [load(value_in, u4.at[:, pl.ds(0, half)], n + 4),
                  load(query_in, u4.at[:, pl.ds(half, narrow)], n + 5),
                  load(key_in, u4.at[:, pl.ds(half + narrow, narrow)], n + 6)]
    down_give(3)
    residual_load.wait()
    feed_round.finish(grad_halves)

    @pl.loop(0, quarter // 128)
    def _(r):
        at = tile(r, 128)
        part, gain_part = norm_back(value_q[at, :], grad_q[at, :], gain_f[...], norm_epsilon)
        cot_at = pl.ds(pl.multiple_of(wires.tensor * quarter + r * 128, 128), 128)
        total = u0[cot_at, :].astype(F32) + part
        grad_q[at, :] = total
        stage[at, :] = total.astype(BF16)
        vec_t[1:2, :] += jnp.sum(gain_part, axis=0, keepdims=True)

    branch_spread = Spread(0, stage, branch_land)
    branch_spread.start()
    relay(G_DOWN)
    relay(N_GRADS)
    near(G_HIDDEN, u2, hid, (2, 3, 0))

    down_load.wait()

    def output_terms(at, h):
        return jnp.dot(act[at, :], u1[:, h * half : (h + 1) * half], preferred_element_type=F32)

    branch_spread.near.wait_recv()
    output_round.give(output_terms)
    output_round.keep(output_terms, value_halves, True)
    branch_spread.pass_on()
    output_round.hand_over(output_terms)
    branch_spread.sent()
    out_load = load(out_full, u1, n)
    branch_loads = [load(branch_land.at[at], u0.at[at], n + 7 + i) for i, at in
                    enumerate((mine, near_rows, across_rows))]
    mixed_load = load(mixed_in, act, n + 1)
    branch_spread.far.wait_recv()
    branch_loads.append(load(branch_land.at[corner_rows], u0.at[corner_rows], n + 2))
    wait_all(branch_loads)
    out_load.wait()

    hold = both

    def gate_tile(at, r_ref, g_ref):
        grads = back_dot(u0[at, :], u1[...])
        for h in range(heads):
            cols = slice(h * DV, (h + 1) * DV)
            x, g, m = r_ref[:, cols], g_ref[:, cols], grads[:, cols]
            scale = gain_g[:, cols]
            sig = 1.0 / (1.0 + jnp.exp(-g))
            swish = g * sig
            center = x - jnp.mean(x, axis=-1, keepdims=True)
            inverse = lax.rsqrt(jnp.mean(center * center, axis=-1, keepdims=True) + group_epsilon)
            unit = center * inverse
            passed = m * swish
            hid[at, cols] = (m * unit * scale * (sig * (1.0 + g * (1.0 - sig)))).astype(BF16)
            vec_g[:, cols] += jnp.sum(passed * unit, axis=0, keepdims=True)
            u = passed * scale
            mean = jnp.mean(u, axis=-1, keepdims=True)
            slope = jnp.mean(u * unit, axis=-1, keepdims=True)
            hold[at, cols] = ((u - mean - unit * slope) * inverse).astype(BF16)

    mixed_load.wait()
    far(G_OUT, u0, act)
    near(G_HIDDEN, u2, hid, (1,))
    stream(retained_in, gate_in, gate_tile)
    relay(G_HIDDEN)
    mixer_load.wait()
    near(G_UP, u2, upg)
    value_loads = load_tall(value_full, u2, n + 1)
    far(G_GATE, u3, hid)
    wait_all(core_loads)

    side = DK // 2
    turn_load = load(turns, fb, n + 8)
    turn_load.wait()

    def turned_back(grads, r, count):
        a, b = grads[:, :side], grads[:, side:]
        c = jnp.concatenate([fb[0, :, (r + i) * side : (r + i + 1) * side] for i in range(count)], axis=0)
        s = jnp.concatenate([fb[1, :, (r + i) * side : (r + i + 1) * side] for i in range(count)], axis=0)
        return (a * c + b * s).astype(BF16), (b * c - a * s).astype(BF16)

    for h in range(heads):
        vcols = slice(h * DV, (h + 1) * DV)
        qcols = slice(half + h * DK, half + (h + 1) * DK)
        kcols = slice(half + narrow + h * DK, half + narrow + (h + 1) * DK)
        for r in range(length // PART):
            at = slice(r * PART, (r + 1) * PART)
            upto = (r + 1) * PART
            raw = back_dot(u4[at, qcols], u4[:upto, kcols])
            place = lax.broadcasted_iota(jnp.int32, (PART, upto), 0) + r * PART
            under = place >= lax.broadcasted_iota(jnp.int32, (PART, upto), 1)
            fade = keyd[heads + h : heads + h + 1, at].reshape(PART, 1) * keyd[h : h + 1, :upto]
            fade = jnp.where(under, fade, 0.0)
            scores = raw * fade
            total = jnp.sum(scores, axis=-1, keepdims=True)
            inverse = lax.rsqrt(total * total + 1.0)
            u1[at, :upto] = (scores * inverse).astype(BF16)
            grads = back_dot(hold[at, vcols], u4[:upto, vcols])
            inner = jnp.sum(grads * scores, axis=-1, keepdims=True)
            drop = inner * total * inverse * inverse * inverse
            raw_grad = ((grads * inverse - drop) * fade).astype(BF16)
            u1[at, half : half + upto] = raw_grad
            query_grad = jnp.dot(raw_grad, u4[:upto, kcols], preferred_element_type=F32)
            lo, hi = turned_back(query_grad, r, 1)
            upg[at, h * DK : h * DK + side] = lo
            upg[at, h * DK + side : (h + 1) * DK] = hi
        for c in range(rows):
            at = slice(c * STEP, (c + 1) * STEP)
            after = slice(c * STEP, length)
            for i in range(1, STEP // PART):
                spare = slice(c * STEP, c * STEP + i * PART)
                late = slice(c * STEP + i * PART, c * STEP + (i + 1) * PART)
                u1[spare, late] = jnp.zeros((i * PART, PART), BF16)
                u1[spare, half + c * STEP + i * PART : half + c * STEP + (i + 1) * PART] = jnp.zeros(
                    (i * PART, PART), BF16
                )
            hold_grad = rows_dot(u1[after, c * STEP : (c + 1) * STEP], hold[after, vcols])
            key_grad = rows_dot(u1[after, half + c * STEP : half + (c + 1) * STEP], u4[after, qcols])
            hold[at, vcols] = hold_grad.astype(BF16)
            lo, hi = turned_back(key_grad, c * (STEP // PART), STEP // PART)
            upg[at, narrow + h * DK : narrow + h * DK + side] = lo
            upg[at, narrow + h * DK + side : narrow + (h + 1) * DK] = hi

    gate_loads = load_tall(gate_full, u1, n + 3)
    both_loads = []
    for h in range(2):
        source = pl.ds(h * half, half)
        both_loads.append(load(query_full.at[source], u4.at[:, pl.ds(h * half, narrow)], n + 5 + 2 * h))
        both_loads.append(load(key_full.at[source], u4.at[:, pl.ds(h * half + narrow, narrow)], n + 6 + 2 * h))

    down_sum()
    relay(G_UP)

    output_round.finish(value_halves)
    ysend[...] = value_q[...].astype(BF16)
    wait_all(true_blocks(ysend, stage, 0))
    output_spread = Spread(1, stage, output)
    output_spread.start()
    token_loads = []
    for place in range(2 * outer):
        at = pl.multiple_of(wires.block_at(place) * block, block)
        token_loads.append(load(tokens.at[mine, pl.ds(at, block)], ysend.at[:, pl.ds(place * block, block)], place))
    wait_all(token_loads)
    for r in range(2):
        at = slice(r * (quarter // 2), (r + 1) * (quarter // 2))
        value_q[at, :] = ysend[at, :].astype(F32)
    near(G_OUT, u0, act)
    far(G_VALUE, u3, hold)
    wait_all(gate_loads)
    wait_all(both_loads)
    wait_all(value_loads)
    mixer_terms = tall_terms(((upg, u4), (hold, u2), (hid, u1)))
    output_spread.near.wait_recv()
    mixer_round.give(mixer_terms)
    output_spread.pass_on()
    mixer_round.hand_over(mixer_terms)
    mixer_round.keep(mixer_terms, mixer_halves, False)
    relay(G_OUT)
    mixer_round.finish(mixer_halves)
    output_spread.sent()

    @pl.loop(0, quarter // 128)
    def _(r):
        at = tile(r, 128)
        grads = jnp.concatenate([fa[0, at, :], fa[1, at, :]], axis=1)
        part, gain_part = norm_back(value_q[at, :], grads, gain_m[...], norm_epsilon)
        ysend[at, :] = (grad_q[at, :] + part).astype(BF16)
        vec_t[0:1, :] += jnp.sum(gain_part, axis=0, keepdims=True)

    def vector_team(i, device):
        return remote(vec_t, vec_tr.at[i], vs.at[i], vr.at[i], device)

    team = (wires.sibling(), wires.across(), wires.corner())
    for i, device in enumerate(team):
        vector_team(i, device).start()
    wait_all(true_blocks(ysend, stage, 0))
    tokens_spread = Spread(2, stage, tokens_out)
    tokens_spread.start()
    near(G_GATE, u3, hid)
    far(G_BOTH, u3, upg, (2, 3))
    for i, device in enumerate(team):
        vector_team(i, device).wait_recv()
    summed = vec_t[0:2, :]
    for i in range(3):
        summed = summed + vec_tr[i, 0:2, :]
    for place in range(2 * outer):
        vec_d[place, 0:2, :] = summed[:, place * block : (place + 1) * block]
        for i in range(heads * DV // block):
            vec_d[place, 2 + i : 3 + i, :] = vec_g[:, i * block : (i + 1) * block]

    def vector_data(place):
        device = (wires.block_at(place), wires.tensor)
        return remote(vec_d.at[place], vec_dr.at[place], vs.at[3 + place], vr.at[3 + place], device)

    for place in range(1, 2 * outer):
        vector_data(place).start()
    tokens_spread.pass_on()
    relay(G_GATE)
    near(G_VALUE, u3, hold)
    relay(G_VALUE)
    far(G_BOTH, u3, upg, (1, 0), x_copy(G_BOTH, 2))
    x_copy(G_DOWN, 0).start()
    near(G_BOTH, u3, upg, (2, 3))
    near(G_BOTH, u3, upg, (1,))
    relay(G_BOTH)
    near(G_BOTH, u3, upg, (0,))
    vectors = vec_d[0]
    for place in range(1, 2 * outer):
        vector_data(place).wait_recv()
        vectors = vectors + vec_dr[place]
    vec_d[0] = vectors
    vector_store = load(vec_d.at[0], vector_out, 0)

    vector_store.wait()
    branch_spread.far.wait_send()
    output_spread.end()
    tokens_spread.near.wait_recv()
    tokens_spread.end()
    tokens_spread.sent()
    for i, device in enumerate(team):
        vector_team(i, device).wait_send()
    for place in range(1, 2 * outer):
        vector_data(place).wait_send()
    acc_copy(N_GRADS - 1).wait()
    x_copy(G_DOWN, 0).wait()
    for item in (N_GRADS - 2, N_GRADS - 1):
        for s in range(outer):
            if (item, s) != (G_BOTH, 2):
                x_copy(item, s).wait_send()
        for s in range(1, outer):
            z_copy(item, s).wait_send()
    for item in range(N_GRADS):
        for s in (1, outer - 1):
            z_copy(item, s).wait_recv()


def backward_fast(dp_size, tokens, cotangent, fulls, kept, tables):
    outer = dp_size // 2
    length, model = tokens.shape
    block = model // dp_size
    gains, query_full, key_full, value_full, gate_full, out_full, hidden_full, up_full, down_full = fulls
    (mixer_input, turned_query, turned_keys, values, retained, gate_in, mixed, residual, feed_input, hidden_pre,
     up_pre, activity) = kept
    heads = query_full.shape[1] // DK
    units = hidden_full.shape[1]
    quarter = length // 4
    shape = jax.ShapeDtypeStruct
    out_shape = [
        shape((length, model), BF16),
        shape((length, model), BF16),
        shape((N_GRADS, block, units), F32),
        shape((N_GRADS + 1, outer - 1, block, units), BF16),
        shape((8, block), F32),
        shape((N_GRADS, outer, block, units), BF16),
        shape((length, model), BF16),
    ]
    dma = pltpu.SemaphoreType.DMA
    vmem = pltpu.VMEM
    scratch = [vmem((length, model), BF16)] * 5 + [vmem((length, units), BF16)] * 4
    scratch += [vmem((2, STEP, units), F32), vmem((2, PART, units), F32)]
    scratch += [
        vmem((2 * outer, block, units), BF16),
        vmem((block, units), BF16),
        vmem((2 * (outer - 1), block, units), BF16),
        vmem((4, block, units), BF16),
        vmem((block, units), F32),
        vmem((2, quarter, model), BF16),
        vmem((2, quarter, model), BF16),
        vmem((quarter, model), BF16),
        vmem((quarter, model), BF16),
        vmem((quarter, model), BF16),
        vmem((quarter, model), F32),
        vmem((quarter, model), F32),
        vmem(tables[1].shape, F32),
        vmem(gains.shape, BF16),
        vmem((1, model), F32),
        vmem((1, model), F32),
        vmem((1, heads * DV), F32),
        vmem((8, model), F32),
        vmem((3, 8, model), F32),
        vmem((dp_size, 8, block), F32),
        vmem((dp_size, 8, block), F32),
        vmem((1, heads * DV), F32),
        dma((N_GRADS, outer)),
        dma((N_GRADS, outer)),
        dma((N_GRADS + 1, outer)),
        dma((N_GRADS + 1, outer)),
        dma((3, 3)),
        dma((3, 3)),
        dma((3, 4)),
        dma((3, 4)),
        dma((3 + dp_size,)),
        dma((3 + dp_size,)),
        dma((dp_size + 13,)),
        dma((2, 2)),
        dma((N_GRADS + 1, outer)),
        dma((N_GRADS,)),
    ]

    def kernel(*refs):
        backward_kernel(outer, heads, (length, model, block, units), *refs)

    operands = (tokens, cotangent, *fulls, *kept, *tables)
    return pl.pallas_call(
        kernel,
        out_shape=out_shape,
        in_specs=[ANY] * len(operands),
        out_specs=[ANY] * len(out_shape),
        scratch_shapes=scratch,
        compiler_params=pltpu.CompilerParams(
            collective_id=1, has_side_effects=True, vmem_limit_bytes=63 * 1024 * 1024
        ),
    )(*operands)


def finish(near_sums, z_land, x_land, tokens_grad, output):
    steps = 8
    _, block, units = near_sums.shape
    length, model = output.shape
    rows, across = block // steps, block // 128
    side = units * across // steps
    turned = (G_DOWN, G_OUT)
    order = (G_BOTH, G_VALUE, G_GATE, G_OUT, G_HIDDEN, G_UP, G_DOWN)
    operands, in_specs, out_specs, out_shape = [], [], [], []

    def add(array, lead, item):
        operands.append(array)
        if item in turned:
            in_specs.append(pl.BlockSpec((1,) * len(lead) + (128, side), lambda i: (*lead, i % across, i // across)))
        else:
            in_specs.append(pl.BlockSpec((1,) * len(lead) + (rows, units), lambda i: (*lead, i, 0)))

    for item in order:
        add(near_sums, (item,), item)
        add(z_land, (item, 0), item)
        add(z_land, (item, 2), item)
        if item == G_DOWN:
            add(x_land, (item, 0), item)
        if item == G_BOTH:
            shapes = [((block, units // 2), (rows, units // 2))] * 2
        else:
            shapes = [((block, units), (rows, units))]
        for whole, part in shapes:
            if item in turned:
                out_shape.append(jax.ShapeDtypeStruct((units, block), F32))
                out_specs.append(pl.BlockSpec((side, 128), lambda i: (i // across, i % across)))
            else:
                out_shape.append(jax.ShapeDtypeStruct(whole, F32))
                out_specs.append(pl.BlockSpec(part, lambda i: (i, 0)))
    for array, kind in ((tokens_grad, F32), (output, BF16)):
        operands.append(array)
        spec = pl.BlockSpec((length // steps, model), lambda i: (i, 0))
        in_specs.append(spec)
        out_specs.append(spec)
        out_shape.append(jax.ShapeDtypeStruct(array.shape, kind))

    def kernel(*refs):
        ins, outs = list(refs[: len(operands)]), list(refs[len(operands) :])
        for item in order:
            total = ins.pop(0)[0]
            for _ in range(3 if item == G_DOWN else 2):
                total = total + ins.pop(0)[0, 0].astype(F32)
            if item == G_BOTH:
                outs.pop(0)[...] = total[:, : units // 2]
                outs.pop(0)[...] = total[:, units // 2 :]
            else:
                outs.pop(0)[...] = total.T if item in turned else total
        for source, target in zip(ins, outs):
            target[...] = source[...].astype(target.dtype)

    return pl.pallas_call(
        kernel,
        grid=(steps,),
        out_shape=out_shape,
        in_specs=in_specs,
        out_specs=out_specs,
        compiler_params=pltpu.CompilerParams(vmem_limit_bytes=62 * 1024 * 1024),
    )(*operands)


def on_device(
    dp_size,
    tensor_size,
    tokens,
    mixer_gain,
    query_weight,
    key_weight,
    value_weight,
    gate_weight,
    out_weight,
    group_gain,
    feed_gain,
    hidden_weight,
    up_weight,
    down_weight,
    cotangent,
):
    data = Ring("dp", dp_size)
    team = Ring("tensor", tensor_size)
    length, model = tokens.shape
    quarter = length // tensor_size
    heads_here = query_weight.shape[1] // DK

    block = mixer_gain.shape[0]
    width = query_weight.shape[1]
    group_block = group_gain.shape[1]
    head_ids = (lax.axis_index("tensor") * heads_here + jnp.arange(heads_here)).astype(F32)
    decays = decay_table(head_ids, length)
    inputs = data.own_order(tokens, 1)
    cot = data.own_order(cotangent, 1)

    def my_rows(array):
        return lax.dynamic_slice_in_dim(array, team.me * quarter, quarter, 0)

    def row_terms(left, right):
        return lambda start, rows: plain_product(
            lax.dynamic_slice_in_dim(left, start, rows, 0), right
        )

    units = hidden_weight.shape[1]
    even = units == 2 * width == heads_here * DV == model // 2 and heads_here * DV // block <= 6
    if even and block % 128 == 0 and tensor_size == 4 and dp_size == 8 and length % 1024 == 0:
        group_line = lax.dynamic_update_slice(
            jnp.zeros((heads_here, DV), BF16), group_gain, (0, data.me * group_block)
        )
        gains = jnp.concatenate([mixer_gain, feed_gain, group_line.reshape(-1)])
        gains = jnp.broadcast_to(gains[None, :], (16, gains.shape[0]))
        cosine, sine, turns, row_decays, key_decays = position_tables(length, query_weight.shape[1] * tensor_size // DK)
        first = lax.axis_index("tensor") * heads_here
        row_decay = lax.dynamic_slice_in_dim(row_decays, first, heads_here, 0)
        key_decay = lax.dynamic_slice_in_dim(key_decays, first, heads_here, 0)
        tables = (cosine, sine, row_decay.T, key_decay)
        back_tables = (turns, jnp.concatenate([key_decay, row_decay]))
        fulls, kept = forward_fast(
            dp_size,
            tokens,
            cotangent,
            gains,
            tables,
            (query_weight, key_weight, value_weight, gate_weight, out_weight, hidden_weight, up_weight, down_weight),
        )
        output, tokens_grad, near_sums, landed, vectors, crossed, _ = backward_fast(
            dp_size, tokens, cotangent, fulls, kept, back_tables
        )
        (query_grad, key_grad, value_grad, gate_grad, out_grad, hidden_grad, up_grad, down_grad, tokens_grad,
         output) = finish(near_sums, landed, crossed, tokens_grad, output)
        group_scale_grad = vectors[2 : 2 + heads_here * DV // block].reshape(heads_here, DV)
        return (
            output,
            tokens_grad,
            vectors[0],
            query_grad,
            key_grad,
            value_grad,
            gate_grad,
            out_grad,
            lax.dynamic_slice_in_dim(group_scale_grad, data.me * group_block, group_block, 1),
            vectors[1],
            hidden_grad,
            up_grad,
            down_grad,
        )
    else:
        gains = jnp.concatenate([mixer_gain, feed_gain, group_gain.reshape(-1)])[None, :]
        gains = data.gather(gains, 0)
        mixer_scale = gains[:, :block].reshape(-1).astype(F32)
        feed_scale = gains[:, block : 2 * block].reshape(-1).astype(F32)
        group_scale = data.true_order(gains[:, 2 * block :], 0).astype(F32)
        group_scale = group_scale.reshape(dp_size, heads_here, -1).swapaxes(0, 1).reshape(heads_here, -1)

        query_key = data.gather(jnp.concatenate([query_weight, key_weight], axis=1), 0)
        value_full = data.gather(value_weight, 0)
        gate_full = data.gather(gate_weight, 0)
        out_full = data.gather(out_weight, 1)
        hidden_full = data.gather(hidden_weight, 0)
        up_full = data.gather(up_weight, 0)
        down_full = data.gather(down_weight, 1)

        mixer_input = layer_norm(inputs.astype(F32), mixer_scale).astype(BF16)

        both = plain_product(mixer_input, query_key)
        query = both[:, :width]
        keyset = both[:, width:]
        values = plain_product(mixer_input, value_full).astype(BF16)
        gate_in = plain_product(mixer_input, gate_full)
        turned_query = rotate(query, heads_here, 1.0).astype(BF16).reshape(length, heads_here, DK)
        turned_keys = rotate(keyset, heads_here, 1.0).astype(BF16).reshape(length, heads_here, DK)
        scores, row_totals, denominators = core_scores(turned_query, turned_keys, decays)
        weights = (scores / denominators).astype(BF16)
        value_heads = values.reshape(length, heads_here, DV)
        retained = jnp.einsum("hqk,khd->qhd", weights, value_heads, preferred_element_type=F32)
        retained = retained.reshape(length, heads_here * DV)
        mixed = gate_piece(retained, gate_in, group_scale).astype(BF16)

        branch = token_sum(team, row_terms(mixed, out_full), length)
        residual = my_rows(inputs).astype(F32) + branch
        feed_input = token_gather(team, layer_norm(residual, feed_scale).astype(BF16))
        hidden_pre = plain_product(feed_input, hidden_full)
        up_pre = plain_product(feed_input, up_full)

    activity, feed_back = jax.vjp(feed_piece, hidden_pre, up_pre)
    activity = activity.astype(BF16)
    activity_grad = back_product(cot, down_full)
    hidden_grad, up_grad = feed_back(activity_grad)
    hidden_grad = hidden_grad.astype(BF16)
    up_grad = up_grad.astype(BF16)

    def feed_rows(start, rows):
        return back_product(
            lax.dynamic_slice_in_dim(hidden_grad, start, rows, 0), hidden_full
        ) + back_product(lax.dynamic_slice_in_dim(up_grad, start, rows, 0), up_full)

    feed_input_grad = token_sum(team, feed_rows, length)
    _, feed_norm_back = jax.vjp(layer_norm, residual, feed_scale)
    residual_part, feed_scale_grad = feed_norm_back(feed_input_grad)
    residual_grad = my_rows(cot).astype(F32) + residual_part
    branch_grad = token_gather(team, residual_grad.astype(BF16))

    hidden_weight_grad = data.scatter_sum(
        lambda turn: row_product(half_of(feed_input, turn, 1), hidden_grad), 0
    )
    up_weight_grad = data.scatter_sum(
        lambda turn: row_product(half_of(feed_input, turn, 1), up_grad), 0
    )
    down_grad = data.scatter_sum(lambda turn: row_product(activity, half_of(cot, turn, 1)), 1)

    feed_out = token_sum(team, row_terms(activity, down_full), length)
    output = token_gather(team, (residual + feed_out).astype(BF16))
    output = data.true_order(output, 1)

    mixed_grad = back_product(branch_grad, out_full)
    _, gate_back = jax.vjp(gate_piece, retained, gate_in, group_scale)
    retained_grad, gate_grad, group_scale_grad = gate_back(mixed_grad)
    retained_grad = retained_grad.astype(BF16)
    gate_grad = gate_grad.astype(BF16)
    out_weight_grad = data.scatter_sum(
        lambda turn: row_product(mixed, half_of(branch_grad, turn, 1)), 1
    )
    gate_weight_grad = data.scatter_sum(
        lambda turn: row_product(half_of(mixer_input, turn, 1), gate_grad), 0
    )

    grad_heads = retained_grad.reshape(length, heads_here, DV)
    weights_grad = jnp.einsum("qhd,khd->hqk", grad_heads, value_heads, preferred_element_type=F32)
    value_parts = jnp.einsum("hqk,qhd->khd", weights, grad_heads, preferred_element_type=F32)
    value_parts = value_parts.reshape(length, heads_here * DV).astype(BF16)
    value_weight_grad = data.scatter_sum(
        lambda turn: row_product(half_of(mixer_input, turn, 1), value_parts), 0
    )
    inner_totals = jnp.sum(weights_grad * scores, axis=-1, keepdims=True)
    slope = row_totals / denominators
    scores_grad = weights_grad / denominators - inner_totals / (denominators * denominators) * slope
    raw_grad = (scores_grad * DK ** (-0.5) * decays).astype(BF16)
    turned_query_grad = jnp.einsum("hqk,khd->qhd", raw_grad, turned_keys, preferred_element_type=F32)
    turned_key_grad = jnp.einsum("hqk,qhd->khd", raw_grad, turned_query, preferred_element_type=F32)
    query_parts = rotate(turned_query_grad.reshape(length, width), heads_here, -1.0).astype(BF16)
    key_parts = rotate(turned_key_grad.reshape(length, width), heads_here, -1.0).astype(BF16)
    both_parts = jnp.concatenate([query_parts, key_parts], axis=1)
    both_grad = data.scatter_sum(
        lambda turn: row_product(half_of(mixer_input, turn, 1), both_parts), 0
    )
    query_weight_grad = both_grad[:, :width]
    key_weight_grad = both_grad[:, width:]

    def mixer_rows(start, rows):
        def cut(array):
            return lax.dynamic_slice_in_dim(array, start, rows, 0)

        return (
            back_product(cut(both_parts), query_key)
            + back_product(cut(value_parts), value_full)
            + back_product(cut(gate_grad), gate_full)
        )

    mixer_input_grad = token_sum(team, mixer_rows, length)
    _, mixer_norm_back = jax.vjp(layer_norm, my_rows(inputs).astype(F32), mixer_scale)
    input_part, mixer_scale_grad = mixer_norm_back(mixer_input_grad)
    tokens_grad = token_gather(team, (residual_grad + input_part).astype(BF16))
    tokens_grad = data.true_order(tokens_grad, 1).astype(F32)

    norm_grads = jnp.concatenate([mixer_scale_grad, feed_scale_grad]).reshape(2, -1)
    norm_grads = lax.psum(data.true_order(norm_grads, 1), ("dp", "tensor"))
    norm_grads = lax.dynamic_slice_in_dim(norm_grads, data.me * block, block, 1)
    group_scale_grad = lax.psum(group_scale_grad, "dp")
    group_scale_grad = lax.dynamic_slice_in_dim(group_scale_grad, data.me * group_block, group_block, 1)
    return (
        output,
        tokens_grad,
        norm_grads[0],
        query_weight_grad,
        key_weight_grad,
        value_weight_grad,
        gate_weight_grad,
        out_weight_grad,
        group_scale_grad,
        norm_grads[1],
        hidden_weight_grad,
        up_weight_grad,
        down_grad,
    )


def solution(mesh):
    columns = P("dp", "tensor")
    rows = P("tensor", "dp")
    placed = (
        P("dp", None),
        P("dp"),
        columns,
        columns,
        columns,
        columns,
        rows,
        rows,
        P("dp"),
        columns,
        columns,
        rows,
        P("dp", None),
    )
    given = (
        P("dp", None),
        P("dp", None),
        P("dp"),
        columns,
        columns,
        columns,
        columns,
        rows,
        rows,
        P("dp"),
        columns,
        columns,
        rows,
    )

    def body(*arrays):
        return on_device(mesh.shape["dp"], mesh.shape["tensor"], *arrays)

    return jax.shard_map(body, mesh=mesh, in_specs=placed, out_specs=given, check_vma=False)
```

```python
import jax
import jax.numpy as jnp
import numpy as np
from jax import lax
from jax.experimental import pallas as pl
from jax.experimental.pallas import tpu as pltpu
from jax.sharding import PartitionSpec as P

DK = 256
DV = 512

norm_epsilon = 1e-05
group_epsilon = 0.01
F32 = jnp.float32
BF16 = jnp.bfloat16


def layer_norm(values, scale_gain, epsilon=norm_epsilon):
    center = values - jnp.mean(values, axis=-1, keepdims=True)
    spread = jnp.mean(center * center, axis=-1, keepdims=True)
    return center * lax.rsqrt(spread + epsilon) * scale_gain


def group_norm(retained, scale_gain):
    shaped = retained.reshape(retained.shape[0], scale_gain.shape[0], scale_gain.shape[1])
    return layer_norm(shaped, scale_gain, group_epsilon).reshape(retained.shape)


def rotate(values, head_count, direction):
    length = values.shape[0]
    head_width = values.shape[1] // head_count
    half_width = head_width // 2
    places = jnp.arange(length, dtype=F32)[:, None]
    speeds = 10000.0 ** (-jnp.arange(half_width, dtype=F32) / half_width)
    angles = places * speeds[None, :]
    cosine = jnp.cos(angles)[:, None, :]
    sine_part = direction * jnp.sin(angles)[:, None, :]
    shaped = values.reshape(length, head_count, 2, half_width)
    front_half = shaped[:, :, 0]
    back_half = shaped[:, :, 1]
    turned = jnp.stack(
        [front_half * cosine - back_half * sine_part, front_half * sine_part + back_half * cosine],
        axis=2,
    )
    return turned.reshape(length, head_count * head_width)


def decays_plain(head_ids, length):
    log_rates = jnp.log1p(-jnp.exp2(-5.0 - head_ids))
    row_place = jnp.arange(length)[:, None]
    key_place = jnp.arange(length)[None, :]
    distance = jnp.maximum(row_place - key_place, 0).astype(F32)
    decays = jnp.where(
        (row_place >= key_place)[None], jnp.exp(log_rates[:, None, None] * distance[None]), 0.0
    )
    return decays


def decay_table(head_ids, length):
    decays = decays_plain(head_ids, length)
    return decays * lax.rsqrt(jnp.sum(decays, axis=-1, keepdims=True))


def plain_product(left, right):
    return jnp.dot(left, right, preferred_element_type=F32)


def row_product(left, right):
    return lax.dot_general(left, right, (((0,), (0,)), ((), ())), preferred_element_type=F32)


def back_product(left, right):
    return lax.dot_general(left, right, (((1,), (1,)), ((), ())), preferred_element_type=F32)


def core_scores(turned_query, turned_keys, decays):
    raw_scores = jnp.einsum("qhd,khd->hqk", turned_query, turned_keys, preferred_element_type=F32)
    scores = raw_scores * DK ** (-0.5) * decays
    row_totals = jnp.sum(scores, axis=-1, keepdims=True)
    denominators = jnp.sqrt(row_totals * row_totals + 1.0)
    return (scores, row_totals, denominators)


def feed_piece(hidden_pre, up_pre):
    return jax.nn.gelu(hidden_pre) * up_pre


def gate_piece(retained, gate_in, group_scale):
    return jax.nn.silu(gate_in) * group_norm(retained, group_scale)


class Ring:
    def __init__(self, name, size):
        self.name = name
        self.size = size
        self.outer = size // 2
        self.me = lax.axis_index(name)
        self.swap_pairs = [(i, i ^ 1) for i in range(size)]

    def swap(self, block):
        return lax.ppermute(block, self.name, self.swap_pairs)

    def shift(self, block, step):
        pairs = [
            (i, ((i // 2 + step) % self.outer) * 2 + i % 2) for i in range(self.size)
        ]
        return lax.ppermute(block, self.name, pairs)

    def block_at(self, place):
        turn, step = place // self.outer, place % self.outer
        outer = (self.me // 2 + self.outer - step) % self.outer
        return outer * 2 + (self.me % 2 + turn) % 2

    def place_of(self, block):
        turn = (block % 2 + self.me % 2) % 2
        step = (self.me // 2 + self.outer - block // 2) % self.outer
        return turn * self.outer + step

    def own_order(self, array, axis):
        width = array.shape[axis] // self.size
        return jnp.concatenate(
            [
                lax.dynamic_slice_in_dim(array, self.block_at(p) * width, width, axis)
                for p in range(self.size)
            ],
            axis=axis,
        )

    def true_order(self, array, axis):
        width = array.shape[axis] // self.size
        return jnp.concatenate(
            [
                lax.dynamic_slice_in_dim(array, self.place_of(b) * width, width, axis)
                for b in range(self.size)
            ],
            axis=axis,
        )

    def gather(self, block, axis):
        near = jnp.concatenate(
            [block] + [self.shift(block, s) for s in range(1, self.outer)], axis=axis
        )
        return jnp.concatenate([near, self.swap(near)], axis=axis)

    def scatter_sum(self, make_half, axis):
        far = self.swap(make_half(1).astype(BF16))
        near = make_half(0) + far.astype(F32)
        width = near.shape[axis] // self.outer
        total = lax.slice_in_dim(near, 0, width, axis=axis)
        for s in range(1, self.outer):
            part = lax.slice_in_dim(near, s * width, (s + 1) * width, axis=axis).astype(BF16)
            total = total + self.shift(part, -s).astype(F32)
        return total


def half_of(array, turn, axis):
    width = array.shape[axis] // 2
    return lax.slice_in_dim(array, turn * width, (turn + 1) * width, axis=axis)


def token_sum(ring, make_rows, rows):
    width = rows // ring.size
    outer, inner = ring.me // 2, ring.me % 2
    far = [make_rows((((outer + s) % ring.outer) * 2 + 1 - inner) * width, width) for s in range(ring.outer)]
    got = ring.swap(jnp.concatenate(far, axis=0).astype(BF16)).astype(F32)
    near = [
        make_rows((((outer + s) % ring.outer) * 2 + inner) * width, width)
        + lax.slice_in_dim(got, s * width, (s + 1) * width, axis=0)
        for s in range(ring.outer)
    ]
    total = near[0]
    for s in range(1, ring.outer):
        total = total + ring.shift(near[s].astype(BF16), s).astype(F32)
    return total


def token_gather(ring, block):
    return ring.true_order(ring.gather(block, 0), 0)


MESH = pl.DeviceIdType.MESH
ANY = pl.BlockSpec(memory_space=pl.ANY)


class Wires:
    def __init__(self, outer):
        self.outer = outer
        self.dp = lax.axis_index("dp")
        self.tensor = lax.axis_index("tensor")
        self.ring = self.dp // 2
        self.turn = self.dp % 2
        self.row = self.tensor // 2
        self.core = self.tensor % 2
        self.order = [1, outer - 1] + list(range(2, outer - 1))

    def far(self, step):
        return (lax.rem(self.ring + step, self.outer) * 2 + self.turn, self.tensor)

    def peer(self):
        return (self.ring * 2 + 1 - self.turn, self.tensor)

    def sibling(self):
        return (self.dp, self.row * 2 + 1 - self.core)

    def across(self):
        return (self.dp, (1 - self.row) * 2 + self.core)

    def block_at(self, place):
        turn, step = place // self.outer, place % self.outer
        return lax.rem(self.ring + self.outer - step, self.outer) * 2 + lax.rem(self.turn + turn, 2)

    def corner(self):
        return (self.dp, (1 - self.row) * 2 + 1 - self.core)

    def greet_all(self):
        barrier = pltpu.get_barrier_semaphore()
        partners = [(self.block_at(place), self.tensor) for place in range(1, 2 * self.outer)]
        partners += [self.sibling(), self.across(), self.corner()]
        for partner in partners:
            pl.semaphore_signal(barrier, inc=1, device_id=partner, device_id_type=MESH)
        pl.semaphore_wait(barrier, len(partners))


def remote(src, dst, send, recv, device):
    return pltpu.make_async_remote_copy(
        src_ref=src, dst_ref=dst, send_sem=send, recv_sem=recv, device_id=device, device_id_type=MESH
    )


def tile(index, rows):
    return pl.ds(pl.multiple_of(index * rows, rows), rows)


def norm_rows(values, gain, epsilon):
    center = values - jnp.mean(values, axis=-1, keepdims=True)
    spread = jnp.mean(center * center, axis=-1, keepdims=True)
    return center * lax.rsqrt(spread + epsilon) * gain


def silu(v):
    return v * (1.0 / (1.0 + jnp.exp(-v)))


N_ITEMS = 9
GAINS, QUERY, KEY, VALUE, GATE, OUT, HIDDEN, UP, DOWN = range(N_ITEMS)
STEP = 256
PART = 128


def forward_kernel(outer, heads, dims, *refs):
    length, model, block = dims
    quarter = length // 4
    tokens, cotangent, gains, cosine, sine, decays = refs[:6]
    items = (gains,) + refs[6:14]
    fulls = refs[14:23]
    (mixer_out, query_out, key_out, value_out, retained_out, gate_out, mixed_out, residual_out,
     feed_out, hidden_out, up_out, activity_out) = refs[23:35]
    (slot_a, slot_b, slot_o, wide, mixer, rq, rk, values, kept, gate_in, mixed, residual, csend, crecv, ysend,
     yrecv, cos_v, sin_v, keyd, gain_v, gain_m, gain_f, gain_g,
     loc, zs, zr, xs, xr, ts, tr, ls, os_) = refs[35:]
    wires = Wires(outer)
    rows = length // STEP
    units = slot_a.shape[1]

    def piece(item, place):
        if item in (OUT, DOWN):
            return fulls[item].at[:, pl.ds(place * block, block)]
        height = items[item].shape[0]
        return fulls[item].at[pl.ds(place * height, height)]

    last = outer - 1
    up = wires.ring < last
    down = wires.ring > 0

    def along(item, source, place, step):
        device = (jnp.clip(wires.ring + step, 0, last) * 2 + wires.turn, wires.tensor)
        return remote(source, piece(item, place), zs.at[item, place], zr.at[item, place], device)

    def climb(item, source, base):
        @pl.when(up)
        def _():
            along(item, source, base + 1, 1).start()

        @pl.when(down)
        def _():
            along(item, source, base + last, -1).start()

    def beside(item, step):
        src = items[item] if step == 0 else piece(item, step)
        return remote(src, piece(item, outer + step), xs.at[item, step], xr.at[item, step], wires.peer())

    def own(item):
        return pltpu.make_async_copy(items[item], piece(item, 0), loc.at[item])

    def issue(item, cross=True):
        climb(item, items[item], 0)
        if cross:
            beside(item, 0).start()

    def hops(item, base, cross, which=None):
        for hop in which or range(1, outer):
            @pl.when(hop <= wires.ring)
            def _():
                along(item, piece(item, base + hop), base + hop, 1).wait_recv()
                if hop < last:
                    @pl.when(up)
                    def _():
                        along(item, piece(item, base + hop), base + hop + 1, 1).start()
                if cross:
                    beside(item, hop).start()

            @pl.when(hop <= last - wires.ring)
            def _():
                place = outer - hop
                along(item, piece(item, base + place), base + place, 1).wait_recv()
                if hop < last:
                    @pl.when(down)
                    def _():
                        along(item, piece(item, base + place), base + place - 1, -1).start()
                if cross:
                    beside(item, place).start()

    def pass_on(item):
        hops(item, 0, item != DOWN)

    def climb_sent(item, base):
        @pl.when(up)
        def _():
            along(item, piece(item, base), base + 1, 1).wait_send()

        @pl.when(down)
        def _():
            along(item, piece(item, base), base + last, -1).wait_send()

        for hop in range(1, last):
            @pl.when((hop <= wires.ring) & up)
            def _():
                along(item, piece(item, base + hop), base + hop + 1, 1).wait_send()

            @pl.when((hop <= last - wires.ring) & down)
            def _():
                along(item, piece(item, base + outer - hop), base + outer - hop - 1, -1).wait_send()

    def arrived(item):
        if item != UP:
            own(item).wait()
        for step in range(outer if item != DOWN else 1):
            beside(item, step).wait_recv()

    def load(src, dst, index):
        copy = pltpu.make_async_copy(src, dst, ls.at[index])
        copy.start()
        return copy

    stores = []

    def store(src, dst):
        copy = pltpu.make_async_copy(src, dst, os_.at[len(stores)])
        copy.start()
        stores.append(copy)
        return copy

    def gain_copy(place):
        turn, step = place // outer, place % outer
        there = piece(GAINS, turn * outer + (outer - step) % outer)
        device = (wires.block_at(place), wires.tensor)
        return remote(gains, there, zs.at[GAINS, place], zr.at[GAINS, turn * outer + (outer - step) % outer], device)

    wires.greet_all()
    for place in range(1, 2 * outer):
        gain_copy(place).start()
    for item in range(N_ITEMS):
        own(item).start()
    issue(QUERY)
    issue(KEY)
    issue(VALUE)
    beside(DOWN, 0).start()

    def own_blocks(source, target):
        copies = []
        for place in range(2 * outer):
            at = pl.multiple_of(wires.block_at(place) * block, block)
            copies.append(load(source.at[:, pl.ds(at, block)], target.at[:, pl.ds(place * block, block)], place))
        return copies

    first = 2 * outer
    loads = own_blocks(tokens, wide)
    loads.append(load(cosine, cos_v, first))
    loads.append(load(sine, sin_v, first + 1))
    loads.append(load(decays.at[wires.tensor], keyd, first + 2))
    own(GAINS).wait()
    for place in range(1, 2 * outer):
        gain_copy(place).wait_recv()
    for copy in loads:
        copy.wait()
    copy = load(fulls[GAINS], gain_v, 0)
    copy.wait()
    group = jnp.zeros((1, heads * DV), F32)
    for place in range(2 * outer):
        line = gain_v[place * 16 : place * 16 + 1, :].astype(F32)
        gain_m[:, place * block : (place + 1) * block] = line[:, :block]
        gain_f[:, place * block : (place + 1) * block] = line[:, block : 2 * block]
        group = group + line[:, 2 * block :]
    gain_g[...] = group

    @pl.loop(0, length // 128)
    def _(r):
        at = tile(r, 128)
        mixer[at, :] = norm_rows(wide[at, :].astype(F32), gain_m[...], norm_epsilon).astype(BF16)

    mine = tile(wires.tensor, quarter)
    residual[...] = wide[mine, :].astype(F32)
    mixer_store = store(mixer, mixer_out)
    pass_on(QUERY)
    pass_on(KEY)
    issue(GATE)
    pass_on(VALUE)
    issue(OUT)
    hops(GATE, 0, True, (1,))
    arrived(QUERY)
    arrived(KEY)
    narrow = heads * DK
    copy = load(fulls[QUERY], slot_a.at[:, pl.ds(0, narrow)], 0)
    other = load(fulls[KEY], slot_a.at[:, pl.ds(narrow, narrow)], 1)
    copy.wait()
    other.wait()

    @pl.loop(0, rows)
    def _(r):
        at = tile(r, STEP)
        both = jnp.dot(mixer[at, :], slot_a[...], preferred_element_type=F32)
        c, s = cos_v[at, :], sin_v[at, :]
        half = DK // 2
        for target, base in ((rq, 0), (rk, narrow)):
            for h in range(heads):
                lo = base + h * DK
                a, b = both[:, lo : lo + half], both[:, lo + half : lo + DK]
                target[at, h * DK : h * DK + half] = (a * c - b * s).astype(BF16)
                target[at, h * DK + half : (h + 1) * DK] = (a * s + b * c).astype(BF16)

    store(rq, query_out)
    store(rk, key_out)
    hops(GATE, 0, True, (2, 3))
    issue(HIDDEN)
    hops(OUT, 0, True, (1,))
    arrived(VALUE)
    load(fulls[VALUE], slot_b, 0).wait()

    @pl.loop(0, rows)
    def _(r):
        at = tile(r, STEP)
        values[at, :] = jnp.dot(mixer[at, :], slot_b[...], preferred_element_type=F32).astype(BF16)

    store(values, value_out)
    for h in range(heads):
        for r in range(rows):
            at = slice(r * STEP, (r + 1) * STEP)
            upto = (r + 1) * STEP
            q = rq[at, h * DK : (h + 1) * DK]
            k = rk[:upto, h * DK : (h + 1) * DK]
            raw = lax.dot_general(q, k, (((1,), (1,)), ((), ())), preferred_element_type=F32)
            fade = keyd[heads + h : heads + h + 1, at].reshape(STEP, 1) * keyd[h : h + 1, :upto]
            place = lax.broadcasted_iota(jnp.int32, (STEP, upto), 0) + r * STEP
            under = place >= lax.broadcasted_iota(jnp.int32, (STEP, upto), 1)
            scores = raw * jnp.where(under, fade, 0.0)
            total = jnp.sum(scores, axis=-1, keepdims=True)
            share = (scores * lax.rsqrt(total * total + 1.0)).astype(BF16)
            kept[at, h * DV : (h + 1) * DV] = jnp.dot(
                share, values[:upto, h * DV : (h + 1) * DV], preferred_element_type=F32
            )
    kept_store = store(kept, retained_out)
    hops(OUT, 0, True, (2, 3))
    issue(UP)
    hops(HIDDEN, 0, True, (1,))
    arrived(GATE)
    load(fulls[GATE], slot_a, 0).wait()

    @pl.loop(0, rows)
    def _(r):
        at = tile(r, STEP)
        gate = jnp.dot(mixer[at, :], slot_a[...], preferred_element_type=F32)
        gate_in[at, :] = gate
        for h in range(heads):
            cols = slice(h * DV, (h + 1) * DV)
            normed = norm_rows(kept[at, cols], gain_g[:, cols], group_epsilon)
            mixed[at, cols] = (silu(gate[:, cols]) * normed).astype(BF16)

    mixer_store.wait()
    cot_loads = own_blocks(cotangent, mixer)
    gate_store = store(gate_in, gate_out)
    mixed_store = store(mixed, mixed_out)
    hops(HIDDEN, 0, True, (2, 3))
    hops(UP, 0, True, (1,))
    issue(DOWN, False)
    arrived(DOWN)
    climb(DOWN, piece(DOWN, outer), outer)
    arrived(OUT)
    load(fulls[OUT], slot_o, first).wait()

    def branch_rows(index):
        return jnp.dot(mixed[tile(index, quarter), :], slot_o[...], preferred_element_type=F32)

    def to_sibling(s):
        return remote(csend.at[s], crecv.at[s], ts.at[s], tr.at[s], wires.sibling())

    cross = remote(ysend, yrecv, ts.at[2], tr.at[2], wires.across())
    for s in (1, 0):
        owner = lax.rem(wires.row + s, 2) * 2 + 1 - wires.core
        csend[s] = branch_rows(owner).astype(BF16)
        to_sibling(s).start()
    part = branch_rows((1 - wires.row) * 2 + wires.core)
    to_sibling(1).wait_recv()
    ysend[...] = (part + crecv[1].astype(F32)).astype(BF16)
    cross.start()
    residual[...] += branch_rows(wires.tensor)
    to_sibling(0).wait_recv()
    residual[...] += crecv[0].astype(F32)
    hops(UP, 0, True, (2, 3))
    hops(DOWN, 0, False, (1,))
    cross.wait_recv()
    residual[...] += yrecv[...].astype(F32)
    store(residual, residual_out)
    feed_mine = wide.at[mine]

    @pl.loop(0, quarter // 128)
    def _(r):
        at = tile(r, 128)
        ysend_rows = norm_rows(residual[at, :], gain_f[...], norm_epsilon).astype(BF16)
        feed_mine[at, :] = ysend_rows

    feed_cross = remote(feed_mine, feed_mine, ts.at[3], tr.at[3], wires.across())
    feed_near = remote(feed_mine, feed_mine, ts.at[4], tr.at[4], wires.sibling())
    theirs = wide.at[tile((1 - wires.row) * 2 + wires.core, quarter)]
    feed_far = remote(theirs, theirs, ts.at[5], tr.at[5], wires.sibling())
    feed_cross.start()
    feed_near.start()
    hops(DOWN, 0, False, (2, 3))
    hops(DOWN, outer, False, (1,))
    feed_cross.wait_recv()
    feed_far.start()
    near_cols, far_cols = pl.ds(0, model // 2), pl.ds(model // 2, model // 2)
    down_load = load(fulls[DOWN].at[:, near_cols], slot_o.at[:, near_cols], first + 1)
    own(UP).wait()
    up_load = load(fulls[UP].at[near_cols], slot_a.at[near_cols], first + 2)
    for copy in cot_loads:
        copy.wait()
    down_load.wait()
    gate_store.wait()

    def grads_half(at, cols):
        return lax.dot_general(
            mixer[at, cols], slot_o[:, cols], (((1,), (1,)), ((), ())), preferred_element_type=F32
        )

    @pl.loop(0, rows)
    def _(r):
        at = tile(r, STEP)
        gate_in[at, :] = grads_half(at, near_cols)

    hops(DOWN, outer, False, (2,))
    arrived(HIDDEN)
    load(fulls[HIDDEN], slot_b, first).wait()
    feed_near.wait_recv()
    feed_far.wait_recv()
    store(wide, feed_out)
    kept_store.wait()

    @pl.loop(0, rows)
    def _(r):
        at = tile(r, STEP)
        kept[at, :] = jnp.dot(wide[at, :], slot_b[...], preferred_element_type=F32)

    hops(DOWN, outer, False, (3,))
    load(fulls[DOWN].at[:, far_cols], slot_o.at[:, far_cols], first + 1).wait()

    @pl.loop(0, rows)
    def _(r):
        at = tile(r, STEP)
        gate_in[at, :] += grads_half(at, far_cols)

    arrived(UP)
    load(fulls[UP].at[far_cols], slot_a.at[far_cols], first).wait()
    up_load.wait()
    mixed_store.wait()

    for part in range(2):
        @pl.loop(part * (length // PART // 2), (part + 1) * (length // PART // 2))
        def _(r):
            at = tile(r, PART)
            u = jnp.dot(wide[at, :], slot_a[...], preferred_element_type=F32)
            h, grads = kept[at, :], gate_in[at, :]
            t = jnp.tanh(SQRT_2_PI * (h + CUBIC * h * h * h))
            gelu = 0.5 * h * (1.0 + t)
            slope = 0.5 * (1.0 + t) + 0.5 * h * (1.0 - t * t) * (SQRT_2_PI * (1.0 + 3.0 * CUBIC * h * h))
            mixed[at, :] = (gelu * u).astype(BF16)
            slot_b[at, :] = (grads * u * slope).astype(BF16)
            slot_o[at, pl.ds(0, units)] = (grads * gelu).astype(BF16)

        done = pl.ds(part * (length // 2), length // 2)
        store(mixed.at[done], activity_out.at[done])
        store(slot_b.at[done], hidden_out.at[done])
        store(slot_o.at[done, pl.ds(0, units)], up_out.at[done])

    for copy in stores:
        if not any(copy is done for done in (kept_store, gate_store, mixer_store, mixed_store)):
            copy.wait()
    for s in range(2):
        to_sibling(s).wait_send()
    for copy in (cross, feed_cross, feed_near, feed_far):
        copy.wait_send()
    for place in range(1, 2 * outer):
        gain_copy(place).wait_send()
    for item in range(1, N_ITEMS):
        climb_sent(item, 0)
        for step in range(outer if item != DOWN else 1):
            beside(item, step).wait_send()
    climb_sent(DOWN, outer)


def position_tables(length, teams, heads):
    half = DK // 2
    speeds = 10000.0 ** (-np.arange(half, dtype=np.float32) / np.float32(half))
    angles = np.arange(length, dtype=np.float32)[:, None] * speeds.astype(np.float32)[None, :]
    pair = [np.cos(angles), np.sin(angles)]
    turns = [t.reshape(length // PART, PART, half).swapaxes(0, 1).reshape(PART, -1) for t in pair]
    rates = np.log1p(-np.exp2(-5.0 - np.arange(teams * heads, dtype=np.float64)))[:, None]
    places = np.arange(length, dtype=np.float64)[None, :]
    sums = np.expm1(rates * (places + 1)) / np.expm1(rates)
    row_decay = np.exp(rates * (places - length // 2)) / np.sqrt(sums) * DK**-0.5
    key_decay = np.exp(rates * (length // 2 - places))
    fades = np.zeros((teams, 8, length))
    fades[:, :heads] = key_decay.reshape(teams, heads, length)
    fades[:, heads : 2 * heads] = row_decay.reshape(teams, heads, length)
    return [jnp.asarray(np.asarray(t, np.float32)) for t in (*pair, np.stack(turns), fades)]


def forward_fast(dp_size, tokens, cotangent, gains, tables, weights):
    outer = dp_size // 2
    length, model = tokens.shape
    block = model // dp_size
    heads = weights[0].shape[1] // DK
    units = weights[3].shape[1]
    wide = units
    shapes = [(gains.shape[0] * dp_size, gains.shape[1])]
    for place, weight in enumerate(weights):
        if place + 1 in (OUT, DOWN):
            shapes.append((weight.shape[0], model))
        else:
            shapes.append((model, weight.shape[1]))
    out_shape = [jax.ShapeDtypeStruct(s, BF16) for s in shapes]
    half = heads * DK
    for shape, kind in (
        ((length, model), BF16),
        ((length, half), BF16),
        ((length, half), BF16),
        ((length, wide), BF16),
        ((length, wide), F32),
        ((length, wide), F32),
        ((length, wide), BF16),
        ((length // 4, model), F32),
        ((length, model), BF16),
        ((length, units), BF16),
        ((length, units), BF16),
        ((length, units), BF16),
    ):
        out_shape.append(jax.ShapeDtypeStruct(shape, kind))
    quarter = length // 4
    dma = pltpu.SemaphoreType.DMA
    scratch = [
        pltpu.VMEM((model, wide), BF16),
        pltpu.VMEM((model, wide), BF16),
        pltpu.VMEM((wide, model), BF16),
        pltpu.VMEM((length, model), BF16),
        pltpu.VMEM((length, model), BF16),
        pltpu.VMEM((length, half), BF16),
        pltpu.VMEM((length, half), BF16),
        pltpu.VMEM((length, wide), BF16),
        pltpu.VMEM((length, wide), F32),
        pltpu.VMEM((length, wide), F32),
        pltpu.VMEM((length, wide), BF16),
        pltpu.VMEM((quarter, model), F32),
        pltpu.VMEM((2, quarter, model), BF16),
        pltpu.VMEM((2, quarter, model), BF16),
        pltpu.VMEM((quarter, model), BF16),
        pltpu.VMEM((quarter, model), BF16),
        pltpu.VMEM(tables[0].shape, F32),
        pltpu.VMEM(tables[1].shape, F32),
        pltpu.VMEM(tables[2].shape[1:], F32),
        pltpu.VMEM(shapes[0], BF16),
        pltpu.VMEM((1, model), F32),
        pltpu.VMEM((1, model), F32),
        pltpu.VMEM((1, heads * DV), F32),
        dma((N_ITEMS,)),
        dma((N_ITEMS, 2 * outer)),
        dma((N_ITEMS, 2 * outer)),
        dma((N_ITEMS, outer)),
        dma((N_ITEMS, outer)),
        dma((6,)),
        dma((6,)),
        dma((2 * outer + 4,)),
        dma((16,)),
    ]

    def kernel(*refs):
        forward_kernel(outer, heads, (length, model, block), *refs)

    results = pl.pallas_call(
        kernel,
        out_shape=out_shape,
        in_specs=[ANY] * (6 + len(weights)),
        out_specs=[ANY] * len(out_shape),
        scratch_shapes=scratch,
        compiler_params=pltpu.CompilerParams(
            collective_id=0, has_side_effects=True, vmem_limit_bytes=58 * 1024 * 1024
        ),
    )(tokens, cotangent, gains, *tables, *weights)
    return results[: N_ITEMS], results[N_ITEMS:]


N_GRADS = 7
(G_DOWN, G_HIDDEN, G_UP, G_OUT, G_GATE, G_VALUE, G_BOTH) = range(N_GRADS)
FLOW = (2, 3, 1, 0)
SQRT_2_PI = 0.7978845608028654
CUBIC = 0.044715


def rows_dot(left, right):
    return lax.dot_general(left, right, (((0,), (0,)), ((), ())), preferred_element_type=F32)


def back_dot(left, right):
    return lax.dot_general(left, right, (((1,), (1,)), ((), ())), preferred_element_type=F32)


def norm_back(values, grads, gain, epsilon):
    center = values - jnp.mean(values, axis=-1, keepdims=True)
    inverse = lax.rsqrt(jnp.mean(center * center, axis=-1, keepdims=True) + epsilon)
    unit = center * inverse
    u = grads * gain
    mean = jnp.mean(u, axis=-1, keepdims=True)
    slope = jnp.mean(u * unit, axis=-1, keepdims=True)
    return (u - mean - unit * slope) * inverse, grads * unit


def backward_kernel(outer, heads, dims, *refs):
    length, model, block, units = dims
    quarter = length // 4
    half = model // 2
    (tokens, cotangent, gains, query_full, key_full, value_full, gate_full, out_full, hidden_full, up_full,
     down_full, mixer_in, query_in, key_in, value_in, retained_in, gate_in, mixed_in, residual_in, feed_in,
     hidden_in, up_in, activity_in, turns, key_decay) = refs[:25]
    (output, tokens_out, near_out, z_land, vector_out, x_land, branch_land) = refs[25:32]
    (u0, u1, u2, u3, u4, act, hid, upg, both, fa, fb, x_ring, x_extra, z_ring, x_stage, acc, csend, crecv, ysend, yrecv,
     stage, grad_q, value_q, keyd, gain_v, gain_m, gain_f, gain_g,
     vec_t, vec_tr, vec_d, vec_dr, vec_g,
     xs, xr, zs, zr, ts, tr, gs, gr, vs, vr, ls, fs, st, ac) = refs[32:]
    wires = Wires(outer)
    rows = length // STEP
    mine = tile(wires.tensor, quarter)
    near_rows = tile(wires.row * 2 + 1 - wires.core, quarter)
    across_index = (1 - wires.row) * 2 + wires.core
    across_rows = tile(across_index, quarter)
    corner_rows = tile((1 - wires.row) * 2 + 1 - wires.core, quarter)

    def load(src, dst, index):
        copy = pltpu.make_async_copy(src, dst, ls.at[index])
        copy.start()
        return copy

    def load_tall(src, dst, index):
        return [load(src.at[pl.ds(h * half, half)], dst.at[:, pl.ds(h * half, half)], index + h) for h in range(2)]

    def wait_all(copies):
        for copy in copies:
            copy.wait()

    def own_blocks(src, dst, index):
        copies = []
        for place in range(2 * outer):
            at = pl.multiple_of(wires.block_at(place) * block, block)
            copies.append(load(src.at[:, pl.ds(at, block)], dst.at[:, pl.ds(place * block, block)], index + place))
        return copies

    def true_blocks(src, dst, index):
        copies = []
        for place in range(2 * outer):
            at = pl.multiple_of(wires.block_at(place) * block, block)
            copies.append(load(src.at[:, pl.ds(place * block, block)], dst.at[:, pl.ds(at, block)], index + place))
        return copies

    def x_copy(item, s):
        source = x_extra if item == G_DOWN else x_ring.at[(item % 2) * outer + s]
        return remote(source, x_land.at[item, s], xs.at[item, s], xr.at[item, s], wires.peer())

    def z_copy(item, s):
        step = outer - 1 if s != outer - 1 else 1
        device = (lax.rem(wires.ring + step, outer) * 2 + wires.turn, wires.tensor)
        slot = (item % 2) * (outer - 1) + s - 1
        return remote(z_ring.at[slot], z_land.at[item, s - 1], zs.at[item, s], zr.at[item, s], device)

    def columns(place):
        return pl.ds(pl.multiple_of(place * block, block), block)

    def far(item, left, right, flow=FLOW, behind=None):
        for s in flow:
            if item >= 3:
                x_copy(item - 2, s).wait_send()
            product = rows_dot(left[:, columns(outer + s)], right[...])
            x_ring[(item % 2) * outer + s] = product.astype(BF16)
            if behind is None:
                x_copy(item, s).start()
        if behind is not None:
            behind.wait_send()
            for s in flow:
                x_copy(item, s).start()

    def acc_copy(item):
        return pltpu.make_async_copy(acc, near_out.at[item], ac.at[item])

    def staged(item, place, source):
        copy = pltpu.make_async_copy(source, x_stage.at[place], st.at[item, place])
        copy.start()
        return copy

    sides = ((0, G_DOWN), (1, N_GRADS))

    def down_product(turn, s):
        return rows_dot(u0[:, columns(turn * outer + s)], act[...])

    def down_give(s):
        for turn, item in sides:
            z_ring[(item % 2) * (outer - 1) + s - 1] = down_product(turn, s).astype(BF16)
            z_copy(item, s).start()

    def down_first():
        down_give(2)
        for turn, item in sides:
            z_ring[(item % 2) * (outer - 1)] = down_product(turn, 1).astype(BF16)
        x_extra[...] = down_product(1, 0).astype(BF16)
        acc[...] = down_product(0, 0)
        acc_copy(G_DOWN).start()

    def relay(item):
        z_copy(item, 2).wait_recv()
        staged(item, 2, z_land.at[item, 1]).wait()
        slot = (item % 2) * (outer - 1)
        z_ring[slot] = (z_ring[slot].astype(F32) + x_stage[2].astype(F32)).astype(BF16)
        z_copy(item, 1).start()

    def down_sum():
        z_copy(N_GRADS, 3).wait_recv()
        copy = staged(N_GRADS, 2, z_land.at[N_GRADS, 2])
        z_copy(N_GRADS, 1).wait_recv()
        other = staged(N_GRADS, 3, z_land.at[N_GRADS, 0])
        copy.wait()
        other.wait()
        total = x_extra[...].astype(F32) + x_stage[2].astype(F32) + x_stage[3].astype(F32)
        x_extra[...] = total.astype(BF16)

    def near(item, left, right, flow=FLOW):
        before = N_GRADS if item == 1 else item - 2
        for s in flow:
            x_copy(item, s).wait_recv()
            copy = staged(item, s % 2, x_land.at[item, s])
            if s:
                z_copy(before, s).wait_send()
            if s == 0:
                acc_copy(item - 1).wait()
            product = rows_dot(left[:, columns(s)], right[...])
            copy.wait()
            product = product + x_stage[s % 2].astype(F32)
            if s == 0:
                acc[...] = product
                acc_copy(item).start()
                continue
            z_ring[(item % 2) * (outer - 1) + s - 1] = product.astype(BF16)
            if s > 1:
                z_copy(item, s).start()

    class Round:
        def __init__(self, index):
            self.index = index
            self.cross = remote(ysend, yrecv, ts.at[index, 2], tr.at[index, 2], wires.across())

        def to_sibling(self, s):
            return remote(csend.at[s], crecv.at[s], ts.at[self.index, s], tr.at[self.index, s], wires.sibling())

        def give(self, terms):
            for s in (1, 0):
                owner = lax.rem(wires.row + s, 2) * 2 + 1 - wires.core
                for h in range(2):
                    cols = slice(h * half, (h + 1) * half)
                    csend[s, :, cols] = terms(tile(owner, quarter), h).astype(BF16)
                self.to_sibling(s).start()

        def hand_over(self, terms):
            self.to_sibling(1).wait_recv()
            for h in range(2):
                cols = slice(h * half, (h + 1) * half)
                ysend[:, cols] = (terms(across_rows, h) + crecv[1, :, cols].astype(F32)).astype(BF16)
            self.cross.start()

        def keep(self, terms, totals, add):
            for h in range(2):
                part = terms(mine, h)
                totals[h][...] = totals[h][...] + part if add else part
            self.to_sibling(0).wait_recv()
            for h in range(2):
                totals[h][...] += crecv[0, :, h * half : (h + 1) * half].astype(F32)

        def finish(self, totals):
            self.cross.wait_recv()
            for h in range(2):
                totals[h][...] += yrecv[:, h * half : (h + 1) * half].astype(F32)
            for s in range(2):
                self.to_sibling(s).wait_send()
            self.cross.wait_send()

    class Spread:
        def __init__(self, index, source, land):
            self.cross = remote(source, land.at[mine], gs.at[index, 0], gr.at[index, 0], wires.across())
            self.near = remote(source, land.at[mine], gs.at[index, 1], gr.at[index, 1], wires.sibling())
            there = land.at[across_rows]
            self.far = remote(there, there, gs.at[index, 2], gr.at[index, 2], wires.sibling())
            self.own = pltpu.make_async_copy(source, land.at[mine], gs.at[index, 3])

        def start(self):
            self.cross.start()
            self.near.start()
            self.own.start()

        def pass_on(self):
            self.cross.wait_recv()
            self.far.start()

        def sent(self):
            self.cross.wait_send()
            self.near.wait_send()
            self.own.wait()

        def end(self):
            self.far.wait_recv()
            self.far.wait_send()

    def stream(src_a, src_b, body):
        def copies(r, slot):
            at = tile(r, PART)
            return (
                pltpu.make_async_copy(src_a.at[at], fa.at[slot, pl.ds(0, PART)], fs.at[0, slot]),
                pltpu.make_async_copy(src_b.at[at], fb.at[slot], fs.at[1, slot]),
            )

        for copy in copies(0, 0):
            copy.start()

        @pl.loop(0, length // PART)
        def _(r):
            slot = lax.rem(r, 2)

            @pl.when(r + 1 < length // PART)
            def _():
                for copy in copies(r + 1, 1 - slot):
                    copy.start()

            for copy in copies(r, slot):
                copy.wait()
            body(tile(r, PART), fa.at[slot, pl.ds(0, PART)], fb.at[slot])

    wires.greet_all()
    n = 2 * outer
    hid_load = load(hidden_in, hid, n + 10)
    far_half, near_half = pl.ds(half, half), pl.ds(0, half)
    feed_load = load(feed_in.at[:, far_half], u2.at[:, far_half], n + 2)
    act_load = load(activity_in, act, n + 9)
    cot_loads = own_blocks(cotangent, u0, 0)
    upg_load = load(up_in, upg, n + 11)
    hidden_loads = load_tall(hidden_full, u3, n + 3)
    up_loads = load_tall(up_full, u4, n + 5)
    down_load = load(down_full, u1, n)
    gain_load = load(gains, gain_v, n + 1)
    residual_load = load(residual_in, value_q, n + 7)
    table_load = load(key_decay.at[wires.tensor], keyd, n + 8)
    near_load = load(feed_in.at[:, near_half], u2.at[:, near_half], n + 12)
    hid_load.wait()
    feed_load.wait()
    far(G_HIDDEN, u2, hid)
    act_load.wait()
    wait_all(cot_loads)
    down_first()
    upg_load.wait()
    wait_all(hidden_loads)
    wait_all(up_loads)
    near_load.wait()

    def tall_terms(pairs):
        def terms(at, h):
            cols = slice(h * half, (h + 1) * half)
            total = None
            for left, right in pairs:
                part = back_dot(left[at, :], right[:, cols])
                total = part if total is None else total + part
            return total

        return terms

    feed_terms = tall_terms(((hid, u3), (upg, u4)))
    feed_round, output_round, mixer_round = Round(0), Round(1), Round(2)
    feed_round.give(feed_terms)
    far(G_UP, u2, upg)
    feed_round.hand_over(feed_terms)
    grad_halves = [grad_q.at[:, pl.ds(h * half, half)] for h in range(2)]
    value_halves = [value_q.at[:, pl.ds(h * half, half)] for h in range(2)]
    mixer_halves = [fa.at[h] for h in range(2)]
    feed_round.keep(feed_terms, grad_halves, False)
    table_load.wait()
    gain_load.wait()
    group = jnp.zeros((1, heads * DV), F32)
    for place in range(2 * outer):
        line = gain_v[place * 16 : place * 16 + 1, :].astype(F32)
        gain_m[:, place * block : (place + 1) * block] = line[:, :block]
        gain_f[:, place * block : (place + 1) * block] = line[:, block : 2 * block]
        group = group + line[:, 2 * block :]
    gain_g[...] = group
    vec_t[...] = jnp.zeros_like(vec_t)
    vec_d[...] = jnp.zeros_like(vec_d)
    vec_g[...] = jnp.zeros_like(vec_g)
    mixer_load = load(mixer_in, u3, n + 3)
    narrow = heads * DK
    core_loads = [load(value_in, u4.at[:, pl.ds(0, half)], n + 4),
                  load(query_in, u4.at[:, pl.ds(half, narrow)], n + 5),
                  load(key_in, u4.at[:, pl.ds(half + narrow, narrow)], n + 6)]
    down_give(3)
    residual_load.wait()
    feed_round.finish(grad_halves)

    @pl.loop(0, quarter // 128)
    def _(r):
        at = tile(r, 128)
        part, gain_part = norm_back(value_q[at, :], grad_q[at, :], gain_f[...], norm_epsilon)
        cot_at = pl.ds(pl.multiple_of(wires.tensor * quarter + r * 128, 128), 128)
        total = u0[cot_at, :].astype(F32) + part
        grad_q[at, :] = total
        stage[at, :] = total.astype(BF16)
        vec_t[1:2, :] += jnp.sum(gain_part, axis=0, keepdims=True)

    branch_spread = Spread(0, stage, branch_land)
    branch_spread.start()
    relay(G_DOWN)
    relay(N_GRADS)
    near(G_HIDDEN, u2, hid, (2, 3, 0))

    down_load.wait()

    def output_terms(at, h):
        return jnp.dot(act[at, :], u1[:, h * half : (h + 1) * half], preferred_element_type=F32)

    branch_spread.near.wait_recv()
    output_round.give(output_terms)
    output_round.keep(output_terms, value_halves, True)
    branch_spread.pass_on()
    output_round.hand_over(output_terms)
    branch_spread.sent()
    out_load = load(out_full, u1, n)
    branch_loads = [load(branch_land.at[at], u0.at[at], n + 7 + i) for i, at in
                    enumerate((mine, near_rows, across_rows))]
    mixed_load = load(mixed_in, act, n + 1)
    branch_spread.far.wait_recv()
    branch_loads.append(load(branch_land.at[corner_rows], u0.at[corner_rows], n + 2))
    wait_all(branch_loads)
    out_load.wait()

    hold = both

    def gate_tile(at, r_ref, g_ref):
        grads = back_dot(u0[at, :], u1[...])
        for h in range(heads):
            cols = slice(h * DV, (h + 1) * DV)
            x, g, m = r_ref[:, cols], g_ref[:, cols], grads[:, cols]
            scale = gain_g[:, cols]
            sig = 1.0 / (1.0 + jnp.exp(-g))
            swish = g * sig
            center = x - jnp.mean(x, axis=-1, keepdims=True)
            inverse = lax.rsqrt(jnp.mean(center * center, axis=-1, keepdims=True) + group_epsilon)
            unit = center * inverse
            passed = m * swish
            hid[at, cols] = (m * unit * scale * (sig * (1.0 + g * (1.0 - sig)))).astype(BF16)
            vec_g[:, cols] += jnp.sum(passed * unit, axis=0, keepdims=True)
            u = passed * scale
            mean = jnp.mean(u, axis=-1, keepdims=True)
            slope = jnp.mean(u * unit, axis=-1, keepdims=True)
            hold[at, cols] = ((u - mean - unit * slope) * inverse).astype(BF16)

    mixed_load.wait()
    far(G_OUT, u0, act)
    near(G_HIDDEN, u2, hid, (1,))
    stream(retained_in, gate_in, gate_tile)
    relay(G_HIDDEN)
    mixer_load.wait()
    near(G_UP, u2, upg)
    value_loads = load_tall(value_full, u2, n + 1)
    far(G_GATE, u3, hid)
    wait_all(core_loads)

    side = DK // 2
    turn_load = load(turns, fb, n + 8)
    turn_load.wait()

    def turned_back(grads, r, count):
        a, b = grads[:, :side], grads[:, side:]
        c = jnp.concatenate([fb[0, :, (r + i) * side : (r + i + 1) * side] for i in range(count)], axis=0)
        s = jnp.concatenate([fb[1, :, (r + i) * side : (r + i + 1) * side] for i in range(count)], axis=0)
        return (a * c + b * s).astype(BF16), (b * c - a * s).astype(BF16)

    for h in range(heads):
        vcols = slice(h * DV, (h + 1) * DV)
        qcols = slice(half + h * DK, half + (h + 1) * DK)
        kcols = slice(half + narrow + h * DK, half + narrow + (h + 1) * DK)
        for r in range(length // PART):
            at = slice(r * PART, (r + 1) * PART)
            upto = (r + 1) * PART
            raw = back_dot(u4[at, qcols], u4[:upto, kcols])
            place = lax.broadcasted_iota(jnp.int32, (PART, upto), 0) + r * PART
            under = place >= lax.broadcasted_iota(jnp.int32, (PART, upto), 1)
            fade = keyd[heads + h : heads + h + 1, at].reshape(PART, 1) * keyd[h : h + 1, :upto]
            fade = jnp.where(under, fade, 0.0)
            scores = raw * fade
            total = jnp.sum(scores, axis=-1, keepdims=True)
            inverse = lax.rsqrt(total * total + 1.0)
            u1[at, :upto] = (scores * inverse).astype(BF16)
            grads = back_dot(hold[at, vcols], u4[:upto, vcols])
            inner = jnp.sum(grads * scores, axis=-1, keepdims=True)
            drop = inner * total * inverse * inverse * inverse
            raw_grad = ((grads * inverse - drop) * fade).astype(BF16)
            u1[at, half : half + upto] = raw_grad
            query_grad = jnp.dot(raw_grad, u4[:upto, kcols], preferred_element_type=F32)
            lo, hi = turned_back(query_grad, r, 1)
            upg[at, h * DK : h * DK + side] = lo
            upg[at, h * DK + side : (h + 1) * DK] = hi
        for c in range(rows):
            at = slice(c * STEP, (c + 1) * STEP)
            after = slice(c * STEP, length)
            for i in range(1, STEP // PART):
                spare = slice(c * STEP, c * STEP + i * PART)
                late = slice(c * STEP + i * PART, c * STEP + (i + 1) * PART)
                u1[spare, late] = jnp.zeros((i * PART, PART), BF16)
                u1[spare, half + c * STEP + i * PART : half + c * STEP + (i + 1) * PART] = jnp.zeros(
                    (i * PART, PART), BF16
                )
            hold_grad = rows_dot(u1[after, c * STEP : (c + 1) * STEP], hold[after, vcols])
            key_grad = rows_dot(u1[after, half + c * STEP : half + (c + 1) * STEP], u4[after, qcols])
            hold[at, vcols] = hold_grad.astype(BF16)
            lo, hi = turned_back(key_grad, c * (STEP // PART), STEP // PART)
            upg[at, narrow + h * DK : narrow + h * DK + side] = lo
            upg[at, narrow + h * DK + side : narrow + (h + 1) * DK] = hi

    gate_loads = load_tall(gate_full, u1, n + 3)
    both_loads = []
    for h in range(2):
        source = pl.ds(h * half, half)
        both_loads.append(load(query_full.at[source], u4.at[:, pl.ds(h * half, narrow)], n + 5 + 2 * h))
        both_loads.append(load(key_full.at[source], u4.at[:, pl.ds(h * half + narrow, narrow)], n + 6 + 2 * h))

    down_sum()
    relay(G_UP)

    output_round.finish(value_halves)
    ysend[...] = value_q[...].astype(BF16)
    wait_all(true_blocks(ysend, stage, 0))
    output_spread = Spread(1, stage, output)
    output_spread.start()
    token_loads = []
    for place in range(2 * outer):
        at = pl.multiple_of(wires.block_at(place) * block, block)
        token_loads.append(load(tokens.at[mine, pl.ds(at, block)], ysend.at[:, pl.ds(place * block, block)], place))
    wait_all(token_loads)
    for r in range(2):
        at = slice(r * (quarter // 2), (r + 1) * (quarter // 2))
        value_q[at, :] = ysend[at, :].astype(F32)
    near(G_OUT, u0, act)
    far(G_VALUE, u3, hold)
    wait_all(gate_loads)
    wait_all(both_loads)
    wait_all(value_loads)
    mixer_terms = tall_terms(((upg, u4), (hold, u2), (hid, u1)))
    output_spread.near.wait_recv()
    mixer_round.give(mixer_terms)
    output_spread.pass_on()
    mixer_round.hand_over(mixer_terms)
    mixer_round.keep(mixer_terms, mixer_halves, False)
    relay(G_OUT)
    mixer_round.finish(mixer_halves)
    output_spread.sent()

    @pl.loop(0, quarter // 128)
    def _(r):
        at = tile(r, 128)
        grads = jnp.concatenate([fa[0, at, :], fa[1, at, :]], axis=1)
        part, gain_part = norm_back(value_q[at, :], grads, gain_m[...], norm_epsilon)
        ysend[at, :] = (grad_q[at, :] + part).astype(BF16)
        vec_t[0:1, :] += jnp.sum(gain_part, axis=0, keepdims=True)

    def vector_team(i, device):
        return remote(vec_t, vec_tr.at[i], vs.at[i], vr.at[i], device)

    team = (wires.sibling(), wires.across(), wires.corner())
    for i, device in enumerate(team):
        vector_team(i, device).start()
    wait_all(true_blocks(ysend, stage, 0))
    tokens_spread = Spread(2, stage, tokens_out)
    tokens_spread.start()
    near(G_GATE, u3, hid)
    far(G_BOTH, u3, upg, (2, 3))
    for i, device in enumerate(team):
        vector_team(i, device).wait_recv()
    summed = vec_t[0:2, :]
    for i in range(3):
        summed = summed + vec_tr[i, 0:2, :]
    for place in range(2 * outer):
        vec_d[place, 0:2, :] = summed[:, place * block : (place + 1) * block]
        for i in range(heads * DV // block):
            vec_d[place, 2 + i : 3 + i, :] = vec_g[:, i * block : (i + 1) * block]

    def vector_data(place):
        device = (wires.block_at(place), wires.tensor)
        return remote(vec_d.at[place], vec_dr.at[place], vs.at[3 + place], vr.at[3 + place], device)

    for place in range(1, 2 * outer):
        vector_data(place).start()
    tokens_spread.pass_on()
    relay(G_GATE)
    near(G_VALUE, u3, hold)
    relay(G_VALUE)
    far(G_BOTH, u3, upg, (1, 0), x_copy(G_BOTH, 2))
    x_copy(G_DOWN, 0).start()
    near(G_BOTH, u3, upg, (2, 3))
    near(G_BOTH, u3, upg, (1,))
    relay(G_BOTH)
    near(G_BOTH, u3, upg, (0,))
    vectors = vec_d[0]
    for place in range(1, 2 * outer):
        vector_data(place).wait_recv()
        vectors = vectors + vec_dr[place]
    vec_d[0] = vectors
    vector_store = load(vec_d.at[0], vector_out, 0)

    vector_store.wait()
    branch_spread.far.wait_send()
    output_spread.end()
    tokens_spread.near.wait_recv()
    tokens_spread.end()
    tokens_spread.sent()
    for i, device in enumerate(team):
        vector_team(i, device).wait_send()
    for place in range(1, 2 * outer):
        vector_data(place).wait_send()
    acc_copy(N_GRADS - 1).wait()
    x_copy(G_DOWN, 0).wait()
    for item in (N_GRADS - 2, N_GRADS - 1):
        for s in range(outer):
            if (item, s) != (G_BOTH, 2):
                x_copy(item, s).wait_send()
        for s in range(1, outer):
            z_copy(item, s).wait_send()
    for item in range(N_GRADS):
        for s in (1, outer - 1):
            z_copy(item, s).wait_recv()


def backward_fast(dp_size, tokens, cotangent, fulls, kept, tables):
    outer = dp_size // 2
    length, model = tokens.shape
    block = model // dp_size
    gains, query_full, key_full, value_full, gate_full, out_full, hidden_full, up_full, down_full = fulls
    (mixer_input, turned_query, turned_keys, values, retained, gate_in, mixed, residual, feed_input, hidden_pre,
     up_pre, activity) = kept
    heads = query_full.shape[1] // DK
    units = hidden_full.shape[1]
    quarter = length // 4
    shape = jax.ShapeDtypeStruct
    out_shape = [
        shape((length, model), BF16),
        shape((length, model), BF16),
        shape((N_GRADS, block, units), F32),
        shape((N_GRADS + 1, outer - 1, block, units), BF16),
        shape((8, block), F32),
        shape((N_GRADS, outer, block, units), BF16),
        shape((length, model), BF16),
    ]
    dma = pltpu.SemaphoreType.DMA
    vmem = pltpu.VMEM
    scratch = [vmem((length, model), BF16)] * 5 + [vmem((length, units), BF16)] * 4
    scratch += [vmem((2, STEP, units), F32), vmem((2, PART, units), F32)]
    scratch += [
        vmem((2 * outer, block, units), BF16),
        vmem((block, units), BF16),
        vmem((2 * (outer - 1), block, units), BF16),
        vmem((4, block, units), BF16),
        vmem((block, units), F32),
        vmem((2, quarter, model), BF16),
        vmem((2, quarter, model), BF16),
        vmem((quarter, model), BF16),
        vmem((quarter, model), BF16),
        vmem((quarter, model), BF16),
        vmem((quarter, model), F32),
        vmem((quarter, model), F32),
        vmem(tables[1].shape[1:], F32),
        vmem(gains.shape, BF16),
        vmem((1, model), F32),
        vmem((1, model), F32),
        vmem((1, heads * DV), F32),
        vmem((8, model), F32),
        vmem((3, 8, model), F32),
        vmem((dp_size, 8, block), F32),
        vmem((dp_size, 8, block), F32),
        vmem((1, heads * DV), F32),
        dma((N_GRADS, outer)),
        dma((N_GRADS, outer)),
        dma((N_GRADS + 1, outer)),
        dma((N_GRADS + 1, outer)),
        dma((3, 3)),
        dma((3, 3)),
        dma((3, 4)),
        dma((3, 4)),
        dma((3 + dp_size,)),
        dma((3 + dp_size,)),
        dma((dp_size + 13,)),
        dma((2, 2)),
        dma((N_GRADS + 1, outer)),
        dma((N_GRADS,)),
    ]

    def kernel(*refs):
        backward_kernel(outer, heads, (length, model, block, units), *refs)

    operands = (tokens, cotangent, *fulls, *kept, *tables)
    return pl.pallas_call(
        kernel,
        out_shape=out_shape,
        in_specs=[ANY] * len(operands),
        out_specs=[ANY] * len(out_shape),
        scratch_shapes=scratch,
        compiler_params=pltpu.CompilerParams(
            collective_id=1, has_side_effects=True, vmem_limit_bytes=63 * 1024 * 1024
        ),
    )(*operands)


def finish(near_sums, z_land, x_land, tokens_grad, output):
    steps = 8
    _, block, units = near_sums.shape
    length, model = output.shape
    rows, across = block // steps, block // 128
    side = units * across // steps
    turned = (G_DOWN, G_OUT)
    order = (G_BOTH, G_VALUE, G_GATE, G_OUT, G_HIDDEN, G_UP, G_DOWN)
    operands, in_specs, out_specs, out_shape = [], [], [], []

    def add(array, lead, item):
        operands.append(array)
        if item in turned:
            in_specs.append(pl.BlockSpec((1,) * len(lead) + (128, side), lambda i: (*lead, i % across, i // across)))
        else:
            in_specs.append(pl.BlockSpec((1,) * len(lead) + (rows, units), lambda i: (*lead, i, 0)))

    for item in order:
        add(near_sums, (item,), item)
        add(z_land, (item, 0), item)
        add(z_land, (item, 2), item)
        if item == G_DOWN:
            add(x_land, (item, 0), item)
        if item == G_BOTH:
            shapes = [((block, units // 2), (rows, units // 2))] * 2
        else:
            shapes = [((block, units), (rows, units))]
        for whole, part in shapes:
            if item in turned:
                out_shape.append(jax.ShapeDtypeStruct((units, block), F32))
                out_specs.append(pl.BlockSpec((side, 128), lambda i: (i // across, i % across)))
            else:
                out_shape.append(jax.ShapeDtypeStruct(whole, F32))
                out_specs.append(pl.BlockSpec(part, lambda i: (i, 0)))
    for array, kind in ((tokens_grad, F32), (output, BF16)):
        operands.append(array)
        spec = pl.BlockSpec((length // steps, model), lambda i: (i, 0))
        in_specs.append(spec)
        out_specs.append(spec)
        out_shape.append(jax.ShapeDtypeStruct(array.shape, kind))

    def kernel(*refs):
        ins, outs = list(refs[: len(operands)]), list(refs[len(operands) :])
        for item in order:
            total = ins.pop(0)[0]
            for _ in range(3 if item == G_DOWN else 2):
                total = total + ins.pop(0)[0, 0].astype(F32)
            if item == G_BOTH:
                outs.pop(0)[...] = total[:, : units // 2]
                outs.pop(0)[...] = total[:, units // 2 :]
            else:
                outs.pop(0)[...] = total.T if item in turned else total
        for source, target in zip(ins, outs):
            target[...] = source[...].astype(target.dtype)

    return pl.pallas_call(
        kernel,
        grid=(steps,),
        out_shape=out_shape,
        in_specs=in_specs,
        out_specs=out_specs,
        compiler_params=pltpu.CompilerParams(vmem_limit_bytes=62 * 1024 * 1024),
    )(*operands)


def on_device(
    dp_size,
    tensor_size,
    tokens,
    mixer_gain,
    query_weight,
    key_weight,
    value_weight,
    gate_weight,
    out_weight,
    group_gain,
    feed_gain,
    hidden_weight,
    up_weight,
    down_weight,
    cotangent,
):
    data = Ring("dp", dp_size)
    team = Ring("tensor", tensor_size)
    length, model = tokens.shape
    quarter = length // tensor_size
    heads_here = query_weight.shape[1] // DK

    block = mixer_gain.shape[0]
    width = query_weight.shape[1]
    group_block = group_gain.shape[1]
    head_ids = (lax.axis_index("tensor") * heads_here + jnp.arange(heads_here)).astype(F32)
    decays = decay_table(head_ids, length)
    inputs = data.own_order(tokens, 1)
    cot = data.own_order(cotangent, 1)

    def my_rows(array):
        return lax.dynamic_slice_in_dim(array, team.me * quarter, quarter, 0)

    def row_terms(left, right):
        return lambda start, rows: plain_product(
            lax.dynamic_slice_in_dim(left, start, rows, 0), right
        )

    units = hidden_weight.shape[1]
    even = units == 2 * width == heads_here * DV == model // 2 and heads_here * DV // block <= 6 and heads_here <= 4
    if even and block % 128 == 0 and tensor_size == 4 and dp_size == 8 and length % 1024 == 0:
        group_line = lax.dynamic_update_slice(
            jnp.zeros((heads_here, DV), BF16), group_gain, (0, data.me * group_block)
        )
        gains = jnp.concatenate([mixer_gain, feed_gain, group_line.reshape(-1)])
        gains = jnp.broadcast_to(gains[None, :], (16, gains.shape[0]))
        cosine, sine, turns, fades = position_tables(length, tensor_size, heads_here)
        tables = (cosine, sine, fades)
        back_tables = (turns, fades)
        fulls, kept = forward_fast(
            dp_size,
            tokens,
            cotangent,
            gains,
            tables,
            (query_weight, key_weight, value_weight, gate_weight, out_weight, hidden_weight, up_weight, down_weight),
        )
        output, tokens_grad, near_sums, landed, vectors, crossed, _ = backward_fast(
            dp_size, tokens, cotangent, fulls, kept, back_tables
        )
        (query_grad, key_grad, value_grad, gate_grad, out_grad, hidden_grad, up_grad, down_grad, tokens_grad,
         output) = finish(near_sums, landed, crossed, tokens_grad, output)
        group_scale_grad = vectors[2 : 2 + heads_here * DV // block].reshape(heads_here, DV)
        return (
            output,
            tokens_grad,
            vectors[0],
            query_grad,
            key_grad,
            value_grad,
            gate_grad,
            out_grad,
            lax.dynamic_slice_in_dim(group_scale_grad, data.me * group_block, group_block, 1),
            vectors[1],
            hidden_grad,
            up_grad,
            down_grad,
        )
    else:
        gains = jnp.concatenate([mixer_gain, feed_gain, group_gain.reshape(-1)])[None, :]
        gains = data.gather(gains, 0)
        mixer_scale = gains[:, :block].reshape(-1).astype(F32)
        feed_scale = gains[:, block : 2 * block].reshape(-1).astype(F32)
        group_scale = data.true_order(gains[:, 2 * block :], 0).astype(F32)
        group_scale = group_scale.reshape(dp_size, heads_here, -1).swapaxes(0, 1).reshape(heads_here, -1)

        query_key = data.gather(jnp.concatenate([query_weight, key_weight], axis=1), 0)
        value_full = data.gather(value_weight, 0)
        gate_full = data.gather(gate_weight, 0)
        out_full = data.gather(out_weight, 1)
        hidden_full = data.gather(hidden_weight, 0)
        up_full = data.gather(up_weight, 0)
        down_full = data.gather(down_weight, 1)

        mixer_input = layer_norm(inputs.astype(F32), mixer_scale).astype(BF16)

        both = plain_product(mixer_input, query_key)
        query = both[:, :width]
        keyset = both[:, width:]
        values = plain_product(mixer_input, value_full).astype(BF16)
        gate_in = plain_product(mixer_input, gate_full)
        turned_query = rotate(query, heads_here, 1.0).astype(BF16).reshape(length, heads_here, DK)
        turned_keys = rotate(keyset, heads_here, 1.0).astype(BF16).reshape(length, heads_here, DK)
        scores, row_totals, denominators = core_scores(turned_query, turned_keys, decays)
        weights = (scores / denominators).astype(BF16)
        value_heads = values.reshape(length, heads_here, DV)
        retained = jnp.einsum("hqk,khd->qhd", weights, value_heads, preferred_element_type=F32)
        retained = retained.reshape(length, heads_here * DV)
        mixed = gate_piece(retained, gate_in, group_scale).astype(BF16)

        branch = token_sum(team, row_terms(mixed, out_full), length)
        residual = my_rows(inputs).astype(F32) + branch
        feed_input = token_gather(team, layer_norm(residual, feed_scale).astype(BF16))
        hidden_pre = plain_product(feed_input, hidden_full)
        up_pre = plain_product(feed_input, up_full)

    activity, feed_back = jax.vjp(feed_piece, hidden_pre, up_pre)
    activity = activity.astype(BF16)
    activity_grad = back_product(cot, down_full)
    hidden_grad, up_grad = feed_back(activity_grad)
    hidden_grad = hidden_grad.astype(BF16)
    up_grad = up_grad.astype(BF16)

    def feed_rows(start, rows):
        return back_product(
            lax.dynamic_slice_in_dim(hidden_grad, start, rows, 0), hidden_full
        ) + back_product(lax.dynamic_slice_in_dim(up_grad, start, rows, 0), up_full)

    feed_input_grad = token_sum(team, feed_rows, length)
    _, feed_norm_back = jax.vjp(layer_norm, residual, feed_scale)
    residual_part, feed_scale_grad = feed_norm_back(feed_input_grad)
    residual_grad = my_rows(cot).astype(F32) + residual_part
    branch_grad = token_gather(team, residual_grad.astype(BF16))

    hidden_weight_grad = data.scatter_sum(
        lambda turn: row_product(half_of(feed_input, turn, 1), hidden_grad), 0
    )
    up_weight_grad = data.scatter_sum(
        lambda turn: row_product(half_of(feed_input, turn, 1), up_grad), 0
    )
    down_grad = data.scatter_sum(lambda turn: row_product(activity, half_of(cot, turn, 1)), 1)

    feed_out = token_sum(team, row_terms(activity, down_full), length)
    output = token_gather(team, (residual + feed_out).astype(BF16))
    output = data.true_order(output, 1)

    mixed_grad = back_product(branch_grad, out_full)
    _, gate_back = jax.vjp(gate_piece, retained, gate_in, group_scale)
    retained_grad, gate_grad, group_scale_grad = gate_back(mixed_grad)
    retained_grad = retained_grad.astype(BF16)
    gate_grad = gate_grad.astype(BF16)
    out_weight_grad = data.scatter_sum(
        lambda turn: row_product(mixed, half_of(branch_grad, turn, 1)), 1
    )
    gate_weight_grad = data.scatter_sum(
        lambda turn: row_product(half_of(mixer_input, turn, 1), gate_grad), 0
    )

    grad_heads = retained_grad.reshape(length, heads_here, DV)
    weights_grad = jnp.einsum("qhd,khd->hqk", grad_heads, value_heads, preferred_element_type=F32)
    value_parts = jnp.einsum("hqk,qhd->khd", weights, grad_heads, preferred_element_type=F32)
    value_parts = value_parts.reshape(length, heads_here * DV).astype(BF16)
    value_weight_grad = data.scatter_sum(
        lambda turn: row_product(half_of(mixer_input, turn, 1), value_parts), 0
    )
    inner_totals = jnp.sum(weights_grad * scores, axis=-1, keepdims=True)
    slope = row_totals / denominators
    scores_grad = weights_grad / denominators - inner_totals / (denominators * denominators) * slope
    raw_grad = (scores_grad * DK ** (-0.5) * decays).astype(BF16)
    turned_query_grad = jnp.einsum("hqk,khd->qhd", raw_grad, turned_keys, preferred_element_type=F32)
    turned_key_grad = jnp.einsum("hqk,qhd->khd", raw_grad, turned_query, preferred_element_type=F32)
    query_parts = rotate(turned_query_grad.reshape(length, width), heads_here, -1.0).astype(BF16)
    key_parts = rotate(turned_key_grad.reshape(length, width), heads_here, -1.0).astype(BF16)
    both_parts = jnp.concatenate([query_parts, key_parts], axis=1)
    both_grad = data.scatter_sum(
        lambda turn: row_product(half_of(mixer_input, turn, 1), both_parts), 0
    )
    query_weight_grad = both_grad[:, :width]
    key_weight_grad = both_grad[:, width:]

    def mixer_rows(start, rows):
        def cut(array):
            return lax.dynamic_slice_in_dim(array, start, rows, 0)

        return (
            back_product(cut(both_parts), query_key)
            + back_product(cut(value_parts), value_full)
            + back_product(cut(gate_grad), gate_full)
        )

    mixer_input_grad = token_sum(team, mixer_rows, length)
    _, mixer_norm_back = jax.vjp(layer_norm, my_rows(inputs).astype(F32), mixer_scale)
    input_part, mixer_scale_grad = mixer_norm_back(mixer_input_grad)
    tokens_grad = token_gather(team, (residual_grad + input_part).astype(BF16))
    tokens_grad = data.true_order(tokens_grad, 1).astype(F32)

    norm_grads = jnp.concatenate([mixer_scale_grad, feed_scale_grad]).reshape(2, -1)
    norm_grads = lax.psum(data.true_order(norm_grads, 1), ("dp", "tensor"))
    norm_grads = lax.dynamic_slice_in_dim(norm_grads, data.me * block, block, 1)
    group_scale_grad = lax.psum(group_scale_grad, "dp")
    group_scale_grad = lax.dynamic_slice_in_dim(group_scale_grad, data.me * group_block, group_block, 1)
    return (
        output,
        tokens_grad,
        norm_grads[0],
        query_weight_grad,
        key_weight_grad,
        value_weight_grad,
        gate_weight_grad,
        out_weight_grad,
        group_scale_grad,
        norm_grads[1],
        hidden_weight_grad,
        up_weight_grad,
        down_grad,
    )


def solution(mesh):
    columns = P("dp", "tensor")
    rows = P("tensor", "dp")
    placed = (
        P("dp", None),
        P("dp"),
        columns,
        columns,
        columns,
        columns,
        rows,
        rows,
        P("dp"),
        columns,
        columns,
        rows,
        P("dp", None),
    )
    given = (
        P("dp", None),
        P("dp", None),
        P("dp"),
        columns,
        columns,
        columns,
        columns,
        rows,
        rows,
        P("dp"),
        columns,
        columns,
        rows,
    )

    def body(*arrays):
        return on_device(mesh.shape["dp"], mesh.shape["tensor"], *arrays)

    return jax.shard_map(body, mesh=mesh, in_specs=placed, out_specs=given, check_vma=False)
```

```python
import jax
import jax.numpy as jnp
import numpy as np
from jax import lax
from jax.experimental import pallas as pl
from jax.experimental.pallas import tpu as pltpu
from jax.sharding import PartitionSpec as P

DK = 256
DV = 512

norm_epsilon = 1e-05
group_epsilon = 0.01
F32 = jnp.float32
BF16 = jnp.bfloat16


def layer_norm(values, scale_gain, epsilon=norm_epsilon):
    center = values - jnp.mean(values, axis=-1, keepdims=True)
    spread = jnp.mean(center * center, axis=-1, keepdims=True)
    return center * lax.rsqrt(spread + epsilon) * scale_gain


def group_norm(retained, scale_gain):
    shaped = retained.reshape(retained.shape[0], scale_gain.shape[0], scale_gain.shape[1])
    return layer_norm(shaped, scale_gain, group_epsilon).reshape(retained.shape)


def rotate(values, head_count, direction):
    length = values.shape[0]
    head_width = values.shape[1] // head_count
    half_width = head_width // 2
    places = jnp.arange(length, dtype=F32)[:, None]
    speeds = 10000.0 ** (-jnp.arange(half_width, dtype=F32) / half_width)
    angles = places * speeds[None, :]
    cosine = jnp.cos(angles)[:, None, :]
    sine_part = direction * jnp.sin(angles)[:, None, :]
    shaped = values.reshape(length, head_count, 2, half_width)
    front_half = shaped[:, :, 0]
    back_half = shaped[:, :, 1]
    turned = jnp.stack(
        [front_half * cosine - back_half * sine_part, front_half * sine_part + back_half * cosine],
        axis=2,
    )
    return turned.reshape(length, head_count * head_width)


def decays_plain(head_ids, length):
    log_rates = jnp.log1p(-jnp.exp2(-5.0 - head_ids))
    row_place = jnp.arange(length)[:, None]
    key_place = jnp.arange(length)[None, :]
    distance = jnp.maximum(row_place - key_place, 0).astype(F32)
    decays = jnp.where(
        (row_place >= key_place)[None], jnp.exp(log_rates[:, None, None] * distance[None]), 0.0
    )
    return decays


def decay_table(head_ids, length):
    decays = decays_plain(head_ids, length)
    return decays * lax.rsqrt(jnp.sum(decays, axis=-1, keepdims=True))


def plain_product(left, right):
    return jnp.dot(left, right, preferred_element_type=F32)


def row_product(left, right):
    return lax.dot_general(left, right, (((0,), (0,)), ((), ())), preferred_element_type=F32)


def back_product(left, right):
    return lax.dot_general(left, right, (((1,), (1,)), ((), ())), preferred_element_type=F32)


def core_scores(turned_query, turned_keys, decays):
    raw_scores = jnp.einsum("qhd,khd->hqk", turned_query, turned_keys, preferred_element_type=F32)
    scores = raw_scores * DK ** (-0.5) * decays
    row_totals = jnp.sum(scores, axis=-1, keepdims=True)
    denominators = jnp.sqrt(row_totals * row_totals + 1.0)
    return (scores, row_totals, denominators)


def feed_piece(hidden_pre, up_pre):
    return jax.nn.gelu(hidden_pre) * up_pre


def gate_piece(retained, gate_in, group_scale):
    return jax.nn.silu(gate_in) * group_norm(retained, group_scale)


class Ring:
    def __init__(self, name, size):
        self.name = name
        self.size = size
        self.outer = size // 2
        self.me = lax.axis_index(name)
        self.swap_pairs = [(i, i ^ 1) for i in range(size)]

    def swap(self, block):
        return lax.ppermute(block, self.name, self.swap_pairs)

    def shift(self, block, step):
        pairs = [
            (i, ((i // 2 + step) % self.outer) * 2 + i % 2) for i in range(self.size)
        ]
        return lax.ppermute(block, self.name, pairs)

    def block_at(self, place):
        turn, step = place // self.outer, place % self.outer
        outer = (self.me // 2 + self.outer - step) % self.outer
        return outer * 2 + (self.me % 2 + turn) % 2

    def place_of(self, block):
        turn = (block % 2 + self.me % 2) % 2
        step = (self.me // 2 + self.outer - block // 2) % self.outer
        return turn * self.outer + step

    def own_order(self, array, axis):
        width = array.shape[axis] // self.size
        return jnp.concatenate(
            [
                lax.dynamic_slice_in_dim(array, self.block_at(p) * width, width, axis)
                for p in range(self.size)
            ],
            axis=axis,
        )

    def true_order(self, array, axis):
        width = array.shape[axis] // self.size
        return jnp.concatenate(
            [
                lax.dynamic_slice_in_dim(array, self.place_of(b) * width, width, axis)
                for b in range(self.size)
            ],
            axis=axis,
        )

    def gather(self, block, axis):
        near = jnp.concatenate(
            [block] + [self.shift(block, s) for s in range(1, self.outer)], axis=axis
        )
        return jnp.concatenate([near, self.swap(near)], axis=axis)

    def scatter_sum(self, make_half, axis):
        far = self.swap(make_half(1).astype(BF16))
        near = make_half(0) + far.astype(F32)
        width = near.shape[axis] // self.outer
        total = lax.slice_in_dim(near, 0, width, axis=axis)
        for s in range(1, self.outer):
            part = lax.slice_in_dim(near, s * width, (s + 1) * width, axis=axis).astype(BF16)
            total = total + self.shift(part, -s).astype(F32)
        return total


def half_of(array, turn, axis):
    width = array.shape[axis] // 2
    return lax.slice_in_dim(array, turn * width, (turn + 1) * width, axis=axis)


def token_sum(ring, make_rows, rows):
    width = rows // ring.size
    outer, inner = ring.me // 2, ring.me % 2
    far = [make_rows((((outer + s) % ring.outer) * 2 + 1 - inner) * width, width) for s in range(ring.outer)]
    got = ring.swap(jnp.concatenate(far, axis=0).astype(BF16)).astype(F32)
    near = [
        make_rows((((outer + s) % ring.outer) * 2 + inner) * width, width)
        + lax.slice_in_dim(got, s * width, (s + 1) * width, axis=0)
        for s in range(ring.outer)
    ]
    total = near[0]
    for s in range(1, ring.outer):
        total = total + ring.shift(near[s].astype(BF16), s).astype(F32)
    return total


def token_gather(ring, block):
    return ring.true_order(ring.gather(block, 0), 0)


MESH = pl.DeviceIdType.MESH
ANY = pl.BlockSpec(memory_space=pl.ANY)


class Wires:
    def __init__(self, outer):
        self.outer = outer
        self.dp = lax.axis_index("dp")
        self.tensor = lax.axis_index("tensor")
        self.ring = self.dp // 2
        self.turn = self.dp % 2
        self.row = self.tensor // 2
        self.core = self.tensor % 2
        self.order = [1, outer - 1] + list(range(2, outer - 1))

    def far(self, step):
        return (lax.rem(self.ring + step, self.outer) * 2 + self.turn, self.tensor)

    def peer(self):
        return (self.ring * 2 + 1 - self.turn, self.tensor)

    def sibling(self):
        return (self.dp, self.row * 2 + 1 - self.core)

    def across(self):
        return (self.dp, (1 - self.row) * 2 + self.core)

    def block_at(self, place):
        turn, step = place // self.outer, place % self.outer
        return lax.rem(self.ring + self.outer - step, self.outer) * 2 + lax.rem(self.turn + turn, 2)

    def corner(self):
        return (self.dp, (1 - self.row) * 2 + 1 - self.core)

    def greet_all(self):
        barrier = pltpu.get_barrier_semaphore()
        partners = [(self.block_at(place), self.tensor) for place in range(1, 2 * self.outer)]
        partners += [self.sibling(), self.across(), self.corner()]
        for partner in partners:
            pl.semaphore_signal(barrier, inc=1, device_id=partner, device_id_type=MESH)
        pl.semaphore_wait(barrier, len(partners))


def remote(src, dst, send, recv, device):
    return pltpu.make_async_remote_copy(
        src_ref=src, dst_ref=dst, send_sem=send, recv_sem=recv, device_id=device, device_id_type=MESH
    )


def tile(index, rows):
    return pl.ds(pl.multiple_of(index * rows, rows), rows)


def norm_rows(values, gain, epsilon):
    center = values - jnp.mean(values, axis=-1, keepdims=True)
    spread = jnp.mean(center * center, axis=-1, keepdims=True)
    return center * lax.rsqrt(spread + epsilon) * gain


def silu(v):
    return v * (1.0 / (1.0 + jnp.exp(-v)))


N_ITEMS = 9
GAINS, QUERY, KEY, VALUE, GATE, OUT, HIDDEN, UP, DOWN = range(N_ITEMS)
STEP = 256
PART = 128


def forward_kernel(outer, heads, dims, *refs):
    length, model, block = dims
    quarter = length // 4
    tokens, cotangent, gains, cosine, sine, decays = refs[:6]
    items = (gains,) + refs[6:14]
    fulls = refs[14:23]
    (mixer_out, query_out, key_out, value_out, retained_out, gate_out, mixed_out, residual_out,
     feed_out, hidden_out, up_out, activity_out) = refs[23:35]
    (slot_a, slot_b, slot_o, wide, mixer, rq, rk, values, kept, gate_in, mixed, residual, csend, crecv, ysend,
     yrecv, cos_v, sin_v, keyd, gain_v, gain_m, gain_f, gain_g,
     loc, zs, zr, xs, xr, ts, tr, ls, os_) = refs[35:]
    wires = Wires(outer)
    rows = length // STEP
    units = slot_a.shape[1]

    def piece(item, place):
        if item in (OUT, DOWN):
            return fulls[item].at[:, pl.ds(place * block, block)]
        height = items[item].shape[0]
        return fulls[item].at[pl.ds(place * height, height)]

    last = outer - 1
    up = wires.ring < last
    down = wires.ring > 0

    def along(item, source, place, step):
        device = (jnp.clip(wires.ring + step, 0, last) * 2 + wires.turn, wires.tensor)
        return remote(source, piece(item, place), zs.at[item, place], zr.at[item, place], device)

    def climb(item, source, base):
        @pl.when(up)
        def _():
            along(item, source, base + 1, 1).start()

        @pl.when(down)
        def _():
            along(item, source, base + last, -1).start()

    def beside(item, step):
        src = items[item] if step == 0 else piece(item, step)
        return remote(src, piece(item, outer + step), xs.at[item, step], xr.at[item, step], wires.peer())

    def own(item):
        return pltpu.make_async_copy(items[item], piece(item, 0), loc.at[item])

    def issue(item, cross=True):
        climb(item, items[item], 0)
        if cross:
            beside(item, 0).start()

    def hops(item, base, cross, which=None):
        for hop in which or range(1, outer):
            @pl.when(hop <= wires.ring)
            def _():
                along(item, piece(item, base + hop), base + hop, 1).wait_recv()
                if hop < last:
                    @pl.when(up)
                    def _():
                        along(item, piece(item, base + hop), base + hop + 1, 1).start()
                if cross:
                    beside(item, hop).start()

            @pl.when(hop <= last - wires.ring)
            def _():
                place = outer - hop
                along(item, piece(item, base + place), base + place, 1).wait_recv()
                if hop < last:
                    @pl.when(down)
                    def _():
                        along(item, piece(item, base + place), base + place - 1, -1).start()
                if cross:
                    beside(item, place).start()

    def pass_on(item):
        hops(item, 0, item != DOWN)

    def climb_sent(item, base):
        @pl.when(up)
        def _():
            along(item, piece(item, base), base + 1, 1).wait_send()

        @pl.when(down)
        def _():
            along(item, piece(item, base), base + last, -1).wait_send()

        for hop in range(1, last):
            @pl.when((hop <= wires.ring) & up)
            def _():
                along(item, piece(item, base + hop), base + hop + 1, 1).wait_send()

            @pl.when((hop <= last - wires.ring) & down)
            def _():
                along(item, piece(item, base + outer - hop), base + outer - hop - 1, -1).wait_send()

    def arrived(item):
        if item != UP:
            own(item).wait()
        for step in range(outer if item != DOWN else 1):
            beside(item, step).wait_recv()

    def load(src, dst, index):
        copy = pltpu.make_async_copy(src, dst, ls.at[index])
        copy.start()
        return copy

    stores = []

    def store(src, dst):
        copy = pltpu.make_async_copy(src, dst, os_.at[len(stores)])
        copy.start()
        stores.append(copy)
        return copy

    def gain_copy(place):
        turn, step = place // outer, place % outer
        there = piece(GAINS, turn * outer + (outer - step) % outer)
        device = (wires.block_at(place), wires.tensor)
        return remote(gains, there, zs.at[GAINS, place], zr.at[GAINS, turn * outer + (outer - step) % outer], device)

    wires.greet_all()
    for place in range(1, 2 * outer):
        gain_copy(place).start()
    for item in range(N_ITEMS):
        own(item).start()
    issue(QUERY)
    issue(KEY)
    issue(VALUE)
    beside(DOWN, 0).start()

    def own_blocks(source, target):
        copies = []
        for place in range(2 * outer):
            at = pl.multiple_of(wires.block_at(place) * block, block)
            copies.append(load(source.at[:, pl.ds(at, block)], target.at[:, pl.ds(place * block, block)], place))
        return copies

    first = 2 * outer
    loads = own_blocks(tokens, wide)
    loads.append(load(cosine, cos_v, first))
    loads.append(load(sine, sin_v, first + 1))
    loads.append(load(decays.at[wires.tensor], keyd, first + 2))
    own(GAINS).wait()
    for place in range(1, 2 * outer):
        gain_copy(place).wait_recv()
    for copy in loads:
        copy.wait()
    copy = load(fulls[GAINS], gain_v, 0)
    copy.wait()
    group = jnp.zeros((1, heads * DV), F32)
    for place in range(2 * outer):
        line = gain_v[place * 16 : place * 16 + 1, :].astype(F32)
        gain_m[:, place * block : (place + 1) * block] = line[:, :block]
        gain_f[:, place * block : (place + 1) * block] = line[:, block : 2 * block]
        group = group + line[:, 2 * block :]
    gain_g[...] = group

    @pl.loop(0, length // 128)
    def _(r):
        at = tile(r, 128)
        mixer[at, :] = norm_rows(wide[at, :].astype(F32), gain_m[...], norm_epsilon).astype(BF16)

    mine = tile(wires.tensor, quarter)
    residual[...] = wide[mine, :].astype(F32)
    mixer_store = store(mixer, mixer_out)
    pass_on(QUERY)
    pass_on(KEY)
    issue(GATE)
    pass_on(VALUE)
    issue(OUT)
    hops(GATE, 0, True, (1,))
    arrived(QUERY)
    arrived(KEY)
    narrow = heads * DK
    copy = load(fulls[QUERY], slot_a.at[:, pl.ds(0, narrow)], 0)
    other = load(fulls[KEY], slot_a.at[:, pl.ds(narrow, narrow)], 1)
    copy.wait()
    other.wait()

    @pl.loop(0, rows)
    def _(r):
        at = tile(r, STEP)
        both = jnp.dot(mixer[at, :], slot_a[...], preferred_element_type=F32)
        c, s = cos_v[at, :], sin_v[at, :]
        half = DK // 2
        for target, base in ((rq, 0), (rk, narrow)):
            for h in range(heads):
                lo = base + h * DK
                a, b = both[:, lo : lo + half], both[:, lo + half : lo + DK]
                target[at, h * DK : h * DK + half] = (a * c - b * s).astype(BF16)
                target[at, h * DK + half : (h + 1) * DK] = (a * s + b * c).astype(BF16)

    store(rq, query_out)
    store(rk, key_out)
    hops(GATE, 0, True, (2, 3))
    issue(HIDDEN)
    hops(OUT, 0, True, (1,))
    arrived(VALUE)
    load(fulls[VALUE], slot_b, 0).wait()

    @pl.loop(0, rows)
    def _(r):
        at = tile(r, STEP)
        values[at, :] = jnp.dot(mixer[at, :], slot_b[...], preferred_element_type=F32).astype(BF16)

    store(values, value_out)
    for h in range(heads):
        for r in range(rows):
            at = slice(r * STEP, (r + 1) * STEP)
            upto = (r + 1) * STEP
            q = rq[at, h * DK : (h + 1) * DK]
            k = rk[:upto, h * DK : (h + 1) * DK]
            raw = lax.dot_general(q, k, (((1,), (1,)), ((), ())), preferred_element_type=F32)
            fade = keyd[heads + h : heads + h + 1, at].reshape(STEP, 1) * keyd[h : h + 1, :upto]
            place = lax.broadcasted_iota(jnp.int32, (STEP, upto), 0) + r * STEP
            under = place >= lax.broadcasted_iota(jnp.int32, (STEP, upto), 1)
            scores = raw * jnp.where(under, fade, 0.0)
            total = jnp.sum(scores, axis=-1, keepdims=True)
            share = (scores * lax.rsqrt(total * total + 1.0)).astype(BF16)
            kept[at, h * DV : (h + 1) * DV] = jnp.dot(
                share, values[:upto, h * DV : (h + 1) * DV], preferred_element_type=F32
            )
    kept_store = store(kept, retained_out)
    hops(OUT, 0, True, (2, 3))
    issue(UP)
    hops(HIDDEN, 0, True, (1,))
    arrived(GATE)
    load(fulls[GATE], slot_a, 0).wait()

    @pl.loop(0, rows)
    def _(r):
        at = tile(r, STEP)
        gate = jnp.dot(mixer[at, :], slot_a[...], preferred_element_type=F32)
        gate_in[at, :] = gate
        for h in range(heads):
            cols = slice(h * DV, (h + 1) * DV)
            normed = norm_rows(kept[at, cols], gain_g[:, cols], group_epsilon)
            mixed[at, cols] = (silu(gate[:, cols]) * normed).astype(BF16)

    mixer_store.wait()
    cot_loads = own_blocks(cotangent, mixer)
    gate_store = store(gate_in, gate_out)
    mixed_store = store(mixed, mixed_out)
    hops(HIDDEN, 0, True, (2, 3))
    hops(UP, 0, True, (1,))
    issue(DOWN, False)
    arrived(DOWN)
    climb(DOWN, piece(DOWN, outer), outer)
    arrived(OUT)
    load(fulls[OUT], slot_o, first).wait()

    def branch_rows(index):
        return jnp.dot(mixed[tile(index, quarter), :], slot_o[...], preferred_element_type=F32)

    def to_sibling(s):
        return remote(csend.at[s], crecv.at[s], ts.at[s], tr.at[s], wires.sibling())

    cross = remote(ysend, yrecv, ts.at[2], tr.at[2], wires.across())
    for s in (1, 0):
        owner = lax.rem(wires.row + s, 2) * 2 + 1 - wires.core
        csend[s] = branch_rows(owner).astype(BF16)
        to_sibling(s).start()
    part = branch_rows((1 - wires.row) * 2 + wires.core)
    to_sibling(1).wait_recv()
    ysend[...] = (part + crecv[1].astype(F32)).astype(BF16)
    cross.start()
    residual[...] += branch_rows(wires.tensor)
    to_sibling(0).wait_recv()
    residual[...] += crecv[0].astype(F32)
    hops(UP, 0, True, (2, 3))
    hops(DOWN, 0, False, (1,))
    cross.wait_recv()
    residual[...] += yrecv[...].astype(F32)
    store(residual, residual_out)
    feed_mine = wide.at[mine]

    @pl.loop(0, quarter // 128)
    def _(r):
        at = tile(r, 128)
        ysend_rows = norm_rows(residual[at, :], gain_f[...], norm_epsilon).astype(BF16)
        feed_mine[at, :] = ysend_rows

    feed_cross = remote(feed_mine, feed_mine, ts.at[3], tr.at[3], wires.across())
    feed_near = remote(feed_mine, feed_mine, ts.at[4], tr.at[4], wires.sibling())
    theirs = wide.at[tile((1 - wires.row) * 2 + wires.core, quarter)]
    feed_far = remote(theirs, theirs, ts.at[5], tr.at[5], wires.sibling())
    feed_cross.start()
    feed_near.start()
    hops(DOWN, 0, False, (2, 3))
    hops(DOWN, outer, False, (1,))
    feed_cross.wait_recv()
    feed_far.start()
    near_cols, far_cols = pl.ds(0, model // 2), pl.ds(model // 2, model // 2)
    down_load = load(fulls[DOWN].at[:, near_cols], slot_o.at[:, near_cols], first + 1)
    own(UP).wait()
    up_load = load(fulls[UP].at[near_cols], slot_a.at[near_cols], first + 2)
    for copy in cot_loads:
        copy.wait()
    down_load.wait()
    gate_store.wait()

    def grads_half(at, cols):
        return lax.dot_general(
            mixer[at, cols], slot_o[:, cols], (((1,), (1,)), ((), ())), preferred_element_type=F32
        )

    @pl.loop(0, rows)
    def _(r):
        at = tile(r, STEP)
        gate_in[at, :] = grads_half(at, near_cols)

    hops(DOWN, outer, False, (2,))
    arrived(HIDDEN)
    load(fulls[HIDDEN], slot_b, first).wait()
    feed_near.wait_recv()
    feed_far.wait_recv()
    store(wide, feed_out)
    kept_store.wait()

    @pl.loop(0, rows)
    def _(r):
        at = tile(r, STEP)
        kept[at, :] = jnp.dot(wide[at, :], slot_b[...], preferred_element_type=F32)

    hops(DOWN, outer, False, (3,))
    load(fulls[DOWN].at[:, far_cols], slot_o.at[:, far_cols], first + 1).wait()

    @pl.loop(0, rows)
    def _(r):
        at = tile(r, STEP)
        gate_in[at, :] += grads_half(at, far_cols)

    arrived(UP)
    load(fulls[UP].at[far_cols], slot_a.at[far_cols], first).wait()
    up_load.wait()
    mixed_store.wait()

    for part in range(2):
        @pl.loop(part * (length // PART // 2), (part + 1) * (length // PART // 2), unroll=True)
        def _(r):
            at = tile(r, PART)
            u = jnp.dot(wide[at, :], slot_a[...], preferred_element_type=F32)
            h, grads = kept[at, :], gate_in[at, :]
            t = jnp.tanh(SQRT_2_PI * (h + CUBIC * h * h * h))
            gelu = 0.5 * h * (1.0 + t)
            slope = 0.5 * (1.0 + t) + 0.5 * h * (1.0 - t * t) * (SQRT_2_PI * (1.0 + 3.0 * CUBIC * h * h))
            mixed[at, :] = (gelu * u).astype(BF16)
            slot_b[at, :] = (grads * u * slope).astype(BF16)
            slot_o[at, pl.ds(0, units)] = (grads * gelu).astype(BF16)

        done = pl.ds(part * (length // 2), length // 2)
        store(mixed.at[done], activity_out.at[done])
        store(slot_b.at[done], hidden_out.at[done])
        store(slot_o.at[done, pl.ds(0, units)], up_out.at[done])

    for copy in stores:
        if not any(copy is done for done in (kept_store, gate_store, mixer_store, mixed_store)):
            copy.wait()
    for s in range(2):
        to_sibling(s).wait_send()
    for copy in (cross, feed_cross, feed_near, feed_far):
        copy.wait_send()
    for place in range(1, 2 * outer):
        gain_copy(place).wait_send()
    for item in range(1, N_ITEMS):
        climb_sent(item, 0)
        for step in range(outer if item != DOWN else 1):
            beside(item, step).wait_send()
    climb_sent(DOWN, outer)


def position_tables(length, teams, heads):
    half = DK // 2
    speeds = 10000.0 ** (-np.arange(half, dtype=np.float32) / np.float32(half))
    angles = np.arange(length, dtype=np.float32)[:, None] * speeds.astype(np.float32)[None, :]
    pair = [np.cos(angles), np.sin(angles)]
    turns = [t.reshape(length // PART, PART, half).swapaxes(0, 1).reshape(PART, -1) for t in pair]
    rates = np.log1p(-np.exp2(-5.0 - np.arange(teams * heads, dtype=np.float64)))[:, None]
    places = np.arange(length, dtype=np.float64)[None, :]
    sums = np.expm1(rates * (places + 1)) / np.expm1(rates)
    row_decay = np.exp(rates * (places - length // 2)) / np.sqrt(sums) * DK**-0.5
    key_decay = np.exp(rates * (length // 2 - places))
    fades = np.zeros((teams, 8, length))
    fades[:, :heads] = key_decay.reshape(teams, heads, length)
    fades[:, heads : 2 * heads] = row_decay.reshape(teams, heads, length)
    return [jnp.asarray(np.asarray(t, np.float32)) for t in (*pair, np.stack(turns), fades)]


def forward_fast(dp_size, tokens, cotangent, gains, tables, weights):
    outer = dp_size // 2
    length, model = tokens.shape
    block = model // dp_size
    heads = weights[0].shape[1] // DK
    units = weights[3].shape[1]
    wide = units
    shapes = [(gains.shape[0] * dp_size, gains.shape[1])]
    for place, weight in enumerate(weights):
        if place + 1 in (OUT, DOWN):
            shapes.append((weight.shape[0], model))
        else:
            shapes.append((model, weight.shape[1]))
    out_shape = [jax.ShapeDtypeStruct(s, BF16) for s in shapes]
    half = heads * DK
    for shape, kind in (
        ((length, model), BF16),
        ((length, half), BF16),
        ((length, half), BF16),
        ((length, wide), BF16),
        ((length, wide), F32),
        ((length, wide), F32),
        ((length, wide), BF16),
        ((length // 4, model), F32),
        ((length, model), BF16),
        ((length, units), BF16),
        ((length, units), BF16),
        ((length, units), BF16),
    ):
        out_shape.append(jax.ShapeDtypeStruct(shape, kind))
    quarter = length // 4
    dma = pltpu.SemaphoreType.DMA
    scratch = [
        pltpu.VMEM((model, wide), BF16),
        pltpu.VMEM((model, wide), BF16),
        pltpu.VMEM((wide, model), BF16),
        pltpu.VMEM((length, model), BF16),
        pltpu.VMEM((length, model), BF16),
        pltpu.VMEM((length, half), BF16),
        pltpu.VMEM((length, half), BF16),
        pltpu.VMEM((length, wide), BF16),
        pltpu.VMEM((length, wide), F32),
        pltpu.VMEM((length, wide), F32),
        pltpu.VMEM((length, wide), BF16),
        pltpu.VMEM((quarter, model), F32),
        pltpu.VMEM((2, quarter, model), BF16),
        pltpu.VMEM((2, quarter, model), BF16),
        pltpu.VMEM((quarter, model), BF16),
        pltpu.VMEM((quarter, model), BF16),
        pltpu.VMEM(tables[0].shape, F32),
        pltpu.VMEM(tables[1].shape, F32),
        pltpu.VMEM(tables[2].shape[1:], F32),
        pltpu.VMEM(shapes[0], BF16),
        pltpu.VMEM((1, model), F32),
        pltpu.VMEM((1, model), F32),
        pltpu.VMEM((1, heads * DV), F32),
        dma((N_ITEMS,)),
        dma((N_ITEMS, 2 * outer)),
        dma((N_ITEMS, 2 * outer)),
        dma((N_ITEMS, outer)),
        dma((N_ITEMS, outer)),
        dma((6,)),
        dma((6,)),
        dma((2 * outer + 4,)),
        dma((16,)),
    ]

    def kernel(*refs):
        forward_kernel(outer, heads, (length, model, block), *refs)

    results = pl.pallas_call(
        kernel,
        out_shape=out_shape,
        in_specs=[ANY] * (6 + len(weights)),
        out_specs=[ANY] * len(out_shape),
        scratch_shapes=scratch,
        compiler_params=pltpu.CompilerParams(
            collective_id=0, has_side_effects=True, vmem_limit_bytes=58 * 1024 * 1024
        ),
    )(tokens, cotangent, gains, *tables, *weights)
    return results[: N_ITEMS], results[N_ITEMS:]


N_GRADS = 7
(G_DOWN, G_HIDDEN, G_UP, G_OUT, G_GATE, G_VALUE, G_BOTH) = range(N_GRADS)
FLOW = (2, 3, 1, 0)
SQRT_2_PI = 0.7978845608028654
CUBIC = 0.044715


def rows_dot(left, right):
    return lax.dot_general(left, right, (((0,), (0,)), ((), ())), preferred_element_type=F32)


def back_dot(left, right):
    return lax.dot_general(left, right, (((1,), (1,)), ((), ())), preferred_element_type=F32)


def norm_back(values, grads, gain, epsilon):
    center = values - jnp.mean(values, axis=-1, keepdims=True)
    inverse = lax.rsqrt(jnp.mean(center * center, axis=-1, keepdims=True) + epsilon)
    unit = center * inverse
    u = grads * gain
    mean = jnp.mean(u, axis=-1, keepdims=True)
    slope = jnp.mean(u * unit, axis=-1, keepdims=True)
    return (u - mean - unit * slope) * inverse, grads * unit


def backward_kernel(outer, heads, dims, *refs):
    length, model, block, units = dims
    quarter = length // 4
    half = model // 2
    (tokens, cotangent, gains, query_full, key_full, value_full, gate_full, out_full, hidden_full, up_full,
     down_full, mixer_in, query_in, key_in, value_in, retained_in, gate_in, mixed_in, residual_in, feed_in,
     hidden_in, up_in, activity_in, turns, key_decay) = refs[:25]
    (output, tokens_out, near_out, z_land, vector_out, x_land, branch_land) = refs[25:32]
    (u0, u1, u2, u3, u4, act, hid, upg, both, fa, fb, x_ring, x_extra, z_ring, x_stage, acc, csend, crecv, ysend, yrecv,
     stage, grad_q, value_q, keyd, gain_v, gain_m, gain_f, gain_g,
     vec_t, vec_tr, vec_d, vec_dr, vec_g,
     xs, xr, zs, zr, ts, tr, gs, gr, vs, vr, ls, fs, st, ac) = refs[32:]
    wires = Wires(outer)
    rows = length // STEP
    mine = tile(wires.tensor, quarter)
    near_rows = tile(wires.row * 2 + 1 - wires.core, quarter)
    across_index = (1 - wires.row) * 2 + wires.core
    across_rows = tile(across_index, quarter)
    corner_rows = tile((1 - wires.row) * 2 + 1 - wires.core, quarter)

    def load(src, dst, index):
        copy = pltpu.make_async_copy(src, dst, ls.at[index])
        copy.start()
        return copy

    def load_tall(src, dst, index):
        return [load(src.at[pl.ds(h * half, half)], dst.at[:, pl.ds(h * half, half)], index + h) for h in range(2)]

    def wait_all(copies):
        for copy in copies:
            copy.wait()

    def own_blocks(src, dst, index):
        copies = []
        for place in range(2 * outer):
            at = pl.multiple_of(wires.block_at(place) * block, block)
            copies.append(load(src.at[:, pl.ds(at, block)], dst.at[:, pl.ds(place * block, block)], index + place))
        return copies

    def true_blocks(src, dst, index):
        copies = []
        for place in range(2 * outer):
            at = pl.multiple_of(wires.block_at(place) * block, block)
            copies.append(load(src.at[:, pl.ds(place * block, block)], dst.at[:, pl.ds(at, block)], index + place))
        return copies

    def x_copy(item, s):
        source = x_extra if item == G_DOWN else x_ring.at[(item % 2) * outer + s]
        return remote(source, x_land.at[item, s], xs.at[item, s], xr.at[item, s], wires.peer())

    def z_copy(item, s):
        step = outer - 1 if s != outer - 1 else 1
        device = (lax.rem(wires.ring + step, outer) * 2 + wires.turn, wires.tensor)
        slot = (item % 2) * (outer - 1) + s - 1
        return remote(z_ring.at[slot], z_land.at[item, s - 1], zs.at[item, s], zr.at[item, s], device)

    def columns(place):
        return pl.ds(pl.multiple_of(place * block, block), block)

    def far(item, left, right, flow=FLOW, behind=None):
        for s in flow:
            if item >= 3:
                x_copy(item - 2, s).wait_send()
            product = rows_dot(left[:, columns(outer + s)], right[...])
            x_ring[(item % 2) * outer + s] = product.astype(BF16)
            if behind is None:
                x_copy(item, s).start()
        if behind is not None:
            behind.wait_send()
            for s in flow:
                x_copy(item, s).start()

    def acc_copy(item):
        return pltpu.make_async_copy(acc, near_out.at[item], ac.at[item])

    def staged(item, place, source):
        copy = pltpu.make_async_copy(source, x_stage.at[place], st.at[item, place])
        copy.start()
        return copy

    sides = ((0, G_DOWN), (1, N_GRADS))

    def down_product(turn, s):
        return rows_dot(u0[:, columns(turn * outer + s)], act[...])

    def down_give(s):
        for turn, item in sides:
            z_ring[(item % 2) * (outer - 1) + s - 1] = down_product(turn, s).astype(BF16)
            z_copy(item, s).start()

    def down_first():
        down_give(2)
        for turn, item in sides:
            z_ring[(item % 2) * (outer - 1)] = down_product(turn, 1).astype(BF16)
        x_extra[...] = down_product(1, 0).astype(BF16)
        acc[...] = down_product(0, 0)
        acc_copy(G_DOWN).start()

    def relay(item):
        z_copy(item, 2).wait_recv()
        staged(item, 2, z_land.at[item, 1]).wait()
        slot = (item % 2) * (outer - 1)
        z_ring[slot] = (z_ring[slot].astype(F32) + x_stage[2].astype(F32)).astype(BF16)
        z_copy(item, 1).start()

    def down_sum():
        z_copy(N_GRADS, 3).wait_recv()
        copy = staged(N_GRADS, 2, z_land.at[N_GRADS, 2])
        z_copy(N_GRADS, 1).wait_recv()
        other = staged(N_GRADS, 3, z_land.at[N_GRADS, 0])
        copy.wait()
        other.wait()
        total = x_extra[...].astype(F32) + x_stage[2].astype(F32) + x_stage[3].astype(F32)
        x_extra[...] = total.astype(BF16)

    def near(item, left, right, flow=FLOW):
        before = N_GRADS if item == 1 else item - 2
        for s in flow:
            x_copy(item, s).wait_recv()
            copy = staged(item, s % 2, x_land.at[item, s])
            if s:
                z_copy(before, s).wait_send()
            if s == 0:
                acc_copy(item - 1).wait()
            product = rows_dot(left[:, columns(s)], right[...])
            copy.wait()
            product = product + x_stage[s % 2].astype(F32)
            if s == 0:
                acc[...] = product
                acc_copy(item).start()
                continue
            z_ring[(item % 2) * (outer - 1) + s - 1] = product.astype(BF16)
            if s > 1:
                z_copy(item, s).start()

    class Round:
        def __init__(self, index):
            self.index = index
            self.cross = remote(ysend, yrecv, ts.at[index, 2], tr.at[index, 2], wires.across())

        def to_sibling(self, s):
            return remote(csend.at[s], crecv.at[s], ts.at[self.index, s], tr.at[self.index, s], wires.sibling())

        def give(self, terms):
            for s in (1, 0):
                owner = lax.rem(wires.row + s, 2) * 2 + 1 - wires.core
                for h in range(2):
                    cols = slice(h * half, (h + 1) * half)
                    csend[s, :, cols] = terms(tile(owner, quarter), h).astype(BF16)
                self.to_sibling(s).start()

        def hand_over(self, terms):
            self.to_sibling(1).wait_recv()
            for h in range(2):
                cols = slice(h * half, (h + 1) * half)
                ysend[:, cols] = (terms(across_rows, h) + crecv[1, :, cols].astype(F32)).astype(BF16)
            self.cross.start()

        def keep(self, terms, totals, add):
            for h in range(2):
                part = terms(mine, h)
                totals[h][...] = totals[h][...] + part if add else part
            self.to_sibling(0).wait_recv()
            for h in range(2):
                totals[h][...] += crecv[0, :, h * half : (h + 1) * half].astype(F32)

        def finish(self, totals):
            self.cross.wait_recv()
            for h in range(2):
                totals[h][...] += yrecv[:, h * half : (h + 1) * half].astype(F32)
            for s in range(2):
                self.to_sibling(s).wait_send()
            self.cross.wait_send()

    class Spread:
        def __init__(self, index, source, land):
            self.cross = remote(source, land.at[mine], gs.at[index, 0], gr.at[index, 0], wires.across())
            self.near = remote(source, land.at[mine], gs.at[index, 1], gr.at[index, 1], wires.sibling())
            there = land.at[across_rows]
            self.far = remote(there, there, gs.at[index, 2], gr.at[index, 2], wires.sibling())
            self.own = pltpu.make_async_copy(source, land.at[mine], gs.at[index, 3])

        def start(self):
            self.cross.start()
            self.near.start()
            self.own.start()

        def pass_on(self):
            self.cross.wait_recv()
            self.far.start()

        def sent(self):
            self.cross.wait_send()
            self.near.wait_send()
            self.own.wait()

        def end(self):
            self.far.wait_recv()
            self.far.wait_send()

    def stream(src_a, src_b, body):
        def copies(r, slot):
            at = tile(r, PART)
            return (
                pltpu.make_async_copy(src_a.at[at], fa.at[slot, pl.ds(0, PART)], fs.at[0, slot]),
                pltpu.make_async_copy(src_b.at[at], fb.at[slot], fs.at[1, slot]),
            )

        for copy in copies(0, 0):
            copy.start()

        @pl.loop(0, length // PART)
        def _(r):
            slot = lax.rem(r, 2)

            @pl.when(r + 1 < length // PART)
            def _():
                for copy in copies(r + 1, 1 - slot):
                    copy.start()

            for copy in copies(r, slot):
                copy.wait()
            body(tile(r, PART), fa.at[slot, pl.ds(0, PART)], fb.at[slot])

    wires.greet_all()
    n = 2 * outer
    hid_load = load(hidden_in, hid, n + 10)
    far_half, near_half = pl.ds(half, half), pl.ds(0, half)
    feed_load = load(feed_in.at[:, far_half], u2.at[:, far_half], n + 2)
    act_load = load(activity_in, act, n + 9)
    cot_loads = own_blocks(cotangent, u0, 0)
    upg_load = load(up_in, upg, n + 11)
    hidden_loads = load_tall(hidden_full, u3, n + 3)
    up_loads = load_tall(up_full, u4, n + 5)
    down_load = load(down_full, u1, n)
    gain_load = load(gains, gain_v, n + 1)
    residual_load = load(residual_in, value_q, n + 7)
    table_load = load(key_decay.at[wires.tensor], keyd, n + 8)
    near_load = load(feed_in.at[:, near_half], u2.at[:, near_half], n + 12)
    hid_load.wait()
    feed_load.wait()
    far(G_HIDDEN, u2, hid)
    act_load.wait()
    wait_all(cot_loads)
    down_first()
    upg_load.wait()
    wait_all(hidden_loads)
    wait_all(up_loads)
    near_load.wait()

    def tall_terms(pairs):
        def terms(at, h):
            cols = slice(h * half, (h + 1) * half)
            total = None
            for left, right in pairs:
                part = back_dot(left[at, :], right[:, cols])
                total = part if total is None else total + part
            return total

        return terms

    feed_terms = tall_terms(((hid, u3), (upg, u4)))
    feed_round, output_round, mixer_round = Round(0), Round(1), Round(2)
    feed_round.give(feed_terms)
    far(G_UP, u2, upg)
    feed_round.hand_over(feed_terms)
    grad_halves = [grad_q.at[:, pl.ds(h * half, half)] for h in range(2)]
    value_halves = [value_q.at[:, pl.ds(h * half, half)] for h in range(2)]
    mixer_halves = [fa.at[h] for h in range(2)]
    feed_round.keep(feed_terms, grad_halves, False)
    table_load.wait()
    gain_load.wait()
    group = jnp.zeros((1, heads * DV), F32)
    for place in range(2 * outer):
        line = gain_v[place * 16 : place * 16 + 1, :].astype(F32)
        gain_m[:, place * block : (place + 1) * block] = line[:, :block]
        gain_f[:, place * block : (place + 1) * block] = line[:, block : 2 * block]
        group = group + line[:, 2 * block :]
    gain_g[...] = group
    vec_t[...] = jnp.zeros_like(vec_t)
    vec_d[...] = jnp.zeros_like(vec_d)
    vec_g[...] = jnp.zeros_like(vec_g)
    mixer_load = load(mixer_in, u3, n + 3)
    narrow = heads * DK
    core_loads = [load(value_in, u4.at[:, pl.ds(0, half)], n + 4),
                  load(query_in, u4.at[:, pl.ds(half, narrow)], n + 5),
                  load(key_in, u4.at[:, pl.ds(half + narrow, narrow)], n + 6)]
    down_give(3)
    residual_load.wait()
    feed_round.finish(grad_halves)

    @pl.loop(0, quarter // 128)
    def _(r):
        at = tile(r, 128)
        part, gain_part = norm_back(value_q[at, :], grad_q[at, :], gain_f[...], norm_epsilon)
        cot_at = pl.ds(pl.multiple_of(wires.tensor * quarter + r * 128, 128), 128)
        total = u0[cot_at, :].astype(F32) + part
        grad_q[at, :] = total
        stage[at, :] = total.astype(BF16)
        vec_t[1:2, :] += jnp.sum(gain_part, axis=0, keepdims=True)

    branch_spread = Spread(0, stage, branch_land)
    branch_spread.start()
    relay(G_DOWN)
    relay(N_GRADS)
    near(G_HIDDEN, u2, hid, (2, 3, 0))

    down_load.wait()

    def output_terms(at, h):
        return jnp.dot(act[at, :], u1[:, h * half : (h + 1) * half], preferred_element_type=F32)

    branch_spread.near.wait_recv()
    output_round.give(output_terms)
    output_round.keep(output_terms, value_halves, True)
    branch_spread.pass_on()
    output_round.hand_over(output_terms)
    branch_spread.sent()
    out_load = load(out_full, u1, n)
    branch_loads = [load(branch_land.at[at], u0.at[at], n + 7 + i) for i, at in
                    enumerate((mine, near_rows, across_rows))]
    mixed_load = load(mixed_in, act, n + 1)
    branch_spread.far.wait_recv()
    branch_loads.append(load(branch_land.at[corner_rows], u0.at[corner_rows], n + 2))
    wait_all(branch_loads)
    out_load.wait()

    hold = both

    def gate_tile(at, r_ref, g_ref):
        grads = back_dot(u0[at, :], u1[...])
        for h in range(heads):
            cols = slice(h * DV, (h + 1) * DV)
            x, g, m = r_ref[:, cols], g_ref[:, cols], grads[:, cols]
            scale = gain_g[:, cols]
            sig = 1.0 / (1.0 + jnp.exp(-g))
            swish = g * sig
            center = x - jnp.mean(x, axis=-1, keepdims=True)
            inverse = lax.rsqrt(jnp.mean(center * center, axis=-1, keepdims=True) + group_epsilon)
            unit = center * inverse
            passed = m * swish
            hid[at, cols] = (m * unit * scale * (sig * (1.0 + g * (1.0 - sig)))).astype(BF16)
            vec_g[:, cols] += jnp.sum(passed * unit, axis=0, keepdims=True)
            u = passed * scale
            mean = jnp.mean(u, axis=-1, keepdims=True)
            slope = jnp.mean(u * unit, axis=-1, keepdims=True)
            hold[at, cols] = ((u - mean - unit * slope) * inverse).astype(BF16)

    mixed_load.wait()
    far(G_OUT, u0, act)
    near(G_HIDDEN, u2, hid, (1,))
    stream(retained_in, gate_in, gate_tile)
    relay(G_HIDDEN)
    mixer_load.wait()
    near(G_UP, u2, upg)
    value_loads = load_tall(value_full, u2, n + 1)
    far(G_GATE, u3, hid)
    wait_all(core_loads)

    side = DK // 2
    turn_load = load(turns, fb, n + 8)
    turn_load.wait()

    def turned_back(grads, r, count):
        a, b = grads[:, :side], grads[:, side:]
        c = jnp.concatenate([fb[0, :, (r + i) * side : (r + i + 1) * side] for i in range(count)], axis=0)
        s = jnp.concatenate([fb[1, :, (r + i) * side : (r + i + 1) * side] for i in range(count)], axis=0)
        return (a * c + b * s).astype(BF16), (b * c - a * s).astype(BF16)

    for h in range(heads):
        vcols = slice(h * DV, (h + 1) * DV)
        qcols = slice(half + h * DK, half + (h + 1) * DK)
        kcols = slice(half + narrow + h * DK, half + narrow + (h + 1) * DK)
        for r in range(length // PART):
            at = slice(r * PART, (r + 1) * PART)
            upto = (r + 1) * PART
            raw = back_dot(u4[at, qcols], u4[:upto, kcols])
            place = lax.broadcasted_iota(jnp.int32, (PART, upto), 0) + r * PART
            under = place >= lax.broadcasted_iota(jnp.int32, (PART, upto), 1)
            fade = keyd[heads + h : heads + h + 1, at].reshape(PART, 1) * keyd[h : h + 1, :upto]
            fade = jnp.where(under, fade, 0.0)
            scores = raw * fade
            total = jnp.sum(scores, axis=-1, keepdims=True)
            inverse = lax.rsqrt(total * total + 1.0)
            u1[at, :upto] = (scores * inverse).astype(BF16)
            grads = back_dot(hold[at, vcols], u4[:upto, vcols])
            inner = jnp.sum(grads * scores, axis=-1, keepdims=True)
            drop = inner * total * inverse * inverse * inverse
            raw_grad = ((grads * inverse - drop) * fade).astype(BF16)
            u1[at, half : half + upto] = raw_grad
            query_grad = jnp.dot(raw_grad, u4[:upto, kcols], preferred_element_type=F32)
            lo, hi = turned_back(query_grad, r, 1)
            upg[at, h * DK : h * DK + side] = lo
            upg[at, h * DK + side : (h + 1) * DK] = hi
        for c in range(rows):
            at = slice(c * STEP, (c + 1) * STEP)
            after = slice(c * STEP, length)
            for i in range(1, STEP // PART):
                spare = slice(c * STEP, c * STEP + i * PART)
                late = slice(c * STEP + i * PART, c * STEP + (i + 1) * PART)
                u1[spare, late] = jnp.zeros((i * PART, PART), BF16)
                u1[spare, half + c * STEP + i * PART : half + c * STEP + (i + 1) * PART] = jnp.zeros(
                    (i * PART, PART), BF16
                )
            hold_grad = rows_dot(u1[after, c * STEP : (c + 1) * STEP], hold[after, vcols])
            key_grad = rows_dot(u1[after, half + c * STEP : half + (c + 1) * STEP], u4[after, qcols])
            hold[at, vcols] = hold_grad.astype(BF16)
            lo, hi = turned_back(key_grad, c * (STEP // PART), STEP // PART)
            upg[at, narrow + h * DK : narrow + h * DK + side] = lo
            upg[at, narrow + h * DK + side : narrow + (h + 1) * DK] = hi

    gate_loads = load_tall(gate_full, u1, n + 3)
    both_loads = []
    for h in range(2):
        source = pl.ds(h * half, half)
        both_loads.append(load(query_full.at[source], u4.at[:, pl.ds(h * half, narrow)], n + 5 + 2 * h))
        both_loads.append(load(key_full.at[source], u4.at[:, pl.ds(h * half + narrow, narrow)], n + 6 + 2 * h))

    down_sum()
    relay(G_UP)

    output_round.finish(value_halves)
    ysend[...] = value_q[...].astype(BF16)
    wait_all(true_blocks(ysend, stage, 0))
    output_spread = Spread(1, stage, output)
    output_spread.start()
    token_loads = []
    for place in range(2 * outer):
        at = pl.multiple_of(wires.block_at(place) * block, block)
        token_loads.append(load(tokens.at[mine, pl.ds(at, block)], ysend.at[:, pl.ds(place * block, block)], place))
    wait_all(token_loads)
    for r in range(2):
        at = slice(r * (quarter // 2), (r + 1) * (quarter // 2))
        value_q[at, :] = ysend[at, :].astype(F32)
    near(G_OUT, u0, act)
    far(G_VALUE, u3, hold)
    wait_all(gate_loads)
    wait_all(both_loads)
    wait_all(value_loads)
    mixer_terms = tall_terms(((upg, u4), (hold, u2), (hid, u1)))
    output_spread.near.wait_recv()
    mixer_round.give(mixer_terms)
    output_spread.pass_on()
    mixer_round.hand_over(mixer_terms)
    mixer_round.keep(mixer_terms, mixer_halves, False)
    relay(G_OUT)
    mixer_round.finish(mixer_halves)
    output_spread.sent()

    @pl.loop(0, quarter // 128)
    def _(r):
        at = tile(r, 128)
        grads = jnp.concatenate([fa[0, at, :], fa[1, at, :]], axis=1)
        part, gain_part = norm_back(value_q[at, :], grads, gain_m[...], norm_epsilon)
        ysend[at, :] = (grad_q[at, :] + part).astype(BF16)
        vec_t[0:1, :] += jnp.sum(gain_part, axis=0, keepdims=True)

    def vector_team(i, device):
        return remote(vec_t, vec_tr.at[i], vs.at[i], vr.at[i], device)

    team = (wires.sibling(), wires.across(), wires.corner())
    for i, device in enumerate(team):
        vector_team(i, device).start()
    wait_all(true_blocks(ysend, stage, 0))
    tokens_spread = Spread(2, stage, tokens_out)
    tokens_spread.start()
    near(G_GATE, u3, hid)
    far(G_BOTH, u3, upg, (2, 3))
    for i, device in enumerate(team):
        vector_team(i, device).wait_recv()
    summed = vec_t[0:2, :]
    for i in range(3):
        summed = summed + vec_tr[i, 0:2, :]
    for place in range(2 * outer):
        vec_d[place, 0:2, :] = summed[:, place * block : (place + 1) * block]
        for i in range(heads * DV // block):
            vec_d[place, 2 + i : 3 + i, :] = vec_g[:, i * block : (i + 1) * block]

    def vector_data(place):
        device = (wires.block_at(place), wires.tensor)
        return remote(vec_d.at[place], vec_dr.at[place], vs.at[3 + place], vr.at[3 + place], device)

    for place in range(1, 2 * outer):
        vector_data(place).start()
    tokens_spread.pass_on()
    relay(G_GATE)
    near(G_VALUE, u3, hold)
    relay(G_VALUE)
    far(G_BOTH, u3, upg, (1, 0), x_copy(G_BOTH, 2))
    x_copy(G_DOWN, 0).start()
    near(G_BOTH, u3, upg, (2, 3))
    near(G_BOTH, u3, upg, (1,))
    relay(G_BOTH)
    near(G_BOTH, u3, upg, (0,))
    vectors = vec_d[0]
    for place in range(1, 2 * outer):
        vector_data(place).wait_recv()
        vectors = vectors + vec_dr[place]
    vec_d[0] = vectors
    vector_store = load(vec_d.at[0], vector_out, 0)

    vector_store.wait()
    branch_spread.far.wait_send()
    output_spread.end()
    tokens_spread.near.wait_recv()
    tokens_spread.end()
    tokens_spread.sent()
    for i, device in enumerate(team):
        vector_team(i, device).wait_send()
    for place in range(1, 2 * outer):
        vector_data(place).wait_send()
    acc_copy(N_GRADS - 1).wait()
    x_copy(G_DOWN, 0).wait()
    for item in (N_GRADS - 2, N_GRADS - 1):
        for s in range(outer):
            if (item, s) != (G_BOTH, 2):
                x_copy(item, s).wait_send()
        for s in range(1, outer):
            z_copy(item, s).wait_send()
    for item in range(N_GRADS):
        for s in (1, outer - 1):
            z_copy(item, s).wait_recv()


def backward_fast(dp_size, tokens, cotangent, fulls, kept, tables):
    outer = dp_size // 2
    length, model = tokens.shape
    block = model // dp_size
    gains, query_full, key_full, value_full, gate_full, out_full, hidden_full, up_full, down_full = fulls
    (mixer_input, turned_query, turned_keys, values, retained, gate_in, mixed, residual, feed_input, hidden_pre,
     up_pre, activity) = kept
    heads = query_full.shape[1] // DK
    units = hidden_full.shape[1]
    quarter = length // 4
    shape = jax.ShapeDtypeStruct
    out_shape = [
        shape((length, model), BF16),
        shape((length, model), BF16),
        shape((N_GRADS, block, units), F32),
        shape((N_GRADS + 1, outer - 1, block, units), BF16),
        shape((8, block), F32),
        shape((N_GRADS, outer, block, units), BF16),
        shape((length, model), BF16),
    ]
    dma = pltpu.SemaphoreType.DMA
    vmem = pltpu.VMEM
    scratch = [vmem((length, model), BF16)] * 5 + [vmem((length, units), BF16)] * 4
    scratch += [vmem((2, STEP, units), F32), vmem((2, PART, units), F32)]
    scratch += [
        vmem((2 * outer, block, units), BF16),
        vmem((block, units), BF16),
        vmem((2 * (outer - 1), block, units), BF16),
        vmem((4, block, units), BF16),
        vmem((block, units), F32),
        vmem((2, quarter, model), BF16),
        vmem((2, quarter, model), BF16),
        vmem((quarter, model), BF16),
        vmem((quarter, model), BF16),
        vmem((quarter, model), BF16),
        vmem((quarter, model), F32),
        vmem((quarter, model), F32),
        vmem(tables[1].shape[1:], F32),
        vmem(gains.shape, BF16),
        vmem((1, model), F32),
        vmem((1, model), F32),
        vmem((1, heads * DV), F32),
        vmem((8, model), F32),
        vmem((3, 8, model), F32),
        vmem((dp_size, 8, block), F32),
        vmem((dp_size, 8, block), F32),
        vmem((1, heads * DV), F32),
        dma((N_GRADS, outer)),
        dma((N_GRADS, outer)),
        dma((N_GRADS + 1, outer)),
        dma((N_GRADS + 1, outer)),
        dma((3, 3)),
        dma((3, 3)),
        dma((3, 4)),
        dma((3, 4)),
        dma((3 + dp_size,)),
        dma((3 + dp_size,)),
        dma((dp_size + 13,)),
        dma((2, 2)),
        dma((N_GRADS + 1, outer)),
        dma((N_GRADS,)),
    ]

    def kernel(*refs):
        backward_kernel(outer, heads, (length, model, block, units), *refs)

    operands = (tokens, cotangent, *fulls, *kept, *tables)
    return pl.pallas_call(
        kernel,
        out_shape=out_shape,
        in_specs=[ANY] * len(operands),
        out_specs=[ANY] * len(out_shape),
        scratch_shapes=scratch,
        compiler_params=pltpu.CompilerParams(
            collective_id=1, has_side_effects=True, vmem_limit_bytes=63 * 1024 * 1024
        ),
    )(*operands)


def finish(near_sums, z_land, x_land, tokens_grad, output):
    steps = 8
    _, block, units = near_sums.shape
    length, model = output.shape
    rows, across = block // steps, block // 128
    side = units * across // steps
    turned = (G_DOWN, G_OUT)
    order = (G_BOTH, G_VALUE, G_GATE, G_OUT, G_HIDDEN, G_UP, G_DOWN)
    operands, in_specs, out_specs, out_shape = [], [], [], []

    def add(array, lead, item):
        operands.append(array)
        if item in turned:
            in_specs.append(pl.BlockSpec((1,) * len(lead) + (128, side), lambda i: (*lead, i % across, i // across)))
        else:
            in_specs.append(pl.BlockSpec((1,) * len(lead) + (rows, units), lambda i: (*lead, i, 0)))

    for item in order:
        add(near_sums, (item,), item)
        add(z_land, (item, 0), item)
        add(z_land, (item, 2), item)
        if item == G_DOWN:
            add(x_land, (item, 0), item)
        if item == G_BOTH:
            shapes = [((block, units // 2), (rows, units // 2))] * 2
        else:
            shapes = [((block, units), (rows, units))]
        for whole, part in shapes:
            if item in turned:
                out_shape.append(jax.ShapeDtypeStruct((units, block), F32))
                out_specs.append(pl.BlockSpec((side, 128), lambda i: (i // across, i % across)))
            else:
                out_shape.append(jax.ShapeDtypeStruct(whole, F32))
                out_specs.append(pl.BlockSpec(part, lambda i: (i, 0)))
    for array, kind in ((tokens_grad, F32), (output, BF16)):
        operands.append(array)
        spec = pl.BlockSpec((length // steps, model), lambda i: (i, 0))
        in_specs.append(spec)
        out_specs.append(spec)
        out_shape.append(jax.ShapeDtypeStruct(array.shape, kind))

    def kernel(*refs):
        ins, outs = list(refs[: len(operands)]), list(refs[len(operands) :])
        for item in order:
            total = ins.pop(0)[0]
            for _ in range(3 if item == G_DOWN else 2):
                total = total + ins.pop(0)[0, 0].astype(F32)
            if item == G_BOTH:
                outs.pop(0)[...] = total[:, : units // 2]
                outs.pop(0)[...] = total[:, units // 2 :]
            else:
                outs.pop(0)[...] = total.T if item in turned else total
        for source, target in zip(ins, outs):
            target[...] = source[...].astype(target.dtype)

    return pl.pallas_call(
        kernel,
        grid=(steps,),
        out_shape=out_shape,
        in_specs=in_specs,
        out_specs=out_specs,
        compiler_params=pltpu.CompilerParams(vmem_limit_bytes=62 * 1024 * 1024),
    )(*operands)


def on_device(
    dp_size,
    tensor_size,
    tokens,
    mixer_gain,
    query_weight,
    key_weight,
    value_weight,
    gate_weight,
    out_weight,
    group_gain,
    feed_gain,
    hidden_weight,
    up_weight,
    down_weight,
    cotangent,
):
    data = Ring("dp", dp_size)
    team = Ring("tensor", tensor_size)
    length, model = tokens.shape
    quarter = length // tensor_size
    heads_here = query_weight.shape[1] // DK

    block = mixer_gain.shape[0]
    width = query_weight.shape[1]
    group_block = group_gain.shape[1]
    head_ids = (lax.axis_index("tensor") * heads_here + jnp.arange(heads_here)).astype(F32)
    decays = decay_table(head_ids, length)
    inputs = data.own_order(tokens, 1)
    cot = data.own_order(cotangent, 1)

    def my_rows(array):
        return lax.dynamic_slice_in_dim(array, team.me * quarter, quarter, 0)

    def row_terms(left, right):
        return lambda start, rows: plain_product(
            lax.dynamic_slice_in_dim(left, start, rows, 0), right
        )

    units = hidden_weight.shape[1]
    even = units == 2 * width == heads_here * DV == model // 2 and heads_here * DV // block <= 6 and heads_here <= 4
    if even and block % 128 == 0 and tensor_size == 4 and dp_size == 8 and length % 1024 == 0:
        group_line = lax.dynamic_update_slice(
            jnp.zeros((heads_here, DV), BF16), group_gain, (0, data.me * group_block)
        )
        gains = jnp.concatenate([mixer_gain, feed_gain, group_line.reshape(-1)])
        gains = jnp.broadcast_to(gains[None, :], (16, gains.shape[0]))
        cosine, sine, turns, fades = position_tables(length, tensor_size, heads_here)
        tables = (cosine, sine, fades)
        back_tables = (turns, fades)
        fulls, kept = forward_fast(
            dp_size,
            tokens,
            cotangent,
            gains,
            tables,
            (query_weight, key_weight, value_weight, gate_weight, out_weight, hidden_weight, up_weight, down_weight),
        )
        output, tokens_grad, near_sums, landed, vectors, crossed, _ = backward_fast(
            dp_size, tokens, cotangent, fulls, kept, back_tables
        )
        (query_grad, key_grad, value_grad, gate_grad, out_grad, hidden_grad, up_grad, down_grad, tokens_grad,
         output) = finish(near_sums, landed, crossed, tokens_grad, output)
        group_scale_grad = vectors[2 : 2 + heads_here * DV // block].reshape(heads_here, DV)
        return (
            output,
            tokens_grad,
            vectors[0],
            query_grad,
            key_grad,
            value_grad,
            gate_grad,
            out_grad,
            lax.dynamic_slice_in_dim(group_scale_grad, data.me * group_block, group_block, 1),
            vectors[1],
            hidden_grad,
            up_grad,
            down_grad,
        )
    else:
        gains = jnp.concatenate([mixer_gain, feed_gain, group_gain.reshape(-1)])[None, :]
        gains = data.gather(gains, 0)
        mixer_scale = gains[:, :block].reshape(-1).astype(F32)
        feed_scale = gains[:, block : 2 * block].reshape(-1).astype(F32)
        group_scale = data.true_order(gains[:, 2 * block :], 0).astype(F32)
        group_scale = group_scale.reshape(dp_size, heads_here, -1).swapaxes(0, 1).reshape(heads_here, -1)

        query_key = data.gather(jnp.concatenate([query_weight, key_weight], axis=1), 0)
        value_full = data.gather(value_weight, 0)
        gate_full = data.gather(gate_weight, 0)
        out_full = data.gather(out_weight, 1)
        hidden_full = data.gather(hidden_weight, 0)
        up_full = data.gather(up_weight, 0)
        down_full = data.gather(down_weight, 1)

        mixer_input = layer_norm(inputs.astype(F32), mixer_scale).astype(BF16)

        both = plain_product(mixer_input, query_key)
        query = both[:, :width]
        keyset = both[:, width:]
        values = plain_product(mixer_input, value_full).astype(BF16)
        gate_in = plain_product(mixer_input, gate_full)
        turned_query = rotate(query, heads_here, 1.0).astype(BF16).reshape(length, heads_here, DK)
        turned_keys = rotate(keyset, heads_here, 1.0).astype(BF16).reshape(length, heads_here, DK)
        scores, row_totals, denominators = core_scores(turned_query, turned_keys, decays)
        weights = (scores / denominators).astype(BF16)
        value_heads = values.reshape(length, heads_here, DV)
        retained = jnp.einsum("hqk,khd->qhd", weights, value_heads, preferred_element_type=F32)
        retained = retained.reshape(length, heads_here * DV)
        mixed = gate_piece(retained, gate_in, group_scale).astype(BF16)

        branch = token_sum(team, row_terms(mixed, out_full), length)
        residual = my_rows(inputs).astype(F32) + branch
        feed_input = token_gather(team, layer_norm(residual, feed_scale).astype(BF16))
        hidden_pre = plain_product(feed_input, hidden_full)
        up_pre = plain_product(feed_input, up_full)

    activity, feed_back = jax.vjp(feed_piece, hidden_pre, up_pre)
    activity = activity.astype(BF16)
    activity_grad = back_product(cot, down_full)
    hidden_grad, up_grad = feed_back(activity_grad)
    hidden_grad = hidden_grad.astype(BF16)
    up_grad = up_grad.astype(BF16)

    def feed_rows(start, rows):
        return back_product(
            lax.dynamic_slice_in_dim(hidden_grad, start, rows, 0), hidden_full
        ) + back_product(lax.dynamic_slice_in_dim(up_grad, start, rows, 0), up_full)

    feed_input_grad = token_sum(team, feed_rows, length)
    _, feed_norm_back = jax.vjp(layer_norm, residual, feed_scale)
    residual_part, feed_scale_grad = feed_norm_back(feed_input_grad)
    residual_grad = my_rows(cot).astype(F32) + residual_part
    branch_grad = token_gather(team, residual_grad.astype(BF16))

    hidden_weight_grad = data.scatter_sum(
        lambda turn: row_product(half_of(feed_input, turn, 1), hidden_grad), 0
    )
    up_weight_grad = data.scatter_sum(
        lambda turn: row_product(half_of(feed_input, turn, 1), up_grad), 0
    )
    down_grad = data.scatter_sum(lambda turn: row_product(activity, half_of(cot, turn, 1)), 1)

    feed_out = token_sum(team, row_terms(activity, down_full), length)
    output = token_gather(team, (residual + feed_out).astype(BF16))
    output = data.true_order(output, 1)

    mixed_grad = back_product(branch_grad, out_full)
    _, gate_back = jax.vjp(gate_piece, retained, gate_in, group_scale)
    retained_grad, gate_grad, group_scale_grad = gate_back(mixed_grad)
    retained_grad = retained_grad.astype(BF16)
    gate_grad = gate_grad.astype(BF16)
    out_weight_grad = data.scatter_sum(
        lambda turn: row_product(mixed, half_of(branch_grad, turn, 1)), 1
    )
    gate_weight_grad = data.scatter_sum(
        lambda turn: row_product(half_of(mixer_input, turn, 1), gate_grad), 0
    )

    grad_heads = retained_grad.reshape(length, heads_here, DV)
    weights_grad = jnp.einsum("qhd,khd->hqk", grad_heads, value_heads, preferred_element_type=F32)
    value_parts = jnp.einsum("hqk,qhd->khd", weights, grad_heads, preferred_element_type=F32)
    value_parts = value_parts.reshape(length, heads_here * DV).astype(BF16)
    value_weight_grad = data.scatter_sum(
        lambda turn: row_product(half_of(mixer_input, turn, 1), value_parts), 0
    )
    inner_totals = jnp.sum(weights_grad * scores, axis=-1, keepdims=True)
    slope = row_totals / denominators
    scores_grad = weights_grad / denominators - inner_totals / (denominators * denominators) * slope
    raw_grad = (scores_grad * DK ** (-0.5) * decays).astype(BF16)
    turned_query_grad = jnp.einsum("hqk,khd->qhd", raw_grad, turned_keys, preferred_element_type=F32)
    turned_key_grad = jnp.einsum("hqk,qhd->khd", raw_grad, turned_query, preferred_element_type=F32)
    query_parts = rotate(turned_query_grad.reshape(length, width), heads_here, -1.0).astype(BF16)
    key_parts = rotate(turned_key_grad.reshape(length, width), heads_here, -1.0).astype(BF16)
    both_parts = jnp.concatenate([query_parts, key_parts], axis=1)
    both_grad = data.scatter_sum(
        lambda turn: row_product(half_of(mixer_input, turn, 1), both_parts), 0
    )
    query_weight_grad = both_grad[:, :width]
    key_weight_grad = both_grad[:, width:]

    def mixer_rows(start, rows):
        def cut(array):
            return lax.dynamic_slice_in_dim(array, start, rows, 0)

        return (
            back_product(cut(both_parts), query_key)
            + back_product(cut(value_parts), value_full)
            + back_product(cut(gate_grad), gate_full)
        )

    mixer_input_grad = token_sum(team, mixer_rows, length)
    _, mixer_norm_back = jax.vjp(layer_norm, my_rows(inputs).astype(F32), mixer_scale)
    input_part, mixer_scale_grad = mixer_norm_back(mixer_input_grad)
    tokens_grad = token_gather(team, (residual_grad + input_part).astype(BF16))
    tokens_grad = data.true_order(tokens_grad, 1).astype(F32)

    norm_grads = jnp.concatenate([mixer_scale_grad, feed_scale_grad]).reshape(2, -1)
    norm_grads = lax.psum(data.true_order(norm_grads, 1), ("dp", "tensor"))
    norm_grads = lax.dynamic_slice_in_dim(norm_grads, data.me * block, block, 1)
    group_scale_grad = lax.psum(group_scale_grad, "dp")
    group_scale_grad = lax.dynamic_slice_in_dim(group_scale_grad, data.me * group_block, group_block, 1)
    return (
        output,
        tokens_grad,
        norm_grads[0],
        query_weight_grad,
        key_weight_grad,
        value_weight_grad,
        gate_weight_grad,
        out_weight_grad,
        group_scale_grad,
        norm_grads[1],
        hidden_weight_grad,
        up_weight_grad,
        down_grad,
    )


def solution(mesh):
    columns = P("dp", "tensor")
    rows = P("tensor", "dp")
    placed = (
        P("dp", None),
        P("dp"),
        columns,
        columns,
        columns,
        columns,
        rows,
        rows,
        P("dp"),
        columns,
        columns,
        rows,
        P("dp", None),
    )
    given = (
        P("dp", None),
        P("dp", None),
        P("dp"),
        columns,
        columns,
        columns,
        columns,
        rows,
        rows,
        P("dp"),
        columns,
        columns,
        rows,
    )

    def body(*arrays):
        return on_device(mesh.shape["dp"], mesh.shape["tensor"], *arrays)

    return jax.shard_map(body, mesh=mesh, in_specs=placed, out_specs=given, check_vma=False)
```
